32 devices in a mesh: grp: 2 (over x), seq: 16 (over z, y, core).
Axes of the slice: x: 2, y: 2, z: 4, core: 2. Of those that a mesh axis runs over, the one named last changes fastest.
Arguments:
- normed_token_features: bfloat16 [4, 1024, 5120], P('grp', 'seq'), parts along dimension 0, may hold values from -6 to 6
- queries: bfloat16 [4, 32, 1024, 128], P('grp', None, 'seq'), parts along dimension 0, may hold values from -8 to 8
- projected_keys: bfloat16 [4, 32, 1024, 128], P('grp', None, 'seq'), parts along dimension 0, may hold values from -8 to 8
- values: bfloat16 [4, 32, 1024, 128], P('grp', None, 'seq'), parts along dimension 0, may hold values from -6 to 6
- adapter_down_factors: bfloat16 [64, 64, 5120], P('seq'), may hold values from -0.078125 to 0.078125
- adapter_up_factors: bfloat16 [64, 64, 4096], P('seq'), may hold values from -1 to 1
- adapter_store_row: int32 [64], replicated, may hold values from 0 to 63, each once
- requests: int32 [4], P('grp'), parts along dimension 0, may hold values from 0 to 63
Outputs:
- attended: bfloat16 [4, 32, 1024, 128], P('grp', None, 'seq'), parts along dimension 0
The draws below stay inside these ranges and needn't reach their ends.
There are 2 independent parts, one for each index of `grp`. The reference program is written for one: setup_inputs(seed, part) draws one part's arguments, and reference() takes and returns one part's arrays. A program takes and returns all parts, laid end to end along the dimension named above; an argument that names none is the same for every part. Nothing has to cross between parts.
Inputs may be any that keep to these rules, and one draw needn't show every extreme that they name: Adapter a's factors are row adapter_store_row[a] of the store, which device adapter_store_row[a] // 4 of seq holds. `requests`: several videos may request the same adapter.
All inputs are finite; a program needn't handle non-finite values.
Results may differ from the reference program's by a relative error of at most 0.0088.
Values may be sent and summed in bfloat16 or wider, within the bound.
No kernel may reach another device: no remote copies, remote signals or barrier semaphores. Data moves between devices by JAX's collectives and lax.ppermute only.
A program may use at most 64 MiB of HBM per device.

```python
import math
import jax
import jax.numpy as jnp
import numpy as np
from jax import lax

MODEL_SIZE = 5120
HEADS = 32
HEAD_DIM = 128
ADAPTER_RANK = 32
SEQS = 2
QUERY_WIDTH = 4096
LEN = 1024
ADAPTER_TOTAL = 64


def draw_queries(key, part):
    key = jax.random.fold_in(key, 5)
    array_extent = (SEQS, HEADS, LEN, HEAD_DIM)
    base = jnp.clip(jax.random.normal(key, array_extent, jnp.float32), -6.0, 6.0)
    return base.astype(jnp.bfloat16)


def draw_projected_keys(key, part):
    key = jax.random.fold_in(key, 9)
    array_extent = (SEQS, HEADS, LEN, HEAD_DIM)
    base = jnp.clip(jax.random.normal(key, array_extent, jnp.float32), -6.0, 6.0)
    return base.astype(jnp.bfloat16)


def shard_levels(rng, extent, cuts, low, top_value):
    level = 1.0
    for dim, parts in cuts:
        draws = jax.random.uniform(jax.random.fold_in(jax.random.fold_in(rng, 6), dim), (parts,), jnp.float32, low / len(cuts), top_value / len(cuts))
        level = level * jnp.repeat(jnp.exp(draws), extent[dim] // parts).reshape((-1,) + (1,) * (len(extent) - 1 - dim))
    return level


def rank_bounds(amount, slope):
    loads = [(1 << 20) // math.isqrt(rank ** slope) + 1 for rank in range(1, amount + 1)]
    deviation = 1 + sum(loads) // (1 << 30)
    return np.cumsum(np.array([max(1, weight // deviation) for weight in loads]))


def ranked(stream_key, shape, amount, lean):
    grid = rank_bounds(amount, lean)
    ticket = jax.random.randint(jax.random.fold_in(stream_key, 1), shape, 0, int(grid[amount - 1]))
    rank = jnp.searchsorted(jnp.asarray(grid, jnp.int32), ticket, side="right")
    return jax.random.permutation(jax.random.fold_in(stream_key, 2), amount)[rank].astype(jnp.int32)


def centred(stream_key, shape, deviation, reach, cuts=(), dtype=jnp.bfloat16):
    entries = jax.random.normal(stream_key, shape, jnp.float32) * deviation
    if len(cuts) > 0:
        entries = shard_levels(stream_key, shape, cuts, -0.22, 0.18) * entries
    return jnp.clip(entries, min=-reach, max=reach).astype(dtype)


def setup_inputs(seed: int = 0, part: int = 0) -> dict:
    streams_of = jax.random.split(jax.random.key(seed), 9)
    part_keys = jax.random.split(jax.random.fold_in(streams_of[8], part), 9)
    normed_token_features = centred(part_keys[0], (SEQS, LEN, MODEL_SIZE), 1.0, 6.0, ((1, 16),))
    queries = draw_queries(jax.random.fold_in(jax.random.fold_in(streams_of[8], part), 71), part)
    projected_keys = draw_projected_keys(jax.random.fold_in(jax.random.fold_in(streams_of[8], part), 71), part)
    values = centred(part_keys[3], (SEQS, HEADS, LEN, HEAD_DIM), 1.0, 6.0, ((2, 16),))
    adapter_down_factors = centred(streams_of[4], (ADAPTER_TOTAL, 2 * ADAPTER_RANK, MODEL_SIZE), MODEL_SIZE ** -0.5, 0.078125, ((0, 16),))
    adapter_up_factors = centred(streams_of[5], (ADAPTER_TOTAL, 2 * ADAPTER_RANK, QUERY_WIDTH), ADAPTER_RANK ** -0.5, 1.0, ((0, 16),))
    adapter_store_row = jax.random.permutation(streams_of[6], ADAPTER_TOTAL).astype(jnp.int32)
    requests = ranked(part_keys[7], (SEQS,), ADAPTER_TOTAL, 2)
    return {"normed_token_features": normed_token_features, "queries": queries, "projected_keys": projected_keys, "values": values, "adapter_down_factors": adapter_down_factors, "adapter_up_factors": adapter_up_factors, "adapter_store_row": adapter_store_row, "requests": requests}


def attend_pair(triple):
    q, k, v = triple
    scores = jnp.dot(q, k.T, preferred_element_type=jnp.float32) / math.sqrt(HEAD_DIM)
    row_max = lax.optimization_barrier(jnp.max(scores, axis=1, keepdims=True))
    weights = jnp.exp(scores - row_max)
    weights = (weights / lax.optimization_barrier(jnp.sum(weights, axis=1, keepdims=True))).astype(jnp.bfloat16)
    return jnp.dot(weights, v, preferred_element_type=jnp.float32).astype(jnp.bfloat16)

def to_heads(tensor):
    return tensor.reshape(SEQS, LEN, HEADS, HEAD_DIM).transpose(0, 2, 1, 3)

def reference(normed_token_features, queries, projected_keys, values, adapter_down_factors, adapter_up_factors, adapter_store_row, requests):
    token_position = adapter_store_row[requests]
    selected_down = adapter_down_factors[token_position].astype(jnp.float32)
    selected_up = adapter_up_factors[token_position].astype(jnp.float32)
    reduced_activation = jnp.einsum('fiz,fpz->fip', normed_token_features.astype(jnp.float32), selected_down).astype(jnp.bfloat16)
    low_wide = reduced_activation.astype(jnp.float32)
    delta_q = jnp.einsum('slr,srw->slw', low_wide[:, :, :ADAPTER_RANK], selected_up[:, :ADAPTER_RANK])
    delta_v = jnp.einsum('slr,srw->slw', low_wide[:, :, ADAPTER_RANK:], selected_up[:, ADAPTER_RANK:])
    query_mix = (queries.astype(jnp.float32) + to_heads(delta_q)).astype(jnp.bfloat16)
    value_mix = (values.astype(jnp.float32) + to_heads(delta_v)).astype(jnp.bfloat16)

    def flatten(tensor):
        return tensor.reshape(SEQS * HEADS, LEN, HEAD_DIM)
    attended = lax.map(attend_pair, (flatten(query_mix), flatten(projected_keys), flatten(value_mix)))
    return attended.reshape(SEQS, HEADS, LEN, HEAD_DIM)
```

```python
import functools
import math

import jax
import jax.numpy as jnp
from jax import lax
from jax.experimental import pallas as pl
from jax.experimental.pallas import tpu as pltpu
from jax.sharding import PartitionSpec as P

LANES = 128
CHUNKS = 2


def bit_count(n):
    bits = n.bit_length() - 1
    assert 1 << bits == n
    return bits


def reversed_bits(j, bits):
    out = 0
    for i in range(bits):
        out = out | (((j >> i) & 1) << (bits - 1 - i))
    return out


def pick_kernel(tiles, rows, heads, info, down_ref, up_ref, out_ref, *, dest, per_video, videos):
    video = dest(pl.program_id(0), info) // per_video
    owned = info[1 + videos + video] == 1

    @pl.when(owned)
    def _():
        for t in range(tiles):
            out_ref[0, t * rows : (t + 1) * rows, :] = down_ref[0, :, t * LANES : (t + 1) * LANES]
        base = tiles * rows
        ranks = up_ref.shape[1]
        for h in range(heads):
            out_ref[0, base + h * ranks : base + (h + 1) * ranks, :] = up_ref[
                0, :, h * LANES : (h + 1) * LANES
            ]

    @pl.when(jnp.logical_not(owned))
    def _():
        out_ref[...] = jnp.zeros_like(out_ref)


def low_rank_kernel(tiles, rows, col_split, per_video, bits, me_ref, x_ref, g_ref, out_ref, down):
    videos = x_ref.shape[0]
    for j in range(g_ref.shape[0]):
        dev = me_ref[0] ^ reversed_bits(j, bits)
        video = dev // per_video
        place = dev % per_video
        row = pl.multiple_of((place // col_split) * rows, rows)
        for t in range(tiles):
            col = pl.multiple_of(((place % col_split) * tiles + t) * LANES, LANES)
            down[video, pl.ds(row, rows), pl.ds(col, LANES)] = g_ref[j, t * rows : (t + 1) * rows, :]
    parts = [
        lax.dot_general(
            x_ref[s], down[s], (((1,), (1,)), ((), ())), preferred_element_type=jnp.float32
        )
        for s in range(videos)
    ]
    out_ref[...] = jnp.concatenate(parts, axis=1).astype(out_ref.dtype)


def attend_kernel(per_video, block_rows, me_ref, q_ref, k_ref, v_ref, low_ref, up_ref, out_ref, q_mix):
    devs, _, toks, width = q_ref.shape
    length = devs * toks
    ranks = up_ref.shape[0]
    videos = low_ref.shape[2] // ranks
    video = me_ref[0] // per_video
    up = jnp.concatenate([up_ref[...]] * videos, axis=0)
    row = lax.broadcasted_iota(jnp.int32, up.shape, 0)
    here = (row // ranks) == video
    for_q = (row % ranks) < (ranks // 2)
    zero = jnp.zeros_like(up)
    up_q = jnp.where(here & for_q, up, zero)
    up_v = jnp.where(here & jnp.logical_not(for_q), up, zero)
    low = low_ref[...].reshape(length, low_ref.shape[2])
    keys = k_ref[...].reshape(length, width)
    delta_v = jnp.dot(low, up_v, preferred_element_type=jnp.float32)
    vals = (v_ref[...].reshape(length, width).astype(jnp.float32) + delta_v).astype(jnp.bfloat16)
    delta_q = jnp.dot(low, up_q, preferred_element_type=jnp.float32)
    q_mix[...] = (q_ref[...].reshape(length, width).astype(jnp.float32) + delta_q).astype(
        jnp.bfloat16
    )
    scale = math.log2(math.e) / math.sqrt(width)
    devs_block = block_rows // toks
    for b in range(length // block_rows):
        q = q_mix[b * block_rows : (b + 1) * block_rows, :]
        scores = lax.dot_general(
            q, keys, (((1,), (1,)), ((), ())), preferred_element_type=jnp.float32
        )
        top = jnp.max(scores, axis=1, keepdims=True)
        weights = jnp.exp2((scores - top) * scale)
        total = jnp.sum(weights, axis=1, keepdims=True)
        mixed = jnp.dot(weights.astype(jnp.bfloat16), vals, preferred_element_type=jnp.float32)
        out = (mixed / total).astype(out_ref.dtype)
        out_ref[b * devs_block : (b + 1) * devs_block] = out.reshape(devs_block, 1, toks, width)


def body(
    normed_token_features,
    queries,
    projected_keys,
    values,
    adapter_down_factors,
    adapter_up_factors,
    adapter_store_row,
    requests,
):
    videos, toks, model_width = normed_token_features.shape
    heads = queries.shape[1]
    width = queries.shape[3]
    slots, ranks, _ = adapter_down_factors.shape
    devs = lax.axis_size("seq")
    bits = bit_count(devs)
    me = lax.axis_index("seq").astype(jnp.int32)
    pairs = videos * heads // devs
    per_video = devs // videos
    length = devs * toks
    chunks = math.gcd(pairs, CHUNKS)
    in_chunk = pairs // chunks

    def by_pairs(tensor):
        return tensor.reshape(devs, pairs, toks, width)

    sources = [by_pairs(t) for t in (queries, projected_keys, values)]
    arrived = []
    for c in range(chunks):
        packed = jnp.concatenate(
            [t[:, c * in_chunk : (c + 1) * in_chunk] for t in sources], axis=1
        )
        arrived.append(lax.all_to_all(packed, "seq", split_axis=0, concat_axis=0, tiled=True))

    col_split = math.gcd(per_video, model_width // LANES)
    row_split = per_video // col_split
    rows = ranks // row_split
    tiles = model_width // col_split // LANES
    down_rows = tiles * rows
    all_rows = down_rows + pairs * ranks

    store_row = adapter_store_row[requests]
    owned = (store_row // slots == me).astype(jnp.int32)
    info = jnp.concatenate([me[None], store_row % slots, owned]).astype(jnp.int32)

    def dest(j, info_ref):
        return info_ref[0] ^ reversed_bits(j, bits)

    def down_block(j, info_ref):
        dev = dest(j, info_ref)
        video = dev // per_video
        place = dev % per_video
        mine = info_ref[1 + videos + video]
        return (
            info_ref[1 + video] * mine,
            (place // col_split) * mine,
            (place % col_split) * mine,
        )

    def up_block(j, info_ref):
        dev = dest(j, info_ref)
        video = dev // per_video
        mine = info_ref[1 + videos + video]
        return (info_ref[1 + video] * mine, 0, (dev % per_video) * mine)

    picked = pl.pallas_call(
        functools.partial(
            pick_kernel, tiles, rows, pairs, dest=dest, per_video=per_video, videos=videos
        ),
        grid_spec=pltpu.PrefetchScalarGridSpec(
            num_scalar_prefetch=1,
            grid=(devs,),
            in_specs=[
                pl.BlockSpec((1, rows, tiles * LANES), down_block),
                pl.BlockSpec((1, ranks, pairs * LANES), up_block),
            ],
            out_specs=pl.BlockSpec((1, all_rows, LANES), lambda j, info_ref: (j, 0, 0)),
        ),
        out_shape=jax.ShapeDtypeStruct((devs, all_rows, LANES), jnp.bfloat16),
        cost_estimate=pl.CostEstimate(
            flops=0, bytes_accessed=devs * all_rows * LANES * 4, transcendentals=0
        ),
        name="pick_factors",
    )(info, adapter_down_factors, adapter_up_factors)

    def swap(tensor, bit):
        return lax.ppermute(tensor, "seq", [(i, i ^ (1 << bit)) for i in range(devs)])

    held = picked
    for bit in range(bits):
        half = held.shape[0] // 2
        held = held[:half] + swap(held[half:], bit)
    up_here = held[0, down_rows:].reshape(pairs, ranks, LANES)
    gathered = held[:, :down_rows]
    for bit in reversed(range(bits)):
        gathered = jnp.concatenate([gathered, swap(gathered, bit)], axis=0)

    low = pl.pallas_call(
        functools.partial(low_rank_kernel, tiles, rows, col_split, per_video, bits),
        grid_spec=pltpu.PrefetchScalarGridSpec(
            num_scalar_prefetch=1,
            grid=(1,),
            in_specs=[
                pl.BlockSpec((videos, toks, model_width), lambda i, m: (0, 0, 0)),
                pl.BlockSpec((devs, down_rows, LANES), lambda i, m: (0, 0, 0)),
            ],
            out_specs=pl.BlockSpec((toks, videos * ranks), lambda i, m: (0, 0)),
            scratch_shapes=[pltpu.VMEM((videos, ranks, model_width), jnp.bfloat16)],
        ),
        out_shape=jax.ShapeDtypeStruct((toks, videos * ranks), jnp.bfloat16),
        compiler_params=pltpu.CompilerParams(vmem_limit_bytes=24 << 20),
        cost_estimate=pl.CostEstimate(
            flops=2 * videos * toks * ranks * model_width,
            bytes_accessed=2 * videos * (toks + ranks) * model_width,
            transcendentals=0,
        ),
        name="low_rank",
    )(me[None], normed_token_features, gathered)
    low_all = lax.all_gather(low, "seq", axis=0)

    block_rows = math.gcd(length, 512)

    def attend(packed, up):
        count = packed.shape[1] // 3

        def part(which):
            return pl.BlockSpec(
                (devs, 1, toks, width), lambda p, m, w=which: (0, w * count + p, 0, 0)
            )

        return pl.pallas_call(
            functools.partial(attend_kernel, per_video, block_rows),
            grid_spec=pltpu.PrefetchScalarGridSpec(
                num_scalar_prefetch=1,
                grid=(count,),
                in_specs=[
                    part(0),
                    part(1),
                    part(2),
                    pl.BlockSpec((devs, toks, videos * ranks), lambda p, m: (0, 0, 0)),
                    pl.BlockSpec((pl.squeezed, ranks, LANES), lambda p, m: (p, 0, 0)),
                ],
                out_specs=pl.BlockSpec((devs, 1, toks, width), lambda p, m: (0, p, 0, 0)),
                scratch_shapes=[pltpu.VMEM((length, width), jnp.bfloat16)],
            ),
            out_shape=jax.ShapeDtypeStruct((devs, count, toks, width), jnp.bfloat16),
            compiler_params=pltpu.CompilerParams(vmem_limit_bytes=40 << 20),
            cost_estimate=pl.CostEstimate(
                flops=4 * count * length * length * width,
                bytes_accessed=8 * count * length * width,
                transcendentals=count * length * length,
            ),
            name="attend",
        )(me[None], packed, packed, packed, low_all, up)

    returned = []
    for c in range(chunks):
        mixed = attend(arrived[c], up_here[c * in_chunk : (c + 1) * in_chunk])
        returned.append(lax.all_to_all(mixed, "seq", split_axis=0, concat_axis=0, tiled=True))
    out = jnp.concatenate(returned, axis=1) if chunks > 1 else returned[0]
    return out.reshape(videos, heads, toks, width)


def solution(mesh):
    in_specs = (
        P("grp", "seq", None),
        P("grp", None, "seq", None),
        P("grp", None, "seq", None),
        P("grp", None, "seq", None),
        P("seq", None, None),
        P("seq", None, None),
        P(),
        P("grp"),
    )
    out_specs = P("grp", None, "seq", None)
    return jax.shard_map(body, mesh=mesh, in_specs=in_specs, out_specs=out_specs, check_vma=False)
```

```python
import functools
import math

import jax
import jax.numpy as jnp
from jax import lax
from jax.experimental import pallas as pl
from jax.experimental.pallas import tpu as pltpu
from jax.sharding import PartitionSpec as P

LANES = 128
LOW = 4
ANY = pl.BlockSpec(memory_space=pl.ANY)
VMEM = pl.BlockSpec(memory_space=pltpu.VMEM)
SMEM = pl.BlockSpec(memory_space=pltpu.SMEM)


def bit_count(n):
    bits = n.bit_length() - 1
    assert 1 << bits == n
    return bits


def reversed_bits(j, bits):
    out = 0
    for i in range(bits):
        out = out | (((j >> i) & 1) << (bits - 1 - i))
    return out


def after(arrays, *others):
    return lax.optimization_barrier((tuple(arrays), others))[0]


def run_copies(copies):
    for copy in copies:
        copy.start()
    for copy in copies:
        copy.wait()


def pack_kernel(devs, pairs, me_ref, q_ref, k_ref, v_ref, *refs):
    outs, sems = refs[:-1], refs[-1]
    copies = []
    for k in range(devs):
        first = (me_ref[0] ^ k) * pairs
        for i, (src, dst) in enumerate(
            ((k_ref, outs[k].at[0]), (v_ref, outs[k].at[1]), (q_ref, outs[devs + k]))
        ):
            copies.append(
                pltpu.make_async_copy(src.at[pl.ds(first, pairs)], dst, sems.at[3 * k + i])
            )
    run_copies(copies)


def unpack_kernel(devs, pairs, me_ref, *refs):
    ins, out, sems = refs[:devs], refs[devs], refs[devs + 1]
    run_copies(
        [
            pltpu.make_async_copy(
                ins[k], out.at[pl.ds((me_ref[0] ^ k) * pairs, pairs)], sems.at[k]
            )
            for k in range(devs)
        ]
    )


def pick_kernel(
    shape, me_ref, row_ref, req_ref, down_ref, up_ref, *refs
):
    devs, bits, per_video, pairs, col_split, rows, tiles = shape
    downs, ups = refs[: bits + 1], refs[bits + 1 : 2 * bits + 2]
    down, up, sems = refs[2 * bits + 2 :]
    slots, ranks, _ = down_ref.shape
    videos = down.shape[0]
    me = me_ref[0]
    for s in range(videos):
        place = row_ref[req_ref[s]]
        slot = place % slots
        owned = place // slots == me
        copies = [
            pltpu.make_async_copy(down_ref.at[slot], down.at[s], sems.at[2 * s]),
            pltpu.make_async_copy(up_ref.at[slot], up.at[s], sems.at[2 * s + 1]),
        ]

        @pl.when(owned)
        def _():
            run_copies(copies)

        @pl.when(jnp.logical_not(owned))
        def _():
            down[s] = jnp.zeros(down.shape[1:], down.dtype)
            up[s] = jnp.zeros(up.shape[1:], up.dtype)

    for j in range(devs):
        step = bits - j.bit_length()
        at = j - (1 << (j.bit_length() - 1)) if j else 0
        dev = me ^ reversed_bits(j, bits)
        video = dev // per_video
        place = dev % per_video
        row = pl.multiple_of((place // col_split) * rows, rows)
        for t in range(tiles):
            col = pl.multiple_of(((place % col_split) * tiles + t) * LANES, LANES)
            downs[step][at, t * rows : (t + 1) * rows, :] = down[
                video, pl.ds(row, rows), pl.ds(col, LANES)
            ]
        for p in range(pairs):
            col = pl.multiple_of((place * pairs + p) * LANES, LANES)
            ups[step][at, p * ranks : (p + 1) * ranks, :] = up[video, :, pl.ds(col, LANES)]


def low_rank_kernel(shape, me_ref, x_ref, g_ref, out_ref, down):
    devs, bits, per_video, _, col_split, rows, tiles = shape
    for j in range(devs):
        dev = me_ref[0] ^ reversed_bits(j, bits)
        video = dev // per_video
        place = dev % per_video
        row = pl.multiple_of((place // col_split) * rows, rows)
        for t in range(tiles):
            col = pl.multiple_of(((place % col_split) * tiles + t) * LANES, LANES)
            down[video, pl.ds(row, rows), pl.ds(col, LANES)] = g_ref[j, t * rows : (t + 1) * rows, :]
    parts = [
        lax.dot_general(
            x_ref[s], down[s], (((1,), (1,)), ((), ())), preferred_element_type=jnp.float32
        )
        for s in range(x_ref.shape[0])
    ]
    out_ref[...] = jnp.concatenate(parts, axis=1).astype(out_ref.dtype)


def up_part(up_ref, video, videos, second):
    up = jnp.concatenate([up_ref[...]] * videos, axis=0)
    ranks = up_ref.shape[0]
    row = lax.broadcasted_iota(jnp.int32, up.shape, 0)
    half = (row % ranks) // (ranks // 2)
    keep = (row // ranks == video) & (half == second)
    return jnp.where(keep, up, jnp.zeros_like(up))


def low_rows(low_refs, ks):
    return jnp.concatenate([low_refs[k % LOW][k // LOW] for k in ks], axis=0)


def prepare_kernel(devs, per_video, me_ref, up_ref, *refs):
    low_refs, kv_refs = refs[:LOW], refs[LOW : LOW + devs]
    k_ref, v_ref = refs[LOW + devs :]
    toks = kv_refs[0].shape[1]
    videos = low_refs[0].shape[2] // up_ref.shape[0]
    up = up_part(up_ref, me_ref[0] // per_video, videos, 1)
    delta = jnp.dot(
        low_rows(low_refs, range(devs)), up, preferred_element_type=jnp.float32
    )
    for k in range(devs):
        here = slice(k * toks, (k + 1) * toks)
        k_ref[here, :] = kv_refs[k][0]
        v_ref[here, :] = (kv_refs[k][1].astype(jnp.float32) + delta[here]).astype(v_ref.dtype)


def attend_kernel(ks, block, per_video, me_ref, up_ref, k_ref, v_ref, *refs):
    count = len(ks)
    low_refs, q_refs, out_refs = refs[:LOW], refs[LOW : LOW + count], refs[LOW + count :]
    width = k_ref.shape[1]
    toks = q_refs[0].shape[0]
    videos = low_refs[0].shape[2] // up_ref.shape[0]
    up = up_part(up_ref, me_ref[0] // per_video, videos, 0)
    keys, vals = k_ref[...], v_ref[...]
    scale = math.log2(math.e) / math.sqrt(width)
    for b in range(0, count, block):
        delta = jnp.dot(
            low_rows(low_refs, ks[b : b + block]), up, preferred_element_type=jnp.float32
        )
        q = jnp.concatenate([r[...] for r in q_refs[b : b + block]], axis=0)
        q = (q.astype(jnp.float32) + delta).astype(jnp.bfloat16)
        scores = lax.dot_general(
            q, keys, (((1,), (1,)), ((), ())), preferred_element_type=jnp.float32
        )
        top = jnp.max(scores, axis=1, keepdims=True)
        weights = jnp.exp2((scores - top) * scale)
        total = jnp.sum(weights, axis=1, keepdims=True)
        mixed = jnp.dot(weights.astype(jnp.bfloat16), vals, preferred_element_type=jnp.float32)
        out = (mixed / total).astype(jnp.bfloat16)
        for i in range(block):
            out_refs[b + i][...] = out[i * toks : (i + 1) * toks]


def body(
    normed_token_features,
    queries,
    projected_keys,
    values,
    adapter_down_factors,
    adapter_up_factors,
    adapter_store_row,
    requests,
):
    videos, toks, model_width = normed_token_features.shape
    heads = queries.shape[1]
    width = queries.shape[3]
    _, ranks, up_width = adapter_up_factors.shape
    devs = lax.axis_size("seq")
    bits = bit_count(devs)
    me = lax.axis_index("seq").astype(jnp.int32)[None]
    pairs = videos * heads // devs
    per_video = devs // videos
    length = devs * toks
    col_split = math.gcd(per_video, model_width // LANES)
    rows = ranks * col_split // per_video
    tiles = model_width // col_split // LANES
    shape = (devs, bits, per_video, pairs, col_split, rows, tiles)
    everyone = range(devs)

    def swap(tensor, k):
        return lax.ppermute(tensor, "seq", [(i, i ^ k) for i in everyone])

    def halve(pieces, gate=None):
        got = []
        for i in range(bits):
            h = devs >> (i + 1)
            send = sum((r[h : 2 * h] for r in got), pieces[i])
            if gate is not None:
                (send,) = after((send,), gate[i])
            got.append(swap(send, 1 << i))
        return sum((r[:1] for r in got), pieces[bits]), got

    sizes = [(2, pairs, toks, width)] * devs + [(pairs, toks, width)] * devs
    packed = pl.pallas_call(
        functools.partial(pack_kernel, devs, pairs),
        in_specs=[SMEM, ANY, ANY, ANY],
        out_specs=[ANY] * (2 * devs),
        out_shape=[jax.ShapeDtypeStruct(s, jnp.bfloat16) for s in sizes],
        scratch_shapes=[pltpu.SemaphoreType.DMA((3 * devs,))],
        cost_estimate=pl.CostEstimate(
            flops=0, bytes_accessed=12 * pairs * length * width, transcendentals=0
        ),
        name="pack",
    )(me, *(t.reshape(-1, toks, width) for t in (queries, projected_keys, values)))
    kv, q = list(packed[:devs]), list(packed[devs:])

    steps = [devs >> (i + 1) for i in range(bits)] + [1]
    piece_shapes = [(h, tiles * rows, LANES) for h in steps] + [
        (h, pairs * ranks, LANES) for h in steps
    ]
    pieces = pl.pallas_call(
        functools.partial(pick_kernel, shape),
        in_specs=[SMEM, SMEM, SMEM, ANY, ANY],
        out_specs=[VMEM] * (2 * bits + 2),
        out_shape=[jax.ShapeDtypeStruct(s, jnp.bfloat16) for s in piece_shapes],
        scratch_shapes=[
            pltpu.VMEM((videos, ranks, model_width), jnp.bfloat16),
            pltpu.VMEM((videos, ranks, up_width), jnp.bfloat16),
            pltpu.SemaphoreType.DMA((2 * videos,)),
        ],
        compiler_params=pltpu.CompilerParams(vmem_limit_bytes=24 << 20),
        cost_estimate=pl.CostEstimate(
            flops=0,
            bytes_accessed=4 * videos * ranks * (model_width + up_width),
            transcendentals=0,
        ),
        name="pick_factors",
    )(me, adapter_store_row, requests, adapter_down_factors, adapter_up_factors)

    shard, halved = halve(pieces[: bits + 1])
    gathered = [shard]
    for bit in reversed(range(bits)):
        gathered.append(jnp.concatenate([gathered[-1], swap(gathered[-1], 1 << bit)], axis=0))
    up_here = halve(pieces[bits + 1 :], halved)[0].reshape(pairs, ranks, LANES)

    low = pl.pallas_call(
        functools.partial(low_rank_kernel, shape),
        in_specs=[SMEM, VMEM, VMEM],
        out_specs=VMEM,
        scratch_shapes=[pltpu.VMEM((videos, ranks, model_width), jnp.bfloat16)],
        out_shape=jax.ShapeDtypeStruct((toks, videos * ranks), jnp.bfloat16),
        compiler_params=pltpu.CompilerParams(vmem_limit_bytes=24 << 20),
        cost_estimate=pl.CostEstimate(
            flops=2 * videos * toks * ranks * model_width,
            bytes_accessed=2 * videos * (toks + ranks) * model_width,
            transcendentals=0,
        ),
        name="low_rank",
    )(me, normed_token_features, gathered[-1])
    far = jnp.stack([low] + [swap(low, LOW * i) for i in range(1, devs // LOW)])
    lows = [far] + [swap(far, i) for i in range(1, LOW)]

    top = devs >> 1
    early = [k for k in everyone if k & top and not k & 2]
    middle = [k for k in everyone if k & top and k & 2]
    near = [k for k in range(1, top)]
    gates = {k: None for k in early}
    for i, k in enumerate(middle):
        gates[k] = shard if 2 * i < len(middle) else gathered[min(2, bits)]
    for k in near:
        gates[k] = halved[min(1, bits - 1)] if k < LOW else gathered[min(2, bits)]
    for k in everyone[1:]:
        if gates[k] is not None:
            (kv[k],) = after((kv[k],), gates[k])
        (q[k],) = after((q[k],), gathered[-1] if k & top else low)
    kv_here = [kv[0]] + [swap(kv[k], k) for k in everyone[1:]]
    q_here = [q[0]] + [swap(q[k], k) for k in everyone[1:]]

    low_specs = [pl.BlockSpec((devs // LOW, toks, videos * ranks), lambda p: (0, 0, 0))] * LOW
    up_spec = pl.BlockSpec((pl.squeezed, ranks, LANES), lambda p: (p, 0, 0))
    all_spec = pl.BlockSpec((pl.squeezed, length, width), lambda p: (p, 0, 0))
    part_spec = pl.BlockSpec((pl.squeezed, toks, width), lambda p: (p, 0, 0))
    keys, vals = pl.pallas_call(
        functools.partial(prepare_kernel, devs, per_video),
        grid=(pairs,),
        in_specs=[SMEM, up_spec, *low_specs]
        + [pl.BlockSpec((2, pl.squeezed, toks, width), lambda p: (0, p, 0, 0))] * devs,
        out_specs=[all_spec] * 2,
        out_shape=[jax.ShapeDtypeStruct((pairs, length, width), jnp.bfloat16)] * 2,
        compiler_params=pltpu.CompilerParams(vmem_limit_bytes=40 << 20),
        cost_estimate=pl.CostEstimate(
            flops=2 * pairs * length * width * videos * ranks,
            bytes_accessed=8 * pairs * length * width,
            transcendentals=0,
        ),
        name="prepare",
    )(me, up_here, *lows, *kv_here)

    def attend(ks):
        count = len(ks)
        return pl.pallas_call(
            functools.partial(
                attend_kernel, ks, math.gcd(count, max(1, 256 // toks)), per_video
            ),
            grid=(pairs,),
            in_specs=[SMEM, up_spec, all_spec, all_spec, *low_specs] + [part_spec] * count,
            out_specs=[part_spec] * count,
            out_shape=[jax.ShapeDtypeStruct((pairs, toks, width), jnp.bfloat16)] * count,
            compiler_params=pltpu.CompilerParams(vmem_limit_bytes=40 << 20),
            cost_estimate=pl.CostEstimate(
                flops=4 * pairs * count * toks * length * width,
                bytes_accessed=4 * pairs * (count * toks + length) * width,
                transcendentals=pairs * count * toks * length,
            ),
            name="attend",
        )(me, up_here, keys, vals, *lows, *(q_here[k] for k in ks))

    back = [None] * devs
    half = top // 2
    for ks in (early, middle, near[half - 1 :], [0] + near[: half - 1]):
        for k, out in zip(ks, attend(ks)):
            back[k] = swap(out, k) if k else out

    out = pl.pallas_call(
        functools.partial(unpack_kernel, devs, pairs),
        in_specs=[SMEM] + [ANY] * devs,
        out_specs=ANY,
        out_shape=jax.ShapeDtypeStruct((devs * pairs, toks, width), jnp.bfloat16),
        scratch_shapes=[pltpu.SemaphoreType.DMA((devs,))],
        cost_estimate=pl.CostEstimate(
            flops=0, bytes_accessed=4 * pairs * length * width, transcendentals=0
        ),
        name="unpack",
    )(me, *back)
    return out.reshape(videos, heads, toks, width)


def solution(mesh):
    in_specs = (
        P("grp", "seq", None),
        P("grp", None, "seq", None),
        P("grp", None, "seq", None),
        P("grp", None, "seq", None),
        P("seq", None, None),
        P("seq", None, None),
        P(),
        P("grp"),
    )
    out_specs = P("grp", None, "seq", None)
    return jax.shard_map(body, mesh=mesh, in_specs=in_specs, out_specs=out_specs, check_vma=False)
```

```python
import functools
import math

import jax
import jax.numpy as jnp
from jax import lax
from jax.experimental import pallas as pl
from jax.experimental.pallas import tpu as pltpu
from jax.sharding import PartitionSpec as P

LANES = 128
LOW = 4
VMEM = pl.BlockSpec(memory_space=pltpu.VMEM)
SMEM = pl.BlockSpec(memory_space=pltpu.SMEM)
HBM = pl.BlockSpec(memory_space=pltpu.HBM)


def pick_kernel(per_video, pairs, me_ref, row_ref, req_ref, down_ref, up_ref, out_down, out_up, up, sems):
    slots, ranks, _ = down_ref.shape
    videos = out_down.shape[0]
    devs = out_up.shape[0]
    for s in range(videos):
        place = row_ref[req_ref[s]]
        slot = place % slots
        owned = place // slots == me_ref[0]
        copies = [
            pltpu.make_async_copy(down_ref.at[slot], out_down.at[s], sems.at[2 * s]),
            pltpu.make_async_copy(up_ref.at[slot], up.at[s], sems.at[2 * s + 1]),
        ]

        @pl.when(owned)
        def _():
            for copy in copies:
                copy.start()
            for copy in copies:
                copy.wait()

        @pl.when(jnp.logical_not(owned))
        def _():
            out_down[s] = jnp.zeros(out_down.shape[1:], out_down.dtype)
            up[s] = jnp.zeros(up.shape[1:], up.dtype)

    for d in range(devs):
        for p in range(pairs):
            col = ((d % per_video) * pairs + p) * LANES
            out_up[d, p * ranks : (p + 1) * ranks, :] = up[d // per_video, :, col : col + LANES]


def low_rank_kernel(x_ref, down_ref, out_ref):
    parts = [
        lax.dot_general(
            x_ref[s], down_ref[s], (((1,), (1,)), ((), ())), preferred_element_type=jnp.float32
        )
        for s in range(x_ref.shape[0])
    ]
    out_ref[...] = jnp.concatenate(parts, axis=1).astype(out_ref.dtype)


def up_part(up_ref, video, videos, second):
    up = jnp.concatenate([up_ref[...]] * videos, axis=0)
    ranks = up_ref.shape[0]
    row = lax.broadcasted_iota(jnp.int32, up.shape, 0)
    half = (row % ranks) // (ranks // 2)
    keep = (row // ranks == video) & (half == second)
    return jnp.where(keep, up, jnp.zeros_like(up))


def attend_kernel(per_video, block, me_ref, up_ref, q_ref, k_ref, v_ref, *refs):
    low_refs, out_ref, low, q_mix = refs[:LOW], refs[LOW], refs[LOW + 1], refs[LOW + 2]
    devs, toks, width = q_ref.shape
    length = devs * toks
    videos = low.shape[2] // up_ref.shape[0]
    me = me_ref[0]
    for k in range(devs):
        low[me ^ k] = low_refs[k % LOW][k // LOW]
    low_all = low[...].reshape(length, low.shape[2])
    up_q, up_v = (up_part(up_ref, me // per_video, videos, i) for i in range(2))
    keys = k_ref[...].reshape(length, width)
    delta_v = jnp.dot(low_all, up_v, preferred_element_type=jnp.float32)
    vals = (v_ref[...].reshape(length, width).astype(jnp.float32) + delta_v).astype(jnp.bfloat16)
    delta_q = jnp.dot(low_all, up_q, preferred_element_type=jnp.float32)
    q_mix[...] = (q_ref[...].reshape(length, width).astype(jnp.float32) + delta_q).astype(
        jnp.bfloat16
    )
    scale = math.log2(math.e) / math.sqrt(width)
    for b in range(0, devs, block):
        q = q_mix[b * toks : (b + block) * toks, :]
        scores = lax.dot_general(
            q, keys, (((1,), (1,)), ((), ())), preferred_element_type=jnp.float32
        )
        top = jnp.max(scores, axis=1, keepdims=True)
        weights = jnp.exp2((scores - top) * scale)
        total = jnp.sum(weights, axis=1, keepdims=True)
        mixed = jnp.dot(weights.astype(jnp.bfloat16), vals, preferred_element_type=jnp.float32)
        out_ref[b : b + block] = (mixed / total).astype(jnp.bfloat16).reshape(block, toks, width)


def body(
    normed_token_features,
    queries,
    projected_keys,
    values,
    adapter_down_factors,
    adapter_up_factors,
    adapter_store_row,
    requests,
):
    videos, toks, model_width = normed_token_features.shape
    heads = queries.shape[1]
    width = queries.shape[3]
    _, ranks, up_width = adapter_up_factors.shape
    devs = lax.axis_size("seq")
    me = lax.axis_index("seq").astype(jnp.int32)[None]
    pairs = videos * heads // devs
    per_video = devs // videos
    length = devs * toks

    def swap(tensor, k):
        return lax.ppermute(tensor, "seq", [(i, i ^ k) for i in range(devs)])

    def exchange(tensor):
        blocks = tensor.reshape(devs, pairs, toks, width)
        return lax.all_to_all(blocks, "seq", split_axis=0, concat_axis=0, tiled=True)

    down_part, up_parts = pl.pallas_call(
        functools.partial(pick_kernel, per_video, pairs),
        in_specs=[SMEM, SMEM, SMEM, HBM, HBM],
        out_specs=[VMEM, VMEM],
        out_shape=[
            jax.ShapeDtypeStruct((videos, ranks, model_width), jnp.bfloat16),
            jax.ShapeDtypeStruct((devs, pairs * ranks, LANES), jnp.bfloat16),
        ],
        scratch_shapes=[
            pltpu.VMEM((videos, ranks, up_width), jnp.bfloat16),
            pltpu.SemaphoreType.DMA((2 * videos,)),
        ],
        compiler_params=pltpu.CompilerParams(vmem_limit_bytes=24 << 20),
        cost_estimate=pl.CostEstimate(
            flops=0,
            bytes_accessed=4 * videos * ranks * (model_width + up_width),
            transcendentals=0,
        ),
        name="pick_factors",
    )(me, adapter_store_row, requests, adapter_down_factors, adapter_up_factors)
    down = lax.psum(down_part, "seq")
    up_here = lax.psum_scatter(up_parts, "seq", scatter_dimension=0, tiled=True)
    up_here = up_here.reshape(pairs, ranks, LANES)

    keys, vals, query = (exchange(t) for t in (projected_keys, values, queries))

    low = pl.pallas_call(
        low_rank_kernel,
        in_specs=[VMEM, VMEM],
        out_specs=VMEM,
        out_shape=jax.ShapeDtypeStruct((toks, videos * ranks), jnp.bfloat16),
        compiler_params=pltpu.CompilerParams(vmem_limit_bytes=24 << 20),
        cost_estimate=pl.CostEstimate(
            flops=2 * videos * toks * ranks * model_width,
            bytes_accessed=2 * videos * (toks + ranks) * model_width,
            transcendentals=0,
        ),
        name="low_rank",
    )(normed_token_features, down)
    far = jnp.stack([low] + [swap(low, LOW * i) for i in range(1, devs // LOW)])
    lows = [far] + [swap(far, i) for i in range(1, LOW)]

    low_spec = pl.BlockSpec((devs // LOW, toks, videos * ranks), lambda p: (0, 0, 0))
    part_spec = pl.BlockSpec((devs, pl.squeezed, toks, width), lambda p: (0, p, 0, 0))
    mixed = pl.pallas_call(
        functools.partial(attend_kernel, per_video, math.gcd(devs, max(1, 512 // toks))),
        grid=(pairs,),
        in_specs=[SMEM, pl.BlockSpec((pl.squeezed, ranks, LANES), lambda p: (p, 0, 0))]
        + [part_spec] * 3
        + [low_spec] * LOW,
        out_specs=part_spec,
        out_shape=jax.ShapeDtypeStruct((devs, pairs, toks, width), jnp.bfloat16),
        scratch_shapes=[
            pltpu.VMEM((devs, toks, videos * ranks), jnp.bfloat16),
            pltpu.VMEM((length, width), jnp.bfloat16),
        ],
        compiler_params=pltpu.CompilerParams(vmem_limit_bytes=48 << 20),
        cost_estimate=pl.CostEstimate(
            flops=4 * pairs * length * length * width,
            bytes_accessed=8 * pairs * length * width,
            transcendentals=pairs * length * length,
        ),
        name="attend",
    )(me, up_here, query, keys, vals, *lows)
    return exchange(mixed).reshape(videos, heads, toks, width)


def solution(mesh):
    in_specs = (
        P("grp", "seq", None),
        P("grp", None, "seq", None),
        P("grp", None, "seq", None),
        P("grp", None, "seq", None),
        P("seq", None, None),
        P("seq", None, None),
        P(),
        P("grp"),
    )
    out_specs = P("grp", None, "seq", None)
    return jax.shard_map(body, mesh=mesh, in_specs=in_specs, out_specs=out_specs, check_vma=False)
```

```python
import functools
import math

import jax
import jax.numpy as jnp
from jax import lax
from jax.experimental import pallas as pl
from jax.experimental.pallas import tpu as pltpu
from jax.sharding import PartitionSpec as P

LANES = 128
LOW = 4
ANY = pl.BlockSpec(memory_space=pl.ANY)
VMEM = pl.BlockSpec(memory_space=pltpu.VMEM)
SMEM = pl.BlockSpec(memory_space=pltpu.SMEM)


def bit_count(n):
    bits = n.bit_length() - 1
    assert 1 << bits == n
    return bits


def reversed_bits(j, bits):
    out = 0
    for i in range(bits):
        out = out | (((j >> i) & 1) << (bits - 1 - i))
    return out


def run_copies(copies):
    for copy in copies:
        copy.start()
    for copy in copies:
        copy.wait()


def pack_kernel(devs, pairs, late, me_ref, k_ref, v_ref, q_ref, *outs):
    for k in range(devs):
        here = pl.ds((me_ref[0] ^ k) * pairs, pairs)
        outs[k][0] = k_ref[here]
        outs[k][1] = v_ref[here]
        if k in late:
            outs[devs + late.index(k)][0] = q_ref[here]
        else:
            outs[k][2] = q_ref[here]


def unpack_kernel(devs, pairs, me_ref, *refs):
    ins, out = refs[:devs], refs[devs]
    for k in range(devs):
        out[pl.ds((me_ref[0] ^ k) * pairs, pairs)] = ins[k][...]


def pick_kernel(
    shape, me_ref, row_ref, req_ref, down_ref, up_ref, *refs
):
    devs, bits, per_video, pairs, col_split, rows, tiles = shape
    downs, ups = refs[: bits + 1], refs[bits + 1 : 2 * bits + 2]
    down, up, sems = refs[2 * bits + 2 :]
    slots, ranks, _ = down_ref.shape
    videos = down.shape[0]
    me = me_ref[0]
    for s in range(videos):
        place = row_ref[req_ref[s]]
        slot = place % slots
        owned = place // slots == me
        copies = [
            pltpu.make_async_copy(down_ref.at[slot], down.at[s], sems.at[2 * s]),
            pltpu.make_async_copy(up_ref.at[slot], up.at[s], sems.at[2 * s + 1]),
        ]

        @pl.when(owned)
        def _():
            run_copies(copies)

        @pl.when(jnp.logical_not(owned))
        def _():
            down[s] = jnp.zeros(down.shape[1:], down.dtype)
            up[s] = jnp.zeros(up.shape[1:], up.dtype)

    for j in range(devs):
        step = bits - j.bit_length()
        at = j - (1 << (j.bit_length() - 1)) if j else 0
        dev = me ^ reversed_bits(j, bits)
        video = dev // per_video
        place = dev % per_video
        row = pl.multiple_of((place // col_split) * rows, rows)
        for t in range(tiles):
            col = pl.multiple_of(((place % col_split) * tiles + t) * LANES, LANES)
            downs[step][at, t * rows : (t + 1) * rows, :] = down[
                video, pl.ds(row, rows), pl.ds(col, LANES)
            ]
        for p in range(pairs):
            col = pl.multiple_of((place * pairs + p) * LANES, LANES)
            ups[step][at, p * ranks : (p + 1) * ranks, :] = up[video, :, pl.ds(col, LANES)]


def low_rank_kernel(shape, me_ref, x_ref, g_ref, out_ref, down):
    devs, bits, per_video, _, col_split, rows, tiles = shape
    for j in range(devs):
        dev = me_ref[0] ^ reversed_bits(j, bits)
        video = dev // per_video
        place = dev % per_video
        row = pl.multiple_of((place // col_split) * rows, rows)
        for t in range(tiles):
            col = pl.multiple_of(((place % col_split) * tiles + t) * LANES, LANES)
            down[video, pl.ds(row, rows), pl.ds(col, LANES)] = g_ref[j, t * rows : (t + 1) * rows, :]
    parts = [
        lax.dot_general(
            x_ref[s], down[s], (((1,), (1,)), ((), ())), preferred_element_type=jnp.float32
        )
        for s in range(x_ref.shape[0])
    ]
    out_ref[...] = jnp.concatenate(parts, axis=1).astype(out_ref.dtype)


def up_part(up_ref, video, videos, second):
    up = jnp.concatenate([up_ref[...]] * videos, axis=0)
    ranks = up_ref.shape[0]
    row = lax.broadcasted_iota(jnp.int32, up.shape, 0)
    half = (row % ranks) // (ranks // 2)
    keep = (row // ranks == video) & (half == second)
    return jnp.where(keep, up, jnp.zeros_like(up))


def low_rows(low_refs, ks):
    return jnp.concatenate([low_refs[k % LOW][k // LOW] for k in ks], axis=0)


def prepare_kernel(devs, per_video, me_ref, up_ref, *refs):
    low_refs, kv_refs = refs[:LOW], refs[LOW : LOW + devs]
    k_ref, v_ref = refs[LOW + devs :]
    toks = kv_refs[0].shape[1]
    videos = low_refs[0].shape[2] // up_ref.shape[0]
    up = up_part(up_ref, me_ref[0] // per_video, videos, 1)
    delta = jnp.dot(
        low_rows(low_refs, range(devs)), up, preferred_element_type=jnp.float32
    )
    for k in range(devs):
        here = slice(k * toks, (k + 1) * toks)
        k_ref[here, :] = kv_refs[k][0]
        v_ref[here, :] = (kv_refs[k][1].astype(jnp.float32) + delta[here]).astype(v_ref.dtype)


def attend_kernel(ks, block, per_video, me_ref, up_ref, k_ref, v_ref, *refs):
    count = len(ks)
    low_refs, q_refs, out_refs = refs[:LOW], refs[LOW : LOW + count], refs[LOW + count :]
    width = k_ref.shape[1]
    toks = q_refs[0].shape[0]
    videos = low_refs[0].shape[2] // up_ref.shape[0]
    up = up_part(up_ref, me_ref[0] // per_video, videos, 0)
    keys, vals = k_ref[...], v_ref[...]
    scale = math.log2(math.e) / math.sqrt(width)
    for b in range(0, count, block):
        delta = jnp.dot(
            low_rows(low_refs, ks[b : b + block]), up, preferred_element_type=jnp.float32
        )
        q = jnp.concatenate([r[...] for r in q_refs[b : b + block]], axis=0)
        q = (q.astype(jnp.float32) + delta).astype(jnp.bfloat16)
        scores = lax.dot_general(
            q, keys, (((1,), (1,)), ((), ())), preferred_element_type=jnp.float32
        )
        top = jnp.max(scores, axis=1, keepdims=True)
        weights = jnp.exp2((scores - top) * scale)
        total = jnp.sum(weights, axis=1, keepdims=True)
        mixed = jnp.dot(weights.astype(jnp.bfloat16), vals, preferred_element_type=jnp.float32)
        out = (mixed / total).astype(jnp.bfloat16)
        for i in range(block):
            out_refs[b + i][...] = out[i * toks : (i + 1) * toks]


def body(
    normed_token_features,
    queries,
    projected_keys,
    values,
    adapter_down_factors,
    adapter_up_factors,
    adapter_store_row,
    requests,
):
    videos, toks, model_width = normed_token_features.shape
    heads = queries.shape[1]
    width = queries.shape[3]
    _, ranks, up_width = adapter_up_factors.shape
    devs = lax.axis_size("seq")
    bits = bit_count(devs)
    me = lax.axis_index("seq").astype(jnp.int32)[None]
    pairs = videos * heads // devs
    per_video = devs // videos
    length = devs * toks
    col_split = math.gcd(per_video, model_width // LANES)
    rows = ranks * col_split // per_video
    tiles = model_width // col_split // LANES
    shape = (devs, bits, per_video, pairs, col_split, rows, tiles)
    everyone = range(devs)

    def swap(tensor, k):
        return lax.ppermute(tensor, "seq", [(i, i ^ k) for i in everyone])

    def after(array, *others):
        return lax.optimization_barrier((array, others))[0]

    top = devs >> 1
    plain = [k for k in everyone if k & top and not k & 2]
    crossed = [k for k in everyone if k & top and k & 2]
    near = [k for k in range(1, top) if k < LOW]
    side = [k for k in range(1, top) if k >= LOW]
    ahead = plain[: 3 * len(plain) // 4]
    behind = plain[3 * len(plain) // 4 :]

    sizes = [(2 if k in crossed else 3, pairs, toks, width) for k in everyone]
    sizes += [(1, pairs, toks, width) for k in crossed]
    packed = pl.pallas_call(
        functools.partial(pack_kernel, devs, pairs, crossed),
        in_specs=[SMEM, VMEM, VMEM, VMEM],
        out_specs=[VMEM] * len(sizes),
        out_shape=[jax.ShapeDtypeStruct(s, jnp.bfloat16) for s in sizes],
        compiler_params=pltpu.CompilerParams(vmem_limit_bytes=40 << 20),
        cost_estimate=pl.CostEstimate(
            flops=0, bytes_accessed=12 * pairs * length * width, transcendentals=0
        ),
        name="pack",
    )(me, *(t.reshape(-1, toks, width) for t in (projected_keys, values, queries)))
    blocks = list(packed[:devs])
    late = dict(zip(crossed, packed[devs:]))

    def send(ks, *others):
        for k in ks:
            blocks[k] = swap(after(blocks[k], *others) if others else blocks[k], k)

    def got(ks):
        return [blocks[k] for k in ks]

    steps = [devs >> (i + 1) for i in range(bits)] + [1]
    piece_shapes = [(h, tiles * rows, LANES) for h in steps] + [
        (h, pairs * ranks, LANES) for h in steps
    ]
    pieces = pl.pallas_call(
        functools.partial(pick_kernel, shape),
        in_specs=[SMEM, SMEM, SMEM, ANY, ANY],
        out_specs=[VMEM] * (2 * bits + 2),
        out_shape=[jax.ShapeDtypeStruct(s, jnp.bfloat16) for s in piece_shapes],
        scratch_shapes=[
            pltpu.VMEM((videos, ranks, model_width), jnp.bfloat16),
            pltpu.VMEM((videos, ranks, up_width), jnp.bfloat16),
            pltpu.SemaphoreType.DMA((2 * videos,)),
        ],
        compiler_params=pltpu.CompilerParams(vmem_limit_bytes=24 << 20),
        cost_estimate=pl.CostEstimate(
            flops=0,
            bytes_accessed=4 * videos * ranks * (model_width + up_width),
            transcendentals=0,
        ),
        name="pick_factors",
    )(after(me, blocks[top]), adapter_store_row, requests, adapter_down_factors, adapter_up_factors)
    down_pieces, up_pieces = pieces[: bits + 1], pieces[bits + 1 :]

    def halving(parts, received, i):
        h = devs >> (i + 1) if i < bits else 0
        size = max(h, 1)
        return sum((r[h : h + size] for r in received), parts[i])

    send(ahead)
    down_got, up_got = [], []
    for i in range(bits):
        piece = halving(down_pieces, down_got, i)
        if i == min(2, bits - 1):
            piece = after(piece, *got(ahead[:-1]))
            send(near, down_got[-1])
        if i == bits - 1:
            piece = after(piece, *got(ahead))
        down_got.append(swap(piece, 1 << i))
    gathered = halving(down_pieces, down_got, bits)
    for i in range(2):
        piece = after(halving(up_pieces, up_got, i), down_got[min(i + 1, bits - 1)])
        up_got.append(swap(piece, 1 << i))
    gathered = after(gathered, *got(near), *up_got)
    for i in reversed(range(bits)):
        if i == bits - 2:
            send(behind, gathered)
        if i == 1:
            send(crossed[: len(crossed) // 2], gathered)
        if i == 0:
            gathered = after(gathered, *got(behind))
            send(crossed[len(crossed) // 2 :], gathered)
            send(side[: len(side) // 2], gathered)
        gathered = jnp.concatenate([gathered, swap(gathered, 1 << i)], axis=0)
    gathered = after(gathered, *got(crossed[: len(crossed) // 2]))

    low = pl.pallas_call(
        functools.partial(low_rank_kernel, shape),
        in_specs=[SMEM, VMEM, VMEM],
        out_specs=VMEM,
        scratch_shapes=[pltpu.VMEM((videos, ranks, model_width), jnp.bfloat16)],
        out_shape=jax.ShapeDtypeStruct((toks, videos * ranks), jnp.bfloat16),
        compiler_params=pltpu.CompilerParams(vmem_limit_bytes=24 << 20),
        cost_estimate=pl.CostEstimate(
            flops=2 * videos * toks * ranks * model_width,
            bytes_accessed=2 * videos * (toks + ranks) * model_width,
            transcendentals=0,
        ),
        name="low_rank",
    )(me, normed_token_features, gathered)
    send(side[len(side) // 2 :], low)
    far = jnp.stack([low] + [swap(low, LOW * i) for i in range(1, devs // LOW)])
    for i in range(2, bits):
        piece = after(halving(up_pieces, up_got, i), low)
        up_got.append(swap(piece, 1 << i))
    up_here = halving(up_pieces, up_got, bits).reshape(pairs, ranks, LANES)
    far = after(far, *got(crossed[len(crossed) // 2 :]))
    late = {k: swap(after(late[k], far), k) for k in crossed}
    lows = [far] + [swap(far, i) for i in range(1, LOW)]

    low_specs = [pl.BlockSpec((devs // LOW, toks, videos * ranks), lambda p: (0, 0, 0))] * LOW
    up_spec = pl.BlockSpec((pl.squeezed, ranks, LANES), lambda p: (p, 0, 0))
    all_spec = pl.BlockSpec((pl.squeezed, length, width), lambda p: (p, 0, 0))
    part_spec = pl.BlockSpec((pl.squeezed, toks, width), lambda p: (p, 0, 0))
    keys, vals = pl.pallas_call(
        functools.partial(prepare_kernel, devs, per_video),
        grid=(pairs,),
        in_specs=[SMEM, up_spec, *low_specs]
        + [pl.BlockSpec((2, pl.squeezed, toks, width), lambda p: (0, p, 0, 0))] * devs,
        out_specs=[all_spec] * 2,
        out_shape=[jax.ShapeDtypeStruct((pairs, length, width), jnp.bfloat16)] * 2,
        compiler_params=pltpu.CompilerParams(vmem_limit_bytes=40 << 20),
        cost_estimate=pl.CostEstimate(
            flops=2 * pairs * length * width * videos * ranks,
            bytes_accessed=8 * pairs * length * width,
            transcendentals=0,
        ),
        name="prepare",
    )(me, up_here, *lows, *blocks)

    def query_spec(k):
        first = 0 if k in late else 2
        return pl.BlockSpec((pl.squeezed, pl.squeezed, toks, width), lambda p: (first, p, 0, 0))

    def attend(ks):
        count = len(ks)
        return pl.pallas_call(
            functools.partial(
                attend_kernel, ks, math.gcd(count, max(1, 256 // toks)), per_video
            ),
            grid=(pairs,),
            in_specs=[SMEM, up_spec, all_spec, all_spec, *low_specs] + [query_spec(k) for k in ks],
            out_specs=[part_spec] * count,
            out_shape=[jax.ShapeDtypeStruct((pairs, toks, width), jnp.bfloat16)] * count,
            compiler_params=pltpu.CompilerParams(vmem_limit_bytes=40 << 20),
            cost_estimate=pl.CostEstimate(
                flops=4 * pairs * count * toks * length * width,
                bytes_accessed=4 * pairs * (count * toks + length) * width,
                transcendentals=pairs * count * toks * length,
            ),
            name="attend",
        )(me, up_here, keys, vals, *lows, *(late.get(k, blocks[k]) for k in ks))

    back = [None] * devs
    for ks in (plain, crossed, side, [0] + near):
        for k, out in zip(ks, attend(ks)):
            back[k] = swap(out, k) if k else out

    out = pl.pallas_call(
        functools.partial(unpack_kernel, devs, pairs),
        in_specs=[SMEM] + [VMEM] * devs,
        out_specs=VMEM,
        out_shape=jax.ShapeDtypeStruct((devs * pairs, toks, width), jnp.bfloat16),
        compiler_params=pltpu.CompilerParams(vmem_limit_bytes=24 << 20),
        cost_estimate=pl.CostEstimate(
            flops=0, bytes_accessed=4 * pairs * length * width, transcendentals=0
        ),
        name="unpack",
    )(me, *back)
    return out.reshape(videos, heads, toks, width)


def solution(mesh):
    in_specs = (
        P("grp", "seq", None),
        P("grp", None, "seq", None),
        P("grp", None, "seq", None),
        P("grp", None, "seq", None),
        P("seq", None, None),
        P("seq", None, None),
        P(),
        P("grp"),
    )
    out_specs = P("grp", None, "seq", None)
    return jax.shard_map(body, mesh=mesh, in_specs=in_specs, out_specs=out_specs, check_vma=False)
```

```python
import functools
import math

import jax
import jax.numpy as jnp
from jax import lax
from jax.experimental import pallas as pl
from jax.experimental.pallas import tpu as pltpu
from jax.sharding import PartitionSpec as P

LANES = 128
LOW = 4
ANY = pl.BlockSpec(memory_space=pl.ANY)
VMEM = pl.BlockSpec(memory_space=pltpu.VMEM)
SMEM = pl.BlockSpec(memory_space=pltpu.SMEM)


def bit_count(n):
    bits = n.bit_length() - 1
    assert 1 << bits == n
    return bits


def reversed_bits(j, bits):
    out = 0
    for i in range(bits):
        out = out | (((j >> i) & 1) << (bits - 1 - i))
    return out


def run_copies(copies):
    for copy in copies:
        copy.start()
    for copy in copies:
        copy.wait()


def pack_kernel(devs, pairs, late, me_ref, k_ref, v_ref, q_ref, *outs):
    for k in range(devs):
        here = pl.ds((me_ref[0] ^ k) * pairs, pairs)
        outs[k][0] = k_ref[here]
        outs[k][1] = v_ref[here]
        if k in late:
            outs[devs + late.index(k)][0] = q_ref[here]
        else:
            outs[k][2] = q_ref[here]


def unpack_kernel(devs, pairs, order, me_ref, *refs):
    ins, crossed, out = refs[: len(order)], refs[len(order) : -1], refs[-1]
    for i, k in enumerate(order):
        out[pl.ds((me_ref[0] ^ k) * pairs, pairs)] = ins[i][0]
        size = crossed[0].shape[0]
        out[pl.ds((me_ref[0] ^ 1 ^ k) * pairs, pairs)] = crossed[i // size][i % size]


def pick_kernel(
    shape, me_ref, row_ref, req_ref, down_ref, up_ref, *refs
):
    devs, bits, per_video, pairs, col_split, rows, tiles = shape
    downs, ups = refs[: bits + 1], refs[bits + 1 : 2 * bits + 2]
    down, up, sems = refs[2 * bits + 2 :]
    slots, ranks, _ = down_ref.shape
    videos = down.shape[0]
    me = me_ref[0]
    for s in range(videos):
        place = row_ref[req_ref[s]]
        slot = place % slots
        owned = place // slots == me
        copies = [
            pltpu.make_async_copy(down_ref.at[slot], down.at[s], sems.at[2 * s]),
            pltpu.make_async_copy(up_ref.at[slot], up.at[s], sems.at[2 * s + 1]),
        ]

        @pl.when(owned)
        def _():
            run_copies(copies)

        @pl.when(jnp.logical_not(owned))
        def _():
            down[s] = jnp.zeros(down.shape[1:], down.dtype)
            up[s] = jnp.zeros(up.shape[1:], up.dtype)

    for j in range(devs):
        step = bits - j.bit_length()
        at = j - (1 << (j.bit_length() - 1)) if j else 0
        dev = me ^ reversed_bits(j, bits)
        video = dev // per_video
        place = dev % per_video
        row = pl.multiple_of((place // col_split) * rows, rows)
        for t in range(tiles):
            col = pl.multiple_of(((place % col_split) * tiles + t) * LANES, LANES)
            downs[step][at, t * rows : (t + 1) * rows, :] = down[
                video, pl.ds(row, rows), pl.ds(col, LANES)
            ]
        for p in range(pairs):
            col = pl.multiple_of((place * pairs + p) * LANES, LANES)
            ups[step][at, p * ranks : (p + 1) * ranks, :] = up[video, :, pl.ds(col, LANES)]


def low_rank_kernel(shape, me_ref, x_ref, g_ref, out_ref, down):
    devs, bits, per_video, _, col_split, rows, tiles = shape
    for j in range(devs):
        dev = me_ref[0] ^ reversed_bits(j, bits)
        video = dev // per_video
        place = dev % per_video
        row = pl.multiple_of((place // col_split) * rows, rows)
        for t in range(tiles):
            col = pl.multiple_of(((place % col_split) * tiles + t) * LANES, LANES)
            down[video, pl.ds(row, rows), pl.ds(col, LANES)] = g_ref[j, t * rows : (t + 1) * rows, :]
    parts = [
        lax.dot_general(
            x_ref[s], down[s], (((1,), (1,)), ((), ())), preferred_element_type=jnp.float32
        )
        for s in range(x_ref.shape[0])
    ]
    out_ref[...] = jnp.concatenate(parts, axis=1).astype(out_ref.dtype)


def up_part(up_ref, video, videos, second):
    up = jnp.concatenate([up_ref[...]] * videos, axis=0)
    ranks = up_ref.shape[0]
    row = lax.broadcasted_iota(jnp.int32, up.shape, 0)
    half = (row % ranks) // (ranks // 2)
    keep = (row // ranks == video) & (half == second)
    return jnp.where(keep, up, jnp.zeros_like(up))


def low_rows(low_refs, ks):
    return jnp.concatenate([low_refs[k % LOW][k // LOW] for k in ks], axis=0)


def prepare_kernel(devs, per_video, me_ref, up_ref, *refs):
    low_refs, kv_refs = refs[:LOW], refs[LOW : LOW + devs]
    k_ref, v_ref = refs[LOW + devs :]
    toks = kv_refs[0].shape[1]
    videos = low_refs[0].shape[2] // up_ref.shape[0]
    up = up_part(up_ref, me_ref[0] // per_video, videos, 1)
    delta = jnp.dot(
        low_rows(low_refs, range(devs)), up, preferred_element_type=jnp.float32
    )
    for k in range(devs):
        here = slice(k * toks, (k + 1) * toks)
        k_ref[here, :] = kv_refs[k][0]
        v_ref[here, :] = (kv_refs[k][1].astype(jnp.float32) + delta[here]).astype(v_ref.dtype)


def attend_kernel(ks, block, per_video, me_ref, up_ref, k_ref, v_ref, *refs):
    count = len(ks)
    low_refs, q_refs, out_refs = refs[:LOW], refs[LOW : LOW + count], refs[LOW + count :]
    width = k_ref.shape[1]
    toks = q_refs[0].shape[0]
    videos = low_refs[0].shape[2] // up_ref.shape[0]
    up = up_part(up_ref, me_ref[0] // per_video, videos, 0)
    keys, vals = k_ref[...], v_ref[...]
    scale = math.log2(math.e) / math.sqrt(width)
    for b in range(0, count, block):
        delta = jnp.dot(
            low_rows(low_refs, ks[b : b + block]), up, preferred_element_type=jnp.float32
        )
        q = jnp.concatenate([r[...] for r in q_refs[b : b + block]], axis=0)
        q = (q.astype(jnp.float32) + delta).astype(jnp.bfloat16)
        scores = lax.dot_general(
            q, keys, (((1,), (1,)), ((), ())), preferred_element_type=jnp.float32
        )
        top = jnp.max(scores, axis=1, keepdims=True)
        weights = jnp.exp2((scores - top) * scale)
        total = jnp.sum(weights, axis=1, keepdims=True)
        mixed = jnp.dot(weights.astype(jnp.bfloat16), vals, preferred_element_type=jnp.float32)
        out = (mixed / total).astype(jnp.bfloat16)
        for i in range(b, b + block):
            out_refs[i // 2][i % 2] = out[(i - b) * toks : (i - b + 1) * toks]


def body(
    normed_token_features,
    queries,
    projected_keys,
    values,
    adapter_down_factors,
    adapter_up_factors,
    adapter_store_row,
    requests,
):
    videos, toks, model_width = normed_token_features.shape
    heads = queries.shape[1]
    width = queries.shape[3]
    _, ranks, up_width = adapter_up_factors.shape
    devs = lax.axis_size("seq")
    bits = bit_count(devs)
    me = lax.axis_index("seq").astype(jnp.int32)[None]
    pairs = videos * heads // devs
    per_video = devs // videos
    length = devs * toks
    col_split = math.gcd(per_video, model_width // LANES)
    rows = ranks * col_split // per_video
    tiles = model_width // col_split // LANES
    shape = (devs, bits, per_video, pairs, col_split, rows, tiles)
    everyone = range(devs)

    def swap(tensor, k):
        return lax.ppermute(tensor, "seq", [(i, i ^ k) for i in everyone])

    def after(array, *others):
        return lax.optimization_barrier((array, others))[0]

    top = devs >> 1
    plain = [k for k in everyone if k & top and not k & 2]
    crossed = [k for k in everyone if k & top and k & 2]
    near = [k for k in range(1, top) if k < LOW]
    side = [k for k in range(1, top) if k >= LOW]
    ahead = plain[: 3 * len(plain) // 4]
    behind = plain[3 * len(plain) // 4 :]

    steps = [devs >> (i + 1) for i in range(bits)] + [1]
    piece_shapes = [(h, tiles * rows, LANES) for h in steps] + [
        (h, pairs * ranks, LANES) for h in steps
    ]
    pieces = pl.pallas_call(
        functools.partial(pick_kernel, shape),
        in_specs=[SMEM, SMEM, SMEM, ANY, ANY],
        out_specs=[VMEM] * (2 * bits + 2),
        out_shape=[jax.ShapeDtypeStruct(s, jnp.bfloat16) for s in piece_shapes],
        scratch_shapes=[
            pltpu.VMEM((videos, ranks, model_width), jnp.bfloat16),
            pltpu.VMEM((videos, ranks, up_width), jnp.bfloat16),
            pltpu.SemaphoreType.DMA((2 * videos,)),
        ],
        compiler_params=pltpu.CompilerParams(vmem_limit_bytes=24 << 20),
        cost_estimate=pl.CostEstimate(
            flops=0,
            bytes_accessed=4 * videos * ranks * (model_width + up_width),
            transcendentals=0,
        ),
        name="pick_factors",
    )(me, adapter_store_row, requests, adapter_down_factors, adapter_up_factors)
    down_pieces, up_pieces = pieces[: bits + 1], pieces[bits + 1 :]

    sizes = [(2 if k in crossed else 3, pairs, toks, width) for k in everyone]
    sizes += [(1, pairs, toks, width) for k in crossed]
    packed = pl.pallas_call(
        functools.partial(pack_kernel, devs, pairs, crossed),
        in_specs=[SMEM, VMEM, VMEM, VMEM],
        out_specs=[VMEM] * len(sizes),
        out_shape=[jax.ShapeDtypeStruct(s, jnp.bfloat16) for s in sizes],
        compiler_params=pltpu.CompilerParams(vmem_limit_bytes=40 << 20),
        cost_estimate=pl.CostEstimate(
            flops=0, bytes_accessed=12 * pairs * length * width, transcendentals=0
        ),
        name="pack",
    )(after(me, pieces[0]), *(t.reshape(-1, toks, width) for t in (projected_keys, values, queries)))
    blocks = list(packed[:devs])
    late = dict(zip(crossed, packed[devs:]))

    def send(ks, *others):
        for k in ks:
            blocks[k] = swap(after(blocks[k], *others) if others else blocks[k], k)

    def got(ks):
        return [blocks[k] for k in ks]

    def halving(parts, received, i):
        h = devs >> (i + 1) if i < bits else 0
        size = max(h, 1)
        return sum((r[h : h + size] for r in received), parts[i])

    ahead, behind = plain[: len(plain) // 2], plain[len(plain) // 2 :]
    down_got, up_got = [], []
    for i in range(bits):
        piece = halving(down_pieces, down_got, i)
        if i == 1:
            send(ahead)
        if i == bits - 2:
            piece = after(piece, *got(ahead[: len(ahead) // 2]))
        if i == bits - 1:
            piece = after(piece, *got(ahead))
            send(near, down_got[-1])
            for j in range(2):
                part = after(halving(up_pieces, up_got, j), down_got[-1])
                up_got.append(swap(part, 1 << j))
        down_got.append(swap(piece, 1 << i))
    gathered = halving(down_pieces, down_got, bits)
    for i in reversed(range(bits)):
        if i == bits - 2:
            gathered = after(gathered, *got(near[:2]))
            send(behind[: len(behind) // 2], gathered)
        if i == 1:
            gathered = after(gathered, *got(near), *up_got)
            send(behind[len(behind) // 2 :], gathered)
            send(side[: len(side) // 4], gathered)
        if i == 0:
            gathered = after(gathered, *got(behind[: len(behind) // 2]))
            send(crossed[: len(crossed) // 4], gathered)
        gathered = jnp.concatenate([gathered, swap(gathered, 1 << i)], axis=0)
    gathered = after(gathered, *got(behind))

    low = pl.pallas_call(
        functools.partial(low_rank_kernel, shape),
        in_specs=[SMEM, VMEM, VMEM],
        out_specs=VMEM,
        scratch_shapes=[pltpu.VMEM((videos, ranks, model_width), jnp.bfloat16)],
        out_shape=jax.ShapeDtypeStruct((toks, videos * ranks), jnp.bfloat16),
        compiler_params=pltpu.CompilerParams(vmem_limit_bytes=24 << 20),
        cost_estimate=pl.CostEstimate(
            flops=2 * videos * toks * ranks * model_width,
            bytes_accessed=2 * videos * (toks + ranks) * model_width,
            transcendentals=0,
        ),
        name="low_rank",
    )(me, normed_token_features, gathered)
    send(crossed[len(crossed) // 4 : len(crossed) // 2], low)
    far = jnp.stack([low] + [swap(low, LOW * i) for i in range(1, devs // LOW)])
    far = after(far, *got(crossed[: len(crossed) // 4]), *got(side[: len(side) // 4]))
    send(crossed[len(crossed) // 2 :], far)
    send(side[len(side) // 4 :], far)
    for i in range(2, bits):
        piece = after(halving(up_pieces, up_got, i), low)
        up_got.append(swap(piece, 1 << i))
    up_here = halving(up_pieces, up_got, bits).reshape(pairs, ranks, LANES)
    lows = [far] + [swap(far, i) for i in range(1, LOW)]
    late = {k: swap(after(late[k], far), k) for k in crossed}

    low_specs = [pl.BlockSpec((devs // LOW, toks, videos * ranks), lambda p: (0, 0, 0))] * LOW
    up_spec = pl.BlockSpec((pl.squeezed, ranks, LANES), lambda p: (p, 0, 0))
    all_spec = pl.BlockSpec((pl.squeezed, length, width), lambda p: (p, 0, 0))
    pair_spec = pl.BlockSpec((2, pl.squeezed, toks, width), lambda p: (0, p, 0, 0))
    keys, vals = pl.pallas_call(
        functools.partial(prepare_kernel, devs, per_video),
        grid=(pairs,),
        in_specs=[SMEM, up_spec, *low_specs]
        + [pl.BlockSpec((2, pl.squeezed, toks, width), lambda p: (0, p, 0, 0))] * devs,
        out_specs=[all_spec] * 2,
        out_shape=[jax.ShapeDtypeStruct((pairs, length, width), jnp.bfloat16)] * 2,
        compiler_params=pltpu.CompilerParams(vmem_limit_bytes=40 << 20),
        cost_estimate=pl.CostEstimate(
            flops=2 * pairs * length * width * videos * ranks,
            bytes_accessed=8 * pairs * length * width,
            transcendentals=0,
        ),
        name="prepare",
    )(me, up_here, *lows, *blocks)

    def query_spec(k):
        first = 0 if k in late else 2
        return pl.BlockSpec((pl.squeezed, pl.squeezed, toks, width), lambda p: (first, p, 0, 0))

    def attend(ks, me):
        count = len(ks)
        return pl.pallas_call(
            functools.partial(
                attend_kernel, ks, math.gcd(count, max(1, 256 // toks)), per_video
            ),
            grid=(pairs,),
            in_specs=[SMEM, up_spec, all_spec, all_spec, *low_specs] + [query_spec(k) for k in ks],
            out_specs=[pair_spec] * (count // 2),
            out_shape=[jax.ShapeDtypeStruct((2, pairs, toks, width), jnp.bfloat16)] * (count // 2),
            compiler_params=pltpu.CompilerParams(vmem_limit_bytes=40 << 20),
            cost_estimate=pl.CostEstimate(
                flops=4 * pairs * count * toks * length * width,
                bytes_accessed=4 * pairs * (count * toks + length) * width,
                transcendentals=pairs * count * toks * length,
            ),
            name="attend",
        )(me, up_here, keys, vals, *lows, *(late.get(k, blocks[k]) for k in ks))

    order, back, across = [], [], []
    turn = me
    for ks in (plain, crossed, side, [0] + near):
        outs = attend(ks, turn)
        turn = after(me, outs[0])
        for k, out in zip(ks[::2], outs):
            order.append(k)
            back.append(swap(out, k) if k else out)
    half = len(order) // 2
    for part in (back[:half], back[half:]):
        across.append(swap(jnp.stack([t[1] for t in part]), 1))

    out = pl.pallas_call(
        functools.partial(unpack_kernel, devs, pairs, order),
        in_specs=[SMEM] + [VMEM] * (len(back) + len(across)),
        out_specs=VMEM,
        out_shape=jax.ShapeDtypeStruct((devs * pairs, toks, width), jnp.bfloat16),
        compiler_params=pltpu.CompilerParams(vmem_limit_bytes=24 << 20),
        cost_estimate=pl.CostEstimate(
            flops=0, bytes_accessed=4 * pairs * length * width, transcendentals=0
        ),
        name="unpack",
    )(me, *back, *across)
    return out.reshape(videos, heads, toks, width)


def solution(mesh):
    in_specs = (
        P("grp", "seq", None),
        P("grp", None, "seq", None),
        P("grp", None, "seq", None),
        P("grp", None, "seq", None),
        P("seq", None, None),
        P("seq", None, None),
        P(),
        P("grp"),
    )
    out_specs = P("grp", None, "seq", None)
    return jax.shard_map(body, mesh=mesh, in_specs=in_specs, out_specs=out_specs, check_vma=False)
```

```python
import functools
import math

import jax
import jax.numpy as jnp
from jax import lax
from jax.experimental import pallas as pl
from jax.experimental.pallas import tpu as pltpu
from jax.sharding import PartitionSpec as P

LANES = 128
ANY = pl.BlockSpec(memory_space=pl.ANY)
VMEM = pl.BlockSpec(memory_space=pltpu.VMEM)
SMEM = pl.BlockSpec(memory_space=pltpu.SMEM)


def bit_count(n):
    bits = n.bit_length() - 1
    assert 1 << bits == n
    return bits


def reversed_bits(j, bits):
    out = 0
    for i in range(bits):
        out = out | (((j >> i) & 1) << (bits - 1 - i))
    return out


def pick_kernel(shape, me_ref, row_ref, req_ref, down_ref, up_ref, *refs):
    devs, bits, per_video, pairs, col_split, rows, tiles = shape
    downs, ups = refs[: bits + 1], refs[bits + 1 : 2 * bits + 2]
    down, up, sems = refs[2 * bits + 2 :]
    slots, ranks, _ = down_ref.shape
    videos = down.shape[0]
    me = me_ref[0]
    for s in range(videos):
        place = row_ref[req_ref[s]]
        slot = place % slots
        owned = place // slots == me
        copies = [
            pltpu.make_async_copy(down_ref.at[slot], down.at[s], sems.at[2 * s]),
            pltpu.make_async_copy(up_ref.at[slot], up.at[s], sems.at[2 * s + 1]),
        ]

        @pl.when(owned)
        def _():
            for copy in copies:
                copy.start()
            for copy in copies:
                copy.wait()

        @pl.when(jnp.logical_not(owned))
        def _():
            down[s] = jnp.zeros(down.shape[1:], down.dtype)
            up[s] = jnp.zeros(up.shape[1:], up.dtype)

    for j in range(devs):
        step = bits - j.bit_length()
        at = j - (1 << (j.bit_length() - 1)) if j else 0
        dev = me ^ reversed_bits(j, bits)
        video = dev // per_video
        place = dev % per_video
        row = pl.multiple_of((place // col_split) * rows, rows)
        for t in range(tiles):
            col = pl.multiple_of(((place % col_split) * tiles + t) * LANES, LANES)
            downs[step][at, t * rows : (t + 1) * rows, :] = down[
                video, pl.ds(row, rows), pl.ds(col, LANES)
            ]
        for p in range(pairs):
            col = pl.multiple_of((place * pairs + p) * LANES, LANES)
            ups[step][at, p * ranks : (p + 1) * ranks, :] = up[video, :, pl.ds(col, LANES)]


def low_rank_kernel(shape, x_ref, g_ref, q_ref, out_ref, down):
    devs, _, per_video, _, col_split, rows, tiles = shape
    for dev in range(devs):
        video = dev // per_video
        place = dev % per_video
        row = (place // col_split) * rows
        for t in range(tiles):
            col = ((place % col_split) * tiles + t) * LANES
            down[video, row : row + rows, col : col + LANES] = g_ref[
                dev, t * rows : (t + 1) * rows, :
            ]
    first = q_ref.shape[1]
    out_ref[:, :first] = q_ref[...]
    for s in range(x_ref.shape[0]):
        low = lax.dot_general(
            x_ref[s], down[s], (((1,), (1,)), ((), ())), preferred_element_type=jnp.float32
        ).astype(out_ref.dtype)
        half = low.shape[0] // 2
        low = jnp.concatenate([low[:half], low[half:]], axis=1)
        for dev in range(s * per_video, (s + 1) * per_video):
            out_ref[dev, first:] = low


def add_delta(base, low, up, second):
    devs, toks, width = base.shape
    ranks = up.shape[0]
    row = lax.broadcasted_iota(jnp.int32, up.shape, 0)
    part = jnp.where(row // (ranks // 2) == second, up, jnp.zeros_like(up))
    none = jnp.zeros_like(part)
    deltas = [
        jnp.dot(low, jnp.concatenate(pair, axis=0), preferred_element_type=jnp.float32)
        for pair in ((part, none), (none, part))
    ]
    delta = jnp.concatenate([d.reshape(devs, toks // 2, width) for d in deltas], axis=1)
    return (base.astype(jnp.float32) + delta).astype(base.dtype).reshape(devs * toks, width)


def attend_kernel(block, up_ref, q_ref, low_ref, k_ref, v_ref, out_ref, q_mix):
    devs, toks, width = q_ref.shape
    length = devs * toks
    low = low_ref[...].reshape(length // 2, low_ref.shape[2])
    up = up_ref[...]
    keys = k_ref[...].reshape(length, width)
    vals = add_delta(v_ref[...], low, up, 1)
    q_mix[...] = add_delta(q_ref[...], low, up, 0)
    scale = math.log2(math.e) / math.sqrt(width)
    for b in range(0, devs, block):
        q = q_mix[b * toks : (b + block) * toks, :]
        scores = lax.dot_general(
            q, keys, (((1,), (1,)), ((), ())), preferred_element_type=jnp.float32
        )
        top = jnp.max(scores, axis=1, keepdims=True)
        weights = jnp.exp2((scores - top) * scale)
        total = jnp.sum(weights, axis=1, keepdims=True)
        mixed = jnp.dot(weights.astype(jnp.bfloat16), vals, preferred_element_type=jnp.float32)
        out_ref[b : b + block] = (mixed / total).astype(jnp.bfloat16).reshape(block, toks, width)


def body(
    normed_token_features,
    queries,
    projected_keys,
    values,
    adapter_down_factors,
    adapter_up_factors,
    adapter_store_row,
    requests,
):
    videos, toks, model_width = normed_token_features.shape
    heads = queries.shape[1]
    width = queries.shape[3]
    _, ranks, up_width = adapter_up_factors.shape
    devs = lax.axis_size("seq")
    bits = bit_count(devs)
    me = lax.axis_index("seq").astype(jnp.int32)[None]
    pairs = videos * heads // devs
    per_video = devs // videos
    length = devs * toks
    col_split = math.gcd(per_video, model_width // LANES)
    rows = ranks * col_split // per_video
    tiles = model_width // col_split // LANES
    shape = (devs, bits, per_video, pairs, col_split, rows, tiles)

    def swap(tensor, k):
        return lax.ppermute(tensor, "seq", [(i, i ^ k) for i in range(devs)])

    def exchange(tensor):
        return lax.all_to_all(tensor, "seq", split_axis=0, concat_axis=0, tiled=True)

    def by_pairs(tensor):
        return tensor.reshape(devs, pairs, toks, width)

    def after(array, *others):
        return lax.optimization_barrier((array, others))[0]

    def halving(parts, received, i):
        h = devs >> (i + 1) if i < bits else 0
        size = max(h, 1)
        return sum((r[h : h + size] for r in received), parts[i])

    keys = exchange(by_pairs(projected_keys))

    steps = [devs >> (i + 1) for i in range(bits)] + [1]
    piece_shapes = [(h, tiles * rows, LANES) for h in steps] + [
        (h, pairs * ranks, LANES) for h in steps
    ]
    pieces = pl.pallas_call(
        functools.partial(pick_kernel, shape),
        in_specs=[SMEM, SMEM, SMEM, ANY, ANY],
        out_specs=[VMEM] * (2 * bits + 2),
        out_shape=[jax.ShapeDtypeStruct(s, jnp.bfloat16) for s in piece_shapes],
        scratch_shapes=[
            pltpu.VMEM((videos, ranks, model_width), jnp.bfloat16),
            pltpu.VMEM((videos, ranks, up_width), jnp.bfloat16),
            pltpu.SemaphoreType.DMA((2 * videos,)),
        ],
        compiler_params=pltpu.CompilerParams(vmem_limit_bytes=24 << 20),
        cost_estimate=pl.CostEstimate(
            flops=0,
            bytes_accessed=4 * videos * ranks * (model_width + up_width),
            transcendentals=0,
        ),
        name="pick_factors",
    )(me, adapter_store_row, requests, adapter_down_factors, adapter_up_factors)
    down_pieces, up_pieces = pieces[: bits + 1], pieces[bits + 1 :]

    down_got, up_got = [], []
    for i in range(bits):
        piece = halving(down_pieces, down_got, i)
        if i == 2:
            piece = after(piece, keys)
        down_got.append(swap(piece, 1 << i))
        up_got.append(swap(after(halving(up_pieces, up_got, i), piece), 1 << i))
    shard = halving(down_pieces, down_got, bits)
    up_here = halving(up_pieces, up_got, bits).reshape(pairs, ranks, LANES)
    gathered = lax.all_gather(shard, "seq", axis=0, tiled=True)
    vals = exchange(after(by_pairs(values), shard))

    asked = pl.pallas_call(
        functools.partial(low_rank_kernel, shape),
        in_specs=[VMEM, VMEM, VMEM],
        out_specs=VMEM,
        scratch_shapes=[pltpu.VMEM((videos, ranks, model_width), jnp.bfloat16)],
        out_shape=jax.ShapeDtypeStruct((devs, pairs * toks + toks // 2, width), jnp.bfloat16),
        compiler_params=pltpu.CompilerParams(vmem_limit_bytes=24 << 20),
        cost_estimate=pl.CostEstimate(
            flops=2 * videos * toks * ranks * model_width,
            bytes_accessed=2 * videos * (toks + ranks) * model_width,
            transcendentals=0,
        ),
        name="low_rank",
    )(
        normed_token_features,
        after(gathered, vals, up_here),
        queries.reshape(devs, pairs * toks, width),
    )
    asked = exchange(asked)

    part_spec = pl.BlockSpec((devs, pl.squeezed, toks, width), lambda p: (0, p, 0, 0))
    mixed = pl.pallas_call(
        functools.partial(attend_kernel, math.gcd(devs, max(1, 512 // toks))),
        grid=(pairs,),
        in_specs=[
            pl.BlockSpec((pl.squeezed, ranks, LANES), lambda p: (p, 0, 0)),
            pl.BlockSpec((devs, toks, width), lambda p: (0, p, 0)),
            pl.BlockSpec((devs, toks // 2, width), lambda p: (0, 2 * pairs, 0)),
            part_spec,
            part_spec,
        ],
        out_specs=part_spec,
        out_shape=jax.ShapeDtypeStruct((devs, pairs, toks, width), jnp.bfloat16),
        scratch_shapes=[pltpu.VMEM((length, width), jnp.bfloat16)],
        compiler_params=pltpu.CompilerParams(vmem_limit_bytes=48 << 20),
        cost_estimate=pl.CostEstimate(
            flops=4 * pairs * length * length * width,
            bytes_accessed=8 * pairs * length * width,
            transcendentals=pairs * length * length,
        ),
        name="attend",
    )(up_here, asked, asked, keys, vals)
    return exchange(mixed).reshape(videos, heads, toks, width)


def solution(mesh):
    in_specs = (
        P("grp", "seq", None),
        P("grp", None, "seq", None),
        P("grp", None, "seq", None),
        P("grp", None, "seq", None),
        P("seq", None, None),
        P("seq", None, None),
        P(),
        P("grp"),
    )
    out_specs = P("grp", None, "seq", None)
    return jax.shard_map(body, mesh=mesh, in_specs=in_specs, out_specs=out_specs, check_vma=False)
```

```python
import functools
import math

import jax
import jax.numpy as jnp
from jax import lax
from jax.experimental import pallas as pl
from jax.experimental.pallas import tpu as pltpu
from jax.sharding import PartitionSpec as P

LANES = 128
LOW = 4
ANY = pl.BlockSpec(memory_space=pl.ANY)
VMEM = pl.BlockSpec(memory_space=pltpu.VMEM)
SMEM = pl.BlockSpec(memory_space=pltpu.SMEM)


def bit_count(n):
    bits = n.bit_length() - 1
    assert 1 << bits == n
    return bits


def reversed_bits(j, bits):
    out = 0
    for i in range(bits):
        out = out | (((j >> i) & 1) << (bits - 1 - i))
    return out


def pick_kernel(shape, me_ref, row_ref, req_ref, down_ref, up_ref, *refs):
    devs, bits, per_video, pairs, col_split, rows, tiles = shape
    downs, ups = refs[: bits + 1], refs[bits + 1 : 2 * bits + 2]
    down, up, sems = refs[2 * bits + 2 :]
    slots, ranks, _ = down_ref.shape
    videos = down.shape[0]
    me = me_ref[0]
    for s in range(videos):
        place = row_ref[req_ref[s]]
        slot = place % slots
        owned = place // slots == me
        copies = [
            pltpu.make_async_copy(down_ref.at[slot], down.at[s], sems.at[2 * s]),
            pltpu.make_async_copy(up_ref.at[slot], up.at[s], sems.at[2 * s + 1]),
        ]

        @pl.when(owned)
        def _():
            for copy in copies:
                copy.start()
            for copy in copies:
                copy.wait()

        @pl.when(jnp.logical_not(owned))
        def _():
            down[s] = jnp.zeros(down.shape[1:], down.dtype)
            up[s] = jnp.zeros(up.shape[1:], up.dtype)

    for j in range(devs):
        step = bits - j.bit_length()
        at = j - (1 << (j.bit_length() - 1)) if j else 0
        dev = me ^ reversed_bits(j, bits)
        video = dev // per_video
        place = dev % per_video
        row = pl.multiple_of((place // col_split) * rows, rows)
        for t in range(tiles):
            col = pl.multiple_of(((place % col_split) * tiles + t) * LANES, LANES)
            downs[step][at, t * rows : (t + 1) * rows, :] = down[
                video, pl.ds(row, rows), pl.ds(col, LANES)
            ]
        for p in range(pairs):
            col = pl.multiple_of((place * pairs + p) * LANES, LANES)
            ups[step][at, p * ranks : (p + 1) * ranks, :] = up[video, :, pl.ds(col, LANES)]


def low_rank_kernel(shape, me_ref, x_ref, g_ref, out_ref, down):
    devs, bits, per_video, _, col_split, rows, tiles = shape
    for j in range(devs):
        dev = me_ref[0] ^ reversed_bits(j, bits)
        video = dev // per_video
        place = dev % per_video
        row = pl.multiple_of((place // col_split) * rows, rows)
        for t in range(tiles):
            col = pl.multiple_of(((place % col_split) * tiles + t) * LANES, LANES)
            down[video, pl.ds(row, rows), pl.ds(col, LANES)] = g_ref[j, t * rows : (t + 1) * rows, :]
    parts = [
        lax.dot_general(
            x_ref[s], down[s], (((1,), (1,)), ((), ())), preferred_element_type=jnp.float32
        )
        for s in range(x_ref.shape[0])
    ]
    out_ref[...] = jnp.concatenate(parts, axis=1).astype(out_ref.dtype)


def up_part(up_ref, video, videos, second):
    up = jnp.concatenate([up_ref[...]] * videos, axis=0)
    ranks = up_ref.shape[0]
    row = lax.broadcasted_iota(jnp.int32, up.shape, 0)
    half = (row % ranks) // (ranks // 2)
    keep = (row // ranks == video) & (half == second)
    return jnp.where(keep, up, jnp.zeros_like(up))


def attend_kernel(per_video, block, me_ref, up_ref, q_ref, k_ref, v_ref, *refs):
    low_refs, out_ref, low, q_mix = refs[:LOW], refs[LOW], refs[LOW + 1], refs[LOW + 2]
    devs, toks, width = q_ref.shape
    length = devs * toks
    videos = low.shape[2] // up_ref.shape[0]
    me = me_ref[0]
    for k in range(devs):
        low[me ^ k] = low_refs[k % LOW][k // LOW]
    low_all = low[...].reshape(length, low.shape[2])
    up_q, up_v = (up_part(up_ref, me // per_video, videos, i) for i in range(2))
    keys = k_ref[...].reshape(length, width)
    delta_v = jnp.dot(low_all, up_v, preferred_element_type=jnp.float32)
    vals = (v_ref[...].reshape(length, width).astype(jnp.float32) + delta_v).astype(jnp.bfloat16)
    delta_q = jnp.dot(low_all, up_q, preferred_element_type=jnp.float32)
    q_mix[...] = (q_ref[...].reshape(length, width).astype(jnp.float32) + delta_q).astype(
        jnp.bfloat16
    )
    scale = math.log2(math.e) / math.sqrt(width)
    for b in range(0, devs, block):
        q = q_mix[b * toks : (b + block) * toks, :]
        scores = lax.dot_general(
            q, keys, (((1,), (1,)), ((), ())), preferred_element_type=jnp.float32
        )
        top = jnp.max(scores, axis=1, keepdims=True)
        weights = jnp.exp2((scores - top) * scale)
        total = jnp.sum(weights, axis=1, keepdims=True)
        mixed = jnp.dot(weights.astype(jnp.bfloat16), vals, preferred_element_type=jnp.float32)
        out_ref[b : b + block] = (mixed / total).astype(jnp.bfloat16).reshape(block, toks, width)


def body(
    normed_token_features,
    queries,
    projected_keys,
    values,
    adapter_down_factors,
    adapter_up_factors,
    adapter_store_row,
    requests,
):
    videos, toks, model_width = normed_token_features.shape
    heads = queries.shape[1]
    width = queries.shape[3]
    _, ranks, up_width = adapter_up_factors.shape
    devs = lax.axis_size("seq")
    bits = bit_count(devs)
    me = lax.axis_index("seq").astype(jnp.int32)[None]
    pairs = videos * heads // devs
    per_video = devs // videos
    length = devs * toks
    col_split = math.gcd(per_video, model_width // LANES)
    rows = ranks * col_split // per_video
    tiles = model_width // col_split // LANES
    shape = (devs, bits, per_video, pairs, col_split, rows, tiles)

    def swap(tensor, k):
        return lax.ppermute(tensor, "seq", [(i, i ^ k) for i in range(devs)])

    def exchange(tensor):
        return lax.all_to_all(tensor, "seq", split_axis=0, concat_axis=0, tiled=True)

    def by_pairs(tensor):
        return tensor.reshape(devs, pairs, toks, width)

    def after(array, *others):
        return lax.optimization_barrier((array, others))[0]

    def halving(parts, received, i):
        h = devs >> (i + 1) if i < bits else 0
        size = max(h, 1)
        return sum((r[h : h + size] for r in received), parts[i])

    keys = exchange(by_pairs(projected_keys))

    steps = [devs >> (i + 1) for i in range(bits)] + [1]
    piece_shapes = [(h, tiles * rows, LANES) for h in steps] + [
        (h, pairs * ranks, LANES) for h in steps
    ]
    pieces = pl.pallas_call(
        functools.partial(pick_kernel, shape),
        in_specs=[SMEM, SMEM, SMEM, ANY, ANY],
        out_specs=[VMEM] * (2 * bits + 2),
        out_shape=[jax.ShapeDtypeStruct(s, jnp.bfloat16) for s in piece_shapes],
        scratch_shapes=[
            pltpu.VMEM((videos, ranks, model_width), jnp.bfloat16),
            pltpu.VMEM((videos, ranks, up_width), jnp.bfloat16),
            pltpu.SemaphoreType.DMA((2 * videos,)),
        ],
        compiler_params=pltpu.CompilerParams(vmem_limit_bytes=24 << 20),
        cost_estimate=pl.CostEstimate(
            flops=0,
            bytes_accessed=4 * videos * ranks * (model_width + up_width),
            transcendentals=0,
        ),
        name="pick_factors",
    )(me, adapter_store_row, requests, adapter_down_factors, adapter_up_factors)
    down_pieces, up_pieces = pieces[: bits + 1], pieces[bits + 1 :]

    down_got, up_got = [], []

    def send_up(i, *others):
        up_got.append(swap(after(halving(up_pieces, up_got, i), *others), 1 << i))

    for i in range(bits):
        piece = halving(down_pieces, down_got, i)
        if i == 2:
            piece = after(piece, keys)
        if i >= 2:
            piece = after(piece, up_got[i - 2])
        if 0 < i < bits - 1:
            send_up(i - 1, piece)
        down_got.append(swap(piece, 1 << i))
    gathered = halving(down_pieces, down_got, bits)
    for i in reversed(range(bits)):
        if i >= bits - 3:
            gathered = after(gathered, up_got[2 * bits - 4 - i])
        if i >= bits - 2:
            send_up(2 * bits - 3 - i, gathered)
        if i == 1:
            up_here = halving(up_pieces, up_got, bits).reshape(pairs, ranks, LANES)
            asked = jnp.concatenate([by_pairs(values), by_pairs(queries)], axis=1)
            asked = exchange(after(asked, gathered, up_here))
        gathered = jnp.concatenate([gathered, swap(gathered, 1 << i)], axis=0)

    low = pl.pallas_call(
        functools.partial(low_rank_kernel, shape),
        in_specs=[SMEM, VMEM, VMEM],
        out_specs=VMEM,
        scratch_shapes=[pltpu.VMEM((videos, ranks, model_width), jnp.bfloat16)],
        out_shape=jax.ShapeDtypeStruct((toks, videos * ranks), jnp.bfloat16),
        compiler_params=pltpu.CompilerParams(vmem_limit_bytes=24 << 20),
        cost_estimate=pl.CostEstimate(
            flops=2 * videos * toks * ranks * model_width,
            bytes_accessed=2 * videos * (toks + ranks) * model_width,
            transcendentals=0,
        ),
        name="low_rank",
    )(me, normed_token_features, gathered)
    far = jnp.stack([low] + [swap(low, LOW * i) for i in range(1, devs // LOW)])
    lows = [far] + [swap(far, i) for i in range(1, LOW)]

    low_spec = pl.BlockSpec((devs // LOW, toks, videos * ranks), lambda p: (0, 0, 0))
    part_spec = pl.BlockSpec((devs, pl.squeezed, toks, width), lambda p: (0, p, 0, 0))
    later_spec = pl.BlockSpec((devs, pl.squeezed, toks, width), lambda p: (0, pairs + p, 0, 0))
    mixed = pl.pallas_call(
        functools.partial(attend_kernel, per_video, math.gcd(devs, max(1, 512 // toks))),
        grid=(pairs,),
        in_specs=[SMEM, pl.BlockSpec((pl.squeezed, ranks, LANES), lambda p: (p, 0, 0))]
        + [later_spec, part_spec, part_spec]
        + [low_spec] * LOW,
        out_specs=part_spec,
        out_shape=jax.ShapeDtypeStruct((devs, pairs, toks, width), jnp.bfloat16),
        scratch_shapes=[
            pltpu.VMEM((devs, toks, videos * ranks), jnp.bfloat16),
            pltpu.VMEM((length, width), jnp.bfloat16),
        ],
        compiler_params=pltpu.CompilerParams(vmem_limit_bytes=48 << 20),
        cost_estimate=pl.CostEstimate(
            flops=4 * pairs * length * length * width,
            bytes_accessed=8 * pairs * length * width,
            transcendentals=pairs * length * length,
        ),
        name="attend",
    )(me, up_here, asked, keys, asked, *lows)
    return exchange(mixed).reshape(videos, heads, toks, width)


def solution(mesh):
    in_specs = (
        P("grp", "seq", None),
        P("grp", None, "seq", None),
        P("grp", None, "seq", None),
        P("grp", None, "seq", None),
        P("seq", None, None),
        P("seq", None, None),
        P(),
        P("grp"),
    )
    out_specs = P("grp", None, "seq", None)
    return jax.shard_map(body, mesh=mesh, in_specs=in_specs, out_specs=out_specs, check_vma=False)
```

```python
import functools
import math

import jax
import jax.numpy as jnp
from jax import lax
from jax.experimental import pallas as pl
from jax.experimental.pallas import tpu as pltpu
from jax.sharding import PartitionSpec as P

LANES = 128
LOW = 4
ANY = pl.BlockSpec(memory_space=pl.ANY)
VMEM = pl.BlockSpec(memory_space=pltpu.VMEM)
SMEM = pl.BlockSpec(memory_space=pltpu.SMEM)


def bit_count(n):
    bits = n.bit_length() - 1
    assert 1 << bits == n
    return bits


def reversed_bits(j, bits):
    out = 0
    for i in range(bits):
        out = out | (((j >> i) & 1) << (bits - 1 - i))
    return out


def pick_kernel(shape, me_ref, row_ref, req_ref, down_ref, up_ref, *refs):
    devs, bits, per_video, pairs, col_split, rows, tiles = shape
    downs, ups = refs[:bits], refs[bits : 2 * bits + 1]
    down, up, sems = refs[2 * bits + 1 :]
    slots, ranks, _ = down_ref.shape
    videos = down.shape[0]
    me = me_ref[0]
    for s in range(videos):
        place = row_ref[req_ref[s]]
        slot = place % slots
        owned = place // slots == me
        copies = [
            pltpu.make_async_copy(down_ref.at[slot], down.at[s], sems.at[2 * s]),
            pltpu.make_async_copy(up_ref.at[slot], up.at[s], sems.at[2 * s + 1]),
        ]

        @pl.when(owned)
        def _():
            for copy in copies:
                copy.start()
            for copy in copies:
                copy.wait()

        @pl.when(jnp.logical_not(owned))
        def _():
            down[s] = jnp.zeros(down.shape[1:], down.dtype)
            up[s] = jnp.zeros(up.shape[1:], up.dtype)

    for j in range(devs):
        step = bits - j.bit_length()
        at = j - (1 << (j.bit_length() - 1)) if j else 0
        dev = me ^ reversed_bits(j, bits)
        video = dev // per_video
        place = dev % per_video
        row = pl.multiple_of((place // col_split) * rows, rows)
        for t in range(tiles):
            col = pl.multiple_of(((place % col_split) * tiles + t) * LANES, LANES)
            downs[min(step, bits - 1)][at if j > 1 else j, t * rows : (t + 1) * rows, :] = down[
                video, pl.ds(row, rows), pl.ds(col, LANES)
            ]
        for p in range(pairs):
            col = pl.multiple_of((place * pairs + p) * LANES, LANES)
            ups[step][at, p * ranks : (p + 1) * ranks, :] = up[video, :, pl.ds(col, LANES)]


def low_rank_kernel(shape, me_ref, x_ref, g_ref, out_ref, down):
    devs, bits, per_video, _, col_split, rows, tiles = shape
    for j in range(devs):
        dev = me_ref[0] ^ reversed_bits(j, bits)
        video = dev // per_video
        place = dev % per_video
        row = pl.multiple_of((place // col_split) * rows, rows)
        for t in range(tiles):
            col = pl.multiple_of(((place % col_split) * tiles + t) * LANES, LANES)
            down[video, pl.ds(row, rows), pl.ds(col, LANES)] = g_ref[j, t * rows : (t + 1) * rows, :]
    parts = [
        lax.dot_general(
            x_ref[s], down[s], (((1,), (1,)), ((), ())), preferred_element_type=jnp.float32
        )
        for s in range(x_ref.shape[0])
    ]
    out_ref[...] = jnp.concatenate(parts, axis=1).astype(out_ref.dtype)


def up_part(up_ref, video, videos, second):
    up = jnp.concatenate([up_ref[...]] * videos, axis=0)
    ranks = up_ref.shape[0]
    row = lax.broadcasted_iota(jnp.int32, up.shape, 0)
    half = (row % ranks) // (ranks // 2)
    keep = (row // ranks == video) & (half == second)
    return jnp.where(keep, up, jnp.zeros_like(up))


def attend_kernel(per_video, block, me_ref, up_ref, q_ref, k_ref, v_ref, *refs):
    low_refs, out_ref, low, q_mix = refs[:LOW], refs[LOW], refs[LOW + 1], refs[LOW + 2]
    devs, toks, width = q_ref.shape
    length = devs * toks
    videos = low.shape[2] // up_ref.shape[0]
    me = me_ref[0]
    for k in range(devs):
        low[me ^ k] = low_refs[k % LOW][k // LOW]
    low_all = low[...].reshape(length, low.shape[2])
    up_q, up_v = (up_part(up_ref, me // per_video, videos, i) for i in range(2))
    keys = k_ref[...].reshape(length, width)
    delta_v = jnp.dot(low_all, up_v, preferred_element_type=jnp.float32)
    vals = (v_ref[...].reshape(length, width).astype(jnp.float32) + delta_v).astype(jnp.bfloat16)
    delta_q = jnp.dot(low_all, up_q, preferred_element_type=jnp.float32)
    q_mix[...] = (q_ref[...].reshape(length, width).astype(jnp.float32) + delta_q).astype(
        jnp.bfloat16
    )
    scale = math.log2(math.e) / math.sqrt(width)
    for b in range(0, devs, block):
        q = q_mix[b * toks : (b + block) * toks, :]
        scores = lax.dot_general(
            q, keys, (((1,), (1,)), ((), ())), preferred_element_type=jnp.float32
        )
        top = jnp.max(scores, axis=1, keepdims=True)
        weights = jnp.exp2((scores - top) * scale)
        total = jnp.sum(weights, axis=1, keepdims=True)
        mixed = jnp.dot(weights.astype(jnp.bfloat16), vals, preferred_element_type=jnp.float32)
        out_ref[b : b + block] = (mixed / total).astype(jnp.bfloat16).reshape(block, toks, width)


def body(
    normed_token_features,
    queries,
    projected_keys,
    values,
    adapter_down_factors,
    adapter_up_factors,
    adapter_store_row,
    requests,
):
    videos, toks, model_width = normed_token_features.shape
    heads = queries.shape[1]
    width = queries.shape[3]
    _, ranks, up_width = adapter_up_factors.shape
    devs = lax.axis_size("seq")
    bits = bit_count(devs)
    me = lax.axis_index("seq").astype(jnp.int32)[None]
    pairs = videos * heads // devs
    per_video = devs // videos
    length = devs * toks
    col_split = math.gcd(per_video, model_width // LANES)
    rows = ranks * col_split // per_video
    tiles = model_width // col_split // LANES
    shape = (devs, bits, per_video, pairs, col_split, rows, tiles)

    def swap(tensor, k):
        return lax.ppermute(tensor, "seq", [(i, i ^ k) for i in range(devs)])

    def exchange(tensor):
        return lax.all_to_all(tensor, "seq", split_axis=0, concat_axis=0, tiled=True)

    def by_pairs(tensor):
        return tensor.reshape(devs, pairs, toks, width)

    def after(array, *others):
        return lax.optimization_barrier((array, others))[0]

    def halving(parts, received, i):
        h = devs >> (i + 1) if i < bits else 0
        size = max(h, 1)
        return sum((r[h : h + size] for r in received), parts[i])

    keys = exchange(by_pairs(projected_keys))

    steps = [devs >> (i + 1) for i in range(bits)] + [1]
    piece_shapes = [(h, tiles * rows, LANES) for h in steps[: bits - 1] + [2]] + [
        (h, pairs * ranks, LANES) for h in steps
    ]
    pieces = pl.pallas_call(
        functools.partial(pick_kernel, shape),
        in_specs=[SMEM, SMEM, SMEM, ANY, ANY],
        out_specs=[VMEM] * (2 * bits + 1),
        out_shape=[jax.ShapeDtypeStruct(s, jnp.bfloat16) for s in piece_shapes],
        scratch_shapes=[
            pltpu.VMEM((videos, ranks, model_width), jnp.bfloat16),
            pltpu.VMEM((videos, ranks, up_width), jnp.bfloat16),
            pltpu.SemaphoreType.DMA((2 * videos,)),
        ],
        compiler_params=pltpu.CompilerParams(vmem_limit_bytes=24 << 20),
        cost_estimate=pl.CostEstimate(
            flops=0,
            bytes_accessed=4 * videos * ranks * (model_width + up_width),
            transcendentals=0,
        ),
        name="pick_factors",
    )(me, adapter_store_row, requests, adapter_down_factors, adapter_up_factors)
    down_pieces, up_pieces = pieces[:bits], pieces[bits:]

    down_got, up_got = [], []

    def send_up(i, *others):
        up_got.append(swap(after(halving(up_pieces, up_got, i), *others), 1 << i))

    for i in range(bits - 1):
        piece = halving(down_pieces, down_got, i)
        if i == 1:
            send_up(0, piece)
        if i == 2:
            piece = after(piece, keys, up_got[0])
        down_got.append(swap(piece, 1 << i))
    gathered = sum((r[:2] for r in down_got), down_pieces[-1])
    other = swap(gathered, 1 << (bits - 1))
    gathered = gathered + jnp.concatenate([other[1:], other[:1]], axis=0)
    for i in reversed(range(bits - 1)):
        if i == 1:
            asked = jnp.concatenate([by_pairs(values), by_pairs(queries)], axis=1)
            asked = exchange(after(asked, gathered))
            send_up(1, gathered)
        if i == 0:
            gathered = after(gathered, up_got[1])
            for j in range(2, bits - 1):
                send_up(j, gathered)
        gathered = jnp.concatenate([gathered, swap(gathered, 1 << i)], axis=0)

    low = pl.pallas_call(
        functools.partial(low_rank_kernel, shape),
        in_specs=[SMEM, VMEM, VMEM],
        out_specs=VMEM,
        scratch_shapes=[pltpu.VMEM((videos, ranks, model_width), jnp.bfloat16)],
        out_shape=jax.ShapeDtypeStruct((toks, videos * ranks), jnp.bfloat16),
        compiler_params=pltpu.CompilerParams(vmem_limit_bytes=24 << 20),
        cost_estimate=pl.CostEstimate(
            flops=2 * videos * toks * ranks * model_width,
            bytes_accessed=2 * videos * (toks + ranks) * model_width,
            transcendentals=0,
        ),
        name="low_rank",
    )(me, normed_token_features, gathered)
    far = jnp.stack([low] + [swap(low, LOW * i) for i in range(1, devs // LOW)])
    far = after(far, up_got[-1])
    send_up(bits - 1)
    up_here = halving(up_pieces, up_got, bits).reshape(pairs, ranks, LANES)
    lows = [far] + [swap(far, i) for i in range(1, LOW)]

    low_spec = pl.BlockSpec((devs // LOW, toks, videos * ranks), lambda p: (0, 0, 0))
    part_spec = pl.BlockSpec((devs, pl.squeezed, toks, width), lambda p: (0, p, 0, 0))
    later_spec = pl.BlockSpec((devs, pl.squeezed, toks, width), lambda p: (0, pairs + p, 0, 0))
    mixed = pl.pallas_call(
        functools.partial(attend_kernel, per_video, math.gcd(devs, max(1, 512 // toks))),
        grid=(pairs,),
        in_specs=[SMEM, pl.BlockSpec((pl.squeezed, ranks, LANES), lambda p: (p, 0, 0))]
        + [later_spec, part_spec, part_spec]
        + [low_spec] * LOW,
        out_specs=part_spec,
        out_shape=jax.ShapeDtypeStruct((devs, pairs, toks, width), jnp.bfloat16),
        scratch_shapes=[
            pltpu.VMEM((devs, toks, videos * ranks), jnp.bfloat16),
            pltpu.VMEM((length, width), jnp.bfloat16),
        ],
        compiler_params=pltpu.CompilerParams(vmem_limit_bytes=48 << 20),
        cost_estimate=pl.CostEstimate(
            flops=4 * pairs * length * length * width,
            bytes_accessed=8 * pairs * length * width,
            transcendentals=pairs * length * length,
        ),
        name="attend",
    )(me, up_here, asked, keys, asked, *lows)
    return exchange(mixed).reshape(videos, heads, toks, width)


def solution(mesh):
    in_specs = (
        P("grp", "seq", None),
        P("grp", None, "seq", None),
        P("grp", None, "seq", None),
        P("grp", None, "seq", None),
        P("seq", None, None),
        P("seq", None, None),
        P(),
        P("grp"),
    )
    out_specs = P("grp", None, "seq", None)
    return jax.shard_map(body, mesh=mesh, in_specs=in_specs, out_specs=out_specs, check_vma=False)
```

```python
import functools
import math

import jax
import jax.numpy as jnp
from jax import lax
from jax.experimental import pallas as pl
from jax.experimental.pallas import tpu as pltpu
from jax.sharding import PartitionSpec as P

LANES = 128
LOW = 4
ANY = pl.BlockSpec(memory_space=pl.ANY)
VMEM = pl.BlockSpec(memory_space=pltpu.VMEM)
SMEM = pl.BlockSpec(memory_space=pltpu.SMEM)


def bit_count(n):
    bits = n.bit_length() - 1
    assert 1 << bits == n
    return bits


def reversed_bits(j, bits):
    out = 0
    for i in range(bits):
        out = out | (((j >> i) & 1) << (bits - 1 - i))
    return out


def pick_kernel(shape, me_ref, row_ref, req_ref, down_ref, up_ref, *refs):
    devs, bits, per_video, pairs, col_split, rows, tiles = shape
    downs, ups = refs[:bits], refs[bits : 2 * bits + 1]
    down, up, sems = refs[2 * bits + 1 :]
    slots, ranks, _ = down_ref.shape
    videos = down.shape[0]
    me = me_ref[0]
    for s in range(videos):
        place = row_ref[req_ref[s]]
        slot = place % slots
        owned = place // slots == me
        copies = [
            pltpu.make_async_copy(down_ref.at[slot], down.at[s], sems.at[2 * s]),
            pltpu.make_async_copy(up_ref.at[slot], up.at[s], sems.at[2 * s + 1]),
        ]

        @pl.when(owned)
        def _():
            for copy in copies:
                copy.start()
            for copy in copies:
                copy.wait()

        @pl.when(jnp.logical_not(owned))
        def _():
            down[s] = jnp.zeros(down.shape[1:], down.dtype)
            up[s] = jnp.zeros(up.shape[1:], up.dtype)

    for j in range(devs):
        step = bits - j.bit_length()
        at = j - (1 << (j.bit_length() - 1)) if j else 0
        dev = me ^ reversed_bits(j, bits)
        video = dev // per_video
        place = dev % per_video
        row = pl.multiple_of((place // col_split) * rows, rows)
        for t in range(tiles):
            col = pl.multiple_of(((place % col_split) * tiles + t) * LANES, LANES)
            downs[min(step, bits - 1)][at if j > 1 else j, t * rows : (t + 1) * rows, :] = down[
                video, pl.ds(row, rows), pl.ds(col, LANES)
            ]
        for p in range(pairs):
            col = pl.multiple_of((place * pairs + p) * LANES, LANES)
            ups[step][at, p * ranks : (p + 1) * ranks, :] = up[video, :, pl.ds(col, LANES)]


def copy_kernel(in_ref, out_ref):
    out_ref[...] = in_ref[...]


def low_rank_kernel(shape, me_ref, x_ref, g_ref, out_ref, down):
    devs, bits, per_video, _, col_split, rows, tiles = shape
    for j in range(devs):
        dev = me_ref[0] ^ reversed_bits(j, bits)
        video = dev // per_video
        place = dev % per_video
        row = pl.multiple_of((place // col_split) * rows, rows)
        for t in range(tiles):
            col = pl.multiple_of(((place % col_split) * tiles + t) * LANES, LANES)
            down[video, pl.ds(row, rows), pl.ds(col, LANES)] = g_ref[j, t * rows : (t + 1) * rows, :]
    parts = [
        lax.dot_general(
            x_ref[s], down[s], (((1,), (1,)), ((), ())), preferred_element_type=jnp.float32
        )
        for s in range(x_ref.shape[0])
    ]
    out_ref[...] = jnp.concatenate(parts, axis=1).astype(out_ref.dtype)


def up_part(up_ref, video, videos, second):
    up = jnp.concatenate([up_ref[...]] * videos, axis=0)
    ranks = up_ref.shape[0]
    row = lax.broadcasted_iota(jnp.int32, up.shape, 0)
    half = (row % ranks) // (ranks // 2)
    keep = (row // ranks == video) & (half == second)
    return jnp.where(keep, up, jnp.zeros_like(up))


def attend_kernel(per_video, block, me_ref, up_ref, q_ref, k_ref, v_ref, *refs):
    low_refs, out_ref, low, q_mix = refs[:LOW], refs[LOW], refs[LOW + 1], refs[LOW + 2]
    devs, toks, width = q_ref.shape
    length = devs * toks
    videos = low.shape[2] // up_ref.shape[0]
    me = me_ref[0]
    for k in range(devs):
        low[me ^ k] = low_refs[k % LOW][k // LOW]
    low_all = low[...].reshape(length, low.shape[2])
    up_q, up_v = (up_part(up_ref, me // per_video, videos, i) for i in range(2))
    keys = k_ref[...].reshape(length, width)
    delta_v = jnp.dot(low_all, up_v, preferred_element_type=jnp.float32)
    vals = (v_ref[...].reshape(length, width).astype(jnp.float32) + delta_v).astype(jnp.bfloat16)
    delta_q = jnp.dot(low_all, up_q, preferred_element_type=jnp.float32)
    q_mix[...] = (q_ref[...].reshape(length, width).astype(jnp.float32) + delta_q).astype(
        jnp.bfloat16
    )
    scale = math.log2(math.e) / math.sqrt(width)
    for b in range(0, devs, block):
        q = q_mix[b * toks : (b + block) * toks, :]
        scores = lax.dot_general(
            q, keys, (((1,), (1,)), ((), ())), preferred_element_type=jnp.float32
        )
        top = jnp.max(scores, axis=1, keepdims=True)
        weights = jnp.exp2((scores - top) * scale)
        total = jnp.sum(weights, axis=1, keepdims=True)
        mixed = jnp.dot(weights.astype(jnp.bfloat16), vals, preferred_element_type=jnp.float32)
        out_ref[b : b + block] = (mixed / total).astype(jnp.bfloat16).reshape(block, toks, width)


def body(
    normed_token_features,
    queries,
    projected_keys,
    values,
    adapter_down_factors,
    adapter_up_factors,
    adapter_store_row,
    requests,
):
    videos, toks, model_width = normed_token_features.shape
    heads = queries.shape[1]
    width = queries.shape[3]
    _, ranks, up_width = adapter_up_factors.shape
    devs = lax.axis_size("seq")
    bits = bit_count(devs)
    me = lax.axis_index("seq").astype(jnp.int32)[None]
    pairs = videos * heads // devs
    per_video = devs // videos
    length = devs * toks
    col_split = math.gcd(per_video, model_width // LANES)
    rows = ranks * col_split // per_video
    tiles = model_width // col_split // LANES
    shape = (devs, bits, per_video, pairs, col_split, rows, tiles)

    def swap(tensor, k):
        return lax.ppermute(tensor, "seq", [(i, i ^ k) for i in range(devs)])

    def exchange(tensor):
        return lax.all_to_all(tensor, "seq", split_axis=0, concat_axis=0, tiled=True)

    def by_pairs(tensor):
        return tensor.reshape(devs, pairs, toks, width)

    def after(array, *others):
        return lax.optimization_barrier((array, others))[0]

    def halving(parts, received, i):
        h = devs >> (i + 1) if i < bits else 0
        size = max(h, 1)
        return sum((r[h : h + size] for r in received), parts[i])

    keys = exchange(by_pairs(projected_keys))

    steps = [devs >> (i + 1) for i in range(bits)] + [1]
    piece_shapes = [(h, tiles * rows, LANES) for h in steps[: bits - 1] + [2]] + [
        (h, pairs * ranks, LANES) for h in steps
    ]
    pieces = pl.pallas_call(
        functools.partial(pick_kernel, shape),
        in_specs=[SMEM, SMEM, SMEM, ANY, ANY],
        out_specs=[VMEM] * (2 * bits + 1),
        out_shape=[jax.ShapeDtypeStruct(s, jnp.bfloat16) for s in piece_shapes],
        scratch_shapes=[
            pltpu.VMEM((videos, ranks, model_width), jnp.bfloat16),
            pltpu.VMEM((videos, ranks, up_width), jnp.bfloat16),
            pltpu.SemaphoreType.DMA((2 * videos,)),
        ],
        compiler_params=pltpu.CompilerParams(vmem_limit_bytes=24 << 20),
        cost_estimate=pl.CostEstimate(
            flops=0,
            bytes_accessed=4 * videos * ranks * (model_width + up_width),
            transcendentals=0,
        ),
        name="pick_factors",
    )(me, adapter_store_row, requests, adapter_down_factors, adapter_up_factors)
    down_pieces, up_pieces = pieces[:bits], pieces[bits:]

    down_got, up_got = [], []

    def send_up(i, *others):
        up_got.append(swap(after(halving(up_pieces, up_got, i), *others), 1 << i))

    for i in range(bits - 1):
        piece = halving(down_pieces, down_got, i)
        if i == 1:
            send_up(0, piece)
        if i == 2:
            piece = after(piece, keys, up_got[0])
        if i == bits - 2:
            vals = exchange(after(by_pairs(values), piece))
            send_up(1, piece)
        down_got.append(swap(piece, 1 << i))
    gathered = sum((r[:2] for r in down_got), down_pieces[-1])
    for j in range(2, bits - 1):
        send_up(j, gathered)
    other = swap(gathered, 1 << (bits - 1))
    gathered = gathered + jnp.concatenate([other[1:], other[:1]], axis=0)
    gathered = after(gathered, vals)
    asked = pl.pallas_call(
        copy_kernel,
        in_specs=[VMEM],
        out_specs=VMEM,
        out_shape=jax.ShapeDtypeStruct((devs, pairs, toks, width), jnp.bfloat16),
        compiler_params=pltpu.CompilerParams(vmem_limit_bytes=24 << 20),
        cost_estimate=pl.CostEstimate(
            flops=0, bytes_accessed=4 * pairs * length * width, transcendentals=0
        ),
        name="stage_queries",
    )(after(by_pairs(queries), gathered))
    asked = exchange(asked)
    for i in reversed(range(bits - 1)):
        if i == 0:
            gathered = after(gathered, *up_got)
            send_up(bits - 1, gathered)
        gathered = jnp.concatenate([gathered, swap(gathered, 1 << i)], axis=0)

    low = pl.pallas_call(
        functools.partial(low_rank_kernel, shape),
        in_specs=[SMEM, VMEM, VMEM],
        out_specs=VMEM,
        scratch_shapes=[pltpu.VMEM((videos, ranks, model_width), jnp.bfloat16)],
        out_shape=jax.ShapeDtypeStruct((toks, videos * ranks), jnp.bfloat16),
        compiler_params=pltpu.CompilerParams(vmem_limit_bytes=24 << 20),
        cost_estimate=pl.CostEstimate(
            flops=2 * videos * toks * ranks * model_width,
            bytes_accessed=2 * videos * (toks + ranks) * model_width,
            transcendentals=0,
        ),
        name="low_rank",
    )(me, normed_token_features, gathered)
    far = jnp.stack([low] + [swap(low, LOW * i) for i in range(1, devs // LOW)])
    up_here = halving(up_pieces, up_got, bits).reshape(pairs, ranks, LANES)
    lows = [far] + [swap(far, i) for i in range(1, LOW)]

    low_spec = pl.BlockSpec((devs // LOW, toks, videos * ranks), lambda p: (0, 0, 0))
    part_spec = pl.BlockSpec((devs, pl.squeezed, toks, width), lambda p: (0, p, 0, 0))
    mixed = pl.pallas_call(
        functools.partial(attend_kernel, per_video, math.gcd(devs, max(1, 512 // toks))),
        grid=(pairs,),
        in_specs=[SMEM, pl.BlockSpec((pl.squeezed, ranks, LANES), lambda p: (p, 0, 0))]
        + [part_spec] * 3
        + [low_spec] * LOW,
        out_specs=part_spec,
        out_shape=jax.ShapeDtypeStruct((devs, pairs, toks, width), jnp.bfloat16),
        scratch_shapes=[
            pltpu.VMEM((devs, toks, videos * ranks), jnp.bfloat16),
            pltpu.VMEM((length, width), jnp.bfloat16),
        ],
        compiler_params=pltpu.CompilerParams(vmem_limit_bytes=48 << 20),
        cost_estimate=pl.CostEstimate(
            flops=4 * pairs * length * length * width,
            bytes_accessed=8 * pairs * length * width,
            transcendentals=pairs * length * length,
        ),
        name="attend",
    )(me, up_here, asked, keys, vals, *lows)
    return exchange(mixed).reshape(videos, heads, toks, width)


def solution(mesh):
    in_specs = (
        P("grp", "seq", None),
        P("grp", None, "seq", None),
        P("grp", None, "seq", None),
        P("grp", None, "seq", None),
        P("seq", None, None),
        P("seq", None, None),
        P(),
        P("grp"),
    )
    out_specs = P("grp", None, "seq", None)
    return jax.shard_map(body, mesh=mesh, in_specs=in_specs, out_specs=out_specs, check_vma=False)
```

```python
import functools
import math

import jax
import jax.numpy as jnp
from jax import lax
from jax.experimental import pallas as pl
from jax.experimental.pallas import tpu as pltpu
from jax.sharding import PartitionSpec as P

LANES = 128
LOW = 4
ANY = pl.BlockSpec(memory_space=pl.ANY)
VMEM = pl.BlockSpec(memory_space=pltpu.VMEM)
SMEM = pl.BlockSpec(memory_space=pltpu.SMEM)


def bit_count(n):
    bits = n.bit_length() - 1
    assert 1 << bits == n
    return bits


def reversed_bits(j, bits):
    out = 0
    for i in range(bits):
        out = out | (((j >> i) & 1) << (bits - 1 - i))
    return out


def pick_kernel(shape, me_ref, row_ref, req_ref, down_ref, up_ref, *refs):
    devs, bits, per_video, pairs, col_split, rows, tiles = shape
    downs, ups = refs[: bits - 1], refs[bits - 1 : 2 * bits - 2]
    down, up, sems = refs[2 * bits - 2 :]
    slots, ranks, _ = down_ref.shape
    videos = down.shape[0]
    me = me_ref[0]
    for s in range(videos):
        place = row_ref[req_ref[s]]
        slot = place % slots
        owned = place // slots == me
        copies = [
            pltpu.make_async_copy(down_ref.at[slot], down.at[s], sems.at[2 * s]),
            pltpu.make_async_copy(up_ref.at[slot], up.at[s], sems.at[2 * s + 1]),
        ]

        @pl.when(owned)
        def _():
            for copy in copies:
                copy.start()
            for copy in copies:
                copy.wait()

        @pl.when(jnp.logical_not(owned))
        def _():
            down[s] = jnp.zeros(down.shape[1:], down.dtype)
            up[s] = jnp.zeros(up.shape[1:], up.dtype)

    for j in range(devs):
        step = min(bits - j.bit_length(), bits - 2)
        at = j - (1 << (j.bit_length() - 1)) if j >= LOW else j
        dev = me ^ reversed_bits(j, bits)
        video = dev // per_video
        place = dev % per_video
        row = pl.multiple_of((place // col_split) * rows, rows)
        for t in range(tiles):
            col = pl.multiple_of(((place % col_split) * tiles + t) * LANES, LANES)
            downs[step][at, t * rows : (t + 1) * rows, :] = down[
                video, pl.ds(row, rows), pl.ds(col, LANES)
            ]
        for p in range(pairs):
            col = pl.multiple_of((place * pairs + p) * LANES, LANES)
            ups[step][at, p * ranks : (p + 1) * ranks, :] = up[video, :, pl.ds(col, LANES)]


def copy_kernel(in_ref, out_ref):
    out_ref[...] = in_ref[...]


def low_rank_kernel(shape, me_ref, x_ref, g_ref, out_ref, down):
    devs, bits, per_video, _, col_split, rows, tiles = shape
    for j in range(devs):
        dev = me_ref[0] ^ reversed_bits(j, bits)
        video = dev // per_video
        place = dev % per_video
        row = pl.multiple_of((place // col_split) * rows, rows)
        for t in range(tiles):
            col = pl.multiple_of(((place % col_split) * tiles + t) * LANES, LANES)
            down[video, pl.ds(row, rows), pl.ds(col, LANES)] = g_ref[j, t * rows : (t + 1) * rows, :]
    parts = [
        lax.dot_general(
            x_ref[s], down[s], (((1,), (1,)), ((), ())), preferred_element_type=jnp.float32
        )
        for s in range(x_ref.shape[0])
    ]
    out_ref[...] = jnp.concatenate(parts, axis=1).astype(out_ref.dtype)


def up_part(up_ref, video, videos, second):
    up = jnp.concatenate([up_ref[...]] * videos, axis=0)
    ranks = up_ref.shape[0]
    row = lax.broadcasted_iota(jnp.int32, up.shape, 0)
    half = (row % ranks) // (ranks // 2)
    keep = (row // ranks == video) & (half == second)
    return jnp.where(keep, up, jnp.zeros_like(up))


def attend_kernel(per_video, block, me_ref, up_ref, q_ref, k_ref, v_ref, *refs):
    low_refs, out_ref, low, q_mix = refs[:LOW], refs[LOW], refs[LOW + 1], refs[LOW + 2]
    devs, toks, width = q_ref.shape
    length = devs * toks
    videos = low.shape[2] // up_ref.shape[0]
    me = me_ref[0]
    for k in range(devs):
        low[me ^ k] = low_refs[k % LOW][k // LOW]
    low_all = low[...].reshape(length, low.shape[2])
    up_q, up_v = (up_part(up_ref, me // per_video, videos, i) for i in range(2))
    keys = k_ref[...].reshape(length, width)
    delta_v = jnp.dot(low_all, up_v, preferred_element_type=jnp.float32)
    vals = (v_ref[...].reshape(length, width).astype(jnp.float32) + delta_v).astype(jnp.bfloat16)
    delta_q = jnp.dot(low_all, up_q, preferred_element_type=jnp.float32)
    q_mix[...] = (q_ref[...].reshape(length, width).astype(jnp.float32) + delta_q).astype(
        jnp.bfloat16
    )
    scale = math.log2(math.e) / math.sqrt(width)
    for b in range(0, devs, block):
        q = q_mix[b * toks : (b + block) * toks, :]
        scores = lax.dot_general(
            q, keys, (((1,), (1,)), ((), ())), preferred_element_type=jnp.float32
        )
        top = jnp.max(scores, axis=1, keepdims=True)
        weights = jnp.exp2((scores - top) * scale)
        total = jnp.sum(weights, axis=1, keepdims=True)
        mixed = jnp.dot(weights.astype(jnp.bfloat16), vals, preferred_element_type=jnp.float32)
        out_ref[b : b + block] = (mixed / total).astype(jnp.bfloat16).reshape(block, toks, width)


def body(
    normed_token_features,
    queries,
    projected_keys,
    values,
    adapter_down_factors,
    adapter_up_factors,
    adapter_store_row,
    requests,
):
    videos, toks, model_width = normed_token_features.shape
    heads = queries.shape[1]
    width = queries.shape[3]
    _, ranks, up_width = adapter_up_factors.shape
    devs = lax.axis_size("seq")
    bits = bit_count(devs)
    me = lax.axis_index("seq").astype(jnp.int32)[None]
    pairs = videos * heads // devs
    per_video = devs // videos
    length = devs * toks
    col_split = math.gcd(per_video, model_width // LANES)
    rows = ranks * col_split // per_video
    tiles = model_width // col_split // LANES
    shape = (devs, bits, per_video, pairs, col_split, rows, tiles)

    def swap(tensor, k):
        return lax.ppermute(tensor, "seq", [(i, i ^ k) for i in range(devs)])

    def exchange(tensor):
        return lax.all_to_all(tensor, "seq", split_axis=0, concat_axis=0, tiled=True)

    def by_pairs(tensor):
        return tensor.reshape(devs, pairs, toks, width)

    def after(array, *others):
        return lax.optimization_barrier((array, others))[0]

    quarter = devs // LOW
    others = (2 * quarter, quarter, 3 * quarter)

    def halving(parts, received, i):
        size = parts[i].shape[0]
        start = size if i < bits - 2 else 0
        return sum((r[start : start + size] for r in received), parts[i])

    def to_others(shards):
        return [swap(shards[j + 1 : j + 2], k) for j, k in enumerate(others)]

    keys = exchange(by_pairs(projected_keys))

    steps = [devs >> (i + 1) for i in range(bits - 2)] + [LOW]
    piece_shapes = [(h, tiles * rows, LANES) for h in steps] + [
        (h, pairs * ranks, LANES) for h in steps
    ]
    pieces = pl.pallas_call(
        functools.partial(pick_kernel, shape),
        in_specs=[SMEM, SMEM, SMEM, ANY, ANY],
        out_specs=[VMEM] * (2 * bits - 2),
        out_shape=[jax.ShapeDtypeStruct(s, jnp.bfloat16) for s in piece_shapes],
        scratch_shapes=[
            pltpu.VMEM((videos, ranks, model_width), jnp.bfloat16),
            pltpu.VMEM((videos, ranks, up_width), jnp.bfloat16),
            pltpu.SemaphoreType.DMA((2 * videos,)),
        ],
        compiler_params=pltpu.CompilerParams(vmem_limit_bytes=24 << 20),
        cost_estimate=pl.CostEstimate(
            flops=0,
            bytes_accessed=4 * videos * ranks * (model_width + up_width),
            transcendentals=0,
        ),
        name="pick_factors",
    )(me, adapter_store_row, requests, adapter_down_factors, adapter_up_factors)
    down_pieces, up_pieces = pieces[: bits - 1], pieces[bits - 1 :]

    def stage(tensor):
        return pl.pallas_call(
            copy_kernel,
            in_specs=[VMEM],
            out_specs=VMEM,
            out_shape=jax.ShapeDtypeStruct((devs, pairs, toks, width), jnp.bfloat16),
            compiler_params=pltpu.CompilerParams(vmem_limit_bytes=24 << 20),
            cost_estimate=pl.CostEstimate(
                flops=0, bytes_accessed=4 * pairs * length * width, transcendentals=0
            ),
            name="stage",
        )(tensor)

    down_got, up_got = [], []
    for i in range(bits - 2):
        piece = halving(down_pieces, down_got, i)
        if i > 0:
            up_got.append(swap(after(halving(up_pieces, up_got, i - 1), piece), 1 << (i - 1)))
        down_got.append(swap(piece, 1 << i))
    shards = halving(down_pieces, down_got, bits - 2)
    shards = after(shards, keys, *up_got)
    vals = exchange(stage(after(by_pairs(values), shards)))
    up_got.append(swap(after(halving(up_pieces, up_got, bits - 3), shards), 1 << (bits - 3)))
    shard = shards[:1] + sum(to_others(shards))
    shard = after(shard, *up_got)
    up_shards = after(halving(up_pieces, up_got, bits - 2), shard)
    up_here = (up_shards[:1] + sum(to_others(up_shards))).reshape(pairs, ranks, LANES)
    gathered = jnp.concatenate([shard] + [swap(shard, k) for k in others], axis=0)
    gathered = after(gathered, vals)
    asked = exchange(after(by_pairs(queries), vals))
    for i in reversed(range(bits - 2)):
        gathered = jnp.concatenate([gathered, swap(gathered, 1 << i)], axis=0)
    gathered = after(gathered, up_here)

    low = pl.pallas_call(
        functools.partial(low_rank_kernel, shape),
        in_specs=[SMEM, VMEM, VMEM],
        out_specs=VMEM,
        scratch_shapes=[pltpu.VMEM((videos, ranks, model_width), jnp.bfloat16)],
        out_shape=jax.ShapeDtypeStruct((toks, videos * ranks), jnp.bfloat16),
        compiler_params=pltpu.CompilerParams(vmem_limit_bytes=24 << 20),
        cost_estimate=pl.CostEstimate(
            flops=2 * videos * toks * ranks * model_width,
            bytes_accessed=2 * videos * (toks + ranks) * model_width,
            transcendentals=0,
        ),
        name="low_rank",
    )(me, normed_token_features, gathered)
    far = jnp.stack([low] + [swap(low, LOW * i) for i in range(1, devs // LOW)])
    lows = [far] + [swap(far, i) for i in range(1, LOW)]

    low_spec = pl.BlockSpec((devs // LOW, toks, videos * ranks), lambda p: (0, 0, 0))
    part_spec = pl.BlockSpec((devs, pl.squeezed, toks, width), lambda p: (0, p, 0, 0))
    mixed = pl.pallas_call(
        functools.partial(attend_kernel, per_video, math.gcd(devs, max(1, 512 // toks))),
        grid=(pairs,),
        in_specs=[SMEM, pl.BlockSpec((pl.squeezed, ranks, LANES), lambda p: (p, 0, 0))]
        + [part_spec] * 3
        + [low_spec] * LOW,
        out_specs=part_spec,
        out_shape=jax.ShapeDtypeStruct((devs, pairs, toks, width), jnp.bfloat16),
        scratch_shapes=[
            pltpu.VMEM((devs, toks, videos * ranks), jnp.bfloat16),
            pltpu.VMEM((length, width), jnp.bfloat16),
        ],
        compiler_params=pltpu.CompilerParams(vmem_limit_bytes=48 << 20),
        cost_estimate=pl.CostEstimate(
            flops=4 * pairs * length * length * width,
            bytes_accessed=8 * pairs * length * width,
            transcendentals=pairs * length * length,
        ),
        name="attend",
    )(me, up_here, asked, keys, vals, *lows)
    return exchange(mixed).reshape(videos, heads, toks, width)


def solution(mesh):
    in_specs = (
        P("grp", "seq", None),
        P("grp", None, "seq", None),
        P("grp", None, "seq", None),
        P("grp", None, "seq", None),
        P("seq", None, None),
        P("seq", None, None),
        P(),
        P("grp"),
    )
    out_specs = P("grp", None, "seq", None)
    return jax.shard_map(body, mesh=mesh, in_specs=in_specs, out_specs=out_specs, check_vma=False)
```

```python
import functools
import math

import jax
import jax.numpy as jnp
from jax import lax
from jax.experimental import pallas as pl
from jax.experimental.pallas import tpu as pltpu
from jax.sharding import PartitionSpec as P

LANES = 128
LOW = 4
ANY = pl.BlockSpec(memory_space=pl.ANY)
VMEM = pl.BlockSpec(memory_space=pltpu.VMEM)
SMEM = pl.BlockSpec(memory_space=pltpu.SMEM)


def bit_count(n):
    bits = n.bit_length() - 1
    assert 1 << bits == n
    return bits


def reversed_bits(j, bits):
    out = 0
    for i in range(bits):
        out = out | (((j >> i) & 1) << (bits - 1 - i))
    return out


def pick_kernel(shape, me_ref, row_ref, req_ref, down_ref, up_ref, *refs):
    devs, bits, per_video, pairs, col_split, rows, tiles = shape
    downs, ups = refs[: bits - 1], refs[bits - 1 : 2 * bits - 2]
    down, up, sems = refs[2 * bits - 2 :]
    slots, ranks, _ = down_ref.shape
    videos = down.shape[0]
    me = me_ref[0]
    for s in range(videos):
        place = row_ref[req_ref[s]]
        slot = place % slots
        owned = place // slots == me
        copies = [
            pltpu.make_async_copy(down_ref.at[slot], down.at[s], sems.at[2 * s]),
            pltpu.make_async_copy(up_ref.at[slot], up.at[s], sems.at[2 * s + 1]),
        ]

        @pl.when(owned)
        def _():
            for copy in copies:
                copy.start()
            for copy in copies:
                copy.wait()

        @pl.when(jnp.logical_not(owned))
        def _():
            down[s] = jnp.zeros(down.shape[1:], down.dtype)
            up[s] = jnp.zeros(up.shape[1:], up.dtype)

    for j in range(devs):
        step = min(bits - j.bit_length(), bits - 2)
        at = j - (1 << (j.bit_length() - 1)) if j >= LOW else j
        dev = me ^ reversed_bits(j, bits)
        video = dev // per_video
        place = dev % per_video
        row = pl.multiple_of((place // col_split) * rows, rows)
        for t in range(tiles):
            col = pl.multiple_of(((place % col_split) * tiles + t) * LANES, LANES)
            downs[step][at, t * rows : (t + 1) * rows, :] = down[
                video, pl.ds(row, rows), pl.ds(col, LANES)
            ]
        for p in range(pairs):
            col = pl.multiple_of((place * pairs + p) * LANES, LANES)
            ups[step][at, p * ranks : (p + 1) * ranks, :] = up[video, :, pl.ds(col, LANES)]


def low_rank_kernel(shape, me_ref, x_ref, g_ref, out_ref, down):
    devs, bits, per_video, _, col_split, rows, tiles = shape
    for j in range(devs):
        dev = me_ref[0] ^ reversed_bits(j, bits)
        video = dev // per_video
        place = dev % per_video
        row = pl.multiple_of((place // col_split) * rows, rows)
        for t in range(tiles):
            col = pl.multiple_of(((place % col_split) * tiles + t) * LANES, LANES)
            down[video, pl.ds(row, rows), pl.ds(col, LANES)] = g_ref[j, t * rows : (t + 1) * rows, :]
    parts = [
        lax.dot_general(
            x_ref[s], down[s], (((1,), (1,)), ((), ())), preferred_element_type=jnp.float32
        )
        for s in range(x_ref.shape[0])
    ]
    out_ref[...] = jnp.concatenate(parts, axis=1).astype(out_ref.dtype)


def up_part(up_ref, video, videos, second):
    up = jnp.concatenate([up_ref[...]] * videos, axis=0)
    ranks = up_ref.shape[0]
    row = lax.broadcasted_iota(jnp.int32, up.shape, 0)
    half = (row % ranks) // (ranks // 2)
    keep = (row // ranks == video) & (half == second)
    return jnp.where(keep, up, jnp.zeros_like(up))


def attend_kernel(per_video, block, me_ref, up_ref, q_ref, k_ref, v_ref, *refs):
    low_refs, out_ref, low, q_mix = refs[:LOW], refs[LOW], refs[LOW + 1], refs[LOW + 2]
    devs, toks, width = q_ref.shape
    length = devs * toks
    videos = low.shape[2] // up_ref.shape[0]
    me = me_ref[0]
    for k in range(devs):
        low[me ^ k] = low_refs[k % LOW][k // LOW]
    low_all = low[...].reshape(length, low.shape[2])
    up_q, up_v = (up_part(up_ref, me // per_video, videos, i) for i in range(2))
    keys = k_ref[...].reshape(length, width)
    delta_v = jnp.dot(low_all, up_v, preferred_element_type=jnp.float32)
    vals = (v_ref[...].reshape(length, width).astype(jnp.float32) + delta_v).astype(jnp.bfloat16)
    delta_q = jnp.dot(low_all, up_q, preferred_element_type=jnp.float32)
    q_mix[...] = (q_ref[...].reshape(length, width).astype(jnp.float32) + delta_q).astype(
        jnp.bfloat16
    )
    scale = math.log2(math.e) / math.sqrt(width)
    for b in range(0, devs, block):
        q = q_mix[b * toks : (b + block) * toks, :]
        scores = lax.dot_general(
            q, keys, (((1,), (1,)), ((), ())), preferred_element_type=jnp.float32
        )
        top = jnp.max(scores, axis=1, keepdims=True)
        weights = jnp.exp2((scores - top) * scale)
        total = jnp.sum(weights, axis=1, keepdims=True)
        mixed = jnp.dot(weights.astype(jnp.bfloat16), vals, preferred_element_type=jnp.float32)
        out_ref[b : b + block] = (mixed / total).astype(jnp.bfloat16).reshape(block, toks, width)


def body(
    normed_token_features,
    queries,
    projected_keys,
    values,
    adapter_down_factors,
    adapter_up_factors,
    adapter_store_row,
    requests,
):
    videos, toks, model_width = normed_token_features.shape
    heads = queries.shape[1]
    width = queries.shape[3]
    _, ranks, up_width = adapter_up_factors.shape
    devs = lax.axis_size("seq")
    bits = bit_count(devs)
    me = lax.axis_index("seq").astype(jnp.int32)[None]
    pairs = videos * heads // devs
    per_video = devs // videos
    length = devs * toks
    col_split = math.gcd(per_video, model_width // LANES)
    rows = ranks * col_split // per_video
    tiles = model_width // col_split // LANES
    shape = (devs, bits, per_video, pairs, col_split, rows, tiles)

    def swap(tensor, k):
        return lax.ppermute(tensor, "seq", [(i, i ^ k) for i in range(devs)])

    def exchange(tensor):
        return lax.all_to_all(tensor, "seq", split_axis=0, concat_axis=0, tiled=True)

    def by_pairs(tensor):
        return tensor.reshape(devs, pairs, toks, width)

    def after(array, *others):
        return lax.optimization_barrier((array, others))[0]

    quarter = devs // LOW
    others = (2 * quarter, quarter, 3 * quarter)

    def halving(parts, received, i):
        size = parts[i].shape[0]
        start = size if i < bits - 2 else 0
        return sum((r[start : start + size] for r in received), parts[i])

    def to_others(shards):
        return [swap(shards[j + 1 : j + 2], k) for j, k in enumerate(others)]

    keys = exchange(by_pairs(projected_keys))

    steps = [devs >> (i + 1) for i in range(bits - 2)] + [LOW]
    piece_shapes = [(h, tiles * rows, LANES) for h in steps] + [
        (h, pairs * ranks, LANES) for h in steps
    ]
    pieces = pl.pallas_call(
        functools.partial(pick_kernel, shape),
        in_specs=[SMEM, SMEM, SMEM, ANY, ANY],
        out_specs=[VMEM] * (2 * bits - 2),
        out_shape=[jax.ShapeDtypeStruct(s, jnp.bfloat16) for s in piece_shapes],
        scratch_shapes=[
            pltpu.VMEM((videos, ranks, model_width), jnp.bfloat16),
            pltpu.VMEM((videos, ranks, up_width), jnp.bfloat16),
            pltpu.SemaphoreType.DMA((2 * videos,)),
        ],
        compiler_params=pltpu.CompilerParams(vmem_limit_bytes=24 << 20),
        cost_estimate=pl.CostEstimate(
            flops=0,
            bytes_accessed=4 * videos * ranks * (model_width + up_width),
            transcendentals=0,
        ),
        name="pick_factors",
    )(me, adapter_store_row, requests, adapter_down_factors, adapter_up_factors)
    down_pieces, up_pieces = pieces[: bits - 1], pieces[bits - 1 :]

    down_got, up_got = [], []

    def send_up(i, *others):
        up_got.append(swap(after(halving(up_pieces, up_got, i), *others), 1 << i))

    for i in range(bits - 2):
        piece = halving(down_pieces, down_got, i)
        if i > 0:
            send_up(i - 1, piece)
        down_got.append(swap(piece, 1 << i))
    shards = after(halving(down_pieces, down_got, bits - 2), keys, *up_got)
    got = to_others(shards)
    vals = exchange(after(by_pairs(values), got[1]))
    shard = shards[:1] + sum(got)
    send_up(bits - 3, shard)
    spread = [swap(shard, k) for k in others]
    asked = exchange(after(by_pairs(queries), vals, spread[1], up_got[-1]))
    gathered = jnp.concatenate([shard] + spread, axis=0)
    up_shards = after(halving(up_pieces, up_got, bits - 2), vals)
    up_here = (up_shards[:1] + sum(to_others(up_shards))).reshape(pairs, ranks, LANES)
    for i in reversed(range(bits - 2)):
        gathered = jnp.concatenate([gathered, swap(gathered, 1 << i)], axis=0)

    low = pl.pallas_call(
        functools.partial(low_rank_kernel, shape),
        in_specs=[SMEM, VMEM, VMEM],
        out_specs=VMEM,
        scratch_shapes=[pltpu.VMEM((videos, ranks, model_width), jnp.bfloat16)],
        out_shape=jax.ShapeDtypeStruct((toks, videos * ranks), jnp.bfloat16),
        compiler_params=pltpu.CompilerParams(vmem_limit_bytes=24 << 20),
        cost_estimate=pl.CostEstimate(
            flops=2 * videos * toks * ranks * model_width,
            bytes_accessed=2 * videos * (toks + ranks) * model_width,
            transcendentals=0,
        ),
        name="low_rank",
    )(me, normed_token_features, gathered)
    far = jnp.stack([low] + [swap(low, LOW * i) for i in range(1, devs // LOW)])
    far = after(far, up_here)
    lows = [far] + [swap(far, i) for i in range(1, LOW)]

    low_spec = pl.BlockSpec((devs // LOW, toks, videos * ranks), lambda p: (0, 0, 0))
    part_spec = pl.BlockSpec((devs, pl.squeezed, toks, width), lambda p: (0, p, 0, 0))
    mixed = pl.pallas_call(
        functools.partial(attend_kernel, per_video, math.gcd(devs, max(1, 512 // toks))),
        grid=(pairs,),
        in_specs=[SMEM, pl.BlockSpec((pl.squeezed, ranks, LANES), lambda p: (p, 0, 0))]
        + [part_spec] * 3
        + [low_spec] * LOW,
        out_specs=part_spec,
        out_shape=jax.ShapeDtypeStruct((devs, pairs, toks, width), jnp.bfloat16),
        scratch_shapes=[
            pltpu.VMEM((devs, toks, videos * ranks), jnp.bfloat16),
            pltpu.VMEM((length, width), jnp.bfloat16),
        ],
        compiler_params=pltpu.CompilerParams(vmem_limit_bytes=48 << 20),
        cost_estimate=pl.CostEstimate(
            flops=4 * pairs * length * length * width,
            bytes_accessed=8 * pairs * length * width,
            transcendentals=pairs * length * length,
        ),
        name="attend",
    )(me, up_here, asked, keys, vals, *lows)
    return exchange(mixed).reshape(videos, heads, toks, width)


def solution(mesh):
    in_specs = (
        P("grp", "seq", None),
        P("grp", None, "seq", None),
        P("grp", None, "seq", None),
        P("grp", None, "seq", None),
        P("seq", None, None),
        P("seq", None, None),
        P(),
        P("grp"),
    )
    out_specs = P("grp", None, "seq", None)
    return jax.shard_map(body, mesh=mesh, in_specs=in_specs, out_specs=out_specs, check_vma=False)
```

```python
import functools
import math

import jax
import jax.numpy as jnp
from jax import lax
from jax.experimental import pallas as pl
from jax.experimental.pallas import tpu as pltpu
from jax.sharding import PartitionSpec as P

LANES = 128
LOW = 4
ANY = pl.BlockSpec(memory_space=pl.ANY)
VMEM = pl.BlockSpec(memory_space=pltpu.VMEM)
SMEM = pl.BlockSpec(memory_space=pltpu.SMEM)


def bit_count(n):
    bits = n.bit_length() - 1
    assert 1 << bits == n
    return bits


def reversed_bits(j, bits):
    out = 0
    for i in range(bits):
        out = out | (((j >> i) & 1) << (bits - 1 - i))
    return out


def pick_kernel(shape, me_ref, row_ref, req_ref, down_ref, up_ref, *refs):
    devs, bits, per_video, pairs, col_split, rows, tiles = shape
    downs, ups = refs[: bits - 1], refs[bits - 1 : 2 * bits - 2]
    down, up, sems = refs[2 * bits - 2 :]
    slots, ranks, _ = down_ref.shape
    videos = down.shape[0]
    me = me_ref[0]
    for s in range(videos):
        place = row_ref[req_ref[s]]
        slot = place % slots
        owned = place // slots == me
        copies = [
            pltpu.make_async_copy(down_ref.at[slot], down.at[s], sems.at[2 * s]),
            pltpu.make_async_copy(up_ref.at[slot], up.at[s], sems.at[2 * s + 1]),
        ]

        @pl.when(owned)
        def _():
            for copy in copies:
                copy.start()
            for copy in copies:
                copy.wait()

        @pl.when(jnp.logical_not(owned))
        def _():
            down[s] = jnp.zeros(down.shape[1:], down.dtype)
            up[s] = jnp.zeros(up.shape[1:], up.dtype)

    for j in range(devs):
        step = min(bits - j.bit_length(), bits - 2)
        at = j - (1 << (j.bit_length() - 1)) if j >= LOW else j
        dev = me ^ reversed_bits(j, bits)
        video = dev // per_video
        place = dev % per_video
        row = pl.multiple_of((place // col_split) * rows, rows)
        for t in range(tiles):
            col = pl.multiple_of(((place % col_split) * tiles + t) * LANES, LANES)
            downs[step][at, t * rows : (t + 1) * rows, :] = down[
                video, pl.ds(row, rows), pl.ds(col, LANES)
            ]
        for p in range(pairs):
            col = pl.multiple_of((place * pairs + p) * LANES, LANES)
            ups[step][at, p * ranks : (p + 1) * ranks, :] = up[video, :, pl.ds(col, LANES)]


def low_rank_kernel(shape, me_ref, x_ref, g_ref, out_ref, down):
    devs, bits, per_video, _, col_split, rows, tiles = shape
    for j in range(devs):
        dev = me_ref[0] ^ reversed_bits(j, bits)
        video = dev // per_video
        place = dev % per_video
        row = pl.multiple_of((place // col_split) * rows, rows)
        for t in range(tiles):
            col = pl.multiple_of(((place % col_split) * tiles + t) * LANES, LANES)
            down[video, pl.ds(row, rows), pl.ds(col, LANES)] = g_ref[j, t * rows : (t + 1) * rows, :]
    parts = [
        lax.dot_general(
            x_ref[s], down[s], (((1,), (1,)), ((), ())), preferred_element_type=jnp.float32
        )
        for s in range(x_ref.shape[0])
    ]
    out_ref[...] = jnp.concatenate(parts, axis=1).astype(out_ref.dtype)


def up_part(up_ref, video, videos, second):
    up = jnp.concatenate([up_ref[...]] * videos, axis=0)
    ranks = up_ref.shape[0]
    row = lax.broadcasted_iota(jnp.int32, up.shape, 0)
    half = (row % ranks) // (ranks // 2)
    keep = (row // ranks == video) & (half == second)
    return jnp.where(keep, up, jnp.zeros_like(up))


def attend_kernel(per_video, block, me_ref, up_ref, q_ref, k_ref, v_ref, *refs):
    low_refs, out_ref, low, q_mix = refs[:LOW], refs[LOW], refs[LOW + 1], refs[LOW + 2]
    devs, toks, width = q_ref.shape
    length = devs * toks
    videos = low.shape[2] // up_ref.shape[0]
    me = me_ref[0]
    for k in range(devs):
        low[me ^ k] = low_refs[k % LOW][k // LOW]
    low_all = low[...].reshape(length, low.shape[2])
    up_q, up_v = (up_part(up_ref, me // per_video, videos, i) for i in range(2))
    keys = k_ref[...].reshape(length, width)
    delta_v = jnp.dot(low_all, up_v, preferred_element_type=jnp.float32)
    vals = (v_ref[...].reshape(length, width).astype(jnp.float32) + delta_v).astype(jnp.bfloat16)
    delta_q = jnp.dot(low_all, up_q, preferred_element_type=jnp.float32)
    q_mix[...] = (q_ref[...].reshape(length, width).astype(jnp.float32) + delta_q).astype(
        jnp.bfloat16
    )
    scale = math.log2(math.e) / math.sqrt(width)
    for b in range(0, devs, block):
        q = q_mix[b * toks : (b + block) * toks, :]
        scores = lax.dot_general(
            q, keys, (((1,), (1,)), ((), ())), preferred_element_type=jnp.float32
        )
        top = jnp.max(scores, axis=1, keepdims=True)
        weights = jnp.exp2((scores - top) * scale)
        total = jnp.sum(weights, axis=1, keepdims=True)
        mixed = jnp.dot(weights.astype(jnp.bfloat16), vals, preferred_element_type=jnp.float32)
        out_ref[b : b + block] = (mixed / total).astype(jnp.bfloat16).reshape(block, toks, width)


def body(
    normed_token_features,
    queries,
    projected_keys,
    values,
    adapter_down_factors,
    adapter_up_factors,
    adapter_store_row,
    requests,
):
    videos, toks, model_width = normed_token_features.shape
    heads = queries.shape[1]
    width = queries.shape[3]
    _, ranks, up_width = adapter_up_factors.shape
    devs = lax.axis_size("seq")
    bits = bit_count(devs)
    me = lax.axis_index("seq").astype(jnp.int32)[None]
    pairs = videos * heads // devs
    per_video = devs // videos
    length = devs * toks
    col_split = math.gcd(per_video, model_width // LANES)
    rows = ranks * col_split // per_video
    tiles = model_width // col_split // LANES
    shape = (devs, bits, per_video, pairs, col_split, rows, tiles)

    def swap(tensor, k):
        return lax.ppermute(tensor, "seq", [(i, i ^ k) for i in range(devs)])

    def exchange(tensor):
        return lax.all_to_all(tensor, "seq", split_axis=0, concat_axis=0, tiled=True)

    def by_pairs(tensor):
        return tensor.reshape(devs, pairs, toks, width)

    def after(array, *others):
        return lax.optimization_barrier((array, others))[0]

    quarter = devs // LOW
    others = (2 * quarter, quarter, 3 * quarter)

    def halving(parts, received, i):
        size = parts[i].shape[0]
        start = size if i < bits - 2 else 0
        return sum((r[start : start + size] for r in received), parts[i])

    def to_others(shards):
        return [swap(shards[j + 1 : j + 2], k) for j, k in enumerate(others)]

    keys = exchange(by_pairs(projected_keys))

    steps = [devs >> (i + 1) for i in range(bits - 2)] + [LOW]
    piece_shapes = [(h, tiles * rows, LANES) for h in steps] + [
        (h, pairs * ranks, LANES) for h in steps
    ]
    pieces = pl.pallas_call(
        functools.partial(pick_kernel, shape),
        in_specs=[SMEM, SMEM, SMEM, ANY, ANY],
        out_specs=[VMEM] * (2 * bits - 2),
        out_shape=[jax.ShapeDtypeStruct(s, jnp.bfloat16) for s in piece_shapes],
        scratch_shapes=[
            pltpu.VMEM((videos, ranks, model_width), jnp.bfloat16),
            pltpu.VMEM((videos, ranks, up_width), jnp.bfloat16),
            pltpu.SemaphoreType.DMA((2 * videos,)),
        ],
        compiler_params=pltpu.CompilerParams(vmem_limit_bytes=24 << 20),
        cost_estimate=pl.CostEstimate(
            flops=0,
            bytes_accessed=4 * videos * ranks * (model_width + up_width),
            transcendentals=0,
        ),
        name="pick_factors",
    )(me, adapter_store_row, requests, adapter_down_factors, adapter_up_factors)
    down_pieces, up_pieces = pieces[: bits - 1], pieces[bits - 1 :]

    down_got, up_got = [], []

    def send_up(i, *others):
        up_got.append(swap(after(halving(up_pieces, up_got, i), *others), 1 << i))

    for i in range(bits - 2):
        piece = halving(down_pieces, down_got, i)
        if i > 0:
            send_up(i - 1, piece)
        down_got.append(swap(piece, 1 << i))
    shards = after(halving(down_pieces, down_got, bits - 2), keys, *up_got)
    send_up(bits - 3, shards)
    shard = shards[:1] + sum(to_others(shards))
    gathered = jnp.concatenate([shard] + [swap(shard, k) for k in others], axis=0)
    asked = jnp.concatenate([by_pairs(values), by_pairs(queries)], axis=1)
    asked = exchange(after(asked, gathered, up_got[-1]))
    up_shards = after(halving(up_pieces, up_got, bits - 2), gathered)
    up_here = (up_shards[:1] + sum(to_others(up_shards))).reshape(pairs, ranks, LANES)
    for i in reversed(range(bits - 2)):
        gathered = jnp.concatenate([gathered, swap(gathered, 1 << i)], axis=0)

    low = pl.pallas_call(
        functools.partial(low_rank_kernel, shape),
        in_specs=[SMEM, VMEM, VMEM],
        out_specs=VMEM,
        scratch_shapes=[pltpu.VMEM((videos, ranks, model_width), jnp.bfloat16)],
        out_shape=jax.ShapeDtypeStruct((toks, videos * ranks), jnp.bfloat16),
        compiler_params=pltpu.CompilerParams(vmem_limit_bytes=24 << 20),
        cost_estimate=pl.CostEstimate(
            flops=2 * videos * toks * ranks * model_width,
            bytes_accessed=2 * videos * (toks + ranks) * model_width,
            transcendentals=0,
        ),
        name="low_rank",
    )(me, normed_token_features, gathered)
    far = jnp.stack([low] + [swap(low, LOW * i) for i in range(1, devs // LOW)])
    far = after(far, up_here)
    lows = [far] + [swap(far, i) for i in range(1, LOW)]

    low_spec = pl.BlockSpec((devs // LOW, toks, videos * ranks), lambda p: (0, 0, 0))
    part_spec = pl.BlockSpec((devs, pl.squeezed, toks, width), lambda p: (0, p, 0, 0))
    later_spec = pl.BlockSpec((devs, pl.squeezed, toks, width), lambda p: (0, pairs + p, 0, 0))
    mixed = pl.pallas_call(
        functools.partial(attend_kernel, per_video, math.gcd(devs, max(1, 512 // toks))),
        grid=(pairs,),
        in_specs=[SMEM, pl.BlockSpec((pl.squeezed, ranks, LANES), lambda p: (p, 0, 0))]
        + [later_spec, part_spec, part_spec]
        + [low_spec] * LOW,
        out_specs=part_spec,
        out_shape=jax.ShapeDtypeStruct((devs, pairs, toks, width), jnp.bfloat16),
        scratch_shapes=[
            pltpu.VMEM((devs, toks, videos * ranks), jnp.bfloat16),
            pltpu.VMEM((length, width), jnp.bfloat16),
        ],
        compiler_params=pltpu.CompilerParams(vmem_limit_bytes=48 << 20),
        cost_estimate=pl.CostEstimate(
            flops=4 * pairs * length * length * width,
            bytes_accessed=8 * pairs * length * width,
            transcendentals=pairs * length * length,
        ),
        name="attend",
    )(me, up_here, asked, keys, asked, *lows)
    return exchange(mixed).reshape(videos, heads, toks, width)


def solution(mesh):
    in_specs = (
        P("grp", "seq", None),
        P("grp", None, "seq", None),
        P("grp", None, "seq", None),
        P("grp", None, "seq", None),
        P("seq", None, None),
        P("seq", None, None),
        P(),
        P("grp"),
    )
    out_specs = P("grp", None, "seq", None)
    return jax.shard_map(body, mesh=mesh, in_specs=in_specs, out_specs=out_specs, check_vma=False)
```

```python
import functools
import math

import jax
import jax.numpy as jnp
from jax import lax
from jax.experimental import pallas as pl
from jax.experimental.pallas import tpu as pltpu
from jax.sharding import PartitionSpec as P

LANES = 128
LOW = 4
ANY = pl.BlockSpec(memory_space=pl.ANY)
VMEM = pl.BlockSpec(memory_space=pltpu.VMEM)
SMEM = pl.BlockSpec(memory_space=pltpu.SMEM)


def bit_count(n):
    bits = n.bit_length() - 1
    assert 1 << bits == n
    return bits


def reversed_bits(j, bits):
    out = 0
    for i in range(bits):
        out = out | (((j >> i) & 1) << (bits - 1 - i))
    return out


def pick_kernel(shape, me_ref, row_ref, req_ref, down_ref, up_ref, *refs):
    devs, bits, per_video, pairs, col_split, rows, tiles = shape
    downs, ups = refs[: bits - 1], refs[bits - 1 : 2 * bits - 2]
    down, up, sems = refs[2 * bits - 2 :]
    slots, ranks, _ = down_ref.shape
    videos = down.shape[0]
    me = me_ref[0]
    for s in range(videos):
        place = row_ref[req_ref[s]]
        slot = place % slots
        owned = place // slots == me
        copies = [
            pltpu.make_async_copy(down_ref.at[slot], down.at[s], sems.at[2 * s]),
            pltpu.make_async_copy(up_ref.at[slot], up.at[s], sems.at[2 * s + 1]),
        ]

        @pl.when(owned)
        def _():
            for copy in copies:
                copy.start()
            for copy in copies:
                copy.wait()

        @pl.when(jnp.logical_not(owned))
        def _():
            down[s] = jnp.zeros(down.shape[1:], down.dtype)
            up[s] = jnp.zeros(up.shape[1:], up.dtype)

    for j in range(devs):
        step = min(bits - j.bit_length(), bits - 2)
        at = j - (1 << (j.bit_length() - 1)) if j >= LOW else j
        dev = me ^ reversed_bits(j, bits)
        video = dev // per_video
        place = dev % per_video
        row = pl.multiple_of((place // col_split) * rows, rows)
        for t in range(tiles):
            col = pl.multiple_of(((place % col_split) * tiles + t) * LANES, LANES)
            downs[step][at, t * rows : (t + 1) * rows, :] = down[
                video, pl.ds(row, rows), pl.ds(col, LANES)
            ]
        for p in range(pairs):
            col = pl.multiple_of((place * pairs + p) * LANES, LANES)
            ups[step][at, p * ranks : (p + 1) * ranks, :] = up[video, :, pl.ds(col, LANES)]


def low_rank_kernel(shape, me_ref, x_ref, g_ref, q_ref, out_ref, down):
    devs, bits, per_video, _, col_split, rows, tiles = shape
    for j in range(devs):
        dev = me_ref[0] ^ reversed_bits(j, bits)
        video = dev // per_video
        place = dev % per_video
        row = pl.multiple_of((place // col_split) * rows, rows)
        for t in range(tiles):
            col = pl.multiple_of(((place % col_split) * tiles + t) * LANES, LANES)
            down[video, pl.ds(row, rows), pl.ds(col, LANES)] = g_ref[j, t * rows : (t + 1) * rows, :]
    first = q_ref.shape[1]
    out_ref[:, :first] = q_ref[...]
    for s in range(x_ref.shape[0]):
        low = lax.dot_general(
            x_ref[s], down[s], (((1,), (1,)), ((), ())), preferred_element_type=jnp.float32
        ).astype(out_ref.dtype)
        half = low.shape[0] // 2
        low = jnp.concatenate([low[:half], low[half:]], axis=1)
        for dev in range(s * per_video, (s + 1) * per_video):
            out_ref[dev, first:] = low


def add_delta(base, low, up, second):
    devs, toks, width = base.shape
    ranks = up.shape[0]
    row = lax.broadcasted_iota(jnp.int32, up.shape, 0)
    part = jnp.where(row // (ranks // 2) == second, up, jnp.zeros_like(up))
    none = jnp.zeros_like(part)
    deltas = [
        jnp.dot(low, jnp.concatenate(pair, axis=0), preferred_element_type=jnp.float32)
        for pair in ((part, none), (none, part))
    ]
    delta = jnp.concatenate([d.reshape(devs, toks // 2, width) for d in deltas], axis=1)
    return (base.astype(jnp.float32) + delta).astype(base.dtype).reshape(devs * toks, width)


def attend_kernel(block, up_ref, q_ref, low_ref, k_ref, v_ref, out_ref, q_mix):
    devs, toks, width = q_ref.shape
    length = devs * toks
    low = low_ref[...].reshape(length // 2, low_ref.shape[2])
    up = up_ref[...]
    keys = k_ref[...].reshape(length, width)
    vals = add_delta(v_ref[...], low, up, 1)
    q_mix[...] = add_delta(q_ref[...], low, up, 0)
    scale = math.log2(math.e) / math.sqrt(width)
    for b in range(0, devs, block):
        q = q_mix[b * toks : (b + block) * toks, :]
        scores = lax.dot_general(
            q, keys, (((1,), (1,)), ((), ())), preferred_element_type=jnp.float32
        )
        top = jnp.max(scores, axis=1, keepdims=True)
        weights = jnp.exp2((scores - top) * scale)
        total = jnp.sum(weights, axis=1, keepdims=True)
        mixed = jnp.dot(weights.astype(jnp.bfloat16), vals, preferred_element_type=jnp.float32)
        out_ref[b : b + block] = (mixed / total).astype(jnp.bfloat16).reshape(block, toks, width)


def body(
    normed_token_features,
    queries,
    projected_keys,
    values,
    adapter_down_factors,
    adapter_up_factors,
    adapter_store_row,
    requests,
):
    videos, toks, model_width = normed_token_features.shape
    heads = queries.shape[1]
    width = queries.shape[3]
    _, ranks, up_width = adapter_up_factors.shape
    devs = lax.axis_size("seq")
    bits = bit_count(devs)
    me = lax.axis_index("seq").astype(jnp.int32)[None]
    pairs = videos * heads // devs
    per_video = devs // videos
    length = devs * toks
    col_split = math.gcd(per_video, model_width // LANES)
    rows = ranks * col_split // per_video
    tiles = model_width // col_split // LANES
    shape = (devs, bits, per_video, pairs, col_split, rows, tiles)

    def swap(tensor, k):
        return lax.ppermute(tensor, "seq", [(i, i ^ k) for i in range(devs)])

    def exchange(tensor):
        return lax.all_to_all(tensor, "seq", split_axis=0, concat_axis=0, tiled=True)

    def by_pairs(tensor):
        return tensor.reshape(devs, pairs, toks, width)

    def after(array, *others):
        return lax.optimization_barrier((array, others))[0]

    quarter = devs // LOW
    others = (2 * quarter, quarter, 3 * quarter)

    def halving(parts, received, i):
        size = parts[i].shape[0]
        start = size if i < bits - 2 else 0
        return sum((r[start : start + size] for r in received), parts[i])

    def to_others(shards):
        return [swap(shards[j + 1 : j + 2], k) for j, k in enumerate(others)]

    keys = exchange(by_pairs(projected_keys))

    steps = [devs >> (i + 1) for i in range(bits - 2)] + [LOW]
    piece_shapes = [(h, tiles * rows, LANES) for h in steps] + [
        (h, pairs * ranks, LANES) for h in steps
    ]
    pieces = pl.pallas_call(
        functools.partial(pick_kernel, shape),
        in_specs=[SMEM, SMEM, SMEM, ANY, ANY],
        out_specs=[VMEM] * (2 * bits - 2),
        out_shape=[jax.ShapeDtypeStruct(s, jnp.bfloat16) for s in piece_shapes],
        scratch_shapes=[
            pltpu.VMEM((videos, ranks, model_width), jnp.bfloat16),
            pltpu.VMEM((videos, ranks, up_width), jnp.bfloat16),
            pltpu.SemaphoreType.DMA((2 * videos,)),
        ],
        compiler_params=pltpu.CompilerParams(vmem_limit_bytes=24 << 20),
        cost_estimate=pl.CostEstimate(
            flops=0,
            bytes_accessed=4 * videos * ranks * (model_width + up_width),
            transcendentals=0,
        ),
        name="pick_factors",
    )(me, adapter_store_row, requests, adapter_down_factors, adapter_up_factors)
    down_pieces, up_pieces = pieces[: bits - 1], pieces[bits - 1 :]

    down_got, up_got = [], []

    def send_up(i, *others):
        up_got.append(swap(after(halving(up_pieces, up_got, i), *others), 1 << i))

    for i in range(bits - 2):
        piece = halving(down_pieces, down_got, i)
        if i > 0:
            send_up(i - 1, piece)
        down_got.append(swap(piece, 1 << i))
    shards = after(halving(down_pieces, down_got, bits - 2), keys, *up_got)
    send_up(bits - 3, shards)
    shard = shards[:1] + sum(to_others(shards))
    gathered = jnp.concatenate([shard] + [swap(shard, k) for k in others], axis=0)
    vals = exchange(after(by_pairs(values), gathered, up_got[-1]))
    up_shards = after(halving(up_pieces, up_got, bits - 2), gathered)
    up_here = (up_shards[:1] + sum(to_others(up_shards))).reshape(pairs, ranks, LANES)
    for i in reversed(range(bits - 2)):
        gathered = jnp.concatenate([gathered, swap(gathered, 1 << i)], axis=0)

    asked = pl.pallas_call(
        functools.partial(low_rank_kernel, shape),
        in_specs=[SMEM, VMEM, VMEM, VMEM],
        out_specs=VMEM,
        scratch_shapes=[pltpu.VMEM((videos, ranks, model_width), jnp.bfloat16)],
        out_shape=jax.ShapeDtypeStruct((devs, pairs * toks + toks // 2, width), jnp.bfloat16),
        compiler_params=pltpu.CompilerParams(vmem_limit_bytes=24 << 20),
        cost_estimate=pl.CostEstimate(
            flops=2 * videos * toks * ranks * model_width,
            bytes_accessed=2 * videos * (toks + ranks) * model_width,
            transcendentals=0,
        ),
        name="low_rank",
    )(me, normed_token_features, gathered, queries.reshape(devs, pairs * toks, width))
    asked = exchange(asked)

    part_spec = pl.BlockSpec((devs, pl.squeezed, toks, width), lambda p: (0, p, 0, 0))
    mixed = pl.pallas_call(
        functools.partial(attend_kernel, math.gcd(devs, max(1, 512 // toks))),
        grid=(pairs,),
        in_specs=[
            pl.BlockSpec((pl.squeezed, ranks, LANES), lambda p: (p, 0, 0)),
            pl.BlockSpec((devs, toks, width), lambda p: (0, p, 0)),
            pl.BlockSpec((devs, toks // 2, width), lambda p: (0, 2 * pairs, 0)),
            part_spec,
            part_spec,
        ],
        out_specs=part_spec,
        out_shape=jax.ShapeDtypeStruct((devs, pairs, toks, width), jnp.bfloat16),
        scratch_shapes=[pltpu.VMEM((length, width), jnp.bfloat16)],
        compiler_params=pltpu.CompilerParams(vmem_limit_bytes=48 << 20),
        cost_estimate=pl.CostEstimate(
            flops=4 * pairs * length * length * width,
            bytes_accessed=8 * pairs * length * width,
            transcendentals=pairs * length * length,
        ),
        name="attend",
    )(up_here, asked, asked, keys, vals)
    return exchange(mixed).reshape(videos, heads, toks, width)


def solution(mesh):
    in_specs = (
        P("grp", "seq", None),
        P("grp", None, "seq", None),
        P("grp", None, "seq", None),
        P("grp", None, "seq", None),
        P("seq", None, None),
        P("seq", None, None),
        P(),
        P("grp"),
    )
    out_specs = P("grp", None, "seq", None)
    return jax.shard_map(body, mesh=mesh, in_specs=in_specs, out_specs=out_specs, check_vma=False)
```

```python
import functools
import math

import jax
import jax.numpy as jnp
from jax import lax
from jax.experimental import pallas as pl
from jax.experimental.pallas import tpu as pltpu
from jax.sharding import PartitionSpec as P

LANES = 128
LOW = 4
ANY = pl.BlockSpec(memory_space=pl.ANY)
VMEM = pl.BlockSpec(memory_space=pltpu.VMEM)
SMEM = pl.BlockSpec(memory_space=pltpu.SMEM)


def bit_count(n):
    bits = n.bit_length() - 1
    assert 1 << bits == n
    return bits


def reversed_bits(j, bits):
    out = 0
    for i in range(bits):
        out = out | (((j >> i) & 1) << (bits - 1 - i))
    return out


def pick_kernel(shape, me_ref, row_ref, req_ref, down_ref, up_ref, *refs):
    devs, bits, per_video, pairs, col_split, rows, tiles = shape
    downs, ups = refs[: bits - 1], refs[bits - 1 : 2 * bits - 2]
    down, up, sems = refs[2 * bits - 2 :]
    slots, ranks, _ = down_ref.shape
    videos = down.shape[0]
    me = me_ref[0]
    for s in range(videos):
        place = row_ref[req_ref[s]]
        slot = place % slots
        owned = place // slots == me
        copies = [
            pltpu.make_async_copy(down_ref.at[slot], down.at[s], sems.at[2 * s]),
            pltpu.make_async_copy(up_ref.at[slot], up.at[s], sems.at[2 * s + 1]),
        ]

        @pl.when(owned)
        def _():
            for copy in copies:
                copy.start()
            for copy in copies:
                copy.wait()

        @pl.when(jnp.logical_not(owned))
        def _():
            down[s] = jnp.zeros(down.shape[1:], down.dtype)
            up[s] = jnp.zeros(up.shape[1:], up.dtype)

    for j in range(devs):
        step = min(bits - j.bit_length(), bits - 2)
        at = j - (1 << (j.bit_length() - 1)) if j >= LOW else j
        dev = me ^ reversed_bits(j, bits)
        video = dev // per_video
        place = dev % per_video
        row = pl.multiple_of((place // col_split) * rows, rows)
        for t in range(tiles):
            col = pl.multiple_of(((place % col_split) * tiles + t) * LANES, LANES)
            downs[step][at, t * rows : (t + 1) * rows, :] = down[
                video, pl.ds(row, rows), pl.ds(col, LANES)
            ]
        for p in range(pairs):
            col = pl.multiple_of((place * pairs + p) * LANES, LANES)
            ups[step][at, p * ranks : (p + 1) * ranks, :] = up[video, :, pl.ds(col, LANES)]


def low_rank_kernel(shape, me_ref, x_ref, g_ref, q_ref, out_ref, down):
    devs, bits, per_video, _, col_split, rows, tiles = shape
    for j in range(devs):
        dev = me_ref[0] ^ reversed_bits(j, bits)
        video = dev // per_video
        place = dev % per_video
        row = pl.multiple_of((place // col_split) * rows, rows)
        for t in range(tiles):
            col = pl.multiple_of(((place % col_split) * tiles + t) * LANES, LANES)
            down[video, pl.ds(row, rows), pl.ds(col, LANES)] = g_ref[j, t * rows : (t + 1) * rows, :]
    first = q_ref.shape[1]
    out_ref[:, :first] = q_ref[...]
    for s in range(x_ref.shape[0]):
        low = lax.dot_general(
            x_ref[s], down[s], (((1,), (1,)), ((), ())), preferred_element_type=jnp.float32
        ).astype(out_ref.dtype)
        half = low.shape[0] // 2
        low = jnp.concatenate([low[:half], low[half:]], axis=1)
        for dev in range(s * per_video, (s + 1) * per_video):
            out_ref[dev, first:] = low


def add_delta(base, low, up, second):
    devs, toks, width = base.shape
    ranks = up.shape[0]
    row = lax.broadcasted_iota(jnp.int32, up.shape, 0)
    part = jnp.where(row // (ranks // 2) == second, up, jnp.zeros_like(up))
    none = jnp.zeros_like(part)
    deltas = [
        jnp.dot(low, jnp.concatenate(pair, axis=0), preferred_element_type=jnp.float32)
        for pair in ((part, none), (none, part))
    ]
    delta = jnp.concatenate([d.reshape(devs, toks // 2, width) for d in deltas], axis=1)
    return (base.astype(jnp.float32) + delta).astype(base.dtype).reshape(devs * toks, width)


def attend_kernel(block, up_ref, q_ref, low_ref, k_ref, v_ref, out_ref, q_mix):
    devs, toks, width = q_ref.shape
    length = devs * toks
    low = low_ref[...].reshape(length // 2, low_ref.shape[2])
    up = up_ref[...]
    keys = k_ref[...].reshape(length, width)
    vals = add_delta(v_ref[...], low, up, 1)
    q_mix[...] = add_delta(q_ref[...], low, up, 0)
    scale = math.log2(math.e) / math.sqrt(width)
    for b in range(0, devs, block):
        q = q_mix[b * toks : (b + block) * toks, :]
        scores = lax.dot_general(
            q, keys, (((1,), (1,)), ((), ())), preferred_element_type=jnp.float32
        )
        top = jnp.max(scores, axis=1, keepdims=True)
        weights = jnp.exp2((scores - top) * scale)
        total = jnp.sum(weights, axis=1, keepdims=True)
        mixed = jnp.dot(weights.astype(jnp.bfloat16), vals, preferred_element_type=jnp.float32)
        out_ref[b : b + block] = (mixed / total).astype(jnp.bfloat16).reshape(block, toks, width)


def body(
    normed_token_features,
    queries,
    projected_keys,
    values,
    adapter_down_factors,
    adapter_up_factors,
    adapter_store_row,
    requests,
):
    videos, toks, model_width = normed_token_features.shape
    heads = queries.shape[1]
    width = queries.shape[3]
    _, ranks, up_width = adapter_up_factors.shape
    devs = lax.axis_size("seq")
    bits = bit_count(devs)
    me = lax.axis_index("seq").astype(jnp.int32)[None]
    pairs = videos * heads // devs
    per_video = devs // videos
    length = devs * toks
    col_split = math.gcd(per_video, model_width // LANES)
    rows = ranks * col_split // per_video
    tiles = model_width // col_split // LANES
    shape = (devs, bits, per_video, pairs, col_split, rows, tiles)

    def swap(tensor, k):
        return lax.ppermute(tensor, "seq", [(i, i ^ k) for i in range(devs)])

    def exchange(tensor):
        return lax.all_to_all(tensor, "seq", split_axis=0, concat_axis=0, tiled=True)

    def by_pairs(tensor):
        return tensor.reshape(devs, pairs, toks, width)

    def after(array, *others):
        return lax.optimization_barrier((array, others))[0]

    quarter = devs // LOW
    others = (2 * quarter, quarter, 3 * quarter)

    def halving(parts, received, i):
        size = parts[i].shape[0]
        start = size if i < bits - 2 else 0
        return sum((r[start : start + size] for r in received), parts[i])

    def to_others(shards):
        return [swap(shards[j + 1 : j + 2], k) for j, k in enumerate(others)]

    keys = exchange(by_pairs(projected_keys))

    steps = [devs >> (i + 1) for i in range(bits - 2)] + [LOW]
    piece_shapes = [(h, tiles * rows, LANES) for h in steps] + [
        (h, pairs * ranks, LANES) for h in steps
    ]
    pieces = pl.pallas_call(
        functools.partial(pick_kernel, shape),
        in_specs=[SMEM, SMEM, SMEM, ANY, ANY],
        out_specs=[VMEM] * (2 * bits - 2),
        out_shape=[jax.ShapeDtypeStruct(s, jnp.bfloat16) for s in piece_shapes],
        scratch_shapes=[
            pltpu.VMEM((videos, ranks, model_width), jnp.bfloat16),
            pltpu.VMEM((videos, ranks, up_width), jnp.bfloat16),
            pltpu.SemaphoreType.DMA((2 * videos,)),
        ],
        compiler_params=pltpu.CompilerParams(vmem_limit_bytes=24 << 20),
        cost_estimate=pl.CostEstimate(
            flops=0,
            bytes_accessed=4 * videos * ranks * (model_width + up_width),
            transcendentals=0,
        ),
        name="pick_factors",
    )(me, adapter_store_row, requests, adapter_down_factors, adapter_up_factors)
    down_pieces, up_pieces = pieces[: bits - 1], pieces[bits - 1 :]

    down_got, up_got = [], []

    def send_up(i, *others):
        up_got.append(swap(after(halving(up_pieces, up_got, i), *others), 1 << i))

    for i in range(bits - 2):
        piece = halving(down_pieces, down_got, i)
        if i > 0:
            send_up(i - 1, piece)
        down_got.append(swap(piece, 1 << i))
    send_up(bits - 3, piece)
    shards = after(halving(down_pieces, down_got, bits - 2), keys, *up_got[:-1])
    shard = shards[:1] + sum(to_others(shards))
    shard = after(shard, up_got[-1])
    gathered = jnp.concatenate([shard] + [swap(shard, k) for k in others], axis=0)
    vals = exchange(after(by_pairs(values), gathered))
    up_shards = after(halving(up_pieces, up_got, bits - 2), gathered)
    up_here = (up_shards[:1] + sum(to_others(up_shards))).reshape(pairs, ranks, LANES)
    for i in reversed(range(bits - 2)):
        gathered = jnp.concatenate([gathered, swap(gathered, 1 << i)], axis=0)

    gathered = after(gathered, up_here)

    asked = pl.pallas_call(
        functools.partial(low_rank_kernel, shape),
        in_specs=[SMEM, VMEM, VMEM, VMEM],
        out_specs=VMEM,
        scratch_shapes=[pltpu.VMEM((videos, ranks, model_width), jnp.bfloat16)],
        out_shape=jax.ShapeDtypeStruct((devs, pairs * toks + toks // 2, width), jnp.bfloat16),
        compiler_params=pltpu.CompilerParams(vmem_limit_bytes=24 << 20),
        cost_estimate=pl.CostEstimate(
            flops=2 * videos * toks * ranks * model_width,
            bytes_accessed=2 * videos * (toks + ranks) * model_width,
            transcendentals=0,
        ),
        name="low_rank",
    )(me, normed_token_features, gathered, queries.reshape(devs, pairs * toks, width))
    asked = exchange(asked)

    part_spec = pl.BlockSpec((devs, pl.squeezed, toks, width), lambda p: (0, p, 0, 0))
    mixed = pl.pallas_call(
        functools.partial(attend_kernel, math.gcd(devs, max(1, 512 // toks))),
        grid=(pairs,),
        in_specs=[
            pl.BlockSpec((pl.squeezed, ranks, LANES), lambda p: (p, 0, 0)),
            pl.BlockSpec((devs, toks, width), lambda p: (0, p, 0)),
            pl.BlockSpec((devs, toks // 2, width), lambda p: (0, 2 * pairs, 0)),
            part_spec,
            part_spec,
        ],
        out_specs=part_spec,
        out_shape=jax.ShapeDtypeStruct((devs, pairs, toks, width), jnp.bfloat16),
        scratch_shapes=[pltpu.VMEM((length, width), jnp.bfloat16)],
        compiler_params=pltpu.CompilerParams(vmem_limit_bytes=48 << 20),
        cost_estimate=pl.CostEstimate(
            flops=4 * pairs * length * length * width,
            bytes_accessed=8 * pairs * length * width,
            transcendentals=pairs * length * length,
        ),
        name="attend",
    )(up_here, asked, asked, keys, vals)
    return exchange(mixed).reshape(videos, heads, toks, width)


def solution(mesh):
    in_specs = (
        P("grp", "seq", None),
        P("grp", None, "seq", None),
        P("grp", None, "seq", None),
        P("grp", None, "seq", None),
        P("seq", None, None),
        P("seq", None, None),
        P(),
        P("grp"),
    )
    out_specs = P("grp", None, "seq", None)
    return jax.shard_map(body, mesh=mesh, in_specs=in_specs, out_specs=out_specs, check_vma=False)
```

```python
import functools
import math

import jax
import jax.numpy as jnp
from jax import lax
from jax.experimental import pallas as pl
from jax.experimental.pallas import tpu as pltpu
from jax.sharding import PartitionSpec as P

LANES = 128
LOW = 4
ANY = pl.BlockSpec(memory_space=pl.ANY)
VMEM = pl.BlockSpec(memory_space=pltpu.VMEM)
SMEM = pl.BlockSpec(memory_space=pltpu.SMEM)


def bit_count(n):
    bits = n.bit_length() - 1
    assert 1 << bits == n
    return bits


def reversed_bits(j, bits):
    out = 0
    for i in range(bits):
        out = out | (((j >> i) & 1) << (bits - 1 - i))
    return out


def pick_kernel(shape, me_ref, row_ref, req_ref, down_ref, up_ref, *refs):
    devs, bits, per_video, pairs, col_split, rows, tiles = shape
    downs, ups = refs[: bits - 1], refs[bits - 1 : 2 * bits - 2]
    down, up, sems = refs[2 * bits - 2 :]
    slots, ranks, _ = down_ref.shape
    videos = down.shape[0]
    me = me_ref[0]
    for s in range(videos):
        place = row_ref[req_ref[s]]
        slot = place % slots
        owned = place // slots == me
        copies = [
            pltpu.make_async_copy(down_ref.at[slot], down.at[s], sems.at[2 * s]),
            pltpu.make_async_copy(up_ref.at[slot], up.at[s], sems.at[2 * s + 1]),
        ]

        @pl.when(owned)
        def _():
            for copy in copies:
                copy.start()
            for copy in copies:
                copy.wait()

        @pl.when(jnp.logical_not(owned))
        def _():
            down[s] = jnp.zeros(down.shape[1:], down.dtype)
            up[s] = jnp.zeros(up.shape[1:], up.dtype)

    for j in range(devs):
        step = min(bits - j.bit_length(), bits - 2)
        at = j - (1 << (j.bit_length() - 1)) if j >= LOW else j
        dev = me ^ reversed_bits(j, bits)
        video = dev // per_video
        place = dev % per_video
        row = pl.multiple_of((place // col_split) * rows, rows)
        for t in range(tiles):
            col = pl.multiple_of(((place % col_split) * tiles + t) * LANES, LANES)
            downs[step][at, t * rows : (t + 1) * rows, :] = down[
                video, pl.ds(row, rows), pl.ds(col, LANES)
            ]
        for p in range(pairs):
            col = pl.multiple_of((place * pairs + p) * LANES, LANES)
            ups[step][at, p * ranks : (p + 1) * ranks, :] = up[video, :, pl.ds(col, LANES)]


def sum_kernel(picks, *refs):
    outs = refs[-len(picks) :]
    for out, terms in zip(outs, picks):
        size = out.shape[0]
        parts = [refs[i][first : first + size] for i, first in terms]
        out[...] = sum(parts[1:], parts[0])


def join_kernel(*refs):
    out, first = refs[-1], 0
    for ref in refs[:-1]:
        out[first : first + ref.shape[0]] = ref[...]
        first += ref.shape[0]


def on_vmem(kernel, shapes, name, *arrays):
    return pl.pallas_call(
        kernel,
        in_specs=[VMEM] * len(arrays),
        out_specs=[VMEM] * len(shapes),
        out_shape=[jax.ShapeDtypeStruct(s, arrays[0].dtype) for s in shapes],
        compiler_params=pltpu.CompilerParams(vmem_limit_bytes=16 << 20),
        cost_estimate=pl.CostEstimate(
            flops=0, bytes_accessed=2 * sum(a.size for a in arrays), transcendentals=0
        ),
        name=name,
    )(*arrays)


def low_rank_kernel(shape, me_ref, x_ref, q_ref, *refs):
    devs, bits, per_video, _, col_split, rows, tiles = shape
    parts, out_ref, down = refs[:-2], refs[-2], refs[-1]
    blocks = [(ref, i) for ref in parts for i in range(ref.shape[0])]
    for j, (ref, i) in enumerate(blocks):
        dev = me_ref[0] ^ reversed_bits(j, bits)
        video = dev // per_video
        place = dev % per_video
        row = pl.multiple_of((place // col_split) * rows, rows)
        for t in range(tiles):
            col = pl.multiple_of(((place % col_split) * tiles + t) * LANES, LANES)
            down[video, pl.ds(row, rows), pl.ds(col, LANES)] = ref[i, t * rows : (t + 1) * rows, :]
    first = q_ref.shape[1]
    out_ref[:, :first] = q_ref[...]
    for s in range(x_ref.shape[0]):
        low = lax.dot_general(
            x_ref[s], down[s], (((1,), (1,)), ((), ())), preferred_element_type=jnp.float32
        ).astype(out_ref.dtype)
        half = low.shape[0] // 2
        low = jnp.concatenate([low[:half], low[half:]], axis=1)
        for dev in range(s * per_video, (s + 1) * per_video):
            out_ref[dev, first:] = low


def add_delta(base, low, up, second):
    devs, toks, width = base.shape
    ranks = up.shape[0]
    row = lax.broadcasted_iota(jnp.int32, up.shape, 0)
    part = jnp.where(row // (ranks // 2) == second, up, jnp.zeros_like(up))
    none = jnp.zeros_like(part)
    deltas = [
        jnp.dot(low, jnp.concatenate(pair, axis=0), preferred_element_type=jnp.float32)
        for pair in ((part, none), (none, part))
    ]
    delta = jnp.concatenate([d.reshape(devs, toks // 2, width) for d in deltas], axis=1)
    return (base.astype(jnp.float32) + delta).astype(base.dtype).reshape(devs * toks, width)


def attend_kernel(block, up_ref, q_ref, low_ref, k_ref, v_ref, out_ref, q_mix):
    devs, toks, width = q_ref.shape
    length = devs * toks
    low = low_ref[...].reshape(length // 2, low_ref.shape[2])
    up = up_ref[...]
    keys = k_ref[...].reshape(length, width)
    vals = add_delta(v_ref[...], low, up, 1)
    q_mix[...] = add_delta(q_ref[...], low, up, 0)
    scale = math.log2(math.e) / math.sqrt(width)
    for b in range(0, devs, block):
        q = q_mix[b * toks : (b + block) * toks, :]
        scores = lax.dot_general(
            q, keys, (((1,), (1,)), ((), ())), preferred_element_type=jnp.float32
        )
        top = jnp.max(scores, axis=1, keepdims=True)
        weights = jnp.exp2((scores - top) * scale)
        total = jnp.sum(weights, axis=1, keepdims=True)
        mixed = jnp.dot(weights.astype(jnp.bfloat16), vals, preferred_element_type=jnp.float32)
        out_ref[b : b + block] = (mixed / total).astype(jnp.bfloat16).reshape(block, toks, width)


def body(
    normed_token_features,
    queries,
    projected_keys,
    values,
    adapter_down_factors,
    adapter_up_factors,
    adapter_store_row,
    requests,
):
    videos, toks, model_width = normed_token_features.shape
    heads = queries.shape[1]
    width = queries.shape[3]
    _, ranks, up_width = adapter_up_factors.shape
    devs = lax.axis_size("seq")
    bits = bit_count(devs)
    me = lax.axis_index("seq").astype(jnp.int32)[None]
    pairs = videos * heads // devs
    per_video = devs // videos
    length = devs * toks
    col_split = math.gcd(per_video, model_width // LANES)
    rows = ranks * col_split // per_video
    tiles = model_width // col_split // LANES
    shape = (devs, bits, per_video, pairs, col_split, rows, tiles)

    def swap(tensor, k):
        return lax.ppermute(tensor, "seq", [(i, i ^ k) for i in range(devs)])

    def exchange(tensor):
        return lax.all_to_all(tensor, "seq", split_axis=0, concat_axis=0, tiled=True)

    def by_pairs(tensor):
        return tensor.reshape(devs, pairs, toks, width)

    def after(array, *others):
        return lax.optimization_barrier((array, others))[0]

    quarter = devs // LOW
    others = (2 * quarter, quarter, 3 * quarter)

    def halving(parts, received, i):
        size = parts[i].shape[0]
        terms = [(0, 0)] + [(1 + n, size) for n in range(len(received))]
        return on_vmem(
            functools.partial(sum_kernel, [terms]), [parts[i].shape], "halve", parts[i], *received
        )[0]

    def splitting(parts, received):
        size = (1,) + parts[-1].shape[1:]
        picks = [[(n, j) for n in range(1 + len(received))] for j in range(LOW)]
        return on_vmem(
            functools.partial(sum_kernel, picks), [size] * LOW, "split", parts[-1], *received
        )

    def to_others(shards):
        return [swap(shard, k) for shard, k in zip(shards[1:], others)]

    def total(shard, received):
        picks = [[(n, 0) for n in range(LOW)]]
        return on_vmem(
            functools.partial(sum_kernel, picks), [shard.shape], "total", shard, *received
        )[0]

    def join(arrays):
        count = sum(a.shape[0] for a in arrays)
        return on_vmem(join_kernel, [(count,) + arrays[0].shape[1:]], "join", *arrays)[0]

    keys = exchange(by_pairs(projected_keys))

    steps = [devs >> (i + 1) for i in range(bits - 2)] + [LOW]
    piece_shapes = [(h, tiles * rows, LANES) for h in steps] + [
        (h, pairs * ranks, LANES) for h in steps
    ]
    pieces = pl.pallas_call(
        functools.partial(pick_kernel, shape),
        in_specs=[SMEM, SMEM, SMEM, ANY, ANY],
        out_specs=[VMEM] * (2 * bits - 2),
        out_shape=[jax.ShapeDtypeStruct(s, jnp.bfloat16) for s in piece_shapes],
        scratch_shapes=[
            pltpu.VMEM((videos, ranks, model_width), jnp.bfloat16),
            pltpu.VMEM((videos, ranks, up_width), jnp.bfloat16),
            pltpu.SemaphoreType.DMA((2 * videos,)),
        ],
        compiler_params=pltpu.CompilerParams(vmem_limit_bytes=24 << 20),
        cost_estimate=pl.CostEstimate(
            flops=0,
            bytes_accessed=4 * videos * ranks * (model_width + up_width),
            transcendentals=0,
        ),
        name="pick_factors",
    )(me, adapter_store_row, requests, adapter_down_factors, adapter_up_factors)
    down_pieces, up_pieces = pieces[: bits - 1], pieces[bits - 1 :]

    down_got, up_got = [], []

    def send_up(i, *others):
        up_got.append(swap(after(halving(up_pieces, up_got, i), *others), 1 << i))

    for i in range(bits - 2):
        piece = down_pieces[0] if i == 0 else halving(down_pieces, down_got, i)
        if i > 0:
            part = up_pieces[0] if i == 1 else halving(up_pieces, up_got, i - 1)
            up_got.append(swap(after(part, piece), 1 << (i - 1)))
        down_got.append(swap(piece, 1 << i))
    part = after(halving(up_pieces, up_got, bits - 3), piece)
    up_got.append(swap(part, 1 << (bits - 3)))
    held = splitting((after(down_pieces[-1], keys, *up_got[:-1]),), down_got)
    shard = after(total(held[0], to_others(held)), up_got[-1])
    up_held = splitting((after(up_pieces[-1], shard),), up_got)
    gathered = [shard] + [swap(shard, k) for k in others]
    up_here = total(up_held[0], to_others(up_held))
    vals = exchange(after(by_pairs(values), *gathered, up_here))
    up_here = up_here.reshape(pairs, ranks, LANES)
    joined = join(gathered)
    for i in reversed(range(bits - 2)):
        gathered = [joined, swap(joined, 1 << i)]
        if i > 0:
            joined = join(gathered)

    asked = pl.pallas_call(
        functools.partial(low_rank_kernel, shape),
        in_specs=[SMEM, VMEM, VMEM] + [VMEM] * len(gathered),
        out_specs=VMEM,
        scratch_shapes=[pltpu.VMEM((videos, ranks, model_width), jnp.bfloat16)],
        out_shape=jax.ShapeDtypeStruct((devs, pairs * toks + toks // 2, width), jnp.bfloat16),
        compiler_params=pltpu.CompilerParams(vmem_limit_bytes=24 << 20),
        cost_estimate=pl.CostEstimate(
            flops=2 * videos * toks * ranks * model_width,
            bytes_accessed=2 * videos * (toks + ranks) * model_width,
            transcendentals=0,
        ),
        name="low_rank",
    )(me, normed_token_features, queries.reshape(devs, pairs * toks, width), *gathered)
    asked = exchange(asked)

    part_spec = pl.BlockSpec((devs, pl.squeezed, toks, width), lambda p: (0, p, 0, 0))
    mixed = pl.pallas_call(
        functools.partial(attend_kernel, math.gcd(devs, max(1, 512 // toks))),
        grid=(pairs,),
        in_specs=[
            pl.BlockSpec((pl.squeezed, ranks, LANES), lambda p: (p, 0, 0)),
            pl.BlockSpec((devs, toks, width), lambda p: (0, p, 0)),
            pl.BlockSpec((devs, toks // 2, width), lambda p: (0, 2 * pairs, 0)),
            part_spec,
            part_spec,
        ],
        out_specs=part_spec,
        out_shape=jax.ShapeDtypeStruct((devs, pairs, toks, width), jnp.bfloat16),
        scratch_shapes=[pltpu.VMEM((length, width), jnp.bfloat16)],
        compiler_params=pltpu.CompilerParams(vmem_limit_bytes=48 << 20),
        cost_estimate=pl.CostEstimate(
            flops=4 * pairs * length * length * width,
            bytes_accessed=8 * pairs * length * width,
            transcendentals=pairs * length * length,
        ),
        name="attend",
    )(up_here, asked, asked, keys, vals)
    return exchange(mixed).reshape(videos, heads, toks, width)


def solution(mesh):
    in_specs = (
        P("grp", "seq", None),
        P("grp", None, "seq", None),
        P("grp", None, "seq", None),
        P("grp", None, "seq", None),
        P("seq", None, None),
        P("seq", None, None),
        P(),
        P("grp"),
    )
    out_specs = P("grp", None, "seq", None)
    return jax.shard_map(body, mesh=mesh, in_specs=in_specs, out_specs=out_specs, check_vma=False)
```

```python
import functools
import math

import jax
import jax.numpy as jnp
from jax import lax
from jax.experimental import pallas as pl
from jax.experimental.pallas import tpu as pltpu
from jax.sharding import PartitionSpec as P

LANES = 128
LOW = 4
ANY = pl.BlockSpec(memory_space=pl.ANY)
VMEM = pl.BlockSpec(memory_space=pltpu.VMEM)
SMEM = pl.BlockSpec(memory_space=pltpu.SMEM)


def bit_count(n):
    bits = n.bit_length() - 1
    assert 1 << bits == n
    return bits


def reversed_bits(j, bits):
    out = 0
    for i in range(bits):
        out = out | (((j >> i) & 1) << (bits - 1 - i))
    return out


def pick_kernel(shape, me_ref, row_ref, req_ref, down_ref, up_ref, *refs):
    devs, bits, per_video, pairs, col_split, rows, tiles = shape
    downs, ups = refs[: bits - 1], refs[bits - 1 : 2 * bits - 2]
    down, up, sems = refs[2 * bits - 2 :]
    slots, ranks, _ = down_ref.shape
    videos = down.shape[0]
    me = me_ref[0]
    for s in range(videos):
        place = row_ref[req_ref[s]]
        slot = place % slots
        owned = place // slots == me
        copies = [
            pltpu.make_async_copy(down_ref.at[slot], down.at[s], sems.at[2 * s]),
            pltpu.make_async_copy(up_ref.at[slot], up.at[s], sems.at[2 * s + 1]),
        ]

        @pl.when(owned)
        def _():
            for copy in copies:
                copy.start()
            for copy in copies:
                copy.wait()

        @pl.when(jnp.logical_not(owned))
        def _():
            down[s] = jnp.zeros(down.shape[1:], down.dtype)
            up[s] = jnp.zeros(up.shape[1:], up.dtype)

    for j in range(devs):
        step = min(bits - j.bit_length(), bits - 2)
        at = j - (1 << (j.bit_length() - 1)) if j >= LOW else j
        dev = me ^ reversed_bits(j, bits)
        video = dev // per_video
        place = dev % per_video
        row = pl.multiple_of((place // col_split) * rows, rows)
        for t in range(tiles):
            col = pl.multiple_of(((place % col_split) * tiles + t) * LANES, LANES)
            downs[step][at, t * rows : (t + 1) * rows, :] = down[
                video, pl.ds(row, rows), pl.ds(col, LANES)
            ]
        for p in range(pairs):
            col = pl.multiple_of((place * pairs + p) * LANES, LANES)
            ups[step][at, p * ranks : (p + 1) * ranks, :] = up[video, :, pl.ds(col, LANES)]


def sum_kernel(picks, *refs):
    outs = refs[-len(picks) :]
    for out, terms in zip(outs, picks):
        size = out.shape[0]
        parts = [refs[i][first : first + size] for i, first in terms]
        out[...] = sum(parts[1:], parts[0])


def join_kernel(*refs):
    out, first = refs[-1], 0
    for ref in refs[:-1]:
        out[first : first + ref.shape[0]] = ref[...]
        first += ref.shape[0]


def on_vmem(kernel, shapes, name, *arrays):
    return pl.pallas_call(
        kernel,
        in_specs=[VMEM] * len(arrays),
        out_specs=[VMEM] * len(shapes),
        out_shape=[jax.ShapeDtypeStruct(s, arrays[0].dtype) for s in shapes],
        compiler_params=pltpu.CompilerParams(vmem_limit_bytes=16 << 20),
        cost_estimate=pl.CostEstimate(
            flops=0, bytes_accessed=2 * sum(a.size for a in arrays), transcendentals=0
        ),
        name=name,
    )(*arrays)


def low_rank_kernel(shape, me_ref, x_ref, *refs):
    devs, bits, per_video, _, col_split, rows, tiles = shape
    parts, out_ref, down = refs[:-2], refs[-2], refs[-1]
    blocks = [(ref, i) for ref in parts for i in range(ref.shape[0])]
    for j, (ref, i) in enumerate(blocks):
        dev = me_ref[0] ^ reversed_bits(j, bits)
        video = dev // per_video
        place = dev % per_video
        row = pl.multiple_of((place // col_split) * rows, rows)
        for t in range(tiles):
            col = pl.multiple_of(((place % col_split) * tiles + t) * LANES, LANES)
            down[video, pl.ds(row, rows), pl.ds(col, LANES)] = ref[i, t * rows : (t + 1) * rows, :]
    for s in range(x_ref.shape[0]):
        low = lax.dot_general(
            x_ref[s], down[s], (((1,), (1,)), ((), ())), preferred_element_type=jnp.float32
        ).astype(out_ref.dtype)
        half = low.shape[0] // 2
        out_ref[s] = jnp.concatenate([low[:half], low[half:]], axis=1)


def choose_kernel(per_video, me_ref, *refs):
    ins, outs = refs[:LOW], refs[LOW:]
    for i, out in enumerate(outs):
        video = (me_ref[0] ^ (LOW * i)) // per_video
        for j in range(LOW):
            out[j] = ins[j][video]


def add_delta(base, low, up, second):
    devs, toks, width = base.shape
    ranks = up.shape[0]
    row = lax.broadcasted_iota(jnp.int32, up.shape, 0)
    part = jnp.where(row // (ranks // 2) == second, up, jnp.zeros_like(up))
    none = jnp.zeros_like(part)
    deltas = [
        jnp.dot(low, jnp.concatenate(pair, axis=0), preferred_element_type=jnp.float32)
        for pair in ((part, none), (none, part))
    ]
    delta = jnp.concatenate([d.reshape(devs, toks // 2, width) for d in deltas], axis=1)
    return (base.astype(jnp.float32) + delta).astype(base.dtype).reshape(devs * toks, width)


def attend_kernel(block, me_ref, up_ref, q_ref, k_ref, v_ref, *refs):
    low_refs, out_ref, low_all, q_mix = refs[:-3], refs[-3], refs[-2], refs[-1]
    devs, toks, width = q_ref.shape
    length = devs * toks
    for k in range(devs):
        low_all[me_ref[0] ^ k] = low_refs[k // LOW][k % LOW]
    low = low_all[...].reshape(length // 2, low_all.shape[2])
    up = up_ref[...]
    keys = k_ref[...].reshape(length, width)
    vals = add_delta(v_ref[...], low, up, 1)
    q_mix[...] = add_delta(q_ref[...], low, up, 0)
    scale = math.log2(math.e) / math.sqrt(width)
    for b in range(0, devs, block):
        q = q_mix[b * toks : (b + block) * toks, :]
        scores = lax.dot_general(
            q, keys, (((1,), (1,)), ((), ())), preferred_element_type=jnp.float32
        )
        top = jnp.max(scores, axis=1, keepdims=True)
        weights = jnp.exp2((scores - top) * scale)
        total = jnp.sum(weights, axis=1, keepdims=True)
        mixed = jnp.dot(weights.astype(jnp.bfloat16), vals, preferred_element_type=jnp.float32)
        out_ref[b : b + block] = (mixed / total).astype(jnp.bfloat16).reshape(block, toks, width)


def body(
    normed_token_features,
    queries,
    projected_keys,
    values,
    adapter_down_factors,
    adapter_up_factors,
    adapter_store_row,
    requests,
):
    videos, toks, model_width = normed_token_features.shape
    heads = queries.shape[1]
    width = queries.shape[3]
    _, ranks, up_width = adapter_up_factors.shape
    devs = lax.axis_size("seq")
    bits = bit_count(devs)
    me = lax.axis_index("seq").astype(jnp.int32)[None]
    pairs = videos * heads // devs
    per_video = devs // videos
    length = devs * toks
    col_split = math.gcd(per_video, model_width // LANES)
    rows = ranks * col_split // per_video
    tiles = model_width // col_split // LANES
    shape = (devs, bits, per_video, pairs, col_split, rows, tiles)

    def swap(tensor, k):
        return lax.ppermute(tensor, "seq", [(i, i ^ k) for i in range(devs)])

    def exchange(tensor):
        return lax.all_to_all(tensor, "seq", split_axis=0, concat_axis=0, tiled=True)

    def by_pairs(tensor):
        return tensor.reshape(devs, pairs, toks, width)

    def after(array, *others):
        return lax.optimization_barrier((array, others))[0]

    quarter = devs // LOW
    others = (2 * quarter, quarter, 3 * quarter)

    def halving(parts, received, i):
        size = parts[i].shape[0]
        terms = [(0, 0)] + [(1 + n, size) for n in range(len(received))]
        return on_vmem(
            functools.partial(sum_kernel, [terms]), [parts[i].shape], "halve", parts[i], *received
        )[0]

    def splitting(parts, received):
        size = (1,) + parts[-1].shape[1:]
        picks = [[(n, j) for n in range(1 + len(received))] for j in range(LOW)]
        return on_vmem(
            functools.partial(sum_kernel, picks), [size] * LOW, "split", parts[-1], *received
        )

    def to_others(shards):
        return [swap(shard, k) for shard, k in zip(shards[1:], others)]

    def total(shard, received):
        picks = [[(n, 0) for n in range(LOW)]]
        return on_vmem(
            functools.partial(sum_kernel, picks), [shard.shape], "total", shard, *received
        )[0]

    def join(arrays):
        count = sum(a.shape[0] for a in arrays)
        return on_vmem(join_kernel, [(count,) + arrays[0].shape[1:]], "join", *arrays)[0]

    keys = exchange(by_pairs(projected_keys))

    steps = [devs >> (i + 1) for i in range(bits - 2)] + [LOW]
    piece_shapes = [(h, tiles * rows, LANES) for h in steps] + [
        (h, pairs * ranks, LANES) for h in steps
    ]
    pieces = pl.pallas_call(
        functools.partial(pick_kernel, shape),
        in_specs=[SMEM, SMEM, SMEM, ANY, ANY],
        out_specs=[VMEM] * (2 * bits - 2),
        out_shape=[jax.ShapeDtypeStruct(s, jnp.bfloat16) for s in piece_shapes],
        scratch_shapes=[
            pltpu.VMEM((videos, ranks, model_width), jnp.bfloat16),
            pltpu.VMEM((videos, ranks, up_width), jnp.bfloat16),
            pltpu.SemaphoreType.DMA((2 * videos,)),
        ],
        compiler_params=pltpu.CompilerParams(vmem_limit_bytes=24 << 20),
        cost_estimate=pl.CostEstimate(
            flops=0,
            bytes_accessed=4 * videos * ranks * (model_width + up_width),
            transcendentals=0,
        ),
        name="pick_factors",
    )(me, adapter_store_row, requests, adapter_down_factors, adapter_up_factors)
    down_pieces, up_pieces = pieces[: bits - 1], pieces[bits - 1 :]

    down_got, up_got = [], []

    def send_up(i, *others):
        up_got.append(swap(after(halving(up_pieces, up_got, i), *others), 1 << i))

    for i in range(bits - 2):
        piece = down_pieces[0] if i == 0 else halving(down_pieces, down_got, i)
        if i > 0:
            part = up_pieces[0] if i == 1 else halving(up_pieces, up_got, i - 1)
            up_got.append(swap(after(part, piece), 1 << (i - 1)))
        down_got.append(swap(piece, 1 << i))
    part = after(halving(up_pieces, up_got, bits - 3), piece)
    up_got.append(swap(part, 1 << (bits - 3)))
    held = splitting((after(down_pieces[-1], keys, *up_got[:-1]),), down_got)
    shard = after(total(held[0], to_others(held)), up_got[-1])
    gathered = [shard] + [swap(shard, k) for k in others]
    asked = jnp.concatenate([by_pairs(values), by_pairs(queries)], axis=1)
    asked = exchange(after(asked, *gathered))

    up_part = after(up_pieces[-1], *gathered)
    pair_shape = (2,) + up_part.shape[1:]
    near_pair, far_pair = on_vmem(
        functools.partial(sum_kernel, [[(n, 2 * h) for n in range(1 + len(up_got))] for h in (0, 1)]),
        [pair_shape] * 2,
        "split",
        up_part,
        *up_got,
    )
    came = swap(far_pair, quarter)
    one_shape = (1,) + up_part.shape[1:]
    kept, sent = on_vmem(
        functools.partial(sum_kernel, [[(n, h) for n in range(2)] for h in (0, 1)]),
        [one_shape] * 2,
        "split",
        near_pair,
        came,
    )
    last = swap(sent, 2 * quarter)
    up_here = on_vmem(
        functools.partial(sum_kernel, [[(0, 0), (1, 0)]]), [one_shape], "total", kept, last
    )[0].reshape(pairs, ranks, LANES)
    joined = join(gathered)
    for i in reversed(range(bits - 2)):
        gathered = [joined, swap(joined, 1 << i)]
        if i > 0:
            joined = join(gathered)

    low_shape = (videos, toks // 2, 2 * ranks)
    low = pl.pallas_call(
        functools.partial(low_rank_kernel, shape),
        in_specs=[SMEM, VMEM] + [VMEM] * len(gathered),
        out_specs=VMEM,
        scratch_shapes=[pltpu.VMEM((videos, ranks, model_width), jnp.bfloat16)],
        out_shape=jax.ShapeDtypeStruct(low_shape, jnp.bfloat16),
        compiler_params=pltpu.CompilerParams(vmem_limit_bytes=24 << 20),
        cost_estimate=pl.CostEstimate(
            flops=2 * videos * toks * ranks * model_width,
            bytes_accessed=2 * videos * (toks + ranks) * model_width,
            transcendentals=0,
        ),
        name="low_rank",
    )(me, normed_token_features, *gathered)
    nearby = [after(low, came)] + [swap(low, k) for k in range(1, LOW)]
    chosen = pl.pallas_call(
        functools.partial(choose_kernel, per_video),
        in_specs=[SMEM] + [VMEM] * LOW,
        out_specs=[VMEM] * quarter,
        out_shape=[jax.ShapeDtypeStruct((LOW,) + low_shape[1:], jnp.bfloat16)] * quarter,
        cost_estimate=pl.CostEstimate(flops=0, bytes_accessed=8 * low.size, transcendentals=0),
        name="choose",
    )(me, *nearby)
    lows = [chosen[0]] + [swap(chosen[i], LOW * i) for i in range(1, quarter)]

    part_spec = pl.BlockSpec((devs, pl.squeezed, toks, width), lambda p: (0, p, 0, 0))
    later_spec = pl.BlockSpec((devs, pl.squeezed, toks, width), lambda p: (0, pairs + p, 0, 0))
    low_spec = pl.BlockSpec((LOW,) + low_shape[1:], lambda p: (0, 0, 0))
    mixed = pl.pallas_call(
        functools.partial(attend_kernel, math.gcd(devs, max(1, 512 // toks))),
        grid=(pairs,),
        in_specs=[SMEM, pl.BlockSpec((pl.squeezed, ranks, LANES), lambda p: (p, 0, 0))]
        + [later_spec, part_spec, part_spec]
        + [low_spec] * quarter,
        out_specs=part_spec,
        out_shape=jax.ShapeDtypeStruct((devs, pairs, toks, width), jnp.bfloat16),
        scratch_shapes=[
            pltpu.VMEM((devs,) + low_shape[1:], jnp.bfloat16),
            pltpu.VMEM((length, width), jnp.bfloat16),
        ],
        compiler_params=pltpu.CompilerParams(vmem_limit_bytes=48 << 20),
        cost_estimate=pl.CostEstimate(
            flops=4 * pairs * length * length * width,
            bytes_accessed=8 * pairs * length * width,
            transcendentals=pairs * length * length,
        ),
        name="attend",
    )(me, up_here, asked, keys, asked, *lows)
    return exchange(mixed).reshape(videos, heads, toks, width)


def solution(mesh):
    in_specs = (
        P("grp", "seq", None),
        P("grp", None, "seq", None),
        P("grp", None, "seq", None),
        P("grp", None, "seq", None),
        P("seq", None, None),
        P("seq", None, None),
        P(),
        P("grp"),
    )
    out_specs = P("grp", None, "seq", None)
    return jax.shard_map(body, mesh=mesh, in_specs=in_specs, out_specs=out_specs, check_vma=False)
```

```python
import functools
import math

import jax
import jax.numpy as jnp
from jax import lax
from jax.experimental import pallas as pl
from jax.experimental.pallas import tpu as pltpu
from jax.sharding import PartitionSpec as P

LANES = 128
LOW = 4
ANY = pl.BlockSpec(memory_space=pl.ANY)
VMEM = pl.BlockSpec(memory_space=pltpu.VMEM)
SMEM = pl.BlockSpec(memory_space=pltpu.SMEM)


def bit_count(n):
    bits = n.bit_length() - 1
    assert 1 << bits == n
    return bits


def reversed_bits(j, bits):
    out = 0
    for i in range(bits):
        out = out | (((j >> i) & 1) << (bits - 1 - i))
    return out


def pick_kernel(shape, me_ref, row_ref, req_ref, down_ref, up_ref, *refs):
    devs, bits, per_video, pairs, col_split, rows, tiles = shape
    downs, ups = refs[: bits - 1], refs[bits - 1 : 2 * bits - 2]
    down, up, sems = refs[2 * bits - 2 :]
    slots, ranks, _ = down_ref.shape
    videos = down.shape[0]
    me = me_ref[0]
    for s in range(videos):
        place = row_ref[req_ref[s]]
        slot = place % slots
        owned = place // slots == me
        copies = [
            pltpu.make_async_copy(down_ref.at[slot], down.at[s], sems.at[2 * s]),
            pltpu.make_async_copy(up_ref.at[slot], up.at[s], sems.at[2 * s + 1]),
        ]

        @pl.when(owned)
        def _():
            for copy in copies:
                copy.start()
            for copy in copies:
                copy.wait()

        @pl.when(jnp.logical_not(owned))
        def _():
            down[s] = jnp.zeros(down.shape[1:], down.dtype)
            up[s] = jnp.zeros(up.shape[1:], up.dtype)

    for j in range(devs):
        step = min(bits - j.bit_length(), bits - 2)
        at = j - (1 << (j.bit_length() - 1)) if j >= LOW else j
        dev = me ^ reversed_bits(j, bits)
        video = dev // per_video
        place = dev % per_video
        row = pl.multiple_of((place // col_split) * rows, rows)
        for t in range(tiles):
            col = pl.multiple_of(((place % col_split) * tiles + t) * LANES, LANES)
            downs[step][at, t * rows : (t + 1) * rows, :] = down[
                video, pl.ds(row, rows), pl.ds(col, LANES)
            ]
        for p in range(pairs):
            col = pl.multiple_of((place * pairs + p) * LANES, LANES)
            ups[step][at, p * ranks : (p + 1) * ranks, :] = up[video, :, pl.ds(col, LANES)]


def sum_kernel(picks, *refs):
    outs = refs[-len(picks) :]
    for out, terms in zip(outs, picks):
        size = out.shape[0]
        parts = [refs[i][first : first + size] for i, first in terms]
        out[...] = sum(parts[1:], parts[0])


def join_kernel(*refs):
    out, first = refs[-1], 0
    for ref in refs[:-1]:
        out[first : first + ref.shape[0]] = ref[...]
        first += ref.shape[0]


def on_vmem(kernel, shapes, name, *arrays):
    return pl.pallas_call(
        kernel,
        in_specs=[VMEM] * len(arrays),
        out_specs=[VMEM] * len(shapes),
        out_shape=[jax.ShapeDtypeStruct(s, arrays[0].dtype) for s in shapes],
        compiler_params=pltpu.CompilerParams(vmem_limit_bytes=16 << 20),
        cost_estimate=pl.CostEstimate(
            flops=0, bytes_accessed=2 * sum(a.size for a in arrays), transcendentals=0
        ),
        name=name,
    )(*arrays)


def low_rank_kernel(shape, me_ref, x_ref, *refs):
    devs, bits, per_video, _, col_split, rows, tiles = shape
    parts, out_ref, down = refs[:-2], refs[-2], refs[-1]
    blocks = [(ref, i) for ref in parts for i in range(ref.shape[0])]
    for j, (ref, i) in enumerate(blocks):
        dev = me_ref[0] ^ reversed_bits(j, bits)
        video = dev // per_video
        place = dev % per_video
        row = pl.multiple_of((place // col_split) * rows, rows)
        for t in range(tiles):
            col = pl.multiple_of(((place % col_split) * tiles + t) * LANES, LANES)
            down[video, pl.ds(row, rows), pl.ds(col, LANES)] = ref[i, t * rows : (t + 1) * rows, :]
    for s in range(x_ref.shape[0]):
        low = lax.dot_general(
            x_ref[s], down[s], (((1,), (1,)), ((), ())), preferred_element_type=jnp.float32
        ).astype(out_ref.dtype)
        half = low.shape[0] // 2
        out_ref[s] = jnp.concatenate([low[:half], low[half:]], axis=1)


def choose_kernel(per_video, me_ref, *refs):
    ins, outs = refs[:LOW], refs[LOW:]
    for i, out in enumerate(outs):
        video = (me_ref[0] ^ (LOW * i)) // per_video
        for j in range(LOW):
            out[j] = ins[j][video]


def add_delta(base, low, up, second):
    devs, toks, width = base.shape
    ranks = up.shape[0]
    row = lax.broadcasted_iota(jnp.int32, up.shape, 0)
    part = jnp.where(row // (ranks // 2) == second, up, jnp.zeros_like(up))
    none = jnp.zeros_like(part)
    deltas = [
        jnp.dot(low, jnp.concatenate(pair, axis=0), preferred_element_type=jnp.float32)
        for pair in ((part, none), (none, part))
    ]
    delta = jnp.concatenate([d.reshape(devs, toks // 2, width) for d in deltas], axis=1)
    return (base.astype(jnp.float32) + delta).astype(base.dtype).reshape(devs * toks, width)


def attend_kernel(block, me_ref, up_ref, q_ref, k_ref, v_ref, *refs):
    low_refs, out_ref, low_all, q_mix = refs[:-3], refs[-3], refs[-2], refs[-1]
    devs, toks, width = q_ref.shape
    length = devs * toks
    for k in range(devs):
        low_all[me_ref[0] ^ k] = low_refs[k // LOW][k % LOW]
    low = low_all[...].reshape(length // 2, low_all.shape[2])
    up = up_ref[...]
    keys = k_ref[...].reshape(length, width)
    vals = add_delta(v_ref[...], low, up, 1)
    q_mix[...] = add_delta(q_ref[...], low, up, 0)
    scale = math.log2(math.e) / math.sqrt(width)
    for b in range(0, devs, block):
        q = q_mix[b * toks : (b + block) * toks, :]
        scores = lax.dot_general(
            q, keys, (((1,), (1,)), ((), ())), preferred_element_type=jnp.float32
        )
        top = jnp.max(scores, axis=1, keepdims=True)
        weights = jnp.exp2((scores - top) * scale)
        total = jnp.sum(weights, axis=1, keepdims=True)
        mixed = jnp.dot(weights.astype(jnp.bfloat16), vals, preferred_element_type=jnp.float32)
        out_ref[b : b + block] = (mixed / total).astype(jnp.bfloat16).reshape(block, toks, width)


def body(
    normed_token_features,
    queries,
    projected_keys,
    values,
    adapter_down_factors,
    adapter_up_factors,
    adapter_store_row,
    requests,
):
    videos, toks, model_width = normed_token_features.shape
    heads = queries.shape[1]
    width = queries.shape[3]
    _, ranks, up_width = adapter_up_factors.shape
    devs = lax.axis_size("seq")
    bits = bit_count(devs)
    me = lax.axis_index("seq").astype(jnp.int32)[None]
    pairs = videos * heads // devs
    per_video = devs // videos
    length = devs * toks
    col_split = math.gcd(per_video, model_width // LANES)
    rows = ranks * col_split // per_video
    tiles = model_width // col_split // LANES
    shape = (devs, bits, per_video, pairs, col_split, rows, tiles)

    def swap(tensor, k):
        return lax.ppermute(tensor, "seq", [(i, i ^ k) for i in range(devs)])

    def exchange(tensor):
        return lax.all_to_all(tensor, "seq", split_axis=0, concat_axis=0, tiled=True)

    def by_pairs(tensor):
        return tensor.reshape(devs, pairs, toks, width)

    def after(array, *others):
        return lax.optimization_barrier((array, others))[0]

    quarter = devs // LOW
    others = (2 * quarter, quarter, 3 * quarter)

    def halving(parts, received, i):
        size = parts[i].shape[0]
        terms = [(0, 0)] + [(1 + n, size) for n in range(len(received))]
        return on_vmem(
            functools.partial(sum_kernel, [terms]), [parts[i].shape], "halve", parts[i], *received
        )[0]

    def splitting(parts, received):
        size = (1,) + parts[-1].shape[1:]
        picks = [[(n, j) for n in range(1 + len(received))] for j in range(LOW)]
        return on_vmem(
            functools.partial(sum_kernel, picks), [size] * LOW, "split", parts[-1], *received
        )

    def to_others(shards):
        return [swap(shard, k) for shard, k in zip(shards[1:], others)]

    def total(shard, received):
        picks = [[(n, 0) for n in range(LOW)]]
        return on_vmem(
            functools.partial(sum_kernel, picks), [shard.shape], "total", shard, *received
        )[0]

    def join(arrays):
        count = sum(a.shape[0] for a in arrays)
        return on_vmem(join_kernel, [(count,) + arrays[0].shape[1:]], "join", *arrays)[0]

    keys = exchange(by_pairs(projected_keys))

    steps = [devs >> (i + 1) for i in range(bits - 2)] + [LOW]
    piece_shapes = [(h, tiles * rows, LANES) for h in steps] + [
        (h, pairs * ranks, LANES) for h in steps
    ]
    pieces = pl.pallas_call(
        functools.partial(pick_kernel, shape),
        in_specs=[SMEM, SMEM, SMEM, ANY, ANY],
        out_specs=[VMEM] * (2 * bits - 2),
        out_shape=[jax.ShapeDtypeStruct(s, jnp.bfloat16) for s in piece_shapes],
        scratch_shapes=[
            pltpu.VMEM((videos, ranks, model_width), jnp.bfloat16),
            pltpu.VMEM((videos, ranks, up_width), jnp.bfloat16),
            pltpu.SemaphoreType.DMA((2 * videos,)),
        ],
        compiler_params=pltpu.CompilerParams(vmem_limit_bytes=24 << 20),
        cost_estimate=pl.CostEstimate(
            flops=0,
            bytes_accessed=4 * videos * ranks * (model_width + up_width),
            transcendentals=0,
        ),
        name="pick_factors",
    )(me, adapter_store_row, requests, adapter_down_factors, adapter_up_factors)
    down_pieces, up_pieces = pieces[: bits - 1], pieces[bits - 1 :]

    down_got, up_got = [], []

    def send_up(i, *others):
        up_got.append(swap(after(halving(up_pieces, up_got, i), *others), 1 << i))

    for i in range(bits - 2):
        piece = down_pieces[0] if i == 0 else halving(down_pieces, down_got, i)
        if i > 0:
            part = up_pieces[0] if i == 1 else halving(up_pieces, up_got, i - 1)
            up_got.append(swap(after(part, piece), 1 << (i - 1)))
        down_got.append(swap(piece, 1 << i))
    part = after(halving(up_pieces, up_got, bits - 3), piece)
    up_got.append(swap(part, 1 << (bits - 3)))
    held = splitting((after(down_pieces[-1], keys, *up_got[:-1]),), down_got)
    shard = after(total(held[0], to_others(held)), up_got[-1])
    gathered = [shard] + [swap(shard, k) for k in others]
    vals = exchange(after(by_pairs(values), *gathered))
    asked = exchange(after(by_pairs(queries), vals))

    up_part = after(up_pieces[-1], *gathered)
    pair_shape = (2,) + up_part.shape[1:]
    near_pair, far_pair = on_vmem(
        functools.partial(sum_kernel, [[(n, 2 * h) for n in range(1 + len(up_got))] for h in (0, 1)]),
        [pair_shape] * 2,
        "split",
        up_part,
        *up_got,
    )
    came = swap(far_pair, quarter)
    one_shape = (1,) + up_part.shape[1:]
    kept, sent = on_vmem(
        functools.partial(sum_kernel, [[(n, h) for n in range(2)] for h in (0, 1)]),
        [one_shape] * 2,
        "split",
        near_pair,
        came,
    )
    last = swap(sent, 2 * quarter)
    up_here = on_vmem(
        functools.partial(sum_kernel, [[(0, 0), (1, 0)]]), [one_shape], "total", kept, last
    )[0].reshape(pairs, ranks, LANES)
    joined = join(gathered)
    for i in reversed(range(bits - 2)):
        gathered = [joined, swap(joined, 1 << i)]
        if i > 0:
            joined = after(join(gathered), came)

    low_shape = (videos, toks // 2, 2 * ranks)
    low = pl.pallas_call(
        functools.partial(low_rank_kernel, shape),
        in_specs=[SMEM, VMEM] + [VMEM] * len(gathered),
        out_specs=VMEM,
        scratch_shapes=[pltpu.VMEM((videos, ranks, model_width), jnp.bfloat16)],
        out_shape=jax.ShapeDtypeStruct(low_shape, jnp.bfloat16),
        compiler_params=pltpu.CompilerParams(vmem_limit_bytes=24 << 20),
        cost_estimate=pl.CostEstimate(
            flops=2 * videos * toks * ranks * model_width,
            bytes_accessed=2 * videos * (toks + ranks) * model_width,
            transcendentals=0,
        ),
        name="low_rank",
    )(me, normed_token_features, *gathered)
    nearby = [low] + [swap(low, k) for k in range(1, LOW)]
    chosen = pl.pallas_call(
        functools.partial(choose_kernel, per_video),
        in_specs=[SMEM] + [VMEM] * LOW,
        out_specs=[VMEM] * quarter,
        out_shape=[jax.ShapeDtypeStruct((LOW,) + low_shape[1:], jnp.bfloat16)] * quarter,
        cost_estimate=pl.CostEstimate(flops=0, bytes_accessed=8 * low.size, transcendentals=0),
        name="choose",
    )(me, *nearby)
    lows = [chosen[0]] + [swap(chosen[i], LOW * i) for i in range(1, quarter)]

    part_spec = pl.BlockSpec((devs, pl.squeezed, toks, width), lambda p: (0, p, 0, 0))
    low_spec = pl.BlockSpec((LOW,) + low_shape[1:], lambda p: (0, 0, 0))
    mixed = pl.pallas_call(
        functools.partial(attend_kernel, math.gcd(devs, max(1, 512 // toks))),
        grid=(pairs,),
        in_specs=[SMEM, pl.BlockSpec((pl.squeezed, ranks, LANES), lambda p: (p, 0, 0))]
        + [part_spec] * 3
        + [low_spec] * quarter,
        out_specs=part_spec,
        out_shape=jax.ShapeDtypeStruct((devs, pairs, toks, width), jnp.bfloat16),
        scratch_shapes=[
            pltpu.VMEM((devs,) + low_shape[1:], jnp.bfloat16),
            pltpu.VMEM((length, width), jnp.bfloat16),
        ],
        compiler_params=pltpu.CompilerParams(vmem_limit_bytes=48 << 20),
        cost_estimate=pl.CostEstimate(
            flops=4 * pairs * length * length * width,
            bytes_accessed=8 * pairs * length * width,
            transcendentals=pairs * length * length,
        ),
        name="attend",
    )(me, up_here, asked, keys, vals, *lows)
    return exchange(mixed).reshape(videos, heads, toks, width)


def solution(mesh):
    in_specs = (
        P("grp", "seq", None),
        P("grp", None, "seq", None),
        P("grp", None, "seq", None),
        P("grp", None, "seq", None),
        P("seq", None, None),
        P("seq", None, None),
        P(),
        P("grp"),
    )
    out_specs = P("grp", None, "seq", None)
    return jax.shard_map(body, mesh=mesh, in_specs=in_specs, out_specs=out_specs, check_vma=False)
```

```python
import functools
import math

import jax
import jax.numpy as jnp
from jax import lax
from jax.experimental import pallas as pl
from jax.experimental.pallas import tpu as pltpu
from jax.sharding import PartitionSpec as P

LANES = 128
LOW = 4
ANY = pl.BlockSpec(memory_space=pl.ANY)
VMEM = pl.BlockSpec(memory_space=pltpu.VMEM)
SMEM = pl.BlockSpec(memory_space=pltpu.SMEM)


def bit_count(n):
    bits = n.bit_length() - 1
    assert 1 << bits == n
    return bits


def reversed_bits(j, bits):
    out = 0
    for i in range(bits):
        out = out | (((j >> i) & 1) << (bits - 1 - i))
    return out


def pick_kernel(shape, me_ref, row_ref, req_ref, down_ref, up_ref, *refs):
    devs, bits, per_video, pairs, col_split, rows, tiles = shape
    downs, ups = refs[: bits - 1], refs[bits - 1 : 2 * bits - 2]
    down, up, sems = refs[2 * bits - 2 :]
    slots, ranks, _ = down_ref.shape
    videos = down.shape[0]
    me = me_ref[0]
    for s in range(videos):
        place = row_ref[req_ref[s]]
        slot = place % slots
        owned = place // slots == me
        copies = [
            pltpu.make_async_copy(down_ref.at[slot], down.at[s], sems.at[2 * s]),
            pltpu.make_async_copy(up_ref.at[slot], up.at[s], sems.at[2 * s + 1]),
        ]

        @pl.when(owned)
        def _():
            for copy in copies:
                copy.start()
            for copy in copies:
                copy.wait()

        @pl.when(jnp.logical_not(owned))
        def _():
            down[s] = jnp.zeros(down.shape[1:], down.dtype)
            up[s] = jnp.zeros(up.shape[1:], up.dtype)

    for j in range(devs):
        step = min(bits - j.bit_length(), bits - 2)
        at = j - (1 << (j.bit_length() - 1)) if j >= LOW else j
        dev = me ^ reversed_bits(j, bits)
        video = dev // per_video
        place = dev % per_video
        row = pl.multiple_of((place // col_split) * rows, rows)
        for t in range(tiles):
            col = pl.multiple_of(((place % col_split) * tiles + t) * LANES, LANES)
            downs[step][at, t * rows : (t + 1) * rows, :] = down[
                video, pl.ds(row, rows), pl.ds(col, LANES)
            ]
        for p in range(pairs):
            col = pl.multiple_of((place * pairs + p) * LANES, LANES)
            ups[step][at, p * ranks : (p + 1) * ranks, :] = up[video, :, pl.ds(col, LANES)]


def sum_kernel(picks, *refs):
    outs = refs[-len(picks) :]
    for out, terms in zip(outs, picks):
        size = out.shape[0]
        parts = [refs[i][first : first + size] for i, first in terms]
        out[...] = sum(parts[1:], parts[0])


def join_kernel(*refs):
    out, first = refs[-1], 0
    for ref in refs[:-1]:
        out[first : first + ref.shape[0]] = ref[...]
        first += ref.shape[0]


def on_vmem(kernel, shapes, name, *arrays):
    return pl.pallas_call(
        kernel,
        in_specs=[VMEM] * len(arrays),
        out_specs=[VMEM] * len(shapes),
        out_shape=[jax.ShapeDtypeStruct(s, arrays[0].dtype) for s in shapes],
        compiler_params=pltpu.CompilerParams(vmem_limit_bytes=16 << 20),
        cost_estimate=pl.CostEstimate(
            flops=0, bytes_accessed=2 * sum(a.size for a in arrays), transcendentals=0
        ),
        name=name,
    )(*arrays)


def low_rank_kernel(shape, me_ref, x_ref, *refs):
    devs, bits, per_video, _, col_split, rows, tiles = shape
    parts, out_ref, down = refs[:-2], refs[-2], refs[-1]
    blocks = [(ref, i) for ref in parts for i in range(ref.shape[0])]
    for j, (ref, i) in enumerate(blocks):
        dev = me_ref[0] ^ reversed_bits(j, bits)
        video = dev // per_video
        place = dev % per_video
        row = pl.multiple_of((place // col_split) * rows, rows)
        for t in range(tiles):
            col = pl.multiple_of(((place % col_split) * tiles + t) * LANES, LANES)
            down[video, pl.ds(row, rows), pl.ds(col, LANES)] = ref[i, t * rows : (t + 1) * rows, :]
    for s in range(x_ref.shape[0]):
        low = lax.dot_general(
            x_ref[s], down[s], (((1,), (1,)), ((), ())), preferred_element_type=jnp.float32
        ).astype(out_ref.dtype)
        half = low.shape[0] // 2
        out_ref[s] = jnp.concatenate([low[:half], low[half:]], axis=1)


def choose_kernel(per_video, me_ref, *refs):
    ins, outs = refs[:LOW], refs[LOW:]
    for i, out in enumerate(outs):
        video = (me_ref[0] ^ (LOW * i)) // per_video
        for j in range(LOW):
            out[j] = ins[j][video]


def add_delta(base, low, up, second):
    devs, toks, width = base.shape
    ranks = up.shape[0]
    row = lax.broadcasted_iota(jnp.int32, up.shape, 0)
    part = jnp.where(row // (ranks // 2) == second, up, jnp.zeros_like(up))
    none = jnp.zeros_like(part)
    deltas = [
        jnp.dot(low, jnp.concatenate(pair, axis=0), preferred_element_type=jnp.float32)
        for pair in ((part, none), (none, part))
    ]
    delta = jnp.concatenate([d.reshape(devs, toks // 2, width) for d in deltas], axis=1)
    return (base.astype(jnp.float32) + delta).astype(base.dtype).reshape(devs * toks, width)


def attend_kernel(block, me_ref, up_ref, q_ref, k_ref, v_ref, *refs):
    low_refs, out_ref, low_all, q_mix = refs[:-3], refs[-3], refs[-2], refs[-1]
    devs, toks, width = q_ref.shape
    length = devs * toks
    for k in range(devs):
        low_all[me_ref[0] ^ k] = low_refs[k // LOW][k % LOW]
    low = low_all[...].reshape(length // 2, low_all.shape[2])
    up = up_ref[...]
    keys = k_ref[...].reshape(length, width)
    vals = add_delta(v_ref[...], low, up, 1)
    q_mix[...] = add_delta(q_ref[...], low, up, 0)
    scale = math.log2(math.e) / math.sqrt(width)
    for b in range(0, devs, block):
        q = q_mix[b * toks : (b + block) * toks, :]
        scores = lax.dot_general(
            q, keys, (((1,), (1,)), ((), ())), preferred_element_type=jnp.float32
        )
        top = jnp.max(scores, axis=1, keepdims=True)
        weights = jnp.exp2((scores - top) * scale)
        total = jnp.sum(weights, axis=1, keepdims=True)
        mixed = jnp.dot(weights.astype(jnp.bfloat16), vals, preferred_element_type=jnp.float32)
        out_ref[b : b + block] = (mixed / total).astype(jnp.bfloat16).reshape(block, toks, width)


def body(
    normed_token_features,
    queries,
    projected_keys,
    values,
    adapter_down_factors,
    adapter_up_factors,
    adapter_store_row,
    requests,
):
    videos, toks, model_width = normed_token_features.shape
    heads = queries.shape[1]
    width = queries.shape[3]
    _, ranks, up_width = adapter_up_factors.shape
    devs = lax.axis_size("seq")
    bits = bit_count(devs)
    me = lax.axis_index("seq").astype(jnp.int32)[None]
    pairs = videos * heads // devs
    per_video = devs // videos
    length = devs * toks
    col_split = math.gcd(per_video, model_width // LANES)
    rows = ranks * col_split // per_video
    tiles = model_width // col_split // LANES
    shape = (devs, bits, per_video, pairs, col_split, rows, tiles)

    def swap(tensor, k):
        return lax.ppermute(tensor, "seq", [(i, i ^ k) for i in range(devs)])

    def exchange(tensor):
        return lax.all_to_all(tensor, "seq", split_axis=0, concat_axis=0, tiled=True)

    def by_pairs(tensor):
        return tensor.reshape(devs, pairs, toks, width)

    def after(array, *others):
        return lax.optimization_barrier((array, others))[0]

    quarter = devs // LOW
    others = (2 * quarter, quarter, 3 * quarter)

    def halving(parts, received, i):
        size = parts[i].shape[0]
        terms = [(0, 0)] + [(1 + n, size) for n in range(len(received))]
        return on_vmem(
            functools.partial(sum_kernel, [terms]), [parts[i].shape], "halve", parts[i], *received
        )[0]

    def splitting(parts, received):
        size = (1,) + parts[-1].shape[1:]
        picks = [[(n, j) for n in range(1 + len(received))] for j in range(LOW)]
        return on_vmem(
            functools.partial(sum_kernel, picks), [size] * LOW, "split", parts[-1], *received
        )

    def to_others(shards):
        return [swap(shard, k) for shard, k in zip(shards[1:], others)]

    def total(shard, received):
        picks = [[(n, 0) for n in range(LOW)]]
        return on_vmem(
            functools.partial(sum_kernel, picks), [shard.shape], "total", shard, *received
        )[0]

    def join(arrays):
        count = sum(a.shape[0] for a in arrays)
        return on_vmem(join_kernel, [(count,) + arrays[0].shape[1:]], "join", *arrays)[0]

    keys = exchange(by_pairs(projected_keys))

    steps = [devs >> (i + 1) for i in range(bits - 2)] + [LOW]
    piece_shapes = [(h, tiles * rows, LANES) for h in steps] + [
        (h, pairs * ranks, LANES) for h in steps
    ]
    pieces = pl.pallas_call(
        functools.partial(pick_kernel, shape),
        in_specs=[SMEM, SMEM, SMEM, ANY, ANY],
        out_specs=[VMEM] * (2 * bits - 2),
        out_shape=[jax.ShapeDtypeStruct(s, jnp.bfloat16) for s in piece_shapes],
        scratch_shapes=[
            pltpu.VMEM((videos, ranks, model_width), jnp.bfloat16),
            pltpu.VMEM((videos, ranks, up_width), jnp.bfloat16),
            pltpu.SemaphoreType.DMA((2 * videos,)),
        ],
        compiler_params=pltpu.CompilerParams(vmem_limit_bytes=24 << 20),
        cost_estimate=pl.CostEstimate(
            flops=0,
            bytes_accessed=4 * videos * ranks * (model_width + up_width),
            transcendentals=0,
        ),
        name="pick_factors",
    )(me, adapter_store_row, requests, adapter_down_factors, adapter_up_factors)
    down_pieces, up_pieces = pieces[: bits - 1], pieces[bits - 1 :]

    down_got, up_got = [], []

    def send_up(i, *others):
        up_got.append(swap(after(halving(up_pieces, up_got, i), *others), 1 << i))

    for i in range(bits - 2):
        piece = down_pieces[0] if i == 0 else halving(down_pieces, down_got, i)
        if i > 0:
            part = up_pieces[0] if i == 1 else halving(up_pieces, up_got, i - 1)
            up_got.append(swap(after(part, piece), 1 << (i - 1)))
        down_got.append(swap(piece, 1 << i))
    part = after(halving(up_pieces, up_got, bits - 3), piece)
    up_got.append(swap(part, 1 << (bits - 3)))
    held = splitting((after(down_pieces[-1], keys, *up_got[:-1]),), down_got)
    shard = after(total(held[0], to_others(held)), up_got[-1])
    gathered = [shard] + [swap(shard, k) for k in others]
    vals = exchange(after(by_pairs(values), *gathered))

    up_part = after(up_pieces[-1], *gathered)
    pair_shape = (2,) + up_part.shape[1:]
    near_pair, far_pair = on_vmem(
        functools.partial(sum_kernel, [[(n, 2 * h) for n in range(1 + len(up_got))] for h in (0, 1)]),
        [pair_shape] * 2,
        "split",
        up_part,
        *up_got,
    )
    came = swap(far_pair, quarter)
    one_shape = (1,) + up_part.shape[1:]
    kept, sent = on_vmem(
        functools.partial(sum_kernel, [[(n, h) for n in range(2)] for h in (0, 1)]),
        [one_shape] * 2,
        "split",
        near_pair,
        came,
    )
    last = swap(sent, 2 * quarter)
    up_here = on_vmem(
        functools.partial(sum_kernel, [[(0, 0), (1, 0)]]), [one_shape], "total", kept, last
    )[0].reshape(pairs, ranks, LANES)
    joined = join(gathered)
    for i in reversed(range(bits - 2)):
        gathered = [joined, swap(joined, 1 << i)]
        if i > 0:
            joined = after(join(gathered), came)
    asked = exchange(after(by_pairs(queries), vals, joined))

    low_shape = (videos, toks // 2, 2 * ranks)
    low = pl.pallas_call(
        functools.partial(low_rank_kernel, shape),
        in_specs=[SMEM, VMEM] + [VMEM] * len(gathered),
        out_specs=VMEM,
        scratch_shapes=[pltpu.VMEM((videos, ranks, model_width), jnp.bfloat16)],
        out_shape=jax.ShapeDtypeStruct(low_shape, jnp.bfloat16),
        compiler_params=pltpu.CompilerParams(vmem_limit_bytes=24 << 20),
        cost_estimate=pl.CostEstimate(
            flops=2 * videos * toks * ranks * model_width,
            bytes_accessed=2 * videos * (toks + ranks) * model_width,
            transcendentals=0,
        ),
        name="low_rank",
    )(me, normed_token_features, *gathered)
    nearby = [low] + [swap(low, k) for k in range(1, LOW)]
    chosen = pl.pallas_call(
        functools.partial(choose_kernel, per_video),
        in_specs=[SMEM] + [VMEM] * LOW,
        out_specs=[VMEM] * quarter,
        out_shape=[jax.ShapeDtypeStruct((LOW,) + low_shape[1:], jnp.bfloat16)] * quarter,
        cost_estimate=pl.CostEstimate(flops=0, bytes_accessed=8 * low.size, transcendentals=0),
        name="choose",
    )(me, *nearby)
    lows = [chosen[0]] + [swap(chosen[i], LOW * i) for i in range(1, quarter)]

    part_spec = pl.BlockSpec((devs, pl.squeezed, toks, width), lambda p: (0, p, 0, 0))
    low_spec = pl.BlockSpec((LOW,) + low_shape[1:], lambda p: (0, 0, 0))
    mixed = pl.pallas_call(
        functools.partial(attend_kernel, math.gcd(devs, max(1, 512 // toks))),
        grid=(pairs,),
        in_specs=[SMEM, pl.BlockSpec((pl.squeezed, ranks, LANES), lambda p: (p, 0, 0))]
        + [part_spec] * 3
        + [low_spec] * quarter,
        out_specs=part_spec,
        out_shape=jax.ShapeDtypeStruct((devs, pairs, toks, width), jnp.bfloat16),
        scratch_shapes=[
            pltpu.VMEM((devs,) + low_shape[1:], jnp.bfloat16),
            pltpu.VMEM((length, width), jnp.bfloat16),
        ],
        compiler_params=pltpu.CompilerParams(vmem_limit_bytes=48 << 20),
        cost_estimate=pl.CostEstimate(
            flops=4 * pairs * length * length * width,
            bytes_accessed=8 * pairs * length * width,
            transcendentals=pairs * length * length,
        ),
        name="attend",
    )(me, up_here, asked, keys, vals, *lows)
    return exchange(mixed).reshape(videos, heads, toks, width)


def solution(mesh):
    in_specs = (
        P("grp", "seq", None),
        P("grp", None, "seq", None),
        P("grp", None, "seq", None),
        P("grp", None, "seq", None),
        P("seq", None, None),
        P("seq", None, None),
        P(),
        P("grp"),
    )
    out_specs = P("grp", None, "seq", None)
    return jax.shard_map(body, mesh=mesh, in_specs=in_specs, out_specs=out_specs, check_vma=False)
```

```python
import functools
import math

import jax
import jax.numpy as jnp
from jax import lax
from jax.experimental import pallas as pl
from jax.experimental.pallas import tpu as pltpu
from jax.sharding import PartitionSpec as P

LANES = 128
LOW = 4
ANY = pl.BlockSpec(memory_space=pl.ANY)
VMEM = pl.BlockSpec(memory_space=pltpu.VMEM)
SMEM = pl.BlockSpec(memory_space=pltpu.SMEM)


def bit_count(n):
    bits = n.bit_length() - 1
    assert 1 << bits == n
    return bits


def reversed_bits(j, bits):
    out = 0
    for i in range(bits):
        out = out | (((j >> i) & 1) << (bits - 1 - i))
    return out


def pick_kernel(shape, me_ref, row_ref, req_ref, down_ref, up_ref, *refs):
    devs, bits, per_video, pairs, col_split, rows, tiles = shape
    downs, ups = refs[: bits - 1], refs[bits - 1 : 2 * bits - 2]
    down, up, sems = refs[2 * bits - 2 :]
    slots, ranks, _ = down_ref.shape
    videos = down.shape[0]
    me = me_ref[0]
    for s in range(videos):
        place = row_ref[req_ref[s]]
        slot = place % slots
        owned = place // slots == me
        copies = [
            pltpu.make_async_copy(down_ref.at[slot], down.at[s], sems.at[2 * s]),
            pltpu.make_async_copy(up_ref.at[slot], up.at[s], sems.at[2 * s + 1]),
        ]

        @pl.when(owned)
        def _():
            for copy in copies:
                copy.start()
            for copy in copies:
                copy.wait()

        @pl.when(jnp.logical_not(owned))
        def _():
            down[s] = jnp.zeros(down.shape[1:], down.dtype)
            up[s] = jnp.zeros(up.shape[1:], up.dtype)

    for j in range(devs):
        step = min(bits - j.bit_length(), bits - 2)
        at = j - (1 << (j.bit_length() - 1)) if j >= LOW else j
        dev = me ^ reversed_bits(j, bits)
        video = dev // per_video
        place = dev % per_video
        row = pl.multiple_of((place // col_split) * rows, rows)
        for t in range(tiles):
            col = pl.multiple_of(((place % col_split) * tiles + t) * LANES, LANES)
            downs[step][at, t * rows : (t + 1) * rows, :] = down[
                video, pl.ds(row, rows), pl.ds(col, LANES)
            ]
        for p in range(pairs):
            col = pl.multiple_of((place * pairs + p) * LANES, LANES)
            ups[step][at, p * ranks : (p + 1) * ranks, :] = up[video, :, pl.ds(col, LANES)]


def sum_kernel(picks, *refs):
    outs = refs[-len(picks) :]
    for out, terms in zip(outs, picks):
        size = out.shape[0]
        parts = [refs[i][first : first + size] for i, first in terms]
        out[...] = sum(parts[1:], parts[0])


def join_kernel(*refs):
    out, first = refs[-1], 0
    for ref in refs[:-1]:
        out[first : first + ref.shape[0]] = ref[...]
        first += ref.shape[0]


def on_vmem(kernel, shapes, name, *arrays):
    return pl.pallas_call(
        kernel,
        in_specs=[VMEM] * len(arrays),
        out_specs=[VMEM] * len(shapes),
        out_shape=[jax.ShapeDtypeStruct(s, arrays[0].dtype) for s in shapes],
        compiler_params=pltpu.CompilerParams(vmem_limit_bytes=16 << 20),
        cost_estimate=pl.CostEstimate(
            flops=0, bytes_accessed=2 * sum(a.size for a in arrays), transcendentals=0
        ),
        name=name,
    )(*arrays)


def low_rank_kernel(shape, me_ref, x_ref, *refs):
    devs, bits, per_video, _, col_split, rows, tiles = shape
    parts, out_ref, down = refs[:-2], refs[-2], refs[-1]
    blocks = [(ref, i) for ref in parts for i in range(ref.shape[0])]
    for j, (ref, i) in enumerate(blocks):
        dev = me_ref[0] ^ reversed_bits(j, bits)
        video = dev // per_video
        place = dev % per_video
        row = pl.multiple_of((place // col_split) * rows, rows)
        for t in range(tiles):
            col = pl.multiple_of(((place % col_split) * tiles + t) * LANES, LANES)
            down[video, pl.ds(row, rows), pl.ds(col, LANES)] = ref[i, t * rows : (t + 1) * rows, :]
    for s in range(x_ref.shape[0]):
        low = lax.dot_general(
            x_ref[s], down[s], (((1,), (1,)), ((), ())), preferred_element_type=jnp.float32
        ).astype(out_ref.dtype)
        half = low.shape[0] // 2
        out_ref[s] = jnp.concatenate([low[:half], low[half:]], axis=1)


def choose_kernel(per_video, me_ref, *refs):
    ins, outs = refs[:LOW], refs[LOW:]
    for i, out in enumerate(outs):
        video = (me_ref[0] ^ (LOW * i)) // per_video
        for j in range(LOW):
            out[j] = ins[j][video]


def add_delta(base, low, up, second):
    devs, toks, width = base.shape
    ranks = up.shape[0]
    row = lax.broadcasted_iota(jnp.int32, up.shape, 0)
    part = jnp.where(row // (ranks // 2) == second, up, jnp.zeros_like(up))
    none = jnp.zeros_like(part)
    deltas = [
        jnp.dot(low, jnp.concatenate(pair, axis=0), preferred_element_type=jnp.float32)
        for pair in ((part, none), (none, part))
    ]
    delta = jnp.concatenate([d.reshape(devs, toks // 2, width) for d in deltas], axis=1)
    return (base.astype(jnp.float32) + delta).astype(base.dtype).reshape(devs * toks, width)


def attend_kernel(block, me_ref, up_ref, q_ref, k_ref, v_ref, *refs):
    low_refs, out_ref, low_all, q_mix = refs[:-3], refs[-3], refs[-2], refs[-1]
    devs, toks, width = q_ref.shape
    length = devs * toks
    for k in range(devs):
        low_all[me_ref[0] ^ k] = low_refs[k // LOW][k % LOW]
    low = low_all[...].reshape(length // 2, low_all.shape[2])
    up = up_ref[...]
    keys = k_ref[...].reshape(length, width)
    vals = add_delta(v_ref[...], low, up, 1)
    vals = jnp.concatenate([vals, jnp.ones_like(vals)], axis=1)
    q_mix[...] = add_delta(q_ref[...], low, up, 0)
    scale = math.log2(math.e) / math.sqrt(width)

    def score(b):
        q = q_mix[b * toks : (b + block) * toks, :]
        return lax.dot_general(q, keys, (((1,), (1,)), ((), ())), preferred_element_type=jnp.float32)

    coming = score(0)
    for b in range(0, devs, block):
        scores = coming
        if b + block < devs:
            coming = score(b + block)
        top = jnp.max(scores, axis=1, keepdims=True)
        weights = jnp.exp2((scores - top) * scale).astype(jnp.bfloat16)
        mixed = jnp.dot(weights, vals, preferred_element_type=jnp.float32)
        out = mixed[:, :width] / mixed[:, width:]
        out_ref[b : b + block] = out.astype(jnp.bfloat16).reshape(block, toks, width)


def body(
    normed_token_features,
    queries,
    projected_keys,
    values,
    adapter_down_factors,
    adapter_up_factors,
    adapter_store_row,
    requests,
):
    videos, toks, model_width = normed_token_features.shape
    heads = queries.shape[1]
    width = queries.shape[3]
    _, ranks, up_width = adapter_up_factors.shape
    devs = lax.axis_size("seq")
    bits = bit_count(devs)
    me = lax.axis_index("seq").astype(jnp.int32)[None]
    pairs = videos * heads // devs
    per_video = devs // videos
    length = devs * toks
    col_split = math.gcd(per_video, model_width // LANES)
    rows = ranks * col_split // per_video
    tiles = model_width // col_split // LANES
    shape = (devs, bits, per_video, pairs, col_split, rows, tiles)

    def swap(tensor, k):
        return lax.ppermute(tensor, "seq", [(i, i ^ k) for i in range(devs)])

    def exchange(tensor):
        return lax.all_to_all(tensor, "seq", split_axis=0, concat_axis=0, tiled=True)

    def by_pairs(tensor):
        return tensor.reshape(devs, pairs, toks, width)

    def after(array, *others):
        return lax.optimization_barrier((array, others))[0]

    quarter = devs // LOW
    others = (2 * quarter, quarter, 3 * quarter)

    def halving(parts, received, i):
        size = parts[i].shape[0]
        terms = [(0, 0)] + [(1 + n, size) for n in range(len(received))]
        return on_vmem(
            functools.partial(sum_kernel, [terms]), [parts[i].shape], "halve", parts[i], *received
        )[0]

    def splitting(parts, received):
        size = (1,) + parts[-1].shape[1:]
        picks = [[(n, j) for n in range(1 + len(received))] for j in range(LOW)]
        return on_vmem(
            functools.partial(sum_kernel, picks), [size] * LOW, "split", parts[-1], *received
        )

    def to_others(shards):
        return [swap(shard, k) for shard, k in zip(shards[1:], others)]

    def total(shard, received):
        picks = [[(n, 0) for n in range(LOW)]]
        return on_vmem(
            functools.partial(sum_kernel, picks), [shard.shape], "total", shard, *received
        )[0]

    def join(arrays):
        count = sum(a.shape[0] for a in arrays)
        return on_vmem(join_kernel, [(count,) + arrays[0].shape[1:]], "join", *arrays)[0]

    keys = exchange(by_pairs(projected_keys))

    steps = [devs >> (i + 1) for i in range(bits - 2)] + [LOW]
    piece_shapes = [(h, tiles * rows, LANES) for h in steps] + [
        (h, pairs * ranks, LANES) for h in steps
    ]
    pieces = pl.pallas_call(
        functools.partial(pick_kernel, shape),
        in_specs=[SMEM, SMEM, SMEM, ANY, ANY],
        out_specs=[VMEM] * (2 * bits - 2),
        out_shape=[jax.ShapeDtypeStruct(s, jnp.bfloat16) for s in piece_shapes],
        scratch_shapes=[
            pltpu.VMEM((videos, ranks, model_width), jnp.bfloat16),
            pltpu.VMEM((videos, ranks, up_width), jnp.bfloat16),
            pltpu.SemaphoreType.DMA((2 * videos,)),
        ],
        compiler_params=pltpu.CompilerParams(vmem_limit_bytes=24 << 20),
        cost_estimate=pl.CostEstimate(
            flops=0,
            bytes_accessed=4 * videos * ranks * (model_width + up_width),
            transcendentals=0,
        ),
        name="pick_factors",
    )(me, adapter_store_row, requests, adapter_down_factors, adapter_up_factors)
    down_pieces, up_pieces = pieces[: bits - 1], pieces[bits - 1 :]

    down_got, up_got = [], []

    def send_up(i, *others):
        up_got.append(swap(after(halving(up_pieces, up_got, i), *others), 1 << i))

    for i in range(bits - 2):
        piece = down_pieces[0] if i == 0 else halving(down_pieces, down_got, i)
        if i > 0:
            part = up_pieces[0] if i == 1 else halving(up_pieces, up_got, i - 1)
            up_got.append(swap(after(part, piece), 1 << (i - 1)))
        down_got.append(swap(piece, 1 << i))
    part = after(halving(up_pieces, up_got, bits - 3), piece)
    up_got.append(swap(part, 1 << (bits - 3)))
    held = splitting((after(down_pieces[-1], keys, *up_got[:-1]),), down_got)
    shard = after(total(held[0], to_others(held)), up_got[-1])
    gathered = [shard] + [swap(shard, k) for k in others]
    asked = jnp.concatenate([by_pairs(values), by_pairs(queries)], axis=1)
    asked = exchange(after(asked, *gathered))

    up_part = after(up_pieces[-1], *gathered)
    pair_shape = (2,) + up_part.shape[1:]
    near_pair, far_pair = on_vmem(
        functools.partial(sum_kernel, [[(n, 2 * h) for n in range(1 + len(up_got))] for h in (0, 1)]),
        [pair_shape] * 2,
        "split",
        up_part,
        *up_got,
    )
    came = swap(far_pair, quarter)
    one_shape = (1,) + up_part.shape[1:]
    kept, sent = on_vmem(
        functools.partial(sum_kernel, [[(n, h) for n in range(2)] for h in (0, 1)]),
        [one_shape] * 2,
        "split",
        near_pair,
        came,
    )
    last = swap(sent, 2 * quarter)
    up_here = on_vmem(
        functools.partial(sum_kernel, [[(0, 0), (1, 0)]]), [one_shape], "total", kept, last
    )[0].reshape(pairs, ranks, LANES)
    joined = join(gathered)
    for i in reversed(range(bits - 2)):
        gathered = [joined, swap(joined, 1 << i)]
        if i > 0:
            joined = join(gathered)

    low_shape = (videos, toks // 2, 2 * ranks)
    low = pl.pallas_call(
        functools.partial(low_rank_kernel, shape),
        in_specs=[SMEM, VMEM] + [VMEM] * len(gathered),
        out_specs=VMEM,
        scratch_shapes=[pltpu.VMEM((videos, ranks, model_width), jnp.bfloat16)],
        out_shape=jax.ShapeDtypeStruct(low_shape, jnp.bfloat16),
        compiler_params=pltpu.CompilerParams(vmem_limit_bytes=24 << 20),
        cost_estimate=pl.CostEstimate(
            flops=2 * videos * toks * ranks * model_width,
            bytes_accessed=2 * videos * (toks + ranks) * model_width,
            transcendentals=0,
        ),
        name="low_rank",
    )(me, normed_token_features, *gathered)
    nearby = [after(low, came)] + [swap(low, k) for k in range(1, LOW)]
    chosen = pl.pallas_call(
        functools.partial(choose_kernel, per_video),
        in_specs=[SMEM] + [VMEM] * LOW,
        out_specs=[VMEM] * quarter,
        out_shape=[jax.ShapeDtypeStruct((LOW,) + low_shape[1:], jnp.bfloat16)] * quarter,
        cost_estimate=pl.CostEstimate(flops=0, bytes_accessed=8 * low.size, transcendentals=0),
        name="choose",
    )(me, *nearby)
    lows = [chosen[0]] + [swap(chosen[i], LOW * i) for i in range(1, quarter)]

    part_spec = pl.BlockSpec((devs, pl.squeezed, toks, width), lambda p: (0, p, 0, 0))
    later_spec = pl.BlockSpec((devs, pl.squeezed, toks, width), lambda p: (0, pairs + p, 0, 0))
    low_spec = pl.BlockSpec((LOW,) + low_shape[1:], lambda p: (0, 0, 0))
    mixed = pl.pallas_call(
        functools.partial(attend_kernel, math.gcd(devs, max(1, 256 // toks))),
        grid=(pairs,),
        in_specs=[SMEM, pl.BlockSpec((pl.squeezed, ranks, LANES), lambda p: (p, 0, 0))]
        + [later_spec, part_spec, part_spec]
        + [low_spec] * quarter,
        out_specs=part_spec,
        out_shape=jax.ShapeDtypeStruct((devs, pairs, toks, width), jnp.bfloat16),
        scratch_shapes=[
            pltpu.VMEM((devs,) + low_shape[1:], jnp.bfloat16),
            pltpu.VMEM((length, width), jnp.bfloat16),
        ],
        compiler_params=pltpu.CompilerParams(vmem_limit_bytes=48 << 20),
        cost_estimate=pl.CostEstimate(
            flops=4 * pairs * length * length * width,
            bytes_accessed=8 * pairs * length * width,
            transcendentals=pairs * length * length,
        ),
        name="attend",
    )(me, up_here, asked, keys, asked, *lows)
    return exchange(mixed).reshape(videos, heads, toks, width)


def solution(mesh):
    in_specs = (
        P("grp", "seq", None),
        P("grp", None, "seq", None),
        P("grp", None, "seq", None),
        P("grp", None, "seq", None),
        P("seq", None, None),
        P("seq", None, None),
        P(),
        P("grp"),
    )
    out_specs = P("grp", None, "seq", None)
    return jax.shard_map(body, mesh=mesh, in_specs=in_specs, out_specs=out_specs, check_vma=False)
```

```python
import functools
import math

import jax
import jax.numpy as jnp
from jax import lax
from jax.experimental import pallas as pl
from jax.experimental.pallas import tpu as pltpu
from jax.sharding import PartitionSpec as P

LANES = 128
LOW = 4
ANY = pl.BlockSpec(memory_space=pl.ANY)
VMEM = pl.BlockSpec(memory_space=pltpu.VMEM)
SMEM = pl.BlockSpec(memory_space=pltpu.SMEM)


def bit_count(n):
    bits = n.bit_length() - 1
    assert 1 << bits == n
    return bits


def reversed_bits(j, bits):
    out = 0
    for i in range(bits):
        out = out | (((j >> i) & 1) << (bits - 1 - i))
    return out


def pick_kernel(shape, me_ref, row_ref, req_ref, down_ref, up_ref, *refs):
    devs, bits, per_video, pairs, col_split, rows, tiles = shape
    downs, ups = refs[: bits - 1], refs[bits - 1 : 2 * bits - 2]
    down, up, sems = refs[2 * bits - 2 :]
    slots, ranks, _ = down_ref.shape
    videos = down.shape[0]
    me = me_ref[0]
    for s in range(videos):
        place = row_ref[req_ref[s]]
        slot = place % slots
        owned = place // slots == me
        copies = [
            pltpu.make_async_copy(down_ref.at[slot], down.at[s], sems.at[2 * s]),
            pltpu.make_async_copy(up_ref.at[slot], up.at[s], sems.at[2 * s + 1]),
        ]

        @pl.when(owned)
        def _():
            for copy in copies:
                copy.start()
            for copy in copies:
                copy.wait()

        @pl.when(jnp.logical_not(owned))
        def _():
            down[s] = jnp.zeros(down.shape[1:], down.dtype)
            up[s] = jnp.zeros(up.shape[1:], up.dtype)

    for j in range(devs):
        step = min(bits - j.bit_length(), bits - 2)
        at = j - (1 << (j.bit_length() - 1)) if j >= LOW else j
        dev = me ^ reversed_bits(j, bits)
        video = dev // per_video
        place = dev % per_video
        row = pl.multiple_of((place // col_split) * rows, rows)
        for t in range(tiles):
            col = pl.multiple_of(((place % col_split) * tiles + t) * LANES, LANES)
            downs[step][at, t * rows : (t + 1) * rows, :] = down[
                video, pl.ds(row, rows), pl.ds(col, LANES)
            ]
        for p in range(pairs):
            col = pl.multiple_of((place * pairs + p) * LANES, LANES)
            ups[step][at, p * ranks : (p + 1) * ranks, :] = up[video, :, pl.ds(col, LANES)]


def sum_kernel(picks, *refs):
    outs = refs[-len(picks) :]
    for out, terms in zip(outs, picks):
        size = out.shape[0]
        parts = [refs[i][first : first + size] for i, first in terms]
        out[...] = sum(parts[1:], parts[0])


def join_kernel(*refs):
    out, first = refs[-1], 0
    for ref in refs[:-1]:
        out[first : first + ref.shape[0]] = ref[...]
        first += ref.shape[0]


def on_vmem(kernel, shapes, name, *arrays):
    return pl.pallas_call(
        kernel,
        in_specs=[VMEM] * len(arrays),
        out_specs=[VMEM] * len(shapes),
        out_shape=[jax.ShapeDtypeStruct(s, arrays[0].dtype) for s in shapes],
        compiler_params=pltpu.CompilerParams(vmem_limit_bytes=16 << 20),
        cost_estimate=pl.CostEstimate(
            flops=0, bytes_accessed=2 * sum(a.size for a in arrays), transcendentals=0
        ),
        name=name,
    )(*arrays)


def low_rank_kernel(shape, me_ref, x_ref, *refs):
    devs, bits, per_video, _, col_split, rows, tiles = shape
    parts, out_ref, down = refs[:-2], refs[-2], refs[-1]
    blocks = [(ref, i) for ref in parts for i in range(ref.shape[0])]
    for j, (ref, i) in enumerate(blocks):
        dev = me_ref[0] ^ reversed_bits(j, bits)
        video = dev // per_video
        place = dev % per_video
        row = pl.multiple_of((place // col_split) * rows, rows)
        for t in range(tiles):
            col = pl.multiple_of(((place % col_split) * tiles + t) * LANES, LANES)
            down[video, pl.ds(row, rows), pl.ds(col, LANES)] = ref[i, t * rows : (t + 1) * rows, :]
    for s in range(x_ref.shape[0]):
        low = lax.dot_general(
            x_ref[s], down[s], (((1,), (1,)), ((), ())), preferred_element_type=jnp.float32
        ).astype(out_ref.dtype)
        half = low.shape[0] // 2
        out_ref[s] = jnp.concatenate([low[:half], low[half:]], axis=1)


def choose_kernel(per_video, me_ref, *refs):
    ins, outs = refs[:LOW], refs[LOW:]
    for i, out in enumerate(outs):
        video = (me_ref[0] ^ (LOW * i)) // per_video
        for j in range(LOW):
            out[j] = ins[j][video]


def add_delta(base, low, up, second):
    devs, toks, width = base.shape
    ranks = up.shape[0]
    row = lax.broadcasted_iota(jnp.int32, up.shape, 0)
    part = jnp.where(row // (ranks // 2) == second, up, jnp.zeros_like(up))
    none = jnp.zeros_like(part)
    deltas = [
        jnp.dot(low, jnp.concatenate(pair, axis=0), preferred_element_type=jnp.float32)
        for pair in ((part, none), (none, part))
    ]
    delta = jnp.concatenate([d.reshape(devs, toks // 2, width) for d in deltas], axis=1)
    return (base.astype(jnp.float32) + delta).astype(base.dtype).reshape(devs * toks, width)


def attend_kernel(block, me_ref, up_ref, q_ref, k_ref, v_ref, *refs):
    low_refs, out_ref, low_all, q_mix = refs[:-3], refs[-3], refs[-2], refs[-1]
    devs, toks, width = q_ref.shape
    length = devs * toks
    for k in range(devs):
        low_all[me_ref[0] ^ k] = low_refs[k // LOW][k % LOW]
    low = low_all[...].reshape(length // 2, low_all.shape[2])
    up = up_ref[...]
    keys = k_ref[...].reshape(length, width)
    vals = add_delta(v_ref[...], low, up, 1)
    vals = jnp.concatenate([vals, jnp.ones_like(vals)], axis=1)
    q_mix[...] = add_delta(q_ref[...], low, up, 0)
    scale = math.log2(math.e) / math.sqrt(width)

    def score(b):
        q = q_mix[b * toks : (b + block) * toks, :]
        return lax.dot_general(q, keys, (((1,), (1,)), ((), ())), preferred_element_type=jnp.float32)

    coming = score(0)
    for b in range(0, devs, block):
        scores = coming
        if b + block < devs:
            coming = score(b + block)
        top = jnp.max(scores, axis=1, keepdims=True)
        weights = jnp.exp2((scores - top) * scale).astype(jnp.bfloat16)
        mixed = jnp.dot(weights, vals, preferred_element_type=jnp.float32)
        out = mixed[:, :width] / mixed[:, width:]
        out_ref[b : b + block] = out.astype(jnp.bfloat16).reshape(block, toks, width)


def body(
    normed_token_features,
    queries,
    projected_keys,
    values,
    adapter_down_factors,
    adapter_up_factors,
    adapter_store_row,
    requests,
):
    videos, toks, model_width = normed_token_features.shape
    heads = queries.shape[1]
    width = queries.shape[3]
    _, ranks, up_width = adapter_up_factors.shape
    devs = lax.axis_size("seq")
    bits = bit_count(devs)
    me = lax.axis_index("seq").astype(jnp.int32)[None]
    pairs = videos * heads // devs
    per_video = devs // videos
    length = devs * toks
    col_split = math.gcd(per_video, model_width // LANES)
    rows = ranks * col_split // per_video
    tiles = model_width // col_split // LANES
    shape = (devs, bits, per_video, pairs, col_split, rows, tiles)

    def swap(tensor, k):
        return lax.ppermute(tensor, "seq", [(i, i ^ k) for i in range(devs)])

    def exchange(tensor):
        return lax.all_to_all(tensor, "seq", split_axis=0, concat_axis=0, tiled=True)

    def by_pairs(tensor):
        return tensor.reshape(devs, pairs, toks, width)

    def after(array, *others):
        return lax.optimization_barrier((array, others))[0]

    quarter = devs // LOW
    others = (2 * quarter, quarter, 3 * quarter)

    def halving(parts, received, i):
        size = parts[i].shape[0]
        terms = [(0, 0)] + [(1 + n, size) for n in range(len(received))]
        return on_vmem(
            functools.partial(sum_kernel, [terms]), [parts[i].shape], "halve", parts[i], *received
        )[0]

    def splitting(parts, received):
        size = (1,) + parts[-1].shape[1:]
        picks = [[(n, j) for n in range(1 + len(received))] for j in range(LOW)]
        return on_vmem(
            functools.partial(sum_kernel, picks), [size] * LOW, "split", parts[-1], *received
        )

    def to_others(shards):
        return [swap(shard, k) for shard, k in zip(shards[1:], others)]

    def total(shard, received):
        picks = [[(n, 0) for n in range(LOW)]]
        return on_vmem(
            functools.partial(sum_kernel, picks), [shard.shape], "total", shard, *received
        )[0]

    def join(arrays):
        count = sum(a.shape[0] for a in arrays)
        return on_vmem(join_kernel, [(count,) + arrays[0].shape[1:]], "join", *arrays)[0]

    keys = exchange(by_pairs(projected_keys))

    steps = [devs >> (i + 1) for i in range(bits - 2)] + [LOW]
    piece_shapes = [(h, tiles * rows, LANES) for h in steps] + [
        (h, pairs * ranks, LANES) for h in steps
    ]
    pieces = pl.pallas_call(
        functools.partial(pick_kernel, shape),
        in_specs=[SMEM, SMEM, SMEM, ANY, ANY],
        out_specs=[VMEM] * (2 * bits - 2),
        out_shape=[jax.ShapeDtypeStruct(s, jnp.bfloat16) for s in piece_shapes],
        scratch_shapes=[
            pltpu.VMEM((videos, ranks, model_width), jnp.bfloat16),
            pltpu.VMEM((videos, ranks, up_width), jnp.bfloat16),
            pltpu.SemaphoreType.DMA((2 * videos,)),
        ],
        compiler_params=pltpu.CompilerParams(vmem_limit_bytes=24 << 20),
        cost_estimate=pl.CostEstimate(
            flops=0,
            bytes_accessed=4 * videos * ranks * (model_width + up_width),
            transcendentals=0,
        ),
        name="pick_factors",
    )(me, adapter_store_row, requests, adapter_down_factors, adapter_up_factors)
    down_pieces, up_pieces = pieces[: bits - 1], pieces[bits - 1 :]

    down_got, up_got = [], []

    def send_up(i, *others):
        up_got.append(swap(after(halving(up_pieces, up_got, i), *others), 1 << i))

    for i in range(bits - 2):
        piece = down_pieces[0] if i == 0 else halving(down_pieces, down_got, i)
        if i > 0:
            part = up_pieces[0] if i == 1 else halving(up_pieces, up_got, i - 1)
            up_got.append(swap(after(part, piece), 1 << (i - 1)))
        down_got.append(swap(piece, 1 << i))
    part = after(halving(up_pieces, up_got, bits - 3), piece)
    up_got.append(swap(part, 1 << (bits - 3)))
    held = splitting((after(down_pieces[-1], keys, *up_got[:-1]),), down_got)
    shard = after(total(held[0], to_others(held)), up_got[-1])
    gathered = [shard] + [swap(shard, k) for k in others]

    up_part = after(up_pieces[-1], shard)
    near_pair, far_pair = on_vmem(
        functools.partial(sum_kernel, [[(n, 2 * h) for n in range(1 + len(up_got))] for h in (0, 1)]),
        [(2,) + up_part.shape[1:]] * 2,
        "split",
        up_part,
        *up_got,
    )
    came = swap(far_pair, quarter)
    asked = jnp.concatenate([by_pairs(values), by_pairs(queries)], axis=1)
    asked = exchange(after(asked, came, *gathered))
    one_shape = (1,) + up_part.shape[1:]
    kept, sent = on_vmem(
        functools.partial(sum_kernel, [[(n, h) for n in range(2)] for h in (0, 1)]),
        [one_shape] * 2,
        "split",
        after(near_pair, *gathered),
        came,
    )
    last = swap(sent, 2 * quarter)
    up_here = on_vmem(
        functools.partial(sum_kernel, [[(0, 0), (1, 0)]]), [one_shape], "total", kept, last
    )[0].reshape(pairs, ranks, LANES)
    joined = join(gathered)
    for i in reversed(range(bits - 2)):
        gathered = [joined, swap(joined, 1 << i)]
        if i > 0:
            joined = join(gathered)

    low_shape = (videos, toks // 2, 2 * ranks)
    low = pl.pallas_call(
        functools.partial(low_rank_kernel, shape),
        in_specs=[SMEM, VMEM] + [VMEM] * len(gathered),
        out_specs=VMEM,
        scratch_shapes=[pltpu.VMEM((videos, ranks, model_width), jnp.bfloat16)],
        out_shape=jax.ShapeDtypeStruct(low_shape, jnp.bfloat16),
        compiler_params=pltpu.CompilerParams(vmem_limit_bytes=24 << 20),
        cost_estimate=pl.CostEstimate(
            flops=2 * videos * toks * ranks * model_width,
            bytes_accessed=2 * videos * (toks + ranks) * model_width,
            transcendentals=0,
        ),
        name="low_rank",
    )(me, normed_token_features, *gathered)
    nearby = [low] + [swap(low, k) for k in range(1, LOW)]
    chosen = pl.pallas_call(
        functools.partial(choose_kernel, per_video),
        in_specs=[SMEM] + [VMEM] * LOW,
        out_specs=[VMEM] * quarter,
        out_shape=[jax.ShapeDtypeStruct((LOW,) + low_shape[1:], jnp.bfloat16)] * quarter,
        cost_estimate=pl.CostEstimate(flops=0, bytes_accessed=8 * low.size, transcendentals=0),
        name="choose",
    )(me, *nearby)
    lows = [chosen[0]] + [swap(chosen[i], LOW * i) for i in range(1, quarter)]

    part_spec = pl.BlockSpec((devs, pl.squeezed, toks, width), lambda p: (0, p, 0, 0))
    later_spec = pl.BlockSpec((devs, pl.squeezed, toks, width), lambda p: (0, pairs + p, 0, 0))
    low_spec = pl.BlockSpec((LOW,) + low_shape[1:], lambda p: (0, 0, 0))
    mixed = pl.pallas_call(
        functools.partial(attend_kernel, math.gcd(devs, max(1, 256 // toks))),
        grid=(pairs,),
        in_specs=[SMEM, pl.BlockSpec((pl.squeezed, ranks, LANES), lambda p: (p, 0, 0))]
        + [later_spec, part_spec, part_spec]
        + [low_spec] * quarter,
        out_specs=part_spec,
        out_shape=jax.ShapeDtypeStruct((devs, pairs, toks, width), jnp.bfloat16),
        scratch_shapes=[
            pltpu.VMEM((devs,) + low_shape[1:], jnp.bfloat16),
            pltpu.VMEM((length, width), jnp.bfloat16),
        ],
        compiler_params=pltpu.CompilerParams(vmem_limit_bytes=48 << 20),
        cost_estimate=pl.CostEstimate(
            flops=4 * pairs * length * length * width,
            bytes_accessed=8 * pairs * length * width,
            transcendentals=pairs * length * length,
        ),
        name="attend",
    )(me, up_here, asked, keys, asked, *lows)
    return exchange(mixed).reshape(videos, heads, toks, width)


def solution(mesh):
    in_specs = (
        P("grp", "seq", None),
        P("grp", None, "seq", None),
        P("grp", None, "seq", None),
        P("grp", None, "seq", None),
        P("seq", None, None),
        P("seq", None, None),
        P(),
        P("grp"),
    )
    out_specs = P("grp", None, "seq", None)
    return jax.shard_map(body, mesh=mesh, in_specs=in_specs, out_specs=out_specs, check_vma=False)
```

```python
import functools
import math

import jax
import jax.numpy as jnp
from jax import lax
from jax.experimental import pallas as pl
from jax.experimental.pallas import tpu as pltpu
from jax.sharding import PartitionSpec as P

LANES = 128
LOW = 4
ANY = pl.BlockSpec(memory_space=pl.ANY)
VMEM = pl.BlockSpec(memory_space=pltpu.VMEM)
SMEM = pl.BlockSpec(memory_space=pltpu.SMEM)


def bit_count(n):
    bits = n.bit_length() - 1
    assert 1 << bits == n
    return bits


def reversed_bits(j, bits):
    out = 0
    for i in range(bits):
        out = out | (((j >> i) & 1) << (bits - 1 - i))
    return out


def pick_kernel(shape, me_ref, row_ref, req_ref, down_ref, up_ref, *refs):
    devs, bits, per_video, pairs, col_split, rows, tiles = shape
    downs, ups = refs[: bits - 1], refs[bits - 1 : 2 * bits - 2]
    down, up, sems = refs[2 * bits - 2 :]
    slots, ranks, _ = down_ref.shape
    videos = down.shape[0]
    me = me_ref[0]
    for s in range(videos):
        place = row_ref[req_ref[s]]
        slot = place % slots
        owned = place // slots == me
        copies = [
            pltpu.make_async_copy(down_ref.at[slot], down.at[s], sems.at[2 * s]),
            pltpu.make_async_copy(up_ref.at[slot], up.at[s], sems.at[2 * s + 1]),
        ]

        @pl.when(owned)
        def _():
            for copy in copies:
                copy.start()
            for copy in copies:
                copy.wait()

        @pl.when(jnp.logical_not(owned))
        def _():
            down[s] = jnp.zeros(down.shape[1:], down.dtype)
            up[s] = jnp.zeros(up.shape[1:], up.dtype)

    for j in range(devs):
        step = min(bits - j.bit_length(), bits - 2)
        at = j - (1 << (j.bit_length() - 1)) if j >= LOW else j
        dev = me ^ reversed_bits(j, bits)
        video = dev // per_video
        place = dev % per_video
        row = pl.multiple_of((place // col_split) * rows, rows)
        for t in range(tiles):
            col = pl.multiple_of(((place % col_split) * tiles + t) * LANES, LANES)
            downs[step][at, t * rows : (t + 1) * rows, :] = down[
                video, pl.ds(row, rows), pl.ds(col, LANES)
            ]
        for p in range(pairs):
            col = pl.multiple_of((place * pairs + p) * LANES, LANES)
            ups[step][at, p * ranks : (p + 1) * ranks, :] = up[video, :, pl.ds(col, LANES)]


def sum_kernel(picks, *refs):
    outs = refs[-len(picks) :]
    for out, terms in zip(outs, picks):
        size = out.shape[0]
        parts = [refs[i][first : first + size] for i, first in terms]
        out[...] = sum(parts[1:], parts[0])


def join_kernel(*refs):
    out, first = refs[-1], 0
    for ref in refs[:-1]:
        out[first : first + ref.shape[0]] = ref[...]
        first += ref.shape[0]


def on_vmem(kernel, shapes, name, *arrays):
    return pl.pallas_call(
        kernel,
        in_specs=[VMEM] * len(arrays),
        out_specs=[VMEM] * len(shapes),
        out_shape=[jax.ShapeDtypeStruct(s, arrays[0].dtype) for s in shapes],
        compiler_params=pltpu.CompilerParams(vmem_limit_bytes=16 << 20),
        cost_estimate=pl.CostEstimate(
            flops=0, bytes_accessed=2 * sum(a.size for a in arrays), transcendentals=0
        ),
        name=name,
    )(*arrays)


def low_rank_kernel(shape, me_ref, x_ref, *refs):
    devs, bits, per_video, _, col_split, rows, tiles = shape
    parts, out_ref, down = refs[:-2], refs[-2], refs[-1]
    blocks = [(ref, i) for ref in parts for i in range(ref.shape[0])]
    for j, (ref, i) in enumerate(blocks):
        dev = me_ref[0] ^ reversed_bits(j, bits)
        video = dev // per_video
        place = dev % per_video
        row = pl.multiple_of((place // col_split) * rows, rows)
        for t in range(tiles):
            col = pl.multiple_of(((place % col_split) * tiles + t) * LANES, LANES)
            down[video, pl.ds(row, rows), pl.ds(col, LANES)] = ref[i, t * rows : (t + 1) * rows, :]
    for s in range(x_ref.shape[0]):
        low = lax.dot_general(
            x_ref[s], down[s], (((1,), (1,)), ((), ())), preferred_element_type=jnp.float32
        ).astype(out_ref.dtype)
        half = low.shape[0] // 2
        out_ref[s] = jnp.concatenate([low[:half], low[half:]], axis=1)


def choose_kernel(per_video, me_ref, *refs):
    ins, outs = refs[:LOW], refs[LOW:]
    for i, out in enumerate(outs):
        video = (me_ref[0] ^ (LOW * i)) // per_video
        for j in range(LOW):
            out[j] = ins[j][video]


def add_delta(base, low, up, second):
    devs, toks, width = base.shape
    ranks = up.shape[0]
    row = lax.broadcasted_iota(jnp.int32, up.shape, 0)
    part = jnp.where(row // (ranks // 2) == second, up, jnp.zeros_like(up))
    none = jnp.zeros_like(part)
    deltas = [
        jnp.dot(low, jnp.concatenate(pair, axis=0), preferred_element_type=jnp.float32)
        for pair in ((part, none), (none, part))
    ]
    delta = jnp.concatenate([d.reshape(devs, toks // 2, width) for d in deltas], axis=1)
    return (base.astype(jnp.float32) + delta).astype(base.dtype).reshape(devs * toks, width)


def attend_kernel(block, me_ref, up_ref, q_ref, k_ref, v_ref, *refs):
    low_refs, out_ref, low_all, q_mix = refs[:-3], refs[-3], refs[-2], refs[-1]
    devs, toks, width = q_ref.shape
    length = devs * toks
    for k in range(devs):
        low_all[me_ref[0] ^ k] = low_refs[k // LOW][k % LOW]
    low = low_all[...].reshape(length // 2, low_all.shape[2])
    up = up_ref[...]
    keys = k_ref[...].reshape(length, width)
    vals = add_delta(v_ref[...], low, up, 1)
    vals = jnp.concatenate([vals, jnp.ones_like(vals)], axis=1)
    q_mix[...] = add_delta(q_ref[...], low, up, 0)
    scale = math.log2(math.e) / math.sqrt(width)

    def score(b):
        q = q_mix[b * toks : (b + block) * toks, :]
        return lax.dot_general(q, keys, (((1,), (1,)), ((), ())), preferred_element_type=jnp.float32)

    coming = score(0)
    for b in range(0, devs, block):
        scores = coming
        if b + block < devs:
            coming = score(b + block)
        top = jnp.max(scores, axis=1, keepdims=True)
        weights = jnp.exp2((scores - top) * scale).astype(jnp.bfloat16)
        mixed = jnp.dot(weights, vals, preferred_element_type=jnp.float32)
        out = mixed[:, :width] / mixed[:, width:]
        out_ref[b : b + block] = out.astype(jnp.bfloat16).reshape(block, toks, width)


def body(
    normed_token_features,
    queries,
    projected_keys,
    values,
    adapter_down_factors,
    adapter_up_factors,
    adapter_store_row,
    requests,
):
    videos, toks, model_width = normed_token_features.shape
    heads = queries.shape[1]
    width = queries.shape[3]
    _, ranks, up_width = adapter_up_factors.shape
    devs = lax.axis_size("seq")
    bits = bit_count(devs)
    me = lax.axis_index("seq").astype(jnp.int32)[None]
    pairs = videos * heads // devs
    per_video = devs // videos
    length = devs * toks
    col_split = math.gcd(per_video, model_width // LANES)
    rows = ranks * col_split // per_video
    tiles = model_width // col_split // LANES
    shape = (devs, bits, per_video, pairs, col_split, rows, tiles)

    def swap(tensor, k):
        return lax.ppermute(tensor, "seq", [(i, i ^ k) for i in range(devs)])

    def exchange(tensor):
        return lax.all_to_all(tensor, "seq", split_axis=0, concat_axis=0, tiled=True)

    def by_pairs(tensor):
        return tensor.reshape(devs, pairs, toks, width)

    def after(array, *others):
        return lax.optimization_barrier((array, others))[0]

    quarter = devs // LOW
    others = (2 * quarter, quarter, 3 * quarter)

    def halving(parts, received, i):
        size = parts[i].shape[0]
        terms = [(0, 0)] + [(1 + n, size) for n in range(len(received))]
        return on_vmem(
            functools.partial(sum_kernel, [terms]), [parts[i].shape], "halve", parts[i], *received
        )[0]

    def splitting(parts, received):
        size = (1,) + parts[-1].shape[1:]
        picks = [[(n, j) for n in range(1 + len(received))] for j in range(LOW)]
        return on_vmem(
            functools.partial(sum_kernel, picks), [size] * LOW, "split", parts[-1], *received
        )

    def to_others(shards):
        return [swap(shard, k) for shard, k in zip(shards[1:], others)]

    def total(shard, received):
        picks = [[(n, 0) for n in range(LOW)]]
        return on_vmem(
            functools.partial(sum_kernel, picks), [shard.shape], "total", shard, *received
        )[0]

    def join(arrays):
        count = sum(a.shape[0] for a in arrays)
        return on_vmem(join_kernel, [(count,) + arrays[0].shape[1:]], "join", *arrays)[0]

    keys = exchange(by_pairs(projected_keys))

    steps = [devs >> (i + 1) for i in range(bits - 2)] + [LOW]
    piece_shapes = [(h, tiles * rows, LANES) for h in steps] + [
        (h, pairs * ranks, LANES) for h in steps
    ]
    pieces = pl.pallas_call(
        functools.partial(pick_kernel, shape),
        in_specs=[SMEM, SMEM, SMEM, ANY, ANY],
        out_specs=[VMEM] * (2 * bits - 2),
        out_shape=[jax.ShapeDtypeStruct(s, jnp.bfloat16) for s in piece_shapes],
        scratch_shapes=[
            pltpu.VMEM((videos, ranks, model_width), jnp.bfloat16),
            pltpu.VMEM((videos, ranks, up_width), jnp.bfloat16),
            pltpu.SemaphoreType.DMA((2 * videos,)),
        ],
        compiler_params=pltpu.CompilerParams(vmem_limit_bytes=24 << 20),
        cost_estimate=pl.CostEstimate(
            flops=0,
            bytes_accessed=4 * videos * ranks * (model_width + up_width),
            transcendentals=0,
        ),
        name="pick_factors",
    )(me, adapter_store_row, requests, adapter_down_factors, adapter_up_factors)
    down_pieces, up_pieces = pieces[: bits - 1], pieces[bits - 1 :]

    down_got, up_got = [], []

    def send_up(i, *others):
        up_got.append(swap(after(halving(up_pieces, up_got, i), *others), 1 << i))

    for i in range(bits - 2):
        piece = down_pieces[0] if i == 0 else halving(down_pieces, down_got, i)
        if i > 0:
            part = up_pieces[0] if i == 1 else halving(up_pieces, up_got, i - 1)
            up_got.append(swap(after(part, piece), 1 << (i - 1)))
        down_got.append(swap(piece, 1 << i))
    part = after(halving(up_pieces, up_got, bits - 3), piece)
    up_got.append(swap(part, 1 << (bits - 3)))
    held = splitting((after(down_pieces[-1], *up_got[:-1]),), down_got)
    shard = after(total(held[0], to_others(held)), keys, up_got[-1])
    gathered = [shard] + [swap(shard, k) for k in others]

    up_part = after(up_pieces[-1], shard)
    near_pair, far_pair = on_vmem(
        functools.partial(sum_kernel, [[(n, 2 * h) for n in range(1 + len(up_got))] for h in (0, 1)]),
        [(2,) + up_part.shape[1:]] * 2,
        "split",
        up_part,
        *up_got,
    )
    came = swap(far_pair, quarter)
    asked = jnp.concatenate([by_pairs(values), by_pairs(queries)], axis=1)
    asked = exchange(after(asked, came, *gathered))
    one_shape = (1,) + up_part.shape[1:]
    kept, sent = on_vmem(
        functools.partial(sum_kernel, [[(n, h) for n in range(2)] for h in (0, 1)]),
        [one_shape] * 2,
        "split",
        near_pair,
        came,
    )
    last = swap(sent, 2 * quarter)
    up_here = on_vmem(
        functools.partial(sum_kernel, [[(0, 0), (1, 0)]]), [one_shape], "total", kept, last
    )[0].reshape(pairs, ranks, LANES)
    joined = join(gathered)
    for i in reversed(range(bits - 2)):
        gathered = [joined, swap(joined, 1 << i)]
        if i > 0:
            joined = join(gathered)

    low_shape = (videos, toks // 2, 2 * ranks)
    low = pl.pallas_call(
        functools.partial(low_rank_kernel, shape),
        in_specs=[SMEM, VMEM] + [VMEM] * len(gathered),
        out_specs=VMEM,
        scratch_shapes=[pltpu.VMEM((videos, ranks, model_width), jnp.bfloat16)],
        out_shape=jax.ShapeDtypeStruct(low_shape, jnp.bfloat16),
        compiler_params=pltpu.CompilerParams(vmem_limit_bytes=24 << 20),
        cost_estimate=pl.CostEstimate(
            flops=2 * videos * toks * ranks * model_width,
            bytes_accessed=2 * videos * (toks + ranks) * model_width,
            transcendentals=0,
        ),
        name="low_rank",
    )(me, normed_token_features, *gathered)
    nearby = [low] + [swap(low, k) for k in range(1, LOW)]
    chosen = pl.pallas_call(
        functools.partial(choose_kernel, per_video),
        in_specs=[SMEM] + [VMEM] * LOW,
        out_specs=[VMEM] * quarter,
        out_shape=[jax.ShapeDtypeStruct((LOW,) + low_shape[1:], jnp.bfloat16)] * quarter,
        cost_estimate=pl.CostEstimate(flops=0, bytes_accessed=8 * low.size, transcendentals=0),
        name="choose",
    )(me, *nearby)
    lows = [chosen[0]] + [swap(chosen[i], LOW * i) for i in range(1, quarter)]

    part_spec = pl.BlockSpec((devs, pl.squeezed, toks, width), lambda p: (0, p, 0, 0))
    later_spec = pl.BlockSpec((devs, pl.squeezed, toks, width), lambda p: (0, pairs + p, 0, 0))
    low_spec = pl.BlockSpec((LOW,) + low_shape[1:], lambda p: (0, 0, 0))
    mixed = pl.pallas_call(
        functools.partial(attend_kernel, math.gcd(devs, max(1, 256 // toks))),
        grid=(pairs,),
        in_specs=[SMEM, pl.BlockSpec((pl.squeezed, ranks, LANES), lambda p: (p, 0, 0))]
        + [later_spec, part_spec, part_spec]
        + [low_spec] * quarter,
        out_specs=part_spec,
        out_shape=jax.ShapeDtypeStruct((devs, pairs, toks, width), jnp.bfloat16),
        scratch_shapes=[
            pltpu.VMEM((devs,) + low_shape[1:], jnp.bfloat16),
            pltpu.VMEM((length, width), jnp.bfloat16),
        ],
        compiler_params=pltpu.CompilerParams(vmem_limit_bytes=48 << 20),
        cost_estimate=pl.CostEstimate(
            flops=4 * pairs * length * length * width,
            bytes_accessed=8 * pairs * length * width,
            transcendentals=pairs * length * length,
        ),
        name="attend",
    )(me, up_here, asked, keys, asked, *lows)
    return exchange(mixed).reshape(videos, heads, toks, width)


def solution(mesh):
    in_specs = (
        P("grp", "seq", None),
        P("grp", None, "seq", None),
        P("grp", None, "seq", None),
        P("grp", None, "seq", None),
        P("seq", None, None),
        P("seq", None, None),
        P(),
        P("grp"),
    )
    out_specs = P("grp", None, "seq", None)
    return jax.shard_map(body, mesh=mesh, in_specs=in_specs, out_specs=out_specs, check_vma=False)
```

```python
import functools
import math

import jax
import jax.numpy as jnp
from jax import lax
from jax.experimental import pallas as pl
from jax.experimental.pallas import tpu as pltpu
from jax.sharding import PartitionSpec as P

LANES = 128
LOW = 4
ANY = pl.BlockSpec(memory_space=pl.ANY)
VMEM = pl.BlockSpec(memory_space=pltpu.VMEM)
SMEM = pl.BlockSpec(memory_space=pltpu.SMEM)


def bit_count(n):
    bits = n.bit_length() - 1
    assert 1 << bits == n
    return bits


def reversed_bits(j, bits):
    out = 0
    for i in range(bits):
        out = out | (((j >> i) & 1) << (bits - 1 - i))
    return out


def pick_kernel(shape, me_ref, row_ref, req_ref, down_ref, up_ref, *refs):
    devs, bits, per_video, pairs, col_split, rows, tiles = shape
    downs, ups = refs[: bits - 1], refs[bits - 1 : 2 * bits - 2]
    down, up, sems = refs[2 * bits - 2 :]
    slots, ranks, _ = down_ref.shape
    videos = down.shape[0]
    me = me_ref[0]
    for s in range(videos):
        place = row_ref[req_ref[s]]
        slot = place % slots
        owned = place // slots == me
        copies = [
            pltpu.make_async_copy(down_ref.at[slot], down.at[s], sems.at[2 * s]),
            pltpu.make_async_copy(up_ref.at[slot], up.at[s], sems.at[2 * s + 1]),
        ]

        @pl.when(owned)
        def _():
            for copy in copies:
                copy.start()
            for copy in copies:
                copy.wait()

        @pl.when(jnp.logical_not(owned))
        def _():
            down[s] = jnp.zeros(down.shape[1:], down.dtype)
            up[s] = jnp.zeros(up.shape[1:], up.dtype)

    for j in range(devs):
        step = min(bits - j.bit_length(), bits - 2)
        at = j - (1 << (j.bit_length() - 1)) if j >= LOW else j
        dev = me ^ reversed_bits(j, bits)
        video = dev // per_video
        place = dev % per_video
        row = pl.multiple_of((place // col_split) * rows, rows)
        for t in range(tiles):
            col = pl.multiple_of(((place % col_split) * tiles + t) * LANES, LANES)
            downs[step][at, t * rows : (t + 1) * rows, :] = down[
                video, pl.ds(row, rows), pl.ds(col, LANES)
            ]
        for p in range(pairs):
            col = pl.multiple_of((place * pairs + p) * LANES, LANES)
            ups[step][at, p * ranks : (p + 1) * ranks, :] = up[video, :, pl.ds(col, LANES)]


def sum_kernel(picks, *refs):
    outs = refs[-len(picks) :]
    for out, terms in zip(outs, picks):
        size = out.shape[0]
        parts = [refs[i][first : first + size] for i, first in terms]
        out[...] = sum(parts[1:], parts[0])


def join_kernel(*refs):
    out, first = refs[-1], 0
    for ref in refs[:-1]:
        out[first : first + ref.shape[0]] = ref[...]
        first += ref.shape[0]


def on_vmem(kernel, shapes, name, *arrays):
    return pl.pallas_call(
        kernel,
        in_specs=[VMEM] * len(arrays),
        out_specs=[VMEM] * len(shapes),
        out_shape=[jax.ShapeDtypeStruct(s, arrays[0].dtype) for s in shapes],
        compiler_params=pltpu.CompilerParams(vmem_limit_bytes=16 << 20),
        cost_estimate=pl.CostEstimate(
            flops=0, bytes_accessed=2 * sum(a.size for a in arrays), transcendentals=0
        ),
        name=name,
    )(*arrays)


def low_rank_kernel(shape, me_ref, x_ref, *refs):
    devs, bits, per_video, _, col_split, rows, tiles = shape
    parts, out_ref, down = refs[:-2], refs[-2], refs[-1]
    blocks = [(ref, i) for ref in parts for i in range(ref.shape[0])]
    for j, (ref, i) in enumerate(blocks):
        dev = me_ref[0] ^ reversed_bits(j, bits)
        video = dev // per_video
        place = dev % per_video
        row = pl.multiple_of((place // col_split) * rows, rows)
        for t in range(tiles):
            col = pl.multiple_of(((place % col_split) * tiles + t) * LANES, LANES)
            down[video, pl.ds(row, rows), pl.ds(col, LANES)] = ref[i, t * rows : (t + 1) * rows, :]
    for s in range(x_ref.shape[0]):
        low = lax.dot_general(
            x_ref[s], down[s], (((1,), (1,)), ((), ())), preferred_element_type=jnp.float32
        ).astype(out_ref.dtype)
        half = low.shape[0] // 2
        out_ref[s] = jnp.concatenate([low[:half], low[half:]], axis=1)


def choose_kernel(per_video, me_ref, *refs):
    ins, outs = refs[:LOW], refs[LOW:]
    for i, out in enumerate(outs):
        video = (me_ref[0] ^ (LOW * i)) // per_video
        for j in range(LOW):
            out[j] = ins[j][video]


def add_delta(base, low, up, second):
    devs, toks, width = base.shape
    ranks = up.shape[0]
    row = lax.broadcasted_iota(jnp.int32, up.shape, 0)
    part = jnp.where(row // (ranks // 2) == second, up, jnp.zeros_like(up))
    none = jnp.zeros_like(part)
    deltas = [
        jnp.dot(low, jnp.concatenate(pair, axis=0), preferred_element_type=jnp.float32)
        for pair in ((part, none), (none, part))
    ]
    delta = jnp.concatenate([d.reshape(devs, toks // 2, width) for d in deltas], axis=1)
    return (base.astype(jnp.float32) + delta).astype(base.dtype).reshape(devs * toks, width)


def attend_kernel(block, me_ref, up_ref, q_ref, k_ref, v_ref, *refs):
    low_refs, out_ref, low_all, q_mix = refs[:-3], refs[-3], refs[-2], refs[-1]
    devs, toks, width = q_ref.shape
    length = devs * toks
    for k in range(devs):
        low_all[me_ref[0] ^ k] = low_refs[k // LOW][k % LOW]
    low = low_all[...].reshape(length // 2, low_all.shape[2])
    up = up_ref[...]
    keys = k_ref[...].reshape(length, width)
    vals = add_delta(v_ref[...], low, up, 1)
    vals = jnp.concatenate([vals, jnp.ones_like(vals)], axis=1)
    q_mix[...] = add_delta(q_ref[...], low, up, 0)
    scale = math.log2(math.e) / math.sqrt(width)

    def score(b):
        q = q_mix[b * toks : (b + block) * toks, :]
        return lax.dot_general(q, keys, (((1,), (1,)), ((), ())), preferred_element_type=jnp.float32)

    coming = score(0)
    for b in range(0, devs, block):
        scores = coming
        if b + block < devs:
            coming = score(b + block)
        top = jnp.max(scores, axis=1, keepdims=True)
        weights = jnp.exp2((scores - top) * scale).astype(jnp.bfloat16)
        mixed = jnp.dot(weights, vals, preferred_element_type=jnp.float32)
        out = mixed[:, :width] / mixed[:, width:]
        out_ref[b : b + block] = out.astype(jnp.bfloat16).reshape(block, toks, width)


def body(
    normed_token_features,
    queries,
    projected_keys,
    values,
    adapter_down_factors,
    adapter_up_factors,
    adapter_store_row,
    requests,
):
    videos, toks, model_width = normed_token_features.shape
    heads = queries.shape[1]
    width = queries.shape[3]
    _, ranks, up_width = adapter_up_factors.shape
    devs = lax.axis_size("seq")
    bits = bit_count(devs)
    me = lax.axis_index("seq").astype(jnp.int32)[None]
    pairs = videos * heads // devs
    per_video = devs // videos
    length = devs * toks
    col_split = math.gcd(per_video, model_width // LANES)
    rows = ranks * col_split // per_video
    tiles = model_width // col_split // LANES
    shape = (devs, bits, per_video, pairs, col_split, rows, tiles)

    def swap(tensor, k):
        return lax.ppermute(tensor, "seq", [(i, i ^ k) for i in range(devs)])

    def exchange(tensor):
        return lax.all_to_all(tensor, "seq", split_axis=0, concat_axis=0, tiled=True)

    def by_pairs(tensor):
        return tensor.reshape(devs, pairs, toks, width)

    def after(array, *others):
        return lax.optimization_barrier((array, others))[0]

    quarter = devs // LOW
    others = (2 * quarter, quarter, 3 * quarter)

    def halving(parts, received, i):
        size = parts[i].shape[0]
        terms = [(0, 0)] + [(1 + n, size) for n in range(len(received))]
        return on_vmem(
            functools.partial(sum_kernel, [terms]), [parts[i].shape], "halve", parts[i], *received
        )[0]

    def splitting(parts, received):
        size = (1,) + parts[-1].shape[1:]
        picks = [[(n, j) for n in range(1 + len(received))] for j in range(LOW)]
        return on_vmem(
            functools.partial(sum_kernel, picks), [size] * LOW, "split", parts[-1], *received
        )

    def to_others(shards):
        return [swap(shard, k) for shard, k in zip(shards[1:], others)]

    def total(shard, received):
        picks = [[(n, 0) for n in range(LOW)]]
        return on_vmem(
            functools.partial(sum_kernel, picks), [shard.shape], "total", shard, *received
        )[0]

    def join(arrays):
        count = sum(a.shape[0] for a in arrays)
        return on_vmem(join_kernel, [(count,) + arrays[0].shape[1:]], "join", *arrays)[0]

    keys = exchange(by_pairs(projected_keys))

    steps = [devs >> (i + 1) for i in range(bits - 2)] + [LOW]
    piece_shapes = [(h, tiles * rows, LANES) for h in steps] + [
        (h, pairs * ranks, LANES) for h in steps
    ]
    pieces = pl.pallas_call(
        functools.partial(pick_kernel, shape),
        in_specs=[SMEM, SMEM, SMEM, ANY, ANY],
        out_specs=[VMEM] * (2 * bits - 2),
        out_shape=[jax.ShapeDtypeStruct(s, jnp.bfloat16) for s in piece_shapes],
        scratch_shapes=[
            pltpu.VMEM((videos, ranks, model_width), jnp.bfloat16),
            pltpu.VMEM((videos, ranks, up_width), jnp.bfloat16),
            pltpu.SemaphoreType.DMA((2 * videos,)),
        ],
        compiler_params=pltpu.CompilerParams(vmem_limit_bytes=24 << 20),
        cost_estimate=pl.CostEstimate(
            flops=0,
            bytes_accessed=4 * videos * ranks * (model_width + up_width),
            transcendentals=0,
        ),
        name="pick_factors",
    )(me, adapter_store_row, requests, adapter_down_factors, adapter_up_factors)
    down_pieces, up_pieces = pieces[: bits - 1], pieces[bits - 1 :]

    down_got, up_got = [], []

    def send_up(i, *others):
        up_got.append(swap(after(halving(up_pieces, up_got, i), *others), 1 << i))

    for i in range(bits - 2):
        piece = down_pieces[0] if i == 0 else halving(down_pieces, down_got, i)
        if i > 0:
            part = up_pieces[0] if i == 1 else halving(up_pieces, up_got, i - 1)
            up_got.append(swap(after(part, piece), 1 << (i - 1)))
        down_got.append(swap(piece, 1 << i))
    part = after(halving(up_pieces, up_got, bits - 3), piece)
    up_got.append(swap(part, 1 << (bits - 3)))
    held = splitting((after(down_pieces[-1], *up_got[:-1]),), down_got)
    shard = after(total(held[0], to_others(held)), keys, up_got[-1])
    gathered = [shard] + [swap(shard, k) for k in others]

    up_part = after(up_pieces[-1], shard)
    near_pair, far_pair = on_vmem(
        functools.partial(sum_kernel, [[(n, 2 * h) for n in range(1 + len(up_got))] for h in (0, 1)]),
        [(2,) + up_part.shape[1:]] * 2,
        "split",
        up_part,
        *up_got,
    )
    came = swap(far_pair, quarter)
    asked = jnp.concatenate([by_pairs(values), by_pairs(queries)], axis=1)
    joined = join(gathered)
    asked = exchange(after(asked, came, joined))
    one_shape = (1,) + up_part.shape[1:]
    kept, sent = on_vmem(
        functools.partial(sum_kernel, [[(n, h) for n in range(2)] for h in (0, 1)]),
        [one_shape] * 2,
        "split",
        near_pair,
        came,
    )
    last = swap(sent, 2 * quarter)
    up_here = on_vmem(
        functools.partial(sum_kernel, [[(0, 0), (1, 0)]]), [one_shape], "total", kept, last
    )[0].reshape(pairs, ranks, LANES)
    for i in reversed(range(bits - 2)):
        gathered = [joined, swap(joined, 1 << i)]
        if i > 0:
            joined = join(gathered)

    low_shape = (videos, toks // 2, 2 * ranks)
    low = pl.pallas_call(
        functools.partial(low_rank_kernel, shape),
        in_specs=[SMEM, VMEM] + [VMEM] * len(gathered),
        out_specs=VMEM,
        scratch_shapes=[pltpu.VMEM((videos, ranks, model_width), jnp.bfloat16)],
        out_shape=jax.ShapeDtypeStruct(low_shape, jnp.bfloat16),
        compiler_params=pltpu.CompilerParams(vmem_limit_bytes=24 << 20),
        cost_estimate=pl.CostEstimate(
            flops=2 * videos * toks * ranks * model_width,
            bytes_accessed=2 * videos * (toks + ranks) * model_width,
            transcendentals=0,
        ),
        name="low_rank",
    )(me, normed_token_features, *gathered)
    nearby = [low] + [swap(low, k) for k in range(1, LOW)]
    chosen = pl.pallas_call(
        functools.partial(choose_kernel, per_video),
        in_specs=[SMEM] + [VMEM] * LOW,
        out_specs=[VMEM] * quarter,
        out_shape=[jax.ShapeDtypeStruct((LOW,) + low_shape[1:], jnp.bfloat16)] * quarter,
        cost_estimate=pl.CostEstimate(flops=0, bytes_accessed=8 * low.size, transcendentals=0),
        name="choose",
    )(me, *nearby)
    lows = [chosen[0]] + [swap(chosen[i], LOW * i) for i in range(1, quarter)]

    part_spec = pl.BlockSpec((devs, pl.squeezed, toks, width), lambda p: (0, p, 0, 0))
    later_spec = pl.BlockSpec((devs, pl.squeezed, toks, width), lambda p: (0, pairs + p, 0, 0))
    low_spec = pl.BlockSpec((LOW,) + low_shape[1:], lambda p: (0, 0, 0))
    mixed = pl.pallas_call(
        functools.partial(attend_kernel, math.gcd(devs, max(1, 256 // toks))),
        grid=(pairs,),
        in_specs=[SMEM, pl.BlockSpec((pl.squeezed, ranks, LANES), lambda p: (p, 0, 0))]
        + [later_spec, part_spec, part_spec]
        + [low_spec] * quarter,
        out_specs=part_spec,
        out_shape=jax.ShapeDtypeStruct((devs, pairs, toks, width), jnp.bfloat16),
        scratch_shapes=[
            pltpu.VMEM((devs,) + low_shape[1:], jnp.bfloat16),
            pltpu.VMEM((length, width), jnp.bfloat16),
        ],
        compiler_params=pltpu.CompilerParams(vmem_limit_bytes=48 << 20),
        cost_estimate=pl.CostEstimate(
            flops=4 * pairs * length * length * width,
            bytes_accessed=8 * pairs * length * width,
            transcendentals=pairs * length * length,
        ),
        name="attend",
    )(me, up_here, asked, keys, asked, *lows)
    return exchange(mixed).reshape(videos, heads, toks, width)


def solution(mesh):
    in_specs = (
        P("grp", "seq", None),
        P("grp", None, "seq", None),
        P("grp", None, "seq", None),
        P("grp", None, "seq", None),
        P("seq", None, None),
        P("seq", None, None),
        P(),
        P("grp"),
    )
    out_specs = P("grp", None, "seq", None)
    return jax.shard_map(body, mesh=mesh, in_specs=in_specs, out_specs=out_specs, check_vma=False)
```

```python
import functools
import math

import jax
import jax.numpy as jnp
from jax import lax
from jax.experimental import pallas as pl
from jax.experimental.pallas import tpu as pltpu
from jax.sharding import PartitionSpec as P

LANES = 128
LOW = 4
ANY = pl.BlockSpec(memory_space=pl.ANY)
VMEM = pl.BlockSpec(memory_space=pltpu.VMEM)
SMEM = pl.BlockSpec(memory_space=pltpu.SMEM)


def bit_count(n):
    bits = n.bit_length() - 1
    assert 1 << bits == n
    return bits


def reversed_bits(j, bits):
    out = 0
    for i in range(bits):
        out = out | (((j >> i) & 1) << (bits - 1 - i))
    return out


def pick_kernel(shape, me_ref, row_ref, req_ref, down_ref, up_ref, *refs):
    devs, bits, per_video, pairs, col_split, rows, tiles = shape
    downs, ups = refs[: bits - 1], refs[bits - 1 : 2 * bits - 2]
    down, up, sems = refs[2 * bits - 2 :]
    slots, ranks, _ = down_ref.shape
    videos = down.shape[0]
    me = me_ref[0]
    for s in range(videos):
        place = row_ref[req_ref[s]]
        slot = place % slots
        owned = place // slots == me
        copies = [
            pltpu.make_async_copy(down_ref.at[slot], down.at[s], sems.at[2 * s]),
            pltpu.make_async_copy(up_ref.at[slot], up.at[s], sems.at[2 * s + 1]),
        ]

        @pl.when(owned)
        def _():
            for copy in copies:
                copy.start()
            for copy in copies:
                copy.wait()

        @pl.when(jnp.logical_not(owned))
        def _():
            down[s] = jnp.zeros(down.shape[1:], down.dtype)
            up[s] = jnp.zeros(up.shape[1:], up.dtype)

    for j in range(devs):
        step = min(bits - j.bit_length(), bits - 2)
        at = j - (1 << (j.bit_length() - 1)) if j >= LOW else j
        dev = me ^ reversed_bits(j, bits)
        video = dev // per_video
        place = dev % per_video
        row = pl.multiple_of((place // col_split) * rows, rows)
        for t in range(tiles):
            col = pl.multiple_of(((place % col_split) * tiles + t) * LANES, LANES)
            downs[step][at, t * rows : (t + 1) * rows, :] = down[
                video, pl.ds(row, rows), pl.ds(col, LANES)
            ]
        for p in range(pairs):
            col = pl.multiple_of((place * pairs + p) * LANES, LANES)
            ups[step][at, p * ranks : (p + 1) * ranks, :] = up[video, :, pl.ds(col, LANES)]


def sum_kernel(picks, *refs):
    outs = refs[-len(picks) :]
    for out, terms in zip(outs, picks):
        size = out.shape[0]
        parts = [refs[i][first : first + size] for i, first in terms]
        out[...] = sum(parts[1:], parts[0])


def pack_kernel(v_ref, q_ref, out_ref):
    pairs = v_ref.shape[1]
    out_ref[:, :pairs] = v_ref[...]
    out_ref[:, pairs:] = q_ref[...]


def join_kernel(*refs):
    out, first = refs[-1], 0
    for ref in refs[:-1]:
        out[first : first + ref.shape[0]] = ref[...]
        first += ref.shape[0]


def on_vmem(kernel, shapes, name, *arrays):
    return pl.pallas_call(
        kernel,
        in_specs=[VMEM] * len(arrays),
        out_specs=[VMEM] * len(shapes),
        out_shape=[jax.ShapeDtypeStruct(s, arrays[0].dtype) for s in shapes],
        compiler_params=pltpu.CompilerParams(vmem_limit_bytes=24 << 20),
        cost_estimate=pl.CostEstimate(
            flops=0, bytes_accessed=2 * sum(a.size for a in arrays), transcendentals=0
        ),
        name=name,
    )(*arrays)


def low_rank_kernel(shape, me_ref, x_ref, *refs):
    devs, bits, per_video, _, col_split, rows, tiles = shape
    parts, out_ref, down = refs[:-2], refs[-2], refs[-1]
    blocks = [(ref, i) for ref in parts for i in range(ref.shape[0])]
    for j, (ref, i) in enumerate(blocks):
        dev = me_ref[0] ^ reversed_bits(j, bits)
        video = dev // per_video
        place = dev % per_video
        row = pl.multiple_of((place // col_split) * rows, rows)
        for t in range(tiles):
            col = pl.multiple_of(((place % col_split) * tiles + t) * LANES, LANES)
            down[video, pl.ds(row, rows), pl.ds(col, LANES)] = ref[i, t * rows : (t + 1) * rows, :]
    for s in range(x_ref.shape[0]):
        low = lax.dot_general(
            x_ref[s], down[s], (((1,), (1,)), ((), ())), preferred_element_type=jnp.float32
        ).astype(out_ref.dtype)
        half = low.shape[0] // 2
        out_ref[s] = jnp.concatenate([low[:half], low[half:]], axis=1)


def choose_kernel(per_video, me_ref, *refs):
    ins, outs = refs[:LOW], refs[LOW:]
    for i, out in enumerate(outs):
        video = (me_ref[0] ^ (LOW * i)) // per_video
        for j in range(LOW):
            out[j] = ins[j][video]


def add_delta(base, low, up, second):
    devs, toks, width = base.shape
    ranks = up.shape[0]
    row = lax.broadcasted_iota(jnp.int32, up.shape, 0)
    part = jnp.where(row // (ranks // 2) == second, up, jnp.zeros_like(up))
    none = jnp.zeros_like(part)
    deltas = [
        jnp.dot(low, jnp.concatenate(pair, axis=0), preferred_element_type=jnp.float32)
        for pair in ((part, none), (none, part))
    ]
    delta = jnp.concatenate([d.reshape(devs, toks // 2, width) for d in deltas], axis=1)
    return (base.astype(jnp.float32) + delta).astype(base.dtype).reshape(devs * toks, width)


def attend_kernel(block, me_ref, up_ref, q_ref, k_ref, v_ref, *refs):
    low_refs, out_ref, low_all, q_mix = refs[:-3], refs[-3], refs[-2], refs[-1]
    devs, toks, width = q_ref.shape
    length = devs * toks
    for k in range(devs):
        low_all[me_ref[0] ^ k] = low_refs[k // LOW][k % LOW]
    low = low_all[...].reshape(length // 2, low_all.shape[2])
    up = up_ref[...]
    keys = k_ref[...].reshape(length, width)
    vals = add_delta(v_ref[...], low, up, 1)
    vals = jnp.concatenate([vals, jnp.ones_like(vals)], axis=1)
    q_mix[...] = add_delta(q_ref[...], low, up, 0)
    scale = math.log2(math.e) / math.sqrt(width)

    def score(b):
        q = q_mix[b * toks : (b + block) * toks, :]
        return lax.dot_general(q, keys, (((1,), (1,)), ((), ())), preferred_element_type=jnp.float32)

    coming = score(0)
    for b in range(0, devs, block):
        scores = coming
        if b + block < devs:
            coming = score(b + block)
        top = jnp.max(scores, axis=1, keepdims=True)
        weights = jnp.exp2((scores - top) * scale).astype(jnp.bfloat16)
        mixed = jnp.dot(weights, vals, preferred_element_type=jnp.float32)
        out = mixed[:, :width] / mixed[:, width:]
        out_ref[b : b + block] = out.astype(jnp.bfloat16).reshape(block, toks, width)


def body(
    normed_token_features,
    queries,
    projected_keys,
    values,
    adapter_down_factors,
    adapter_up_factors,
    adapter_store_row,
    requests,
):
    videos, toks, model_width = normed_token_features.shape
    heads = queries.shape[1]
    width = queries.shape[3]
    _, ranks, up_width = adapter_up_factors.shape
    devs = lax.axis_size("seq")
    bits = bit_count(devs)
    me = lax.axis_index("seq").astype(jnp.int32)[None]
    pairs = videos * heads // devs
    per_video = devs // videos
    length = devs * toks
    col_split = math.gcd(per_video, model_width // LANES)
    rows = ranks * col_split // per_video
    tiles = model_width // col_split // LANES
    shape = (devs, bits, per_video, pairs, col_split, rows, tiles)

    def swap(tensor, k):
        return lax.ppermute(tensor, "seq", [(i, i ^ k) for i in range(devs)])

    def exchange(tensor):
        return lax.all_to_all(tensor, "seq", split_axis=0, concat_axis=0, tiled=True)

    def by_pairs(tensor):
        return tensor.reshape(devs, pairs, toks, width)

    def after(array, *others):
        return lax.optimization_barrier((array, others))[0]

    quarter = devs // LOW
    others = (2 * quarter, quarter, 3 * quarter)

    def halving(parts, received, i):
        size = parts[i].shape[0]
        terms = [(0, 0)] + [(1 + n, size) for n in range(len(received))]
        return on_vmem(
            functools.partial(sum_kernel, [terms]), [parts[i].shape], "halve", parts[i], *received
        )[0]

    def splitting(parts, received):
        size = (1,) + parts[-1].shape[1:]
        picks = [[(n, j) for n in range(1 + len(received))] for j in range(LOW)]
        return on_vmem(
            functools.partial(sum_kernel, picks), [size] * LOW, "split", parts[-1], *received
        )

    def to_others(shards):
        return [swap(shard, k) for shard, k in zip(shards[1:], others)]

    def total(shard, received):
        picks = [[(n, 0) for n in range(LOW)]]
        return on_vmem(
            functools.partial(sum_kernel, picks), [shard.shape], "total", shard, *received
        )[0]

    def join(arrays):
        count = sum(a.shape[0] for a in arrays)
        return on_vmem(join_kernel, [(count,) + arrays[0].shape[1:]], "join", *arrays)[0]

    keys = exchange(by_pairs(projected_keys))

    steps = [devs >> (i + 1) for i in range(bits - 2)] + [LOW]
    piece_shapes = [(h, tiles * rows, LANES) for h in steps] + [
        (h, pairs * ranks, LANES) for h in steps
    ]
    pieces = pl.pallas_call(
        functools.partial(pick_kernel, shape),
        in_specs=[SMEM, SMEM, SMEM, ANY, ANY],
        out_specs=[VMEM] * (2 * bits - 2),
        out_shape=[jax.ShapeDtypeStruct(s, jnp.bfloat16) for s in piece_shapes],
        scratch_shapes=[
            pltpu.VMEM((videos, ranks, model_width), jnp.bfloat16),
            pltpu.VMEM((videos, ranks, up_width), jnp.bfloat16),
            pltpu.SemaphoreType.DMA((2 * videos,)),
        ],
        compiler_params=pltpu.CompilerParams(vmem_limit_bytes=24 << 20),
        cost_estimate=pl.CostEstimate(
            flops=0,
            bytes_accessed=4 * videos * ranks * (model_width + up_width),
            transcendentals=0,
        ),
        name="pick_factors",
    )(me, adapter_store_row, requests, adapter_down_factors, adapter_up_factors)
    down_pieces, up_pieces = pieces[: bits - 1], pieces[bits - 1 :]

    down_got, up_got = [], []

    def send_up(i, *others):
        up_got.append(swap(after(halving(up_pieces, up_got, i), *others), 1 << i))

    for i in range(bits - 2):
        piece = down_pieces[0] if i == 0 else halving(down_pieces, down_got, i)
        if i > 0:
            part = up_pieces[0] if i == 1 else halving(up_pieces, up_got, i - 1)
            up_got.append(swap(after(part, piece), 1 << (i - 1)))
        down_got.append(swap(piece, 1 << i))
    part = after(halving(up_pieces, up_got, bits - 3), piece)
    up_got.append(swap(part, 1 << (bits - 3)))
    held = splitting((after(down_pieces[-1], *up_got[:-1]),), down_got)
    shard = after(total(held[0], to_others(held)), keys, up_got[-1])
    both = join([shard, swap(shard, 2 * quarter)])

    up_part = after(up_pieces[-1], shard)
    near_pair, far_pair = on_vmem(
        functools.partial(sum_kernel, [[(n, 2 * h) for n in range(1 + len(up_got))] for h in (0, 1)]),
        [(2,) + up_part.shape[1:]] * 2,
        "split",
        up_part,
        *up_got,
    )
    came = swap(far_pair, quarter)
    sources = lax.optimization_barrier((by_pairs(values), by_pairs(queries), both, came))[:2]
    asked = on_vmem(pack_kernel, [(devs, 2 * pairs, toks, width)], "pack", *sources)[0]
    asked = exchange(asked)
    joined = join([both, swap(both, quarter)])
    one_shape = (1,) + up_part.shape[1:]
    kept, sent = on_vmem(
        functools.partial(sum_kernel, [[(n, h) for n in range(2)] for h in (0, 1)]),
        [one_shape] * 2,
        "split",
        near_pair,
        came,
    )
    last = swap(sent, 2 * quarter)
    up_here = on_vmem(
        functools.partial(sum_kernel, [[(0, 0), (1, 0)]]), [one_shape], "total", kept, last
    )[0].reshape(pairs, ranks, LANES)
    for i in reversed(range(bits - 2)):
        gathered = [joined, swap(joined, 1 << i)]
        if i > 0:
            joined = join(gathered)

    low_shape = (videos, toks // 2, 2 * ranks)
    low = pl.pallas_call(
        functools.partial(low_rank_kernel, shape),
        in_specs=[SMEM, VMEM] + [VMEM] * len(gathered),
        out_specs=VMEM,
        scratch_shapes=[pltpu.VMEM((videos, ranks, model_width), jnp.bfloat16)],
        out_shape=jax.ShapeDtypeStruct(low_shape, jnp.bfloat16),
        compiler_params=pltpu.CompilerParams(vmem_limit_bytes=24 << 20),
        cost_estimate=pl.CostEstimate(
            flops=2 * videos * toks * ranks * model_width,
            bytes_accessed=2 * videos * (toks + ranks) * model_width,
            transcendentals=0,
        ),
        name="low_rank",
    )(me, normed_token_features, *gathered)
    nearby = [low] + [swap(low, k) for k in range(1, LOW)]
    chosen = pl.pallas_call(
        functools.partial(choose_kernel, per_video),
        in_specs=[SMEM] + [VMEM] * LOW,
        out_specs=[VMEM] * quarter,
        out_shape=[jax.ShapeDtypeStruct((LOW,) + low_shape[1:], jnp.bfloat16)] * quarter,
        cost_estimate=pl.CostEstimate(flops=0, bytes_accessed=8 * low.size, transcendentals=0),
        name="choose",
    )(me, *nearby)
    lows = [chosen[0]] + [swap(chosen[i], LOW * i) for i in range(1, quarter)]

    part_spec = pl.BlockSpec((devs, pl.squeezed, toks, width), lambda p: (0, p, 0, 0))
    later_spec = pl.BlockSpec((devs, pl.squeezed, toks, width), lambda p: (0, pairs + p, 0, 0))
    low_spec = pl.BlockSpec((LOW,) + low_shape[1:], lambda p: (0, 0, 0))
    mixed = pl.pallas_call(
        functools.partial(attend_kernel, math.gcd(devs, max(1, 256 // toks))),
        grid=(pairs,),
        in_specs=[SMEM, pl.BlockSpec((pl.squeezed, ranks, LANES), lambda p: (p, 0, 0))]
        + [later_spec, part_spec, part_spec]
        + [low_spec] * quarter,
        out_specs=part_spec,
        out_shape=jax.ShapeDtypeStruct((devs, pairs, toks, width), jnp.bfloat16),
        scratch_shapes=[
            pltpu.VMEM((devs,) + low_shape[1:], jnp.bfloat16),
            pltpu.VMEM((length, width), jnp.bfloat16),
        ],
        compiler_params=pltpu.CompilerParams(vmem_limit_bytes=48 << 20),
        cost_estimate=pl.CostEstimate(
            flops=4 * pairs * length * length * width,
            bytes_accessed=8 * pairs * length * width,
            transcendentals=pairs * length * length,
        ),
        name="attend",
    )(me, up_here, asked, keys, asked, *lows)
    return exchange(mixed).reshape(videos, heads, toks, width)


def solution(mesh):
    in_specs = (
        P("grp", "seq", None),
        P("grp", None, "seq", None),
        P("grp", None, "seq", None),
        P("grp", None, "seq", None),
        P("seq", None, None),
        P("seq", None, None),
        P(),
        P("grp"),
    )
    out_specs = P("grp", None, "seq", None)
    return jax.shard_map(body, mesh=mesh, in_specs=in_specs, out_specs=out_specs, check_vma=False)
```

```python
import functools
import math

import jax
import jax.numpy as jnp
from jax import lax
from jax.experimental import pallas as pl
from jax.experimental.pallas import tpu as pltpu
from jax.sharding import PartitionSpec as P

LANES = 128
LOW = 4
ANY = pl.BlockSpec(memory_space=pl.ANY)
VMEM = pl.BlockSpec(memory_space=pltpu.VMEM)
SMEM = pl.BlockSpec(memory_space=pltpu.SMEM)


def bit_count(n):
    bits = n.bit_length() - 1
    assert 1 << bits == n
    return bits


def reversed_bits(j, bits):
    out = 0
    for i in range(bits):
        out = out | (((j >> i) & 1) << (bits - 1 - i))
    return out


def pick_kernel(shape, me_ref, row_ref, req_ref, down_ref, up_ref, *refs):
    devs, bits, per_video, pairs, col_split, rows, tiles = shape
    downs, ups = refs[: bits - 1], refs[bits - 1 : 2 * bits - 2]
    down, up, sems = refs[2 * bits - 2 :]
    slots, ranks, _ = down_ref.shape
    videos = down.shape[0]
    me = me_ref[0]
    for s in range(videos):
        place = row_ref[req_ref[s]]
        slot = place % slots
        owned = place // slots == me
        copies = [
            pltpu.make_async_copy(down_ref.at[slot], down.at[s], sems.at[2 * s]),
            pltpu.make_async_copy(up_ref.at[slot], up.at[s], sems.at[2 * s + 1]),
        ]

        @pl.when(owned)
        def _():
            for copy in copies:
                copy.start()
            for copy in copies:
                copy.wait()

        @pl.when(jnp.logical_not(owned))
        def _():
            down[s] = jnp.zeros(down.shape[1:], down.dtype)
            up[s] = jnp.zeros(up.shape[1:], up.dtype)

    for j in range(devs):
        step = min(bits - j.bit_length(), bits - 2)
        at = j - (1 << (j.bit_length() - 1)) if j >= LOW else j
        dev = me ^ reversed_bits(j, bits)
        video = dev // per_video
        place = dev % per_video
        row = pl.multiple_of((place // col_split) * rows, rows)
        for t in range(tiles):
            col = pl.multiple_of(((place % col_split) * tiles + t) * LANES, LANES)
            downs[step][at, t * rows : (t + 1) * rows, :] = down[
                video, pl.ds(row, rows), pl.ds(col, LANES)
            ]
        for p in range(pairs):
            col = pl.multiple_of((place * pairs + p) * LANES, LANES)
            ups[step][at, p * ranks : (p + 1) * ranks, :] = up[video, :, pl.ds(col, LANES)]


def sum_kernel(picks, *refs):
    outs = refs[-len(picks) :]
    for out, terms in zip(outs, picks):
        size = out.shape[0]
        parts = [refs[i][first : first + size] for i, first in terms]
        out[...] = sum(parts[1:], parts[0])


def join_kernel(*refs):
    out, first = refs[-1], 0
    for ref in refs[:-1]:
        out[first : first + ref.shape[0]] = ref[...]
        first += ref.shape[0]


def on_vmem(kernel, shapes, name, *arrays):
    return pl.pallas_call(
        kernel,
        in_specs=[VMEM] * len(arrays),
        out_specs=[VMEM] * len(shapes),
        out_shape=[jax.ShapeDtypeStruct(s, arrays[0].dtype) for s in shapes],
        compiler_params=pltpu.CompilerParams(vmem_limit_bytes=16 << 20),
        cost_estimate=pl.CostEstimate(
            flops=0, bytes_accessed=2 * sum(a.size for a in arrays), transcendentals=0
        ),
        name=name,
    )(*arrays)


def low_rank_kernel(shape, me_ref, x_ref, *refs):
    devs, bits, per_video, _, col_split, rows, tiles = shape
    parts, out_ref, down = refs[:-2], refs[-2], refs[-1]
    blocks = [(ref, i) for ref in parts for i in range(ref.shape[0])]
    for j, (ref, i) in enumerate(blocks):
        dev = me_ref[0] ^ reversed_bits(j, bits)
        video = dev // per_video
        place = dev % per_video
        row = pl.multiple_of((place // col_split) * rows, rows)
        for t in range(tiles):
            col = pl.multiple_of(((place % col_split) * tiles + t) * LANES, LANES)
            down[video, pl.ds(row, rows), pl.ds(col, LANES)] = ref[i, t * rows : (t + 1) * rows, :]
    for s in range(x_ref.shape[0]):
        low = lax.dot_general(
            x_ref[s], down[s], (((1,), (1,)), ((), ())), preferred_element_type=jnp.float32
        ).astype(out_ref.dtype)
        half = low.shape[0] // 2
        out_ref[s] = jnp.concatenate([low[:half], low[half:]], axis=1)


def choose_kernel(per_video, me_ref, *refs):
    ins, outs = refs[:LOW], refs[LOW:]
    for i, out in enumerate(outs):
        video = (me_ref[0] ^ (LOW * i)) // per_video
        for j in range(LOW):
            out[j] = ins[j][video]


def add_delta(base, low, up, second):
    devs, toks, width = base.shape
    ranks = up.shape[0]
    row = lax.broadcasted_iota(jnp.int32, up.shape, 0)
    part = jnp.where(row // (ranks // 2) == second, up, jnp.zeros_like(up))
    none = jnp.zeros_like(part)
    deltas = [
        jnp.dot(low, jnp.concatenate(pair, axis=0), preferred_element_type=jnp.float32)
        for pair in ((part, none), (none, part))
    ]
    delta = jnp.concatenate([d.reshape(devs, toks // 2, width) for d in deltas], axis=1)
    return (base.astype(jnp.float32) + delta).astype(base.dtype).reshape(devs * toks, width)


def attend_kernel(block, me_ref, up_ref, q_ref, k_ref, v_ref, *refs):
    low_refs, out_ref, low_all, q_mix = refs[:-3], refs[-3], refs[-2], refs[-1]
    devs, toks, width = q_ref.shape
    length = devs * toks
    for k in range(devs):
        low_all[me_ref[0] ^ k] = low_refs[k // LOW][k % LOW]
    low = low_all[...].reshape(length // 2, low_all.shape[2])
    up = up_ref[...]
    keys = k_ref[...].reshape(length, width)
    vals = add_delta(v_ref[...], low, up, 1)
    vals = jnp.concatenate([vals, jnp.ones_like(vals)], axis=1)
    q_mix[...] = add_delta(q_ref[...], low, up, 0)
    scale = math.log2(math.e) / math.sqrt(width)

    def score(b):
        q = q_mix[b * toks : (b + block) * toks, :]
        return lax.dot_general(q, keys, (((1,), (1,)), ((), ())), preferred_element_type=jnp.float32)

    coming = score(0)
    for b in range(0, devs, block):
        scores = coming
        if b + block < devs:
            coming = score(b + block)
        top = jnp.max(scores, axis=1, keepdims=True)
        weights = jnp.exp2((scores - top) * scale).astype(jnp.bfloat16)
        mixed = jnp.dot(weights, vals, preferred_element_type=jnp.float32)
        out = mixed[:, :width] / mixed[:, width:]
        out_ref[b : b + block] = out.astype(jnp.bfloat16).reshape(block, toks, width)


def body(
    normed_token_features,
    queries,
    projected_keys,
    values,
    adapter_down_factors,
    adapter_up_factors,
    adapter_store_row,
    requests,
):
    videos, toks, model_width = normed_token_features.shape
    heads = queries.shape[1]
    width = queries.shape[3]
    _, ranks, up_width = adapter_up_factors.shape
    devs = lax.axis_size("seq")
    bits = bit_count(devs)
    me = lax.axis_index("seq").astype(jnp.int32)[None]
    pairs = videos * heads // devs
    per_video = devs // videos
    length = devs * toks
    col_split = math.gcd(per_video, model_width // LANES)
    rows = ranks * col_split // per_video
    tiles = model_width // col_split // LANES
    shape = (devs, bits, per_video, pairs, col_split, rows, tiles)

    def swap(tensor, k):
        return lax.ppermute(tensor, "seq", [(i, i ^ k) for i in range(devs)])

    def exchange(tensor):
        return lax.all_to_all(tensor, "seq", split_axis=0, concat_axis=0, tiled=True)

    def by_pairs(tensor):
        return tensor.reshape(devs, pairs, toks, width)

    def after(array, *others):
        return lax.optimization_barrier((array, others))[0]

    quarter = devs // LOW
    others = (2 * quarter, quarter, 3 * quarter)

    def halving(parts, received, i):
        size = parts[i].shape[0]
        terms = [(0, 0)] + [(1 + n, size) for n in range(len(received))]
        return on_vmem(
            functools.partial(sum_kernel, [terms]), [parts[i].shape], "halve", parts[i], *received
        )[0]

    def splitting(parts, received):
        size = (1,) + parts[-1].shape[1:]
        picks = [[(n, j) for n in range(1 + len(received))] for j in range(LOW)]
        return on_vmem(
            functools.partial(sum_kernel, picks), [size] * LOW, "split", parts[-1], *received
        )

    def to_others(shards):
        return [swap(shard, k) for shard, k in zip(shards[1:], others)]

    def total(shard, received):
        picks = [[(n, 0) for n in range(LOW)]]
        return on_vmem(
            functools.partial(sum_kernel, picks), [shard.shape], "total", shard, *received
        )[0]

    def join(arrays):
        count = sum(a.shape[0] for a in arrays)
        return on_vmem(join_kernel, [(count,) + arrays[0].shape[1:]], "join", *arrays)[0]

    keys = exchange(by_pairs(projected_keys))

    steps = [devs >> (i + 1) for i in range(bits - 2)] + [LOW]
    piece_shapes = [(h, tiles * rows, LANES) for h in steps] + [
        (h, pairs * ranks, LANES) for h in steps
    ]
    pieces = pl.pallas_call(
        functools.partial(pick_kernel, shape),
        in_specs=[SMEM, SMEM, SMEM, ANY, ANY],
        out_specs=[VMEM] * (2 * bits - 2),
        out_shape=[jax.ShapeDtypeStruct(s, jnp.bfloat16) for s in piece_shapes],
        scratch_shapes=[
            pltpu.VMEM((videos, ranks, model_width), jnp.bfloat16),
            pltpu.VMEM((videos, ranks, up_width), jnp.bfloat16),
            pltpu.SemaphoreType.DMA((2 * videos,)),
        ],
        compiler_params=pltpu.CompilerParams(vmem_limit_bytes=24 << 20),
        cost_estimate=pl.CostEstimate(
            flops=0,
            bytes_accessed=4 * videos * ranks * (model_width + up_width),
            transcendentals=0,
        ),
        name="pick_factors",
    )(me, adapter_store_row, requests, adapter_down_factors, adapter_up_factors)
    down_pieces, up_pieces = pieces[: bits - 1], pieces[bits - 1 :]

    down_got, up_got = [], []

    def send_up(i, *others):
        up_got.append(swap(after(halving(up_pieces, up_got, i), *others), 1 << i))

    for i in range(bits - 2):
        piece = down_pieces[0] if i == 0 else halving(down_pieces, down_got, i)
        if i > 0:
            part = up_pieces[0] if i == 1 else halving(up_pieces, up_got, i - 1)
            up_got.append(swap(after(part, piece), 1 << (i - 1)))
        down_got.append(swap(piece, 1 << i))
    part = after(halving(up_pieces, up_got, bits - 3), piece)
    up_got.append(swap(part, 1 << (bits - 3)))
    held = splitting((after(down_pieces[-1], *up_got[:-1]),), down_got)
    shard = after(total(held[0], to_others(held)), keys, up_got[-1])
    gathered = [shard] + [swap(shard, k) for k in others]

    joined = join(gathered)
    asked = jnp.concatenate([by_pairs(values), by_pairs(queries)], axis=1)
    asked = exchange(after(asked, joined))
    for i in reversed(range(bits - 2)):
        gathered = [joined, swap(joined, 1 << i)]
        if i > 0:
            joined = join(gathered)

    low_shape = (videos, toks // 2, 2 * ranks)
    low = pl.pallas_call(
        functools.partial(low_rank_kernel, shape),
        in_specs=[SMEM, VMEM] + [VMEM] * len(gathered),
        out_specs=VMEM,
        scratch_shapes=[pltpu.VMEM((videos, ranks, model_width), jnp.bfloat16)],
        out_shape=jax.ShapeDtypeStruct(low_shape, jnp.bfloat16),
        compiler_params=pltpu.CompilerParams(vmem_limit_bytes=24 << 20),
        cost_estimate=pl.CostEstimate(
            flops=2 * videos * toks * ranks * model_width,
            bytes_accessed=2 * videos * (toks + ranks) * model_width,
            transcendentals=0,
        ),
        name="low_rank",
    )(me, normed_token_features, *gathered)
    up_part = after(up_pieces[-1], low)
    near_pair, far_pair = on_vmem(
        functools.partial(sum_kernel, [[(n, 2 * h) for n in range(1 + len(up_got))] for h in (0, 1)]),
        [(2,) + up_part.shape[1:]] * 2,
        "split",
        up_part,
        *up_got,
    )
    came = swap(far_pair, quarter)
    one_shape = (1,) + up_part.shape[1:]
    kept, sent = on_vmem(
        functools.partial(sum_kernel, [[(n, h) for n in range(2)] for h in (0, 1)]),
        [one_shape] * 2,
        "split",
        near_pair,
        came,
    )
    last = swap(sent, 2 * quarter)
    up_here = on_vmem(
        functools.partial(sum_kernel, [[(0, 0), (1, 0)]]), [one_shape], "total", kept, last
    )[0].reshape(pairs, ranks, LANES)
    nearby = [low] + [swap(low, k) for k in range(1, LOW)]
    chosen = pl.pallas_call(
        functools.partial(choose_kernel, per_video),
        in_specs=[SMEM] + [VMEM] * LOW,
        out_specs=[VMEM] * quarter,
        out_shape=[jax.ShapeDtypeStruct((LOW,) + low_shape[1:], jnp.bfloat16)] * quarter,
        cost_estimate=pl.CostEstimate(flops=0, bytes_accessed=8 * low.size, transcendentals=0),
        name="choose",
    )(me, *nearby)
    lows = [chosen[0]] + [swap(chosen[i], LOW * i) for i in range(1, quarter)]

    part_spec = pl.BlockSpec((devs, pl.squeezed, toks, width), lambda p: (0, p, 0, 0))
    later_spec = pl.BlockSpec((devs, pl.squeezed, toks, width), lambda p: (0, pairs + p, 0, 0))
    low_spec = pl.BlockSpec((LOW,) + low_shape[1:], lambda p: (0, 0, 0))
    mixed = pl.pallas_call(
        functools.partial(attend_kernel, math.gcd(devs, max(1, 256 // toks))),
        grid=(pairs,),
        in_specs=[SMEM, pl.BlockSpec((pl.squeezed, ranks, LANES), lambda p: (p, 0, 0))]
        + [later_spec, part_spec, part_spec]
        + [low_spec] * quarter,
        out_specs=part_spec,
        out_shape=jax.ShapeDtypeStruct((devs, pairs, toks, width), jnp.bfloat16),
        scratch_shapes=[
            pltpu.VMEM((devs,) + low_shape[1:], jnp.bfloat16),
            pltpu.VMEM((length, width), jnp.bfloat16),
        ],
        compiler_params=pltpu.CompilerParams(vmem_limit_bytes=48 << 20),
        cost_estimate=pl.CostEstimate(
            flops=4 * pairs * length * length * width,
            bytes_accessed=8 * pairs * length * width,
            transcendentals=pairs * length * length,
        ),
        name="attend",
    )(me, up_here, asked, keys, asked, *lows)
    return exchange(mixed).reshape(videos, heads, toks, width)


def solution(mesh):
    in_specs = (
        P("grp", "seq", None),
        P("grp", None, "seq", None),
        P("grp", None, "seq", None),
        P("grp", None, "seq", None),
        P("seq", None, None),
        P("seq", None, None),
        P(),
        P("grp"),
    )
    out_specs = P("grp", None, "seq", None)
    return jax.shard_map(body, mesh=mesh, in_specs=in_specs, out_specs=out_specs, check_vma=False)
```

```python
import functools
import math

import jax
import jax.numpy as jnp
from jax import lax
from jax.experimental import pallas as pl
from jax.experimental.pallas import tpu as pltpu
from jax.sharding import PartitionSpec as P

LANES = 128
LOW = 4
ANY = pl.BlockSpec(memory_space=pl.ANY)
VMEM = pl.BlockSpec(memory_space=pltpu.VMEM)
SMEM = pl.BlockSpec(memory_space=pltpu.SMEM)


def bit_count(n):
    bits = n.bit_length() - 1
    assert 1 << bits == n
    return bits


def reversed_bits(j, bits):
    out = 0
    for i in range(bits):
        out = out | (((j >> i) & 1) << (bits - 1 - i))
    return out


def pick_kernel(shape, me_ref, row_ref, req_ref, down_ref, up_ref, *refs):
    devs, bits, per_video, pairs, col_split, rows, tiles = shape
    downs, ups = refs[: bits - 1], refs[bits - 1 : 2 * bits - 2]
    down, up, sems = refs[2 * bits - 2 :]
    slots, ranks, _ = down_ref.shape
    videos = down.shape[0]
    me = me_ref[0]
    for s in range(videos):
        place = row_ref[req_ref[s]]
        slot = place % slots
        owned = place // slots == me
        copies = [
            pltpu.make_async_copy(down_ref.at[slot], down.at[s], sems.at[2 * s]),
            pltpu.make_async_copy(up_ref.at[slot], up.at[s], sems.at[2 * s + 1]),
        ]

        @pl.when(owned)
        def _():
            for copy in copies:
                copy.start()
            for copy in copies:
                copy.wait()

        @pl.when(jnp.logical_not(owned))
        def _():
            down[s] = jnp.zeros(down.shape[1:], down.dtype)
            up[s] = jnp.zeros(up.shape[1:], up.dtype)

    for j in range(devs):
        step = min(bits - j.bit_length(), bits - 2)
        at = j - (1 << (j.bit_length() - 1)) if j >= LOW else j
        dev = me ^ reversed_bits(j, bits)
        video = dev // per_video
        place = dev % per_video
        row = pl.multiple_of((place // col_split) * rows, rows)
        for t in range(tiles):
            col = pl.multiple_of(((place % col_split) * tiles + t) * LANES, LANES)
            downs[step][at, t * rows : (t + 1) * rows, :] = down[
                video, pl.ds(row, rows), pl.ds(col, LANES)
            ]
        for p in range(pairs):
            col = pl.multiple_of((place * pairs + p) * LANES, LANES)
            ups[step][at, p * ranks : (p + 1) * ranks, :] = up[video, :, pl.ds(col, LANES)]


def sum_kernel(picks, *refs):
    outs = refs[-len(picks) :]
    for out, terms in zip(outs, picks):
        size = out.shape[0]
        parts = [refs[i][first : first + size] for i, first in terms]
        out[...] = sum(parts[1:], parts[0])


def join_kernel(*refs):
    out, first = refs[-1], 0
    for ref in refs[:-1]:
        out[first : first + ref.shape[0]] = ref[...]
        first += ref.shape[0]


def on_vmem(kernel, shapes, name, *arrays):
    return pl.pallas_call(
        kernel,
        in_specs=[VMEM] * len(arrays),
        out_specs=[VMEM] * len(shapes),
        out_shape=[jax.ShapeDtypeStruct(s, arrays[0].dtype) for s in shapes],
        compiler_params=pltpu.CompilerParams(vmem_limit_bytes=16 << 20),
        cost_estimate=pl.CostEstimate(
            flops=0, bytes_accessed=2 * sum(a.size for a in arrays), transcendentals=0
        ),
        name=name,
    )(*arrays)


def low_rank_kernel(shape, me_ref, x_ref, *refs):
    devs, bits, per_video, _, col_split, rows, tiles = shape
    parts, out_ref, down = refs[:-2], refs[-2], refs[-1]
    blocks = [(ref, i) for ref in parts for i in range(ref.shape[0])]
    for j, (ref, i) in enumerate(blocks):
        dev = me_ref[0] ^ reversed_bits(j, bits)
        video = dev // per_video
        place = dev % per_video
        row = pl.multiple_of((place // col_split) * rows, rows)
        for t in range(tiles):
            col = pl.multiple_of(((place % col_split) * tiles + t) * LANES, LANES)
            down[video, pl.ds(row, rows), pl.ds(col, LANES)] = ref[i, t * rows : (t + 1) * rows, :]
    for s in range(x_ref.shape[0]):
        low = lax.dot_general(
            x_ref[s], down[s], (((1,), (1,)), ((), ())), preferred_element_type=jnp.float32
        ).astype(out_ref.dtype)
        half = low.shape[0] // 2
        out_ref[s] = jnp.concatenate([low[:half], low[half:]], axis=1)


def choose_kernel(per_video, me_ref, *refs):
    ins, outs = refs[:LOW], refs[LOW:]
    for i, out in enumerate(outs):
        video = (me_ref[0] ^ (LOW * i)) // per_video
        for j in range(LOW):
            out[j] = ins[j][video]


def add_delta(base, low, up, second):
    devs, toks, width = base.shape
    ranks = up.shape[0]
    row = lax.broadcasted_iota(jnp.int32, up.shape, 0)
    part = jnp.where(row // (ranks // 2) == second, up, jnp.zeros_like(up))
    none = jnp.zeros_like(part)
    deltas = [
        jnp.dot(low, jnp.concatenate(pair, axis=0), preferred_element_type=jnp.float32)
        for pair in ((part, none), (none, part))
    ]
    delta = jnp.concatenate([d.reshape(devs, toks // 2, width) for d in deltas], axis=1)
    return (base.astype(jnp.float32) + delta).astype(base.dtype).reshape(devs * toks, width)


def attend_kernel(block, me_ref, up_ref, q_ref, k_ref, v_ref, *refs):
    low_refs, out_ref, low_all, q_mix = refs[:-3], refs[-3], refs[-2], refs[-1]
    devs, toks, width = q_ref.shape
    length = devs * toks
    for k in range(devs):
        low_all[me_ref[0] ^ k] = low_refs[k // LOW][k % LOW]
    low = low_all[...].reshape(length // 2, low_all.shape[2])
    up = up_ref[...]
    keys = k_ref[...].reshape(length, width)
    vals = add_delta(v_ref[...], low, up, 1)
    vals = jnp.concatenate([vals, jnp.ones_like(vals)], axis=1)
    q_mix[...] = add_delta(q_ref[...], low, up, 0)
    scale = math.log2(math.e) / math.sqrt(width)

    def score(b):
        q = q_mix[b * toks : (b + block) * toks, :]
        return lax.dot_general(q, keys, (((1,), (1,)), ((), ())), preferred_element_type=jnp.float32)

    coming = score(0)
    for b in range(0, devs, block):
        scores = coming
        if b + block < devs:
            coming = score(b + block)
        top = jnp.max(scores, axis=1, keepdims=True)
        weights = jnp.exp2((scores - top) * scale).astype(jnp.bfloat16)
        mixed = jnp.dot(weights, vals, preferred_element_type=jnp.float32)
        out = mixed[:, :width] / mixed[:, width:]
        out_ref[b : b + block] = out.astype(jnp.bfloat16).reshape(block, toks, width)


def body(
    normed_token_features,
    queries,
    projected_keys,
    values,
    adapter_down_factors,
    adapter_up_factors,
    adapter_store_row,
    requests,
):
    videos, toks, model_width = normed_token_features.shape
    heads = queries.shape[1]
    width = queries.shape[3]
    _, ranks, up_width = adapter_up_factors.shape
    devs = lax.axis_size("seq")
    bits = bit_count(devs)
    me = lax.axis_index("seq").astype(jnp.int32)[None]
    pairs = videos * heads // devs
    per_video = devs // videos
    length = devs * toks
    col_split = math.gcd(per_video, model_width // LANES)
    rows = ranks * col_split // per_video
    tiles = model_width // col_split // LANES
    shape = (devs, bits, per_video, pairs, col_split, rows, tiles)

    def swap(tensor, k):
        return lax.ppermute(tensor, "seq", [(i, i ^ k) for i in range(devs)])

    def exchange(tensor):
        return lax.all_to_all(tensor, "seq", split_axis=0, concat_axis=0, tiled=True)

    def by_pairs(tensor):
        return tensor.reshape(devs, pairs, toks, width)

    def after(array, *others):
        return lax.optimization_barrier((array, others))[0]

    quarter = devs // LOW
    others = (2 * quarter, quarter, 3 * quarter)

    def halving(parts, received, i):
        size = parts[i].shape[0]
        terms = [(0, 0)] + [(1 + n, size) for n in range(len(received))]
        return on_vmem(
            functools.partial(sum_kernel, [terms]), [parts[i].shape], "halve", parts[i], *received
        )[0]

    def splitting(parts, received):
        size = (1,) + parts[-1].shape[1:]
        picks = [[(n, j) for n in range(1 + len(received))] for j in range(LOW)]
        return on_vmem(
            functools.partial(sum_kernel, picks), [size] * LOW, "split", parts[-1], *received
        )

    def to_others(shards):
        return [swap(shard, k) for shard, k in zip(shards[1:], others)]

    def total(shard, received):
        picks = [[(n, 0) for n in range(LOW)]]
        return on_vmem(
            functools.partial(sum_kernel, picks), [shard.shape], "total", shard, *received
        )[0]

    def join(arrays):
        count = sum(a.shape[0] for a in arrays)
        return on_vmem(join_kernel, [(count,) + arrays[0].shape[1:]], "join", *arrays)[0]

    keys = exchange(by_pairs(projected_keys))

    steps = [devs >> (i + 1) for i in range(bits - 2)] + [LOW]
    piece_shapes = [(h, tiles * rows, LANES) for h in steps] + [
        (h, pairs * ranks, LANES) for h in steps
    ]
    pieces = pl.pallas_call(
        functools.partial(pick_kernel, shape),
        in_specs=[SMEM, SMEM, SMEM, ANY, ANY],
        out_specs=[VMEM] * (2 * bits - 2),
        out_shape=[jax.ShapeDtypeStruct(s, jnp.bfloat16) for s in piece_shapes],
        scratch_shapes=[
            pltpu.VMEM((videos, ranks, model_width), jnp.bfloat16),
            pltpu.VMEM((videos, ranks, up_width), jnp.bfloat16),
            pltpu.SemaphoreType.DMA((2 * videos,)),
        ],
        compiler_params=pltpu.CompilerParams(vmem_limit_bytes=24 << 20),
        cost_estimate=pl.CostEstimate(
            flops=0,
            bytes_accessed=4 * videos * ranks * (model_width + up_width),
            transcendentals=0,
        ),
        name="pick_factors",
    )(me, adapter_store_row, requests, adapter_down_factors, adapter_up_factors)
    down_pieces, up_pieces = pieces[: bits - 1], pieces[bits - 1 :]

    down_got, up_got = [], []

    def send_up(i, *others):
        up_got.append(swap(after(halving(up_pieces, up_got, i), *others), 1 << i))

    for i in range(bits - 2):
        piece = down_pieces[0] if i == 0 else halving(down_pieces, down_got, i)
        if i > 0:
            part = up_pieces[0] if i == 1 else halving(up_pieces, up_got, i - 1)
            up_got.append(swap(after(part, piece), 1 << (i - 1)))
        down_got.append(swap(piece, 1 << i))
    part = after(halving(up_pieces, up_got, bits - 3), piece)
    up_got.append(swap(part, 1 << (bits - 3)))
    held = splitting((after(down_pieces[-1], *up_got[:-1]),), down_got)
    shard = after(total(held[0], to_others(held)), keys, up_got[-1])
    gathered = [shard] + [swap(shard, k) for k in others]

    joined = join(gathered)
    asked = jnp.concatenate([by_pairs(values), by_pairs(queries)], axis=1)
    asked = exchange(after(asked, joined))
    for i in reversed(range(bits - 2)):
        gathered = [joined, swap(joined, 1 << i)]
        if i > 0:
            joined = join(gathered)

    low_shape = (videos, toks // 2, 2 * ranks)
    low = pl.pallas_call(
        functools.partial(low_rank_kernel, shape),
        in_specs=[SMEM, VMEM] + [VMEM] * len(gathered),
        out_specs=VMEM,
        scratch_shapes=[pltpu.VMEM((videos, ranks, model_width), jnp.bfloat16)],
        out_shape=jax.ShapeDtypeStruct(low_shape, jnp.bfloat16),
        compiler_params=pltpu.CompilerParams(vmem_limit_bytes=24 << 20),
        cost_estimate=pl.CostEstimate(
            flops=2 * videos * toks * ranks * model_width,
            bytes_accessed=2 * videos * (toks + ranks) * model_width,
            transcendentals=0,
        ),
        name="low_rank",
    )(me, normed_token_features, *gathered)
    nearby = [low] + [swap(low, k) for k in range(1, LOW)]
    chosen = pl.pallas_call(
        functools.partial(choose_kernel, per_video),
        in_specs=[SMEM] + [VMEM] * LOW,
        out_specs=[VMEM] * quarter,
        out_shape=[jax.ShapeDtypeStruct((LOW,) + low_shape[1:], jnp.bfloat16)] * quarter,
        cost_estimate=pl.CostEstimate(flops=0, bytes_accessed=8 * low.size, transcendentals=0),
        name="choose",
    )(me, *nearby)
    up_part = after(up_pieces[-1], chosen[0])
    near_pair, far_pair = on_vmem(
        functools.partial(sum_kernel, [[(n, 2 * h) for n in range(1 + len(up_got))] for h in (0, 1)]),
        [(2,) + up_part.shape[1:]] * 2,
        "split",
        up_part,
        *up_got,
    )
    came = swap(far_pair, quarter)
    one_shape = (1,) + up_part.shape[1:]
    kept, sent = on_vmem(
        functools.partial(sum_kernel, [[(n, h) for n in range(2)] for h in (0, 1)]),
        [one_shape] * 2,
        "split",
        near_pair,
        came,
    )
    last = swap(sent, 2 * quarter)
    up_here = on_vmem(
        functools.partial(sum_kernel, [[(0, 0), (1, 0)]]), [one_shape], "total", kept, last
    )[0].reshape(pairs, ranks, LANES)
    lows = [chosen[0]] + [swap(chosen[i], LOW * i) for i in range(1, quarter)]

    part_spec = pl.BlockSpec((devs, pl.squeezed, toks, width), lambda p: (0, p, 0, 0))
    later_spec = pl.BlockSpec((devs, pl.squeezed, toks, width), lambda p: (0, pairs + p, 0, 0))
    low_spec = pl.BlockSpec((LOW,) + low_shape[1:], lambda p: (0, 0, 0))
    mixed = pl.pallas_call(
        functools.partial(attend_kernel, math.gcd(devs, max(1, 256 // toks))),
        grid=(pairs,),
        in_specs=[SMEM, pl.BlockSpec((pl.squeezed, ranks, LANES), lambda p: (p, 0, 0))]
        + [later_spec, part_spec, part_spec]
        + [low_spec] * quarter,
        out_specs=part_spec,
        out_shape=jax.ShapeDtypeStruct((devs, pairs, toks, width), jnp.bfloat16),
        scratch_shapes=[
            pltpu.VMEM((devs,) + low_shape[1:], jnp.bfloat16),
            pltpu.VMEM((length, width), jnp.bfloat16),
        ],
        compiler_params=pltpu.CompilerParams(vmem_limit_bytes=48 << 20),
        cost_estimate=pl.CostEstimate(
            flops=4 * pairs * length * length * width,
            bytes_accessed=8 * pairs * length * width,
            transcendentals=pairs * length * length,
        ),
        name="attend",
    )(me, up_here, asked, keys, asked, *lows)
    return exchange(mixed).reshape(videos, heads, toks, width)


def solution(mesh):
    in_specs = (
        P("grp", "seq", None),
        P("grp", None, "seq", None),
        P("grp", None, "seq", None),
        P("grp", None, "seq", None),
        P("seq", None, None),
        P("seq", None, None),
        P(),
        P("grp"),
    )
    out_specs = P("grp", None, "seq", None)
    return jax.shard_map(body, mesh=mesh, in_specs=in_specs, out_specs=out_specs, check_vma=False)
```

```python
import functools
import math

import jax
import jax.numpy as jnp
from jax import lax
from jax.experimental import pallas as pl
from jax.experimental.pallas import tpu as pltpu
from jax.sharding import PartitionSpec as P

LANES = 128
LOW = 4
ANY = pl.BlockSpec(memory_space=pl.ANY)
VMEM = pl.BlockSpec(memory_space=pltpu.VMEM)
SMEM = pl.BlockSpec(memory_space=pltpu.SMEM)


def bit_count(n):
    bits = n.bit_length() - 1
    assert 1 << bits == n
    return bits


def reversed_bits(j, bits):
    out = 0
    for i in range(bits):
        out = out | (((j >> i) & 1) << (bits - 1 - i))
    return out


def pick_kernel(shape, me_ref, row_ref, req_ref, down_ref, up_ref, *refs):
    devs, bits, per_video, pairs, col_split, rows, tiles = shape
    downs, ups = refs[: bits - 1], refs[bits - 1 : 2 * bits - 2]
    down, up, sems = refs[2 * bits - 2 :]
    slots, ranks, _ = down_ref.shape
    videos = down.shape[0]
    me = me_ref[0]
    for s in range(videos):
        place = row_ref[req_ref[s]]
        slot = place % slots
        owned = place // slots == me
        copies = [
            pltpu.make_async_copy(down_ref.at[slot], down.at[s], sems.at[2 * s]),
            pltpu.make_async_copy(up_ref.at[slot], up.at[s], sems.at[2 * s + 1]),
        ]

        @pl.when(owned)
        def _():
            for copy in copies:
                copy.start()
            for copy in copies:
                copy.wait()

        @pl.when(jnp.logical_not(owned))
        def _():
            down[s] = jnp.zeros(down.shape[1:], down.dtype)
            up[s] = jnp.zeros(up.shape[1:], up.dtype)

    for j in range(devs):
        step = min(bits - j.bit_length(), bits - 2)
        at = j - (1 << (j.bit_length() - 1)) if j >= LOW else j
        dev = me ^ reversed_bits(j, bits)
        video = dev // per_video
        place = dev % per_video
        row = pl.multiple_of((place // col_split) * rows, rows)
        for t in range(tiles):
            col = pl.multiple_of(((place % col_split) * tiles + t) * LANES, LANES)
            downs[step][at, t * rows : (t + 1) * rows, :] = down[
                video, pl.ds(row, rows), pl.ds(col, LANES)
            ]
        for p in range(pairs):
            col = pl.multiple_of((place * pairs + p) * LANES, LANES)
            ups[step][at, p * ranks : (p + 1) * ranks, :] = up[video, :, pl.ds(col, LANES)]


def sum_kernel(picks, *refs):
    outs = refs[-len(picks) :]
    for out, terms in zip(outs, picks):
        size = out.shape[0]
        parts = [refs[i][first : first + size] for i, first in terms]
        out[...] = sum(parts[1:], parts[0])


def join_kernel(*refs):
    out, first = refs[-1], 0
    for ref in refs[:-1]:
        out[first : first + ref.shape[0]] = ref[...]
        first += ref.shape[0]


def on_vmem(kernel, shapes, name, *arrays):
    return pl.pallas_call(
        kernel,
        in_specs=[VMEM] * len(arrays),
        out_specs=[VMEM] * len(shapes),
        out_shape=[jax.ShapeDtypeStruct(s, arrays[0].dtype) for s in shapes],
        compiler_params=pltpu.CompilerParams(vmem_limit_bytes=16 << 20),
        cost_estimate=pl.CostEstimate(
            flops=0, bytes_accessed=2 * sum(a.size for a in arrays), transcendentals=0
        ),
        name=name,
    )(*arrays)


def low_rank_kernel(shape, me_ref, x_ref, *refs):
    devs, bits, per_video, _, col_split, rows, tiles = shape
    parts, out_ref, down = refs[:-2], refs[-2], refs[-1]
    blocks = [(ref, i) for ref in parts for i in range(ref.shape[0])]
    for j, (ref, i) in enumerate(blocks):
        dev = me_ref[0] ^ reversed_bits(j, bits)
        video = dev // per_video
        place = dev % per_video
        row = pl.multiple_of((place // col_split) * rows, rows)
        for t in range(tiles):
            col = pl.multiple_of(((place % col_split) * tiles + t) * LANES, LANES)
            down[video, pl.ds(row, rows), pl.ds(col, LANES)] = ref[i, t * rows : (t + 1) * rows, :]
    for s in range(x_ref.shape[0]):
        low = lax.dot_general(
            x_ref[s], down[s], (((1,), (1,)), ((), ())), preferred_element_type=jnp.float32
        ).astype(out_ref.dtype)
        half = low.shape[0] // 2
        out_ref[s] = jnp.concatenate([low[:half], low[half:]], axis=1)


def choose_kernel(per_video, me_ref, *refs):
    ins, outs = refs[:LOW], refs[LOW:]
    for i, out in enumerate(outs):
        video = (me_ref[0] ^ (LOW * i)) // per_video
        for j in range(LOW):
            out[j] = ins[j][video]


def add_delta(base, low, up, second):
    devs, toks, width = base.shape
    ranks = up.shape[0]
    row = lax.broadcasted_iota(jnp.int32, up.shape, 0)
    part = jnp.where(row // (ranks // 2) == second, up, jnp.zeros_like(up))
    none = jnp.zeros_like(part)
    deltas = [
        jnp.dot(low, jnp.concatenate(pair, axis=0), preferred_element_type=jnp.float32)
        for pair in ((part, none), (none, part))
    ]
    delta = jnp.concatenate([d.reshape(devs, toks // 2, width) for d in deltas], axis=1)
    return (base.astype(jnp.float32) + delta).astype(base.dtype).reshape(devs * toks, width)


def attend_kernel(block, me_ref, up_ref, q_ref, k_ref, v_ref, *refs):
    low_refs, out_ref, low_all, q_mix = refs[:-3], refs[-3], refs[-2], refs[-1]
    devs, toks, width = q_ref.shape
    length = devs * toks
    for k in range(devs):
        low_all[me_ref[0] ^ k] = low_refs[k // LOW][k % LOW]
    low = low_all[...].reshape(length // 2, low_all.shape[2])
    up = up_ref[...]
    keys = k_ref[...].reshape(length, width)
    vals = add_delta(v_ref[...], low, up, 1)
    vals = jnp.concatenate([vals, jnp.ones_like(vals)], axis=1)
    q_mix[...] = add_delta(q_ref[...], low, up, 0)
    scale = 1 / math.sqrt(width)

    def score(b):
        q = q_mix[b * toks : (b + block) * toks, :]
        return lax.dot_general(q, keys, (((1,), (1,)), ((), ())), preferred_element_type=jnp.float32)

    coming = score(0)
    for b in range(0, devs, block):
        scores = coming
        if b + block < devs:
            coming = score(b + block)
        top = jnp.max(scores, axis=1, keepdims=True)
        weights = jnp.exp((scores - top) * scale).astype(jnp.bfloat16)
        mixed = jnp.dot(weights, vals, preferred_element_type=jnp.float32)
        out = mixed[:, :width] / mixed[:, width:]
        out_ref[b : b + block] = out.astype(jnp.bfloat16).reshape(block, toks, width)


def body(
    normed_token_features,
    queries,
    projected_keys,
    values,
    adapter_down_factors,
    adapter_up_factors,
    adapter_store_row,
    requests,
):
    videos, toks, model_width = normed_token_features.shape
    heads = queries.shape[1]
    width = queries.shape[3]
    _, ranks, up_width = adapter_up_factors.shape
    devs = lax.axis_size("seq")
    bits = bit_count(devs)
    me = lax.axis_index("seq").astype(jnp.int32)[None]
    pairs = videos * heads // devs
    per_video = devs // videos
    length = devs * toks
    col_split = math.gcd(per_video, model_width // LANES)
    rows = ranks * col_split // per_video
    tiles = model_width // col_split // LANES
    shape = (devs, bits, per_video, pairs, col_split, rows, tiles)

    def swap(tensor, k):
        return lax.ppermute(tensor, "seq", [(i, i ^ k) for i in range(devs)])

    def exchange(tensor):
        return lax.all_to_all(tensor, "seq", split_axis=0, concat_axis=0, tiled=True)

    def by_pairs(tensor):
        return tensor.reshape(devs, pairs, toks, width)

    def after(array, *others):
        return lax.optimization_barrier((array, others))[0]

    quarter = devs // LOW
    others = (2 * quarter, quarter, 3 * quarter)

    def halving(parts, received, i):
        size = parts[i].shape[0]
        terms = [(0, 0)] + [(1 + n, size) for n in range(len(received))]
        return on_vmem(
            functools.partial(sum_kernel, [terms]), [parts[i].shape], "halve", parts[i], *received
        )[0]

    def splitting(parts, received):
        size = (1,) + parts[-1].shape[1:]
        picks = [[(n, j) for n in range(1 + len(received))] for j in range(LOW)]
        return on_vmem(
            functools.partial(sum_kernel, picks), [size] * LOW, "split", parts[-1], *received
        )

    def to_others(shards):
        return [swap(shard, k) for shard, k in zip(shards[1:], others)]

    def total(shard, received):
        picks = [[(n, 0) for n in range(LOW)]]
        return on_vmem(
            functools.partial(sum_kernel, picks), [shard.shape], "total", shard, *received
        )[0]

    def join(arrays):
        count = sum(a.shape[0] for a in arrays)
        return on_vmem(join_kernel, [(count,) + arrays[0].shape[1:]], "join", *arrays)[0]

    keys = exchange(by_pairs(projected_keys))

    steps = [devs >> (i + 1) for i in range(bits - 2)] + [LOW]
    piece_shapes = [(h, tiles * rows, LANES) for h in steps] + [
        (h, pairs * ranks, LANES) for h in steps
    ]
    pieces = pl.pallas_call(
        functools.partial(pick_kernel, shape),
        in_specs=[SMEM, SMEM, SMEM, ANY, ANY],
        out_specs=[VMEM] * (2 * bits - 2),
        out_shape=[jax.ShapeDtypeStruct(s, jnp.bfloat16) for s in piece_shapes],
        scratch_shapes=[
            pltpu.VMEM((videos, ranks, model_width), jnp.bfloat16),
            pltpu.VMEM((videos, ranks, up_width), jnp.bfloat16),
            pltpu.SemaphoreType.DMA((2 * videos,)),
        ],
        compiler_params=pltpu.CompilerParams(vmem_limit_bytes=24 << 20),
        cost_estimate=pl.CostEstimate(
            flops=0,
            bytes_accessed=4 * videos * ranks * (model_width + up_width),
            transcendentals=0,
        ),
        name="pick_factors",
    )(me, adapter_store_row, requests, adapter_down_factors, adapter_up_factors)
    down_pieces, up_pieces = pieces[: bits - 1], pieces[bits - 1 :]

    down_got, up_got = [], []

    def send_up(i, *others):
        up_got.append(swap(after(halving(up_pieces, up_got, i), *others), 1 << i))

    for i in range(bits - 2):
        piece = down_pieces[0] if i == 0 else halving(down_pieces, down_got, i)
        if i > 0:
            part = up_pieces[0] if i == 1 else halving(up_pieces, up_got, i - 1)
            up_got.append(swap(after(part, piece), 1 << (i - 1)))
        down_got.append(swap(piece, 1 << i))
    part = after(halving(up_pieces, up_got, bits - 3), piece)
    up_got.append(swap(part, 1 << (bits - 3)))
    held = splitting((after(down_pieces[-1], *up_got[:-1]),), down_got)
    shard = after(total(held[0], to_others(held)), keys, up_got[-1])
    gathered = [shard] + [swap(shard, k) for k in others]

    up_part = after(up_pieces[-1], shard)
    near_pair, far_pair = on_vmem(
        functools.partial(sum_kernel, [[(n, 2 * h) for n in range(1 + len(up_got))] for h in (0, 1)]),
        [(2,) + up_part.shape[1:]] * 2,
        "split",
        up_part,
        *up_got,
    )
    came = swap(far_pair, quarter)
    asked = jnp.concatenate([by_pairs(values), by_pairs(queries)], axis=1)
    joined = join(gathered)
    asked = exchange(after(asked, came, joined))
    one_shape = (1,) + up_part.shape[1:]
    kept, sent = on_vmem(
        functools.partial(sum_kernel, [[(n, h) for n in range(2)] for h in (0, 1)]),
        [one_shape] * 2,
        "split",
        near_pair,
        came,
    )
    last = swap(sent, 2 * quarter)
    up_here = on_vmem(
        functools.partial(sum_kernel, [[(0, 0), (1, 0)]]), [one_shape], "total", kept, last
    )[0].reshape(pairs, ranks, LANES)
    for i in reversed(range(bits - 2)):
        gathered = [joined, swap(joined, 1 << i)]
        if i > 0:
            joined = join(gathered)

    low_shape = (videos, toks // 2, 2 * ranks)
    low = pl.pallas_call(
        functools.partial(low_rank_kernel, shape),
        in_specs=[SMEM, VMEM] + [VMEM] * len(gathered),
        out_specs=VMEM,
        scratch_shapes=[pltpu.VMEM((videos, ranks, model_width), jnp.bfloat16)],
        out_shape=jax.ShapeDtypeStruct(low_shape, jnp.bfloat16),
        compiler_params=pltpu.CompilerParams(vmem_limit_bytes=24 << 20),
        cost_estimate=pl.CostEstimate(
            flops=2 * videos * toks * ranks * model_width,
            bytes_accessed=2 * videos * (toks + ranks) * model_width,
            transcendentals=0,
        ),
        name="low_rank",
    )(me, normed_token_features, *gathered)
    nearby = [low] + [swap(low, k) for k in range(1, LOW)]
    chosen = pl.pallas_call(
        functools.partial(choose_kernel, per_video),
        in_specs=[SMEM] + [VMEM] * LOW,
        out_specs=[VMEM] * quarter,
        out_shape=[jax.ShapeDtypeStruct((LOW,) + low_shape[1:], jnp.bfloat16)] * quarter,
        cost_estimate=pl.CostEstimate(flops=0, bytes_accessed=8 * low.size, transcendentals=0),
        name="choose",
    )(me, *nearby)
    lows = [chosen[0]] + [swap(chosen[i], LOW * i) for i in range(1, quarter)]

    part_spec = pl.BlockSpec((devs, pl.squeezed, toks, width), lambda p: (0, p, 0, 0))
    later_spec = pl.BlockSpec((devs, pl.squeezed, toks, width), lambda p: (0, pairs + p, 0, 0))
    low_spec = pl.BlockSpec((LOW,) + low_shape[1:], lambda p: (0, 0, 0))
    mixed = pl.pallas_call(
        functools.partial(attend_kernel, math.gcd(devs, max(1, 256 // toks))),
        grid=(pairs,),
        in_specs=[SMEM, pl.BlockSpec((pl.squeezed, ranks, LANES), lambda p: (p, 0, 0))]
        + [later_spec, part_spec, part_spec]
        + [low_spec] * quarter,
        out_specs=part_spec,
        out_shape=jax.ShapeDtypeStruct((devs, pairs, toks, width), jnp.bfloat16),
        scratch_shapes=[
            pltpu.VMEM((devs,) + low_shape[1:], jnp.bfloat16),
            pltpu.VMEM((length, width), jnp.bfloat16),
        ],
        compiler_params=pltpu.CompilerParams(vmem_limit_bytes=48 << 20),
        cost_estimate=pl.CostEstimate(
            flops=4 * pairs * length * length * width,
            bytes_accessed=8 * pairs * length * width,
            transcendentals=pairs * length * length,
        ),
        name="attend",
    )(me, up_here, asked, keys, asked, *lows)
    return exchange(mixed).reshape(videos, heads, toks, width)


def solution(mesh):
    in_specs = (
        P("grp", "seq", None),
        P("grp", None, "seq", None),
        P("grp", None, "seq", None),
        P("grp", None, "seq", None),
        P("seq", None, None),
        P("seq", None, None),
        P(),
        P("grp"),
    )
    out_specs = P("grp", None, "seq", None)
    return jax.shard_map(body, mesh=mesh, in_specs=in_specs, out_specs=out_specs, check_vma=False)
```

```python
import functools
import math

import jax
import jax.numpy as jnp
from jax import lax
from jax.experimental import pallas as pl
from jax.experimental.pallas import tpu as pltpu
from jax.sharding import PartitionSpec as P

LANES = 128
LOW = 4
ANY = pl.BlockSpec(memory_space=pl.ANY)
VMEM = pl.BlockSpec(memory_space=pltpu.VMEM)
SMEM = pl.BlockSpec(memory_space=pltpu.SMEM)


def bit_count(n):
    bits = n.bit_length() - 1
    assert 1 << bits == n
    return bits


def reversed_bits(j, bits):
    out = 0
    for i in range(bits):
        out = out | (((j >> i) & 1) << (bits - 1 - i))
    return out


def pick_kernel(shape, me_ref, row_ref, req_ref, down_ref, up_ref, *refs):
    devs, bits, per_video, pairs, col_split, rows, tiles = shape
    downs, ups = refs[: bits - 1], refs[bits - 1 : 2 * bits - 2]
    down, up, sems = refs[2 * bits - 2 :]
    slots, ranks, _ = down_ref.shape
    videos = down.shape[0]
    me = me_ref[0]
    for s in range(videos):
        place = row_ref[req_ref[s]]
        slot = place % slots
        owned = place // slots == me
        copies = [
            pltpu.make_async_copy(down_ref.at[slot], down.at[s], sems.at[2 * s]),
            pltpu.make_async_copy(up_ref.at[slot], up.at[s], sems.at[2 * s + 1]),
        ]

        @pl.when(owned)
        def _():
            for copy in copies:
                copy.start()
            for copy in copies:
                copy.wait()

        @pl.when(jnp.logical_not(owned))
        def _():
            down[s] = jnp.zeros(down.shape[1:], down.dtype)
            up[s] = jnp.zeros(up.shape[1:], up.dtype)

    for j in range(devs):
        step = min(bits - j.bit_length(), bits - 2)
        at = j - (1 << (j.bit_length() - 1)) if j >= LOW else j
        dev = me ^ reversed_bits(j, bits)
        video = dev // per_video
        place = dev % per_video
        row = pl.multiple_of((place // col_split) * rows, rows)
        for t in range(tiles):
            col = pl.multiple_of(((place % col_split) * tiles + t) * LANES, LANES)
            downs[step][at, t * rows : (t + 1) * rows, :] = down[
                video, pl.ds(row, rows), pl.ds(col, LANES)
            ]
        for p in range(pairs):
            col = pl.multiple_of((place * pairs + p) * LANES, LANES)
            ups[step][at, p * ranks : (p + 1) * ranks, :] = up[video, :, pl.ds(col, LANES)]


def sum_kernel(picks, *refs):
    outs = refs[-len(picks) :]
    for out, terms in zip(outs, picks):
        size = out.shape[0]
        parts = [refs[i][first : first + size] for i, first in terms]
        out[...] = sum(parts[1:], parts[0])


def join_kernel(*refs):
    out, first = refs[-1], 0
    for ref in refs[:-1]:
        out[first : first + ref.shape[0]] = ref[...]
        first += ref.shape[0]


def on_vmem(kernel, shapes, name, *arrays):
    return pl.pallas_call(
        kernel,
        in_specs=[VMEM] * len(arrays),
        out_specs=[VMEM] * len(shapes),
        out_shape=[jax.ShapeDtypeStruct(s, arrays[0].dtype) for s in shapes],
        compiler_params=pltpu.CompilerParams(vmem_limit_bytes=16 << 20),
        cost_estimate=pl.CostEstimate(
            flops=0, bytes_accessed=2 * sum(a.size for a in arrays), transcendentals=0
        ),
        name=name,
    )(*arrays)


def low_rank_kernel(shape, me_ref, x_ref, *refs):
    devs, bits, per_video, _, col_split, rows, tiles = shape
    parts, out_ref, down = refs[:-2], refs[-2], refs[-1]
    blocks = [(ref, i) for ref in parts for i in range(ref.shape[0])]
    for j, (ref, i) in enumerate(blocks):
        dev = me_ref[0] ^ reversed_bits(j, bits)
        video = dev // per_video
        place = dev % per_video
        row = pl.multiple_of((place // col_split) * rows, rows)
        for t in range(tiles):
            col = pl.multiple_of(((place % col_split) * tiles + t) * LANES, LANES)
            down[video, pl.ds(row, rows), pl.ds(col, LANES)] = ref[i, t * rows : (t + 1) * rows, :]
    for s in range(x_ref.shape[0]):
        low = lax.dot_general(
            x_ref[s], down[s], (((1,), (1,)), ((), ())), preferred_element_type=jnp.float32
        ).astype(out_ref.dtype)
        half = low.shape[0] // 2
        out_ref[s] = jnp.concatenate([low[:half], low[half:]], axis=1)


def choose_kernel(per_video, me_ref, *refs):
    ins, outs = refs[:LOW], refs[LOW:]
    for i, out in enumerate(outs):
        video = (me_ref[0] ^ (LOW * i)) // per_video
        for j in range(LOW):
            out[j] = ins[j][video]


def add_delta(base, low, up, second):
    devs, toks, width = base.shape
    ranks = up.shape[0]
    row = lax.broadcasted_iota(jnp.int32, up.shape, 0)
    part = jnp.where(row // (ranks // 2) == second, up, jnp.zeros_like(up))
    none = jnp.zeros_like(part)
    deltas = [
        jnp.dot(low, jnp.concatenate(pair, axis=0), preferred_element_type=jnp.float32)
        for pair in ((part, none), (none, part))
    ]
    delta = jnp.concatenate([d.reshape(devs, toks // 2, width) for d in deltas], axis=1)
    return (base.astype(jnp.float32) + delta).astype(base.dtype).reshape(devs * toks, width)


def attend_kernel(block, me_ref, up_ref, q_ref, k_ref, v_ref, *refs):
    low_refs, out_ref, low_all, q_mix = refs[:-3], refs[-3], refs[-2], refs[-1]
    devs, toks, width = q_ref.shape
    length = devs * toks
    for k in range(devs):
        low_all[me_ref[0] ^ k] = low_refs[k // LOW][k % LOW]
    low = low_all[...].reshape(length // 2, low_all.shape[2])
    up = up_ref[...]
    keys = k_ref[...].reshape(length, width)
    vals = add_delta(v_ref[...], low, up, 1)
    vals = jnp.concatenate([vals, jnp.ones_like(vals)], axis=1)
    q_mix[...] = add_delta(q_ref[...], low, up, 0)
    scale = math.log2(math.e) / math.sqrt(width)

    def score(b):
        q = q_mix[b * toks : (b + block) * toks, :]
        return lax.dot_general(q, keys, (((1,), (1,)), ((), ())), preferred_element_type=jnp.float32)

    coming = score(0)
    for b in range(0, devs, block):
        scores = coming
        if b + block < devs:
            coming = score(b + block)
        top = jnp.max(scores, axis=1, keepdims=True)
        weights = jnp.exp2((scores - top) * scale).astype(jnp.bfloat16)
        mixed = jnp.dot(weights, vals, preferred_element_type=jnp.float32)
        out = mixed[:, :width] / mixed[:, width:]
        out_ref[b : b + block] = out.astype(jnp.bfloat16).reshape(block, toks, width)


def body(
    normed_token_features,
    queries,
    projected_keys,
    values,
    adapter_down_factors,
    adapter_up_factors,
    adapter_store_row,
    requests,
):
    videos, toks, model_width = normed_token_features.shape
    heads = queries.shape[1]
    width = queries.shape[3]
    _, ranks, up_width = adapter_up_factors.shape
    devs = lax.axis_size("seq")
    bits = bit_count(devs)
    me = lax.axis_index("seq").astype(jnp.int32)[None]
    pairs = videos * heads // devs
    per_video = devs // videos
    length = devs * toks
    col_split = math.gcd(per_video, model_width // LANES)
    rows = ranks * col_split // per_video
    tiles = model_width // col_split // LANES
    shape = (devs, bits, per_video, pairs, col_split, rows, tiles)

    def swap(tensor, k):
        return lax.ppermute(tensor, "seq", [(i, i ^ k) for i in range(devs)])

    def exchange(tensor):
        return lax.all_to_all(tensor, "seq", split_axis=0, concat_axis=0, tiled=True)

    def by_pairs(tensor):
        return tensor.reshape(devs, pairs, toks, width)

    def after(array, *others):
        return lax.optimization_barrier((array, others))[0]

    quarter = devs // LOW
    others = (2 * quarter, quarter, 3 * quarter)

    def halving(parts, received, i):
        size = parts[i].shape[0]
        terms = [(0, 0)] + [(1 + n, size) for n in range(len(received))]
        return on_vmem(
            functools.partial(sum_kernel, [terms]), [parts[i].shape], "halve", parts[i], *received
        )[0]

    def splitting(parts, received):
        size = (1,) + parts[-1].shape[1:]
        picks = [[(n, j) for n in range(1 + len(received))] for j in range(LOW)]
        return on_vmem(
            functools.partial(sum_kernel, picks), [size] * LOW, "split", parts[-1], *received
        )

    def to_others(shards):
        return [swap(shard, k) for shard, k in zip(shards[1:], others)]

    def total(shard, received):
        picks = [[(n, 0) for n in range(LOW)]]
        return on_vmem(
            functools.partial(sum_kernel, picks), [shard.shape], "total", shard, *received
        )[0]

    def join(arrays):
        count = sum(a.shape[0] for a in arrays)
        return on_vmem(join_kernel, [(count,) + arrays[0].shape[1:]], "join", *arrays)[0]

    keys = exchange(by_pairs(projected_keys))

    steps = [devs >> (i + 1) for i in range(bits - 2)] + [LOW]
    piece_shapes = [(h, tiles * rows, LANES) for h in steps] + [
        (h, pairs * ranks, LANES) for h in steps
    ]
    pieces = pl.pallas_call(
        functools.partial(pick_kernel, shape),
        in_specs=[SMEM, SMEM, SMEM, ANY, ANY],
        out_specs=[VMEM] * (2 * bits - 2),
        out_shape=[jax.ShapeDtypeStruct(s, jnp.bfloat16) for s in piece_shapes],
        scratch_shapes=[
            pltpu.VMEM((videos, ranks, model_width), jnp.bfloat16),
            pltpu.VMEM((videos, ranks, up_width), jnp.bfloat16),
            pltpu.SemaphoreType.DMA((2 * videos,)),
        ],
        compiler_params=pltpu.CompilerParams(vmem_limit_bytes=24 << 20),
        cost_estimate=pl.CostEstimate(
            flops=0,
            bytes_accessed=4 * videos * ranks * (model_width + up_width),
            transcendentals=0,
        ),
        name="pick_factors",
    )(me, adapter_store_row, requests, adapter_down_factors, adapter_up_factors)
    down_pieces, up_pieces = pieces[: bits - 1], pieces[bits - 1 :]

    down_got, up_got = [], []

    def send_up(i, *others):
        up_got.append(swap(after(halving(up_pieces, up_got, i), *others), 1 << i))

    for i in range(bits - 2):
        piece = down_pieces[0] if i == 0 else halving(down_pieces, down_got, i)
        if i > 0:
            part = up_pieces[0] if i == 1 else halving(up_pieces, up_got, i - 1)
            up_got.append(swap(after(part, piece), 1 << (i - 1)))
        down_got.append(swap(piece, 1 << i))
    part = after(halving(up_pieces, up_got, bits - 3), piece)
    up_got.append(swap(part, 1 << (bits - 3)))
    held = splitting((after(down_pieces[-1], *up_got[:-1]),), down_got)
    shard = after(total(held[0], to_others(held)), keys, up_got[-1])
    gathered = [shard] + [swap(shard, k) for k in others]

    up_part = after(up_pieces[-1], shard)
    near_pair, far_pair = on_vmem(
        functools.partial(sum_kernel, [[(n, 2 * h) for n in range(1 + len(up_got))] for h in (0, 1)]),
        [(2,) + up_part.shape[1:]] * 2,
        "split",
        up_part,
        *up_got,
    )
    came = swap(far_pair, quarter)
    asked = jnp.concatenate([by_pairs(values), by_pairs(queries)], axis=1)
    joined = join(gathered)
    asked = exchange(after(asked, came, joined))
    one_shape = (1,) + up_part.shape[1:]
    kept, sent = on_vmem(
        functools.partial(sum_kernel, [[(n, h) for n in range(2)] for h in (0, 1)]),
        [one_shape] * 2,
        "split",
        near_pair,
        came,
    )
    last = swap(sent, 2 * quarter)
    up_here = on_vmem(
        functools.partial(sum_kernel, [[(0, 0), (1, 0)]]), [one_shape], "total", kept, last
    )[0].reshape(pairs, ranks, LANES)
    for i in reversed(range(bits - 2)):
        gathered = [joined, swap(joined, 1 << i)]
        if i > 0:
            joined = join(gathered)

    low_shape = (videos, toks // 2, 2 * ranks)
    low = pl.pallas_call(
        functools.partial(low_rank_kernel, shape),
        in_specs=[SMEM, VMEM] + [VMEM] * len(gathered),
        out_specs=VMEM,
        scratch_shapes=[pltpu.VMEM((videos, ranks, model_width), jnp.bfloat16)],
        out_shape=jax.ShapeDtypeStruct(low_shape, jnp.bfloat16),
        compiler_params=pltpu.CompilerParams(vmem_limit_bytes=24 << 20),
        cost_estimate=pl.CostEstimate(
            flops=2 * videos * toks * ranks * model_width,
            bytes_accessed=2 * videos * (toks + ranks) * model_width,
            transcendentals=0,
        ),
        name="low_rank",
    )(me, normed_token_features, *gathered)
    nearby = [low] + [swap(low, k) for k in range(1, LOW)]
    chosen = pl.pallas_call(
        functools.partial(choose_kernel, per_video),
        in_specs=[SMEM] + [VMEM] * LOW,
        out_specs=[VMEM] * quarter,
        out_shape=[jax.ShapeDtypeStruct((LOW,) + low_shape[1:], jnp.bfloat16)] * quarter,
        compiler_params=pltpu.CompilerParams(vmem_limit_bytes=16 << 20),
        cost_estimate=pl.CostEstimate(flops=0, bytes_accessed=8 * low.size, transcendentals=0),
        name="choose",
    )(me, *nearby)
    lows = [chosen[0]] + [swap(chosen[i], LOW * i) for i in range(1, quarter)]

    part_spec = pl.BlockSpec((devs, pl.squeezed, toks, width), lambda p: (0, p, 0, 0))
    later_spec = pl.BlockSpec((devs, pl.squeezed, toks, width), lambda p: (0, pairs + p, 0, 0))
    low_spec = pl.BlockSpec((LOW,) + low_shape[1:], lambda p: (0, 0, 0))
    mixed = pl.pallas_call(
        functools.partial(attend_kernel, math.gcd(devs, max(1, 256 // toks))),
        grid=(pairs,),
        in_specs=[SMEM, pl.BlockSpec((pl.squeezed, ranks, LANES), lambda p: (p, 0, 0))]
        + [later_spec, part_spec, part_spec]
        + [low_spec] * quarter,
        out_specs=part_spec,
        out_shape=jax.ShapeDtypeStruct((devs, pairs, toks, width), jnp.bfloat16),
        scratch_shapes=[
            pltpu.VMEM((devs,) + low_shape[1:], jnp.bfloat16),
            pltpu.VMEM((length, width), jnp.bfloat16),
        ],
        compiler_params=pltpu.CompilerParams(vmem_limit_bytes=48 << 20),
        cost_estimate=pl.CostEstimate(
            flops=4 * pairs * length * length * width,
            bytes_accessed=8 * pairs * length * width,
            transcendentals=pairs * length * length,
        ),
        name="attend",
    )(me, up_here, asked, keys, asked, *lows)
    return exchange(mixed).reshape(videos, heads, toks, width)


def solution(mesh):
    in_specs = (
        P("grp", "seq", None),
        P("grp", None, "seq", None),
        P("grp", None, "seq", None),
        P("grp", None, "seq", None),
        P("seq", None, None),
        P("seq", None, None),
        P(),
        P("grp"),
    )
    out_specs = P("grp", None, "seq", None)
    return jax.shard_map(body, mesh=mesh, in_specs=in_specs, out_specs=out_specs, check_vma=False)
```

```python
import functools
import math

import jax
import jax.numpy as jnp
from jax import lax
from jax.experimental import pallas as pl
from jax.experimental.pallas import tpu as pltpu
from jax.sharding import PartitionSpec as P

LANES = 128
LOW = 4
ANY = pl.BlockSpec(memory_space=pl.ANY)
VMEM = pl.BlockSpec(memory_space=pltpu.VMEM)
SMEM = pl.BlockSpec(memory_space=pltpu.SMEM)


def bit_count(n):
    bits = n.bit_length() - 1
    assert 1 << bits == n
    return bits


def reversed_bits(j, bits):
    out = 0
    for i in range(bits):
        out = out | (((j >> i) & 1) << (bits - 1 - i))
    return out


def pick_kernel(shape, me_ref, row_ref, req_ref, down_ref, up_ref, *refs):
    devs, bits, per_video, pairs, col_split, rows, tiles = shape
    downs, ups = refs[: bits - 1], refs[bits - 1 : 2 * bits - 2]
    down, up, sems = refs[2 * bits - 2 :]
    slots, ranks, _ = down_ref.shape
    videos = down.shape[0]
    me = me_ref[0]
    for s in range(videos):
        place = row_ref[req_ref[s]]
        slot = place % slots
        owned = place // slots == me
        copies = [
            pltpu.make_async_copy(down_ref.at[slot], down.at[s], sems.at[2 * s]),
            pltpu.make_async_copy(up_ref.at[slot], up.at[s], sems.at[2 * s + 1]),
        ]

        @pl.when(owned)
        def _():
            for copy in copies:
                copy.start()
            for copy in copies:
                copy.wait()

        @pl.when(jnp.logical_not(owned))
        def _():
            down[s] = jnp.zeros(down.shape[1:], down.dtype)
            up[s] = jnp.zeros(up.shape[1:], up.dtype)

    for j in range(devs):
        step = min(bits - j.bit_length(), bits - 2)
        at = j - (1 << (j.bit_length() - 1)) if j >= LOW else j
        dev = me ^ reversed_bits(j, bits)
        video = dev // per_video
        place = dev % per_video
        row = pl.multiple_of((place // col_split) * rows, rows)
        for t in range(tiles):
            col = pl.multiple_of(((place % col_split) * tiles + t) * LANES, LANES)
            downs[step][at, t * rows : (t + 1) * rows, :] = down[
                video, pl.ds(row, rows), pl.ds(col, LANES)
            ]
        for p in range(pairs):
            col = pl.multiple_of((place * pairs + p) * LANES, LANES)
            ups[step][at, p * ranks : (p + 1) * ranks, :] = up[video, :, pl.ds(col, LANES)]


def sum_kernel(picks, *refs):
    outs = refs[-len(picks) :]
    for out, terms in zip(outs, picks):
        size = out.shape[0]
        parts = [refs[i][first : first + size] for i, first in terms]
        out[...] = sum(parts[1:], parts[0])


def join_kernel(*refs):
    out, first = refs[-1], 0
    for ref in refs[:-1]:
        out[first : first + ref.shape[0]] = ref[...]
        first += ref.shape[0]


def on_vmem(kernel, shapes, name, *arrays):
    return pl.pallas_call(
        kernel,
        in_specs=[VMEM] * len(arrays),
        out_specs=[VMEM] * len(shapes),
        out_shape=[jax.ShapeDtypeStruct(s, arrays[0].dtype) for s in shapes],
        compiler_params=pltpu.CompilerParams(vmem_limit_bytes=16 << 20),
        cost_estimate=pl.CostEstimate(
            flops=0, bytes_accessed=2 * sum(a.size for a in arrays), transcendentals=0
        ),
        name=name,
    )(*arrays)


def low_rank_kernel(shape, me_ref, x_ref, *refs):
    devs, bits, per_video, _, col_split, rows, tiles = shape
    parts, out_ref, down = refs[:-2], refs[-2], refs[-1]
    blocks = [(ref, i) for ref in parts for i in range(ref.shape[0])]
    for j, (ref, i) in enumerate(blocks):
        dev = me_ref[0] ^ reversed_bits(j, bits)
        video = dev // per_video
        place = dev % per_video
        row = pl.multiple_of((place // col_split) * rows, rows)
        for t in range(tiles):
            col = pl.multiple_of(((place % col_split) * tiles + t) * LANES, LANES)
            down[video, pl.ds(row, rows), pl.ds(col, LANES)] = ref[i, t * rows : (t + 1) * rows, :]
    for s in range(x_ref.shape[0]):
        low = lax.dot_general(
            x_ref[s], down[s], (((1,), (1,)), ((), ())), preferred_element_type=jnp.float32
        ).astype(out_ref.dtype)
        half = low.shape[0] // 2
        out_ref[s] = jnp.concatenate([low[:half], low[half:]], axis=1)


def choose_kernel(per_video, me_ref, *refs):
    ins, outs = refs[:LOW], refs[LOW:]
    for i, out in enumerate(outs):
        video = (me_ref[0] ^ (LOW * i)) // per_video
        for j in range(LOW):
            out[j] = ins[j][video]


def add_delta(base, low, up, second):
    devs, toks, width = base.shape
    ranks = up.shape[0]
    row = lax.broadcasted_iota(jnp.int32, up.shape, 0)
    part = jnp.where(row // (ranks // 2) == second, up, jnp.zeros_like(up))
    none = jnp.zeros_like(part)
    deltas = [
        jnp.dot(low, jnp.concatenate(pair, axis=0), preferred_element_type=jnp.float32)
        for pair in ((part, none), (none, part))
    ]
    delta = jnp.concatenate([d.reshape(devs, toks // 2, width) for d in deltas], axis=1)
    return (base.astype(jnp.float32) + delta).astype(base.dtype).reshape(devs * toks, width)


def attend_kernel(block, me_ref, up_ref, q_ref, k_ref, v_ref, *refs):
    low_refs, out_ref, low_all, q_mix = refs[:-3], refs[-3], refs[-2], refs[-1]
    devs, toks, width = q_ref.shape
    length = devs * toks
    for k in range(devs):
        low_all[me_ref[0] ^ k] = low_refs[k // LOW][k % LOW]
    low = low_all[...].reshape(length // 2, low_all.shape[2])
    up = up_ref[...]
    keys = k_ref[...].reshape(length, width)
    vals = add_delta(v_ref[...], low, up, 1)
    vals = jnp.concatenate([vals, jnp.ones_like(vals)], axis=1)
    q_mix[...] = add_delta(q_ref[...], low, up, 0)
    scale = math.log2(math.e) / math.sqrt(width)

    def score(b):
        q = q_mix[b * toks : (b + block) * toks, :]
        return lax.dot_general(q, keys, (((1,), (1,)), ((), ())), preferred_element_type=jnp.float32)

    coming = score(0)
    for b in range(0, devs, block):
        scores = coming
        if b + block < devs:
            coming = score(b + block)
        top = jnp.max(scores, axis=1, keepdims=True)
        weights = jnp.exp2((scores - top) * scale).astype(jnp.bfloat16)
        mixed = jnp.dot(weights, vals, preferred_element_type=jnp.float32)
        out = mixed[:, :width] / mixed[:, width:]
        out_ref[b : b + block] = out.astype(jnp.bfloat16).reshape(block, toks, width)


def body(
    normed_token_features,
    queries,
    projected_keys,
    values,
    adapter_down_factors,
    adapter_up_factors,
    adapter_store_row,
    requests,
):
    videos, toks, model_width = normed_token_features.shape
    heads = queries.shape[1]
    width = queries.shape[3]
    _, ranks, up_width = adapter_up_factors.shape
    devs = lax.axis_size("seq")
    bits = bit_count(devs)
    me = lax.axis_index("seq").astype(jnp.int32)[None]
    pairs = videos * heads // devs
    per_video = devs // videos
    length = devs * toks
    col_split = math.gcd(per_video, model_width // LANES)
    rows = ranks * col_split // per_video
    tiles = model_width // col_split // LANES
    shape = (devs, bits, per_video, pairs, col_split, rows, tiles)

    def swap(tensor, k):
        return lax.ppermute(tensor, "seq", [(i, i ^ k) for i in range(devs)])

    def exchange(tensor):
        return lax.all_to_all(tensor, "seq", split_axis=0, concat_axis=0, tiled=True)

    def by_pairs(tensor):
        return tensor.reshape(devs, pairs, toks, width)

    def after(array, *others):
        return lax.optimization_barrier((array, others))[0]

    quarter = devs // LOW
    others = (2 * quarter, quarter, 3 * quarter)

    def halving(parts, received, i):
        size = parts[i].shape[0]
        terms = [(0, 0)] + [(1 + n, size) for n in range(len(received))]
        return on_vmem(
            functools.partial(sum_kernel, [terms]), [parts[i].shape], "halve", parts[i], *received
        )[0]

    def splitting(parts, received):
        size = (1,) + parts[-1].shape[1:]
        picks = [[(n, j) for n in range(1 + len(received))] for j in range(LOW)]
        return on_vmem(
            functools.partial(sum_kernel, picks), [size] * LOW, "split", parts[-1], *received
        )

    def to_others(shards):
        return [swap(shard, k) for shard, k in zip(shards[1:], others)]

    def total(shard, received):
        picks = [[(n, 0) for n in range(LOW)]]
        return on_vmem(
            functools.partial(sum_kernel, picks), [shard.shape], "total", shard, *received
        )[0]

    def join(arrays):
        count = sum(a.shape[0] for a in arrays)
        return on_vmem(join_kernel, [(count,) + arrays[0].shape[1:]], "join", *arrays)[0]

    keys = exchange(by_pairs(projected_keys))

    steps = [devs >> (i + 1) for i in range(bits - 2)] + [LOW]
    piece_shapes = [(h, tiles * rows, LANES) for h in steps] + [
        (h, pairs * ranks, LANES) for h in steps
    ]
    pieces = pl.pallas_call(
        functools.partial(pick_kernel, shape),
        in_specs=[SMEM, SMEM, SMEM, ANY, ANY],
        out_specs=[VMEM] * (2 * bits - 2),
        out_shape=[jax.ShapeDtypeStruct(s, jnp.bfloat16) for s in piece_shapes],
        scratch_shapes=[
            pltpu.VMEM((videos, ranks, model_width), jnp.bfloat16),
            pltpu.VMEM((videos, ranks, up_width), jnp.bfloat16),
            pltpu.SemaphoreType.DMA((2 * videos,)),
        ],
        compiler_params=pltpu.CompilerParams(vmem_limit_bytes=24 << 20),
        cost_estimate=pl.CostEstimate(
            flops=0,
            bytes_accessed=4 * videos * ranks * (model_width + up_width),
            transcendentals=0,
        ),
        name="pick_factors",
    )(me, adapter_store_row, requests, adapter_down_factors, adapter_up_factors)
    down_pieces, up_pieces = pieces[: bits - 1], pieces[bits - 1 :]

    down_got, up_got = [], []

    def send_up(i, *others):
        up_got.append(swap(after(halving(up_pieces, up_got, i), *others), 1 << i))

    for i in range(bits - 2):
        piece = down_pieces[0] if i == 0 else halving(down_pieces, down_got, i)
        if i > 0:
            part = up_pieces[0] if i == 1 else halving(up_pieces, up_got, i - 1)
            up_got.append(swap(after(part, piece), 1 << (i - 1)))
        down_got.append(swap(piece, 1 << i))
    part = after(halving(up_pieces, up_got, bits - 3), piece)
    up_got.append(swap(part, 1 << (bits - 3)))
    held = splitting((after(down_pieces[-1], *up_got[:-1]),), down_got)
    shard = after(total(held[0], to_others(held)), keys, up_got[-1])
    gathered = [shard] + [swap(shard, k) for k in others]

    joined = join(gathered)
    asked = jnp.concatenate([by_pairs(values), by_pairs(queries)], axis=1)
    asked = exchange(after(asked, joined))
    for i in reversed(range(bits - 2)):
        gathered = [joined, swap(joined, 1 << i)]
        if i > 0:
            joined = join(gathered)

    low_shape = (videos, toks // 2, 2 * ranks)
    low = pl.pallas_call(
        functools.partial(low_rank_kernel, shape),
        in_specs=[SMEM, VMEM] + [VMEM] * len(gathered),
        out_specs=VMEM,
        scratch_shapes=[pltpu.VMEM((videos, ranks, model_width), jnp.bfloat16)],
        out_shape=jax.ShapeDtypeStruct(low_shape, jnp.bfloat16),
        compiler_params=pltpu.CompilerParams(vmem_limit_bytes=24 << 20),
        cost_estimate=pl.CostEstimate(
            flops=2 * videos * toks * ranks * model_width,
            bytes_accessed=2 * videos * (toks + ranks) * model_width,
            transcendentals=0,
        ),
        name="low_rank",
    )(me, normed_token_features, *gathered)
    up_part = after(up_pieces[-1], low)
    near_pair, far_pair = on_vmem(
        functools.partial(sum_kernel, [[(n, 2 * h) for n in range(1 + len(up_got))] for h in (0, 1)]),
        [(2,) + up_part.shape[1:]] * 2,
        "split",
        up_part,
        *up_got,
    )
    came = swap(far_pair, quarter)
    one_shape = (1,) + up_part.shape[1:]
    kept, sent = on_vmem(
        functools.partial(sum_kernel, [[(n, h) for n in range(2)] for h in (0, 1)]),
        [one_shape] * 2,
        "split",
        near_pair,
        came,
    )
    last = swap(sent, 2 * quarter)
    up_here = on_vmem(
        functools.partial(sum_kernel, [[(0, 0), (1, 0)]]), [one_shape], "total", kept, last
    )[0].reshape(pairs, ranks, LANES)
    nearby = [low] + [swap(low, k) for k in range(1, LOW)]
    chosen = pl.pallas_call(
        functools.partial(choose_kernel, per_video),
        in_specs=[SMEM] + [VMEM] * LOW,
        out_specs=[VMEM] * quarter,
        out_shape=[jax.ShapeDtypeStruct((LOW,) + low_shape[1:], jnp.bfloat16)] * quarter,
        compiler_params=pltpu.CompilerParams(vmem_limit_bytes=16 << 20),
        cost_estimate=pl.CostEstimate(flops=0, bytes_accessed=8 * low.size, transcendentals=0),
        name="choose",
    )(me, *nearby)
    lows = [chosen[0]] + [swap(chosen[i], LOW * i) for i in range(1, quarter)]

    part_spec = pl.BlockSpec((devs, pl.squeezed, toks, width), lambda p: (0, p, 0, 0))
    later_spec = pl.BlockSpec((devs, pl.squeezed, toks, width), lambda p: (0, pairs + p, 0, 0))
    low_spec = pl.BlockSpec((LOW,) + low_shape[1:], lambda p: (0, 0, 0))
    mixed = pl.pallas_call(
        functools.partial(attend_kernel, math.gcd(devs, max(1, 256 // toks))),
        grid=(pairs,),
        in_specs=[SMEM, pl.BlockSpec((pl.squeezed, ranks, LANES), lambda p: (p, 0, 0))]
        + [later_spec, part_spec, part_spec]
        + [low_spec] * quarter,
        out_specs=part_spec,
        out_shape=jax.ShapeDtypeStruct((devs, pairs, toks, width), jnp.bfloat16),
        scratch_shapes=[
            pltpu.VMEM((devs,) + low_shape[1:], jnp.bfloat16),
            pltpu.VMEM((length, width), jnp.bfloat16),
        ],
        compiler_params=pltpu.CompilerParams(vmem_limit_bytes=48 << 20),
        cost_estimate=pl.CostEstimate(
            flops=4 * pairs * length * length * width,
            bytes_accessed=8 * pairs * length * width,
            transcendentals=pairs * length * length,
        ),
        name="attend",
    )(me, up_here, asked, keys, asked, *lows)
    return exchange(mixed).reshape(videos, heads, toks, width)


def solution(mesh):
    in_specs = (
        P("grp", "seq", None),
        P("grp", None, "seq", None),
        P("grp", None, "seq", None),
        P("grp", None, "seq", None),
        P("seq", None, None),
        P("seq", None, None),
        P(),
        P("grp"),
    )
    out_specs = P("grp", None, "seq", None)
    return jax.shard_map(body, mesh=mesh, in_specs=in_specs, out_specs=out_specs, check_vma=False)
```

```python
import functools
import math

import jax
import jax.numpy as jnp
from jax import lax
from jax.experimental import pallas as pl
from jax.experimental.pallas import tpu as pltpu
from jax.sharding import PartitionSpec as P

LANES = 128
LOW = 4
ANY = pl.BlockSpec(memory_space=pl.ANY)
VMEM = pl.BlockSpec(memory_space=pltpu.VMEM)
SMEM = pl.BlockSpec(memory_space=pltpu.SMEM)


def bit_count(n):
    bits = n.bit_length() - 1
    assert 1 << bits == n
    return bits


def reversed_bits(j, bits):
    out = 0
    for i in range(bits):
        out = out | (((j >> i) & 1) << (bits - 1 - i))
    return out


def pick_kernel(shape, me_ref, row_ref, req_ref, down_ref, up_ref, *refs):
    devs, bits, per_video, pairs, col_split, rows, tiles = shape
    downs, ups = refs[: bits - 1], refs[bits - 1 : 2 * bits - 2]
    down, up, sems = refs[2 * bits - 2 :]
    slots, ranks, _ = down_ref.shape
    videos = down.shape[0]
    me = me_ref[0]
    for s in range(videos):
        place = row_ref[req_ref[s]]
        slot = place % slots
        owned = place // slots == me
        copies = [
            pltpu.make_async_copy(down_ref.at[slot], down.at[s], sems.at[2 * s]),
            pltpu.make_async_copy(up_ref.at[slot], up.at[s], sems.at[2 * s + 1]),
        ]

        @pl.when(owned)
        def _():
            for copy in copies:
                copy.start()
            for copy in copies:
                copy.wait()

        @pl.when(jnp.logical_not(owned))
        def _():
            down[s] = jnp.zeros(down.shape[1:], down.dtype)
            up[s] = jnp.zeros(up.shape[1:], up.dtype)

    for j in range(devs):
        step = min(bits - j.bit_length(), bits - 2)
        at = j - (1 << (j.bit_length() - 1)) if j >= LOW else j
        dev = me ^ reversed_bits(j, bits)
        video = dev // per_video
        place = dev % per_video
        row = pl.multiple_of((place // col_split) * rows, rows)
        for t in range(tiles):
            col = pl.multiple_of(((place % col_split) * tiles + t) * LANES, LANES)
            downs[step][at, t * rows : (t + 1) * rows, :] = down[
                video, pl.ds(row, rows), pl.ds(col, LANES)
            ]
        for p in range(pairs):
            col = pl.multiple_of((place * pairs + p) * LANES, LANES)
            ups[step][at, p * ranks : (p + 1) * ranks, :] = up[video, :, pl.ds(col, LANES)]


def sum_kernel(picks, *refs):
    outs = refs[-len(picks) :]
    for out, terms in zip(outs, picks):
        size = out.shape[0]
        parts = [refs[i][first : first + size] for i, first in terms]
        out[...] = sum(parts[1:], parts[0])


def join_kernel(*refs):
    out, first = refs[-1], 0
    for ref in refs[:-1]:
        out[first : first + ref.shape[0]] = ref[...]
        first += ref.shape[0]


def on_vmem(kernel, shapes, name, *arrays):
    return pl.pallas_call(
        kernel,
        in_specs=[VMEM] * len(arrays),
        out_specs=[VMEM] * len(shapes),
        out_shape=[jax.ShapeDtypeStruct(s, arrays[0].dtype) for s in shapes],
        compiler_params=pltpu.CompilerParams(vmem_limit_bytes=8 << 20),
        cost_estimate=pl.CostEstimate(
            flops=0, bytes_accessed=2 * sum(a.size for a in arrays), transcendentals=0
        ),
        name=name,
    )(*arrays)


def low_rank_kernel(shape, me_ref, x_ref, *refs):
    devs, bits, per_video, _, col_split, rows, tiles = shape
    parts, out_ref, down = refs[:-2], refs[-2], refs[-1]
    blocks = [(ref, i) for ref in parts for i in range(ref.shape[0])]
    for j, (ref, i) in enumerate(blocks):
        dev = me_ref[0] ^ reversed_bits(j, bits)
        video = dev // per_video
        place = dev % per_video
        row = pl.multiple_of((place // col_split) * rows, rows)
        for t in range(tiles):
            col = pl.multiple_of(((place % col_split) * tiles + t) * LANES, LANES)
            down[video, pl.ds(row, rows), pl.ds(col, LANES)] = ref[i, t * rows : (t + 1) * rows, :]
    for s in range(x_ref.shape[0]):
        low = lax.dot_general(
            x_ref[s], down[s], (((1,), (1,)), ((), ())), preferred_element_type=jnp.float32
        ).astype(out_ref.dtype)
        half = low.shape[0] // 2
        out_ref[s] = jnp.concatenate([low[:half], low[half:]], axis=1)


def choose_kernel(per_video, me_ref, *refs):
    ins, outs = refs[:LOW], refs[LOW:]
    for i, out in enumerate(outs):
        video = (me_ref[0] ^ (LOW * i)) // per_video
        for j in range(LOW):
            out[j] = ins[j][video]


def add_delta(base, low, up, second):
    devs, toks, width = base.shape
    ranks = up.shape[0]
    row = lax.broadcasted_iota(jnp.int32, up.shape, 0)
    part = jnp.where(row // (ranks // 2) == second, up, jnp.zeros_like(up))
    none = jnp.zeros_like(part)
    deltas = [
        jnp.dot(low, jnp.concatenate(pair, axis=0), preferred_element_type=jnp.float32)
        for pair in ((part, none), (none, part))
    ]
    delta = jnp.concatenate([d.reshape(devs, toks // 2, width) for d in deltas], axis=1)
    return (base.astype(jnp.float32) + delta).astype(base.dtype).reshape(devs * toks, width)


def attend_kernel(block, me_ref, up_ref, q_ref, k_ref, v_ref, *refs):
    low_refs, out_ref, low_all, q_mix = refs[:-3], refs[-3], refs[-2], refs[-1]
    devs, toks, width = q_ref.shape
    length = devs * toks
    for k in range(devs):
        low_all[me_ref[0] ^ k] = low_refs[k // LOW][k % LOW]
    low = low_all[...].reshape(length // 2, low_all.shape[2])
    up = up_ref[...]
    keys = k_ref[...].reshape(length, width)
    vals = add_delta(v_ref[...], low, up, 1)
    vals = jnp.concatenate([vals, jnp.ones_like(vals)], axis=1)
    q_mix[...] = add_delta(q_ref[...], low, up, 0)
    scale = math.log2(math.e) / math.sqrt(width)

    def score(b):
        q = q_mix[b * toks : (b + block) * toks, :]
        return lax.dot_general(q, keys, (((1,), (1,)), ((), ())), preferred_element_type=jnp.float32)

    coming = score(0)
    for b in range(0, devs, block):
        scores = coming
        if b + block < devs:
            coming = score(b + block)
        top = jnp.max(scores, axis=1, keepdims=True)
        weights = jnp.exp2((scores - top) * scale).astype(jnp.bfloat16)
        mixed = jnp.dot(weights, vals, preferred_element_type=jnp.float32)
        out = mixed[:, :width] / mixed[:, width:]
        out_ref[b : b + block] = out.astype(jnp.bfloat16).reshape(block, toks, width)


def body(
    normed_token_features,
    queries,
    projected_keys,
    values,
    adapter_down_factors,
    adapter_up_factors,
    adapter_store_row,
    requests,
):
    videos, toks, model_width = normed_token_features.shape
    heads = queries.shape[1]
    width = queries.shape[3]
    _, ranks, up_width = adapter_up_factors.shape
    devs = lax.axis_size("seq")
    bits = bit_count(devs)
    me = lax.axis_index("seq").astype(jnp.int32)[None]
    pairs = videos * heads // devs
    per_video = devs // videos
    length = devs * toks
    col_split = math.gcd(per_video, model_width // LANES)
    rows = ranks * col_split // per_video
    tiles = model_width // col_split // LANES
    shape = (devs, bits, per_video, pairs, col_split, rows, tiles)

    def swap(tensor, k):
        return lax.ppermute(tensor, "seq", [(i, i ^ k) for i in range(devs)])

    def exchange(tensor):
        return lax.all_to_all(tensor, "seq", split_axis=0, concat_axis=0, tiled=True)

    def by_pairs(tensor):
        return tensor.reshape(devs, pairs, toks, width)

    def after(array, *others):
        return lax.optimization_barrier((array, others))[0]

    quarter = devs // LOW
    others = (2 * quarter, quarter, 3 * quarter)

    def halving(parts, received, i):
        size = parts[i].shape[0]
        terms = [(0, 0)] + [(1 + n, size) for n in range(len(received))]
        return on_vmem(
            functools.partial(sum_kernel, [terms]), [parts[i].shape], "halve", parts[i], *received
        )[0]

    def splitting(parts, received):
        size = (1,) + parts[-1].shape[1:]
        picks = [[(n, j) for n in range(1 + len(received))] for j in range(LOW)]
        return on_vmem(
            functools.partial(sum_kernel, picks), [size] * LOW, "split", parts[-1], *received
        )

    def to_others(shards):
        return [swap(shard, k) for shard, k in zip(shards[1:], others)]

    def total(shard, received):
        picks = [[(n, 0) for n in range(LOW)]]
        return on_vmem(
            functools.partial(sum_kernel, picks), [shard.shape], "total", shard, *received
        )[0]

    def join(arrays):
        count = sum(a.shape[0] for a in arrays)
        return on_vmem(join_kernel, [(count,) + arrays[0].shape[1:]], "join", *arrays)[0]

    keys = exchange(by_pairs(projected_keys))

    steps = [devs >> (i + 1) for i in range(bits - 2)] + [LOW]
    piece_shapes = [(h, tiles * rows, LANES) for h in steps] + [
        (h, pairs * ranks, LANES) for h in steps
    ]
    pieces = pl.pallas_call(
        functools.partial(pick_kernel, shape),
        in_specs=[SMEM, SMEM, SMEM, ANY, ANY],
        out_specs=[VMEM] * (2 * bits - 2),
        out_shape=[jax.ShapeDtypeStruct(s, jnp.bfloat16) for s in piece_shapes],
        scratch_shapes=[
            pltpu.VMEM((videos, ranks, model_width), jnp.bfloat16),
            pltpu.VMEM((videos, ranks, up_width), jnp.bfloat16),
            pltpu.SemaphoreType.DMA((2 * videos,)),
        ],
        compiler_params=pltpu.CompilerParams(vmem_limit_bytes=12 << 20),
        cost_estimate=pl.CostEstimate(
            flops=0,
            bytes_accessed=4 * videos * ranks * (model_width + up_width),
            transcendentals=0,
        ),
        name="pick_factors",
    )(me, adapter_store_row, requests, adapter_down_factors, adapter_up_factors)
    down_pieces, up_pieces = pieces[: bits - 1], pieces[bits - 1 :]

    down_got, up_got = [], []

    def send_up(i, *others):
        up_got.append(swap(after(halving(up_pieces, up_got, i), *others), 1 << i))

    for i in range(bits - 2):
        piece = down_pieces[0] if i == 0 else halving(down_pieces, down_got, i)
        if i > 0:
            part = up_pieces[0] if i == 1 else halving(up_pieces, up_got, i - 1)
            up_got.append(swap(after(part, piece), 1 << (i - 1)))
        down_got.append(swap(piece, 1 << i))
    part = after(halving(up_pieces, up_got, bits - 3), piece)
    up_got.append(swap(part, 1 << (bits - 3)))
    held = splitting((after(down_pieces[-1], *up_got[:-1]),), down_got)
    shard = after(total(held[0], to_others(held)), keys, up_got[-1])
    gathered = [shard] + [swap(shard, k) for k in others]

    joined = join(gathered)
    asked = jnp.concatenate([by_pairs(values), by_pairs(queries)], axis=1)
    asked = exchange(after(asked, joined))
    for i in reversed(range(bits - 2)):
        gathered = [joined, swap(joined, 1 << i)]
        if i > 0:
            joined = join(gathered)

    low_shape = (videos, toks // 2, 2 * ranks)
    low = pl.pallas_call(
        functools.partial(low_rank_kernel, shape),
        in_specs=[SMEM, VMEM] + [VMEM] * len(gathered),
        out_specs=VMEM,
        scratch_shapes=[pltpu.VMEM((videos, ranks, model_width), jnp.bfloat16)],
        out_shape=jax.ShapeDtypeStruct(low_shape, jnp.bfloat16),
        compiler_params=pltpu.CompilerParams(vmem_limit_bytes=12 << 20),
        cost_estimate=pl.CostEstimate(
            flops=2 * videos * toks * ranks * model_width,
            bytes_accessed=2 * videos * (toks + ranks) * model_width,
            transcendentals=0,
        ),
        name="low_rank",
    )(me, normed_token_features, *gathered)
    up_part = after(up_pieces[-1], low)
    near_pair, far_pair = on_vmem(
        functools.partial(sum_kernel, [[(n, 2 * h) for n in range(1 + len(up_got))] for h in (0, 1)]),
        [(2,) + up_part.shape[1:]] * 2,
        "split",
        up_part,
        *up_got,
    )
    came = swap(far_pair, quarter)
    one_shape = (1,) + up_part.shape[1:]
    kept, sent = on_vmem(
        functools.partial(sum_kernel, [[(n, h) for n in range(2)] for h in (0, 1)]),
        [one_shape] * 2,
        "split",
        near_pair,
        came,
    )
    last = swap(sent, 2 * quarter)
    up_here = on_vmem(
        functools.partial(sum_kernel, [[(0, 0), (1, 0)]]), [one_shape], "total", kept, last
    )[0].reshape(pairs, ranks, LANES)
    nearby = [low] + [swap(low, k) for k in range(1, LOW)]
    chosen = pl.pallas_call(
        functools.partial(choose_kernel, per_video),
        in_specs=[SMEM] + [VMEM] * LOW,
        out_specs=[VMEM] * quarter,
        out_shape=[jax.ShapeDtypeStruct((LOW,) + low_shape[1:], jnp.bfloat16)] * quarter,
        compiler_params=pltpu.CompilerParams(vmem_limit_bytes=8 << 20),
        cost_estimate=pl.CostEstimate(flops=0, bytes_accessed=8 * low.size, transcendentals=0),
        name="choose",
    )(me, *nearby)
    lows = [chosen[0]] + [swap(chosen[i], LOW * i) for i in range(1, quarter)]

    part_spec = pl.BlockSpec((devs, pl.squeezed, toks, width), lambda p: (0, p, 0, 0))
    later_spec = pl.BlockSpec((devs, pl.squeezed, toks, width), lambda p: (0, pairs + p, 0, 0))
    low_spec = pl.BlockSpec((LOW,) + low_shape[1:], lambda p: (0, 0, 0))
    mixed = pl.pallas_call(
        functools.partial(attend_kernel, math.gcd(devs, max(1, 256 // toks))),
        grid=(pairs,),
        in_specs=[SMEM, pl.BlockSpec((pl.squeezed, ranks, LANES), lambda p: (p, 0, 0))]
        + [later_spec, part_spec, part_spec]
        + [low_spec] * quarter,
        out_specs=part_spec,
        out_shape=jax.ShapeDtypeStruct((devs, pairs, toks, width), jnp.bfloat16),
        scratch_shapes=[
            pltpu.VMEM((devs,) + low_shape[1:], jnp.bfloat16),
            pltpu.VMEM((length, width), jnp.bfloat16),
        ],
        compiler_params=pltpu.CompilerParams(vmem_limit_bytes=40 << 20),
        cost_estimate=pl.CostEstimate(
            flops=4 * pairs * length * length * width,
            bytes_accessed=8 * pairs * length * width,
            transcendentals=pairs * length * length,
        ),
        name="attend",
    )(me, up_here, asked, keys, asked, *lows)
    return exchange(mixed).reshape(videos, heads, toks, width)


def solution(mesh):
    in_specs = (
        P("grp", "seq", None),
        P("grp", None, "seq", None),
        P("grp", None, "seq", None),
        P("grp", None, "seq", None),
        P("seq", None, None),
        P("seq", None, None),
        P(),
        P("grp"),
    )
    out_specs = P("grp", None, "seq", None)
    return jax.shard_map(body, mesh=mesh, in_specs=in_specs, out_specs=out_specs, check_vma=False)
```

```python
import functools
import math

import jax
import jax.numpy as jnp
from jax import lax
from jax.experimental import pallas as pl
from jax.experimental.pallas import tpu as pltpu
from jax.sharding import PartitionSpec as P

LANES = 128
LOW = 4
ANY = pl.BlockSpec(memory_space=pl.ANY)
VMEM = pl.BlockSpec(memory_space=pltpu.VMEM)
SMEM = pl.BlockSpec(memory_space=pltpu.SMEM)


def bit_count(n):
    bits = n.bit_length() - 1
    assert 1 << bits == n
    return bits


def reversed_bits(j, bits):
    out = 0
    for i in range(bits):
        out = out | (((j >> i) & 1) << (bits - 1 - i))
    return out


def pick_kernel(shape, me_ref, row_ref, req_ref, down_ref, up_ref, *refs):
    devs, bits, per_video, pairs, col_split, rows, tiles = shape
    downs, ups = refs[: bits - 1], refs[bits - 1 : 2 * bits - 2]
    down, up, sems = refs[2 * bits - 2 :]
    slots, ranks, _ = down_ref.shape
    videos = down.shape[0]
    me = me_ref[0]
    for s in range(videos):
        place = row_ref[req_ref[s]]
        slot = place % slots
        owned = place // slots == me
        copies = [
            pltpu.make_async_copy(down_ref.at[slot], down.at[s], sems.at[2 * s]),
            pltpu.make_async_copy(up_ref.at[slot], up.at[s], sems.at[2 * s + 1]),
        ]

        @pl.when(owned)
        def _():
            for copy in copies:
                copy.start()
            for copy in copies:
                copy.wait()

        @pl.when(jnp.logical_not(owned))
        def _():
            down[s] = jnp.zeros(down.shape[1:], down.dtype)
            up[s] = jnp.zeros(up.shape[1:], up.dtype)

    for j in range(devs):
        step = min(bits - j.bit_length(), bits - 2)
        at = j - (1 << (j.bit_length() - 1)) if j >= LOW else j
        dev = me ^ reversed_bits(j, bits)
        video = dev // per_video
        place = dev % per_video
        row = pl.multiple_of((place // col_split) * rows, rows)
        for t in range(tiles):
            col = pl.multiple_of(((place % col_split) * tiles + t) * LANES, LANES)
            downs[step][at, t * rows : (t + 1) * rows, :] = down[
                video, pl.ds(row, rows), pl.ds(col, LANES)
            ]
        for p in range(pairs):
            col = pl.multiple_of((place * pairs + p) * LANES, LANES)
            ups[step][at, p * ranks : (p + 1) * ranks, :] = up[video, :, pl.ds(col, LANES)]


def sum_kernel(picks, *refs):
    outs = refs[-len(picks) :]
    for out, terms in zip(outs, picks):
        size = out.shape[0]
        parts = [refs[i][first : first + size] for i, first in terms]
        out[...] = sum(parts[1:], parts[0])


def join_kernel(*refs):
    out, first = refs[-1], 0
    for ref in refs[:-1]:
        out[first : first + ref.shape[0]] = ref[...]
        first += ref.shape[0]


def on_vmem(kernel, shapes, name, *arrays):
    return pl.pallas_call(
        kernel,
        in_specs=[VMEM] * len(arrays),
        out_specs=[VMEM] * len(shapes),
        out_shape=[jax.ShapeDtypeStruct(s, arrays[0].dtype) for s in shapes],
        compiler_params=pltpu.CompilerParams(vmem_limit_bytes=8 << 20),
        cost_estimate=pl.CostEstimate(
            flops=0, bytes_accessed=2 * sum(a.size for a in arrays), transcendentals=0
        ),
        name=name,
    )(*arrays)


def low_rank_kernel(shape, me_ref, x_ref, *refs):
    devs, bits, per_video, _, col_split, rows, tiles = shape
    parts, out_ref, down = refs[:-2], refs[-2], refs[-1]
    blocks = [(ref, i) for ref in parts for i in range(ref.shape[0])]
    for j, (ref, i) in enumerate(blocks):
        dev = me_ref[0] ^ reversed_bits(j, bits)
        video = dev // per_video
        place = dev % per_video
        row = pl.multiple_of((place // col_split) * rows, rows)
        for t in range(tiles):
            col = pl.multiple_of(((place % col_split) * tiles + t) * LANES, LANES)
            down[video, pl.ds(row, rows), pl.ds(col, LANES)] = ref[i, t * rows : (t + 1) * rows, :]
    for s in range(x_ref.shape[0]):
        low = lax.dot_general(
            x_ref[s], down[s], (((1,), (1,)), ((), ())), preferred_element_type=jnp.float32
        ).astype(out_ref.dtype)
        half = low.shape[0] // 2
        out_ref[s] = jnp.concatenate([low[:half], low[half:]], axis=1)


def choose_kernel(per_video, me_ref, *refs):
    ins, outs = refs[:LOW], refs[LOW:]
    for i, out in enumerate(outs):
        video = (me_ref[0] ^ (LOW * i)) // per_video
        for j in range(LOW):
            out[j] = ins[j][video]


def add_delta(base, low, up, second):
    devs, toks, width = base.shape
    ranks = up.shape[0]
    row = lax.broadcasted_iota(jnp.int32, up.shape, 0)
    part = jnp.where(row // (ranks // 2) == second, up, jnp.zeros_like(up))
    none = jnp.zeros_like(part)
    deltas = [
        jnp.dot(low, jnp.concatenate(pair, axis=0), preferred_element_type=jnp.float32)
        for pair in ((part, none), (none, part))
    ]
    delta = jnp.concatenate([d.reshape(devs, toks // 2, width) for d in deltas], axis=1)
    return (base.astype(jnp.float32) + delta).astype(base.dtype).reshape(devs * toks, width)


def attend_kernel(block, me_ref, up_ref, q_ref, k_ref, v_ref, *refs):
    low_refs, out_ref, low_all, q_mix = refs[:-3], refs[-3], refs[-2], refs[-1]
    devs, toks, width = q_ref.shape
    length = devs * toks
    for k in range(devs):
        low_all[me_ref[0] ^ k] = low_refs[k // LOW][k % LOW]
    low = low_all[...].reshape(length // 2, low_all.shape[2])
    up = up_ref[...]
    keys = k_ref[...].reshape(length, width)
    vals = add_delta(v_ref[...], low, up, 1)
    vals = jnp.concatenate([vals, jnp.ones_like(vals)], axis=1)
    q_mix[...] = add_delta(q_ref[...], low, up, 0)
    scale = math.log2(math.e) / math.sqrt(width)

    def score(b):
        q = q_mix[b * toks : (b + block) * toks, :]
        return lax.dot_general(q, keys, (((1,), (1,)), ((), ())), preferred_element_type=jnp.float32)

    coming = score(0)
    for b in range(0, devs, block):
        scores = coming
        if b + block < devs:
            coming = score(b + block)
        top = jnp.max(scores, axis=1, keepdims=True)
        weights = jnp.exp2((scores - top) * scale).astype(jnp.bfloat16)
        mixed = jnp.dot(weights, vals, preferred_element_type=jnp.float32)
        out = mixed[:, :width] / mixed[:, width:]
        out_ref[b : b + block] = out.astype(jnp.bfloat16).reshape(block, toks, width)


def body(
    normed_token_features,
    queries,
    projected_keys,
    values,
    adapter_down_factors,
    adapter_up_factors,
    adapter_store_row,
    requests,
):
    videos, toks, model_width = normed_token_features.shape
    heads = queries.shape[1]
    width = queries.shape[3]
    _, ranks, up_width = adapter_up_factors.shape
    devs = lax.axis_size("seq")
    bits = bit_count(devs)
    me = lax.axis_index("seq").astype(jnp.int32)[None]
    pairs = videos * heads // devs
    per_video = devs // videos
    length = devs * toks
    col_split = math.gcd(per_video, model_width // LANES)
    rows = ranks * col_split // per_video
    tiles = model_width // col_split // LANES
    shape = (devs, bits, per_video, pairs, col_split, rows, tiles)

    def swap(tensor, k):
        return lax.ppermute(tensor, "seq", [(i, i ^ k) for i in range(devs)])

    def exchange(tensor):
        return lax.all_to_all(tensor, "seq", split_axis=0, concat_axis=0, tiled=True)

    def by_pairs(tensor):
        return tensor.reshape(devs, pairs, toks, width)

    def after(array, *others):
        return lax.optimization_barrier((array, others))[0]

    quarter = devs // LOW
    others = (2 * quarter, quarter, 3 * quarter)

    def halving(parts, received, i):
        size = parts[i].shape[0]
        terms = [(0, 0)] + [(1 + n, size) for n in range(len(received))]
        return on_vmem(
            functools.partial(sum_kernel, [terms]), [parts[i].shape], "halve", parts[i], *received
        )[0]

    def splitting(parts, received):
        size = (1,) + parts[-1].shape[1:]
        picks = [[(n, j) for n in range(1 + len(received))] for j in range(LOW)]
        return on_vmem(
            functools.partial(sum_kernel, picks), [size] * LOW, "split", parts[-1], *received
        )

    def to_others(shards):
        return [swap(shard, k) for shard, k in zip(shards[1:], others)]

    def total(shard, received):
        picks = [[(n, 0) for n in range(LOW)]]
        return on_vmem(
            functools.partial(sum_kernel, picks), [shard.shape], "total", shard, *received
        )[0]

    def join(arrays):
        count = sum(a.shape[0] for a in arrays)
        return on_vmem(join_kernel, [(count,) + arrays[0].shape[1:]], "join", *arrays)[0]

    keys = exchange(by_pairs(projected_keys))

    steps = [devs >> (i + 1) for i in range(bits - 2)] + [LOW]
    piece_shapes = [(h, tiles * rows, LANES) for h in steps] + [
        (h, pairs * ranks, LANES) for h in steps
    ]
    pieces = pl.pallas_call(
        functools.partial(pick_kernel, shape),
        in_specs=[SMEM, SMEM, SMEM, ANY, ANY],
        out_specs=[VMEM] * (2 * bits - 2),
        out_shape=[jax.ShapeDtypeStruct(s, jnp.bfloat16) for s in piece_shapes],
        scratch_shapes=[
            pltpu.VMEM((videos, ranks, model_width), jnp.bfloat16),
            pltpu.VMEM((videos, ranks, up_width), jnp.bfloat16),
            pltpu.SemaphoreType.DMA((2 * videos,)),
        ],
        compiler_params=pltpu.CompilerParams(vmem_limit_bytes=12 << 20),
        cost_estimate=pl.CostEstimate(
            flops=0,
            bytes_accessed=4 * videos * ranks * (model_width + up_width),
            transcendentals=0,
        ),
        name="pick_factors",
    )(me, adapter_store_row, requests, adapter_down_factors, adapter_up_factors)
    down_pieces, up_pieces = pieces[: bits - 1], pieces[bits - 1 :]

    down_got, up_got = [], []

    def send_up(i, *others):
        up_got.append(swap(after(halving(up_pieces, up_got, i), *others), 1 << i))

    for i in range(bits - 2):
        piece = down_pieces[0] if i == 0 else halving(down_pieces, down_got, i)
        if i > 0:
            part = up_pieces[0] if i == 1 else halving(up_pieces, up_got, i - 1)
            up_got.append(swap(after(part, piece), 1 << (i - 1)))
        down_got.append(swap(piece, 1 << i))
    part = after(halving(up_pieces, up_got, bits - 3), piece)
    up_got.append(swap(part, 1 << (bits - 3)))
    held = splitting((after(down_pieces[-1], *up_got[:-1]),), down_got)
    shard = after(total(held[0], to_others(held)), keys, up_got[-1])
    gathered = [shard] + [swap(shard, k) for k in others]

    joined = join(gathered)
    asked = jnp.concatenate([by_pairs(values), by_pairs(queries)], axis=1)
    asked = exchange(after(asked, joined))
    up_part = after(up_pieces[-1], joined)
    near_pair, far_pair = on_vmem(
        functools.partial(sum_kernel, [[(n, 2 * h) for n in range(1 + len(up_got))] for h in (0, 1)]),
        [(2,) + up_part.shape[1:]] * 2,
        "split",
        up_part,
        *up_got,
    )
    came = swap(far_pair, quarter)
    for i in reversed(range(bits - 2)):
        gathered = [joined, swap(joined, 1 << i)]
        if i > 0:
            joined = after(join(gathered), came)

    low_shape = (videos, toks // 2, 2 * ranks)
    low = pl.pallas_call(
        functools.partial(low_rank_kernel, shape),
        in_specs=[SMEM, VMEM] + [VMEM] * len(gathered),
        out_specs=VMEM,
        scratch_shapes=[pltpu.VMEM((videos, ranks, model_width), jnp.bfloat16)],
        out_shape=jax.ShapeDtypeStruct(low_shape, jnp.bfloat16),
        compiler_params=pltpu.CompilerParams(vmem_limit_bytes=12 << 20),
        cost_estimate=pl.CostEstimate(
            flops=2 * videos * toks * ranks * model_width,
            bytes_accessed=2 * videos * (toks + ranks) * model_width,
            transcendentals=0,
        ),
        name="low_rank",
    )(me, normed_token_features, *gathered)
    one_shape = (1,) + up_part.shape[1:]
    kept, sent = on_vmem(
        functools.partial(sum_kernel, [[(n, h) for n in range(2)] for h in (0, 1)]),
        [one_shape] * 2,
        "split",
        near_pair,
        came,
    )
    last = swap(sent, 2 * quarter)
    up_here = on_vmem(
        functools.partial(sum_kernel, [[(0, 0), (1, 0)]]), [one_shape], "total", kept, last
    )[0].reshape(pairs, ranks, LANES)
    nearby = [low] + [swap(low, k) for k in range(1, LOW)]
    chosen = pl.pallas_call(
        functools.partial(choose_kernel, per_video),
        in_specs=[SMEM] + [VMEM] * LOW,
        out_specs=[VMEM] * quarter,
        out_shape=[jax.ShapeDtypeStruct((LOW,) + low_shape[1:], jnp.bfloat16)] * quarter,
        compiler_params=pltpu.CompilerParams(vmem_limit_bytes=8 << 20),
        cost_estimate=pl.CostEstimate(flops=0, bytes_accessed=8 * low.size, transcendentals=0),
        name="choose",
    )(me, *nearby)
    lows = [chosen[0]] + [swap(chosen[i], LOW * i) for i in range(1, quarter)]

    part_spec = pl.BlockSpec((devs, pl.squeezed, toks, width), lambda p: (0, p, 0, 0))
    later_spec = pl.BlockSpec((devs, pl.squeezed, toks, width), lambda p: (0, pairs + p, 0, 0))
    low_spec = pl.BlockSpec((LOW,) + low_shape[1:], lambda p: (0, 0, 0))
    mixed = pl.pallas_call(
        functools.partial(attend_kernel, math.gcd(devs, max(1, 256 // toks))),
        grid=(pairs,),
        in_specs=[SMEM, pl.BlockSpec((pl.squeezed, ranks, LANES), lambda p: (p, 0, 0))]
        + [later_spec, part_spec, part_spec]
        + [low_spec] * quarter,
        out_specs=part_spec,
        out_shape=jax.ShapeDtypeStruct((devs, pairs, toks, width), jnp.bfloat16),
        scratch_shapes=[
            pltpu.VMEM((devs,) + low_shape[1:], jnp.bfloat16),
            pltpu.VMEM((length, width), jnp.bfloat16),
        ],
        compiler_params=pltpu.CompilerParams(vmem_limit_bytes=40 << 20),
        cost_estimate=pl.CostEstimate(
            flops=4 * pairs * length * length * width,
            bytes_accessed=8 * pairs * length * width,
            transcendentals=pairs * length * length,
        ),
        name="attend",
    )(me, up_here, asked, keys, asked, *lows)
    return exchange(mixed).reshape(videos, heads, toks, width)


def solution(mesh):
    in_specs = (
        P("grp", "seq", None),
        P("grp", None, "seq", None),
        P("grp", None, "seq", None),
        P("grp", None, "seq", None),
        P("seq", None, None),
        P("seq", None, None),
        P(),
        P("grp"),
    )
    out_specs = P("grp", None, "seq", None)
    return jax.shard_map(body, mesh=mesh, in_specs=in_specs, out_specs=out_specs, check_vma=False)
```
